32 devices in a mesh: rep: 4 (over y, x), fsdp: 8 (over z, core).
Axes of the slice: x: 2, y: 2, z: 4, core: 2. Of those that a mesh axis runs over, the one named last changes fastest.
Arguments:
- tokens: bfloat16 [32768, 768], P(('rep', 'fsdp')), may hold values from -6 to 6
- lengths: int32 [4, 8], P('rep'), may hold values from 1 to 7680, 8192 in all within a row
- qkv_weight: float32 [768, 2304], P('fsdp'), may hold values from -0.21875 to 0.21875
- out_weight: float32 [768, 768], P('fsdp'), may hold values from -6 to 6
- gate_weight: float32 [768, 3072], P('fsdp'), may hold values from -0.21875 to 0.21875
- up_weight: float32 [768, 3072], P('fsdp'), may hold values from -0.21875 to 0.21875
- down_weight: float32 [3072, 768], P('fsdp'), may hold values from -0.109375 to 0.109375
- norm1_gain: float32 [768], P('fsdp'), may hold values from 0.5 to 1.5
- norm1_bias: float32 [768], P('fsdp'), may hold values from -3 to 3
- norm2_gain: float32 [768], P('fsdp'), may hold values from 0.5 to 1.5
- norm2_bias: float32 [768], P('fsdp'), may hold values from -3 to 3
- cotangent: bfloat16 [32768, 768], P(('rep', 'fsdp')), may hold values from -6 to 6
Outputs:
- layer_out: bfloat16 [32768, 768], P(('rep', 'fsdp'))
- grad_tokens: float32 [32768, 768], P(('rep', 'fsdp'))
- grad_qkv_weight: float32 [768, 2304], P('fsdp')
- grad_out_weight: float32 [768, 768], P('fsdp')
- grad_gate_weight: float32 [768, 3072], P('fsdp')
- grad_up_weight: float32 [768, 3072], P('fsdp')
- grad_down_weight: float32 [3072, 768], P('fsdp')
- grad_norm1_gain: float32 [768], P('fsdp')
- grad_norm1_bias: float32 [768], P('fsdp')
- grad_norm2_gain: float32 [768], P('fsdp')
- grad_norm2_bias: float32 [768], P('fsdp')
The draws below stay inside these ranges and needn't reach their ends.
Inputs may be any that keep to these rules, and one draw needn't show every extreme that they name: Each row lists the lengths of 8 documents that fill one sequence in order; they sum to the sequence's tokens, and the longest covers all but 1024 // 2 of them.
All inputs are finite; a program needn't handle non-finite values.
Results may differ from the reference program's by a relative error of at most 0.018.
The reference program's roundings to bfloat16 on the way count: a program that leaves them out, or rounds other values in their place, can miss the bound.
Values may be sent and summed in bfloat16 or wider, within the bound.
No kernel may reach another device: no remote copies, remote signals or barrier semaphores. Data moves between devices by JAX's collectives and lax.ppermute only.
A program may use at most 320 MiB of HBM per device.

```python
import math
import jax
import jax.numpy as jnp
import numpy as np
from jax import lax

D = 768
HEADS = 12
FF = 3072
TOK_DEV = 1024
WINDOW = 1024
DOCS = 8
HEAD_DIM = 64
SEQ_LEN = 8192
SEQS = 4
TOKENS = 32768
N_FSDP = 8


def block_scale(key, dims, cuts, smallest, high):
    loudness, own = 1.0, jax.random.fold_in(key, 6)
    for axis_at, parts in cuts:
        draws = jnp.exp(jax.random.uniform(jax.random.fold_in(own, axis_at), (parts,), jnp.float32, smallest / len(cuts), high / len(cuts)))
        loudness = loudness * jnp.repeat(draws, dims[axis_at] // parts).reshape([-1 if axis == axis_at else 1 for axis in range(len(dims))])
    return loudness


def profile(amount, total, most, skew):
    weights = [(1 << 20) // math.isqrt(rank ** skew) + 1 for rank in range(2, amount + 1)]
    surplus, given = total - most - (amount - 1), [1] * (amount - 1)
    while surplus > 0:
        movable = [i for i in range(amount - 1) if given[i] < most]
        pool, remaining = sum([weights[i] for i in movable]), surplus
        for i in movable:
            more = min(most - given[i], max(1, remaining * weights[i] // pool), surplus)
            given[i] = given[i] + more
            surplus = surplus - more
    return np.array([most] + given)


def uneven_parts(own_key, count, total, bound, skew):
    if count == 2:
        one = jax.random.randint(own_key, (), max(1, total - bound), min(bound, total - 1) + 1)
        return jnp.stack([one, total - one])
    sizes = jnp.asarray(profile(count, total, bound, skew), jnp.int32)
    pairs = (count - 1) // 2
    giver, receiver = sizes[1:1 + 2 * pairs:2], sizes[2:2 + 2 * pairs:2]
    slack = jnp.minimum(giver - 1, bound - receiver)
    shifted = jax.random.randint(jax.random.fold_in(own_key, 1), (pairs,), 0, 1 << 20) % (slack + 1)
    sizes = sizes.at[1:1 + 2 * pairs:2].set(giver - shifted).at[2:2 + 2 * pairs:2].set(receiver + shifted)
    return sizes[jax.random.permutation(jax.random.fold_in(own_key, 2), count)]


def normal_values(rng, dims, width, most, shards=(), held_as=jnp.bfloat16):
    entries = jax.random.normal(rng, dims, jnp.float32) * width
    if len(shards) > 0:
        entries = block_scale(rng, dims, shards, -0.22, 0.18) * entries
    return jnp.clip(entries, min=-most, max=most).astype(held_as)


def setup_inputs(seed: int = 0) -> dict:
    streams_of = jax.random.split(jax.random.key(seed), 13)
    return {
        "tokens": normal_values(streams_of[0], (TOKENS, D), 1.0, 6.0, ((0, 32),)),
        "lengths": jax.vmap(lambda own: uneven_parts(own, DOCS, TOK_DEV * N_FSDP, TOK_DEV * N_FSDP - TOK_DEV // 2, 2))(jax.random.split(streams_of[1], SEQS)).reshape((SEQS, DOCS)).astype(jnp.int32),
        "qkv_weight": normal_values(streams_of[2], (D, 3 * D), D ** -0.5, 0.21875, ((0, 8),), jnp.float32),
        "out_weight": normal_values(streams_of[3], (D, D), (max(1, D // WINDOW)) ** -0.5, 6.0, ((0, 8),), jnp.float32),
        "gate_weight": normal_values(streams_of[4], (D, FF), D ** -0.5, 0.21875, ((0, 8),), jnp.float32),
        "up_weight": normal_values(streams_of[5], (D, FF), D ** -0.5, 0.21875, ((0, 8),), jnp.float32),
        "down_weight": normal_values(streams_of[6], (FF, D), FF ** -0.5, 0.109375, ((0, 8),), jnp.float32),
        "norm1_gain": jnp.clip(1.0 + 0.1 * jax.random.normal(streams_of[7], (D,), jnp.float32), 0.5, 1.5),
        "norm1_bias": normal_values(streams_of[8], (D,), 0.5, 3.0, ((0, 8),), jnp.float32),
        "norm2_gain": jnp.clip(1.0 + 0.1 * jax.random.normal(streams_of[9], (D,), jnp.float32), 0.5, 1.5),
        "norm2_bias": normal_values(streams_of[10], (D,), 0.5, 3.0, ((0, 8),), jnp.float32),
        "cotangent": normal_values(streams_of[11], (TOKENS, D), 1.0, 6.0, ((0, 32),)),
    }


@jax.custom_vjp
def low(v):
    return lax.optimization_barrier(v.astype(jnp.bfloat16)).astype(jnp.float32)

@jax.custom_vjp
def low_back(v):
    return v

def low_keep(v):
    return (low(v), None)

def low_pass(kept, grad):
    return (grad,)

def back_keep(v):
    return (v, None)

def back_low(kept, grad):
    return (low(grad),)
low.defvjp(low_keep, low_pass)
low_back.defvjp(back_keep, back_low)
epsilon = 1e-06
rope_base = 1000.0
masked_score = -1e+30
highest = lax.Precision.HIGHEST

def layout(doc_lengths, index):
    ends = jnp.cumsum(doc_lengths).astype(jnp.int32)
    after = (index[:, None] >= ends[None, :]).astype(jnp.int32)
    documents = lax.optimization_barrier(jnp.sum(after, axis=1)).astype(jnp.int32)
    starts = lax.optimization_barrier(jnp.sum(after * doc_lengths[None, :], axis=1)).astype(jnp.int32)
    return (documents, (index - starts).astype(jnp.int32))

def rotate(values, position):
    count = values.shape[0]
    half = HEAD_DIM // 2
    frequency = rope_base ** (-2.0 * jnp.arange(half, dtype=jnp.float32) / HEAD_DIM)
    angle = position.astype(jnp.float32)[:, None] * frequency[None, :]
    cosine = jnp.cos(angle)[:, None, :]
    sine = jnp.sin(angle)[:, None, :]
    split = values.reshape(count, HEADS, HEAD_DIM)
    first = split[..., :half]
    second = split[..., half:]
    turned = jnp.concatenate([first * cosine - second * sine, second * cosine + first * sine], axis=-1)
    return turned.reshape(count, D)

def normalize(summed, gain, shift):
    centred = summed - lax.optimization_barrier(jnp.mean(summed, axis=-1, keepdims=True))
    inverse = lax.rsqrt(lax.optimization_barrier(jnp.mean(centred * centred, axis=-1, keepdims=True)) + epsilon)
    return centred * inverse * gain + shift

def attend(queries, keys, values, documents):
    reach = WINDOW // 2
    block = min(512, TOK_DEV)
    span = block + 2 * reach
    scale = 1.0 / math.sqrt(HEAD_DIM)
    key_pad = jnp.pad(keys, ((reach, reach), (0, 0)))
    value_pad = jnp.pad(values, ((reach, reach), (0, 0)))
    doc_pad = jnp.pad(documents, (reach, reach), constant_values=-1)

    def one_block(number):
        start = number * block
        query_rows = lax.dynamic_slice_in_dim(queries, start, block, 0).reshape(block, HEADS, HEAD_DIM)
        key_rows = lax.dynamic_slice_in_dim(key_pad, start, span, 0).reshape(span, HEADS, HEAD_DIM)
        value_rows = lax.dynamic_slice_in_dim(value_pad, start, span, 0).reshape(span, HEADS, HEAD_DIM)
        query_docs = lax.dynamic_slice_in_dim(documents, start, block, 0)
        key_docs = lax.dynamic_slice_in_dim(doc_pad, start, span, 0)
        distance = jnp.arange(block, dtype=jnp.int32)[:, None] + reach - jnp.arange(span, dtype=jnp.int32)[None, :]
        near = (query_docs[:, None] == key_docs[None, :]) & (jnp.abs(distance) <= reach)
        scores = low_back(jnp.einsum('qhd,khd->hqk', query_rows, key_rows, precision=highest) * scale)
        scores = jnp.where(near[None], scores, masked_score)
        peak = lax.optimization_barrier(jnp.max(scores, axis=-1, keepdims=True))
        raised = jnp.exp(scores - peak)
        weights = raised / lax.optimization_barrier(jnp.sum(raised, axis=-1, keepdims=True))
        mixed = jnp.einsum('hqk,khd->qhd', low(weights), value_rows, precision=highest)
        return mixed.reshape(block, D)
    blocks = lax.map(jax.checkpoint(one_block), jnp.arange(SEQ_LEN // block, dtype=jnp.int32))
    return blocks.reshape(SEQ_LEN, D)

def layer(inputs, qkv_weight, out_weight, gate_weight, up_weight, down_weight, norm1_gain, norm1_bias, norm2_gain, norm2_bias, doc_lengths):
    index = jnp.arange(SEQ_LEN, dtype=jnp.int32)
    documents, position = layout(doc_lengths, index)
    joint = low_back(jnp.dot(inputs, low(qkv_weight), precision=highest))
    queries = low(rotate(joint[:, :D], position))
    keys = low(rotate(joint[:, D:2 * D], position))
    values = low(joint[:, 2 * D:])
    attended = low(low_back(attend(queries, keys, values, documents)))
    branch = low_back(jnp.dot(attended, low(out_weight), precision=highest))
    hidden = normalize(inputs + branch, low(norm1_gain), low(norm1_bias))
    hidden_low = low(hidden)
    gate = low_back(jnp.dot(hidden_low, low(gate_weight), precision=highest))
    lift = low_back(jnp.dot(hidden_low, low(up_weight), precision=highest))
    product = low(gate * jax.nn.sigmoid(gate) * lift)
    feed = low_back(jnp.dot(product, low(down_weight), precision=highest))
    return normalize(hidden + feed, low(norm2_gain), low(norm2_bias))

def reference(tokens, lengths, qkv_weight, out_weight, gate_weight, up_weight, down_weight, norm1_gain, norm1_bias, norm2_gain, norm2_bias, cotangent):
    params = (qkv_weight, out_weight, gate_weight, up_weight, down_weight, norm1_gain, norm1_bias, norm2_gain, norm2_bias)
    inputs = tokens.astype(jnp.float32).reshape(SEQS, SEQ_LEN, D)
    grads_in = cotangent.astype(jnp.float32).reshape(SEQS, SEQ_LEN, D)
    zero = tuple((jnp.zeros(p.shape, jnp.float32) for p in params))

    def one_sequence(total, item):
        sequence, grad_seq, doc_lengths = item

        def forward(source, *weights):
            return layer(source, *weights, doc_lengths)
        output, pull = jax.vjp(forward, sequence, *params)
        grads = pull(grad_seq)
        total = tuple((t + g for t, g in zip(total, grads[1:])))
        return (total, (output.astype(jnp.bfloat16), grads[0]))
    total, (outputs, grad_inputs) = lax.scan(one_sequence, zero, (inputs, grads_in, lengths))
    return (outputs.reshape(TOKENS, D), grad_inputs.reshape(TOKENS, D), total[0], total[1], total[2], total[3], total[4], total[5], total[6], total[7], total[8])
```

```python
import functools
import math

import jax
import jax.numpy as jnp
from jax import lax
from jax.experimental import pallas as pl
from jax.experimental.pallas import tpu as pltpu
from jax.sharding import PartitionSpec as P

HEADS = 12
WINDOW = 1024
REACH = WINDOW // 2
HEAD = 64
PAIR = 2 * HEAD
QUERY_BLOCK = 256
TOKEN_BLOCK = 256
VMEM = 56 * 1024 * 1024

epsilon = 1e-06
rope_base = 1000.0
masked_score = -1e30
low = jnp.bfloat16
full = jnp.float32


def dot_nn(a, b):
    return lax.dot_general(a, b, (((1,), (0,)), ((), ())), preferred_element_type=full)


def dot_nt(a, b):
    return lax.dot_general(a, b, (((1,), (1,)), ((), ())), preferred_element_type=full)


def dot_tn(a, b):
    return lax.dot_general(a, b, (((0,), (0,)), ((), ())), preferred_element_type=full)


def params():
    return pltpu.CompilerParams(vmem_limit_bytes=VMEM)


def shape(dims, dtype):
    return jax.ShapeDtypeStruct(dims, dtype)


def tables(position):
    lane = jnp.arange(PAIR, dtype=jnp.int32) % HEAD
    half = HEAD // 2
    frequency = rope_base ** (-2.0 * (lane % half).astype(full) / HEAD)
    angle = position.astype(full)[:, None] * frequency[None, :]
    sign = jnp.where(lane < half, -1.0, 1.0).astype(full)
    return jnp.cos(angle), jnp.sin(angle) * sign[None, :]


def partner(x):
    half = HEAD // 2
    lane = lax.broadcasted_iota(jnp.int32, x.shape, 1) % HEAD
    return jnp.where(lane < half, pltpu.roll(x, PAIR - half, 1), pltpu.roll(x, half, 1))


def turn(x, cosine, sine):
    return x * cosine + partner(x) * sine


def turn_back(x, cosine, sine):
    return x * cosine - partner(x) * sine


def project_kernel(plan, sources, first, count, ids, tok_ref, cos_ref, sin_ref, *refs):
    srcs = refs[:sources]
    q_ref, k_ref, v_ref, weight, sems = refs[sources:]
    step = pl.program_id(0)
    copies = plan(ids, srcs, weight, sems)

    @pl.when(step == 0)
    def _():
        for copy in copies:
            copy.start()
        for copy in copies:
            copy.wait()

    width = tok_ref.shape[1]
    rows = tok_ref[...]
    cosine = cos_ref[...]
    sine = sin_ref[...]
    keys = dot_nn(rows, weight[1])
    for at in range(0, width, PAIR):
        k_ref[:, at : at + PAIR] = turn(keys[:, at : at + PAIR], cosine, sine).astype(low)
    v_ref[...] = dot_nn(rows, weight[2]).astype(low)

    @pl.when((step >= first) & (step < first + count))
    def _():
        queries = dot_nn(rows, weight[0])
        for at in range(0, width, PAIR):
            turned = turn(queries[:, at : at + PAIR], cosine, sine).astype(low)
            q_ref[:, at : at + PAIR] = (turned.astype(full) * (1.0 / math.sqrt(HEAD))).astype(low)


def project(plan, ids, tokens, cosine, sine, sources, rows):
    ext, width = tokens.shape
    block = TOKEN_BLOCK
    first, count = (ext - rows) // 2 // block, rows // block
    tile = lambda w: pl.BlockSpec((block, w), lambda i, *_: (i, 0))
    inner = pl.BlockSpec((block, width), lambda i, *_: (jnp.clip(i - first, 0, count - 1), 0))
    return pl.pallas_call(
        functools.partial(project_kernel, plan, len(sources), first, count),
        grid_spec=pltpu.PrefetchScalarGridSpec(
            num_scalar_prefetch=1,
            grid=(ext // block,),
            in_specs=[tile(width), tile(PAIR), tile(PAIR)]
            + [pl.BlockSpec(memory_space=pl.ANY)] * len(sources),
            out_specs=[inner, tile(width), tile(width)],
            scratch_shapes=[
                pltpu.VMEM((3, width, width), low),
                pltpu.SemaphoreType.DMA((1,)),
            ],
        ),
        out_shape=[shape((rows, width), low), shape((ext, width), low), shape((ext, width), low)],
        compiler_params=params(),
        cost_estimate=pl.CostEstimate(
            flops=2 * width * width * (2 * ext + rows),
            bytes_accessed=12 * ext * width,
            transcendentals=0,
        ),
        name="project",
    )(ids, tokens, cosine, sine, *sources)


def fill_bias(bounds_ref, bias_ref, blocks, span):
    for b in range(blocks):
        lo = bounds_ref[0:1, b * QUERY_BLOCK : (b + 1) * QUERY_BLOCK] - b * QUERY_BLOCK
        hi = bounds_ref[1:2, b * QUERY_BLOCK : (b + 1) * QUERY_BLOCK] - b * QUERY_BLOCK
        at = lax.broadcasted_iota(jnp.int32, (span, QUERY_BLOCK), 0)
        bias_ref[b] = jnp.where((at >= lo) & (at < hi), 0.0, masked_score)


def only(x, head):
    lane = lax.broadcasted_iota(jnp.int32, x.shape, 1)
    return jnp.where((lane >= HEAD) if head else (lane < HEAD), x, jnp.zeros_like(x))


def attend_kernel(chunk, bounds_ref, q_ref, k_ref, v_ref, o_ref, lse_ref, bias_ref, vt_ref, s_ref):
    rows = q_ref.shape[0]
    block = QUERY_BLOCK
    blocks = rows // block
    span = k_ref.shape[0] - rows + block

    @pl.when(pl.program_id(0) == 0)
    def _():
        fill_bias(bounds_ref, bias_ref, blocks, span)

    vt_ref[...] = v_ref[...].T
    chunks = [(c, min(chunk, span - c)) for c in range(0, span, chunk)]
    for b in range(blocks):
        out = []
        for h in range(2):
            query = only(q_ref[b * block : (b + 1) * block, :], h)
            slot = s_ref.at[(2 * b + h) % 2]
            top = None
            for c, n in chunks:
                s = dot_nt(k_ref[b * block + c : b * block + c + n, :], query)
                s = s + bias_ref[b, c : c + n, :]
                slot[c : c + n, :] = s
                t = jnp.max(s.reshape(n // 8, 8, block), axis=0)
                top = t if top is None else jnp.maximum(top, t)
            peak = jnp.max(top, axis=0, keepdims=True)
            total = None
            mixed = None
            for c, n in chunks:
                e = jnp.exp(slot[c : c + n, :] - peak)
                t = jnp.sum(e.reshape(n // 8, 8, block), axis=0)
                total = t if total is None else total + t
                o = dot_nn(
                    vt_ref[h * HEAD : (h + 1) * HEAD, b * block + c : b * block + c + n],
                    e.astype(low),
                )
                mixed = o if mixed is None else mixed + o
            total = jnp.sum(total, axis=0, keepdims=True)
            out.append(mixed / total)
            lse_ref[0, h : h + 1, b * block : (b + 1) * block] = peak + jnp.log(total)
        o_ref[b * block : (b + 1) * block, :] = jnp.concatenate(out, axis=0).T.astype(low)


def attend(bounds, q, k, v, chunk=640):
    rows, width = q.shape
    ext = k.shape[0]
    pairs = width // PAIR
    blocks = rows // QUERY_BLOCK
    span = ext - rows + QUERY_BLOCK
    own = pl.BlockSpec((rows, PAIR), lambda p: (0, p))
    wide = pl.BlockSpec((ext, PAIR), lambda p: (0, p))
    return pl.pallas_call(
        functools.partial(attend_kernel, chunk),
        grid=(pairs,),
        in_specs=[pl.BlockSpec((2, rows), lambda p: (0, 0)), own, wide, wide],
        out_specs=[own, pl.BlockSpec((1, 2, rows), lambda p: (p, 0, 0))],
        out_shape=[shape((rows, width), low), shape((pairs, 2, rows), full)],
        scratch_shapes=[
            pltpu.VMEM((blocks, span, QUERY_BLOCK), full),
            pltpu.VMEM((PAIR, ext), low),
            pltpu.VMEM((2, span, QUERY_BLOCK), full),
        ],
        compiler_params=params(),
        cost_estimate=pl.CostEstimate(
            flops=16 * rows * span * width,
            bytes_accessed=4 * ext * width,
            transcendentals=rows * span * width // HEAD,
        ),
        name="attend",
    )(bounds, q, k, v)


def attend_back_kernel(
    chunk,
    bounds_ref,
    q_ref,
    k_ref,
    v_ref,
    o_ref,
    do_ref,
    lse_ref,
    dq_ref,
    own_ref,
    prior_ref,
    next_ref,
    bias_ref,
    kt_ref,
    dk_ref,
    dv_ref,
):
    rows = q_ref.shape[0]
    ext = k_ref.shape[0]
    block = QUERY_BLOCK
    blocks = rows // block
    reach = (ext - rows) // 2
    span = ext - rows + block

    @pl.when(pl.program_id(0) == 0)
    def _():
        fill_bias(bounds_ref, bias_ref, blocks, span)

    kt_ref[...] = k_ref[...].T
    dk_ref[...] = jnp.zeros_like(dk_ref)
    dv_ref[...] = jnp.zeros_like(dv_ref)
    chunks = [(c, min(chunk, span - c)) for c in range(0, span, chunk)]
    for b in range(blocks):
        at = slice(b * block, (b + 1) * block)
        q = q_ref[at, :]
        do = do_ref[at, :]
        product = (do.astype(full) * o_ref[at, :].astype(full)).T
        query = [only(q, h) for h in range(2)]
        grad = [only(do, h) for h in range(2)]
        delta = [
            jnp.sum(product[h * HEAD : (h + 1) * HEAD], axis=0, keepdims=True) for h in range(2)
        ]
        lse = [lse_ref[0, h : h + 1, at] for h in range(2)]
        dq = [None, None]
        queries = jnp.concatenate(query, axis=0)
        grads = jnp.concatenate(grad, axis=0)
        for c, n in chunks:
            lo = b * block + c
            keys = k_ref[lo : lo + n, :]
            values = v_ref[lo : lo + n, :]
            chances = []
            grad_scores = []
            for h in range(2):
                s = dot_nt(keys, query[h]) + bias_ref[b, c : c + n, :]
                p = jnp.exp(s - lse[h])
                dp = dot_nt(values, grad[h])
                ds = (p * (dp - delta[h])).astype(low)
                chances.append(p.astype(low))
                grad_scores.append(ds)
                t = dot_nn(kt_ref[h * HEAD : (h + 1) * HEAD, lo : lo + n], ds)
                dq[h] = t if dq[h] is None else dq[h] + t
            dv_ref[lo : lo + n, :] += dot_nn(jnp.concatenate(chances, axis=1), grads)
            dk_ref[lo : lo + n, :] += dot_nn(jnp.concatenate(grad_scores, axis=1), queries)
        dq_ref[at, :] = jnp.concatenate(dq, axis=0).T * (1.0 / math.sqrt(HEAD))
    for i, ref in enumerate((dk_ref, dv_ref)):
        prior_ref[i] = ref[:reach, :].astype(low)
        own_ref[i] = ref[reach : reach + rows, :]
        next_ref[i] = ref[reach + rows :, :].astype(low)


def attend_back(bounds, q, k, v, o, do, lse, chunk=1280):
    rows, width = q.shape
    ext = k.shape[0]
    pairs = width // PAIR
    blocks = rows // QUERY_BLOCK
    reach = (ext - rows) // 2
    span = ext - rows + QUERY_BLOCK
    own = pl.BlockSpec((rows, PAIR), lambda p: (0, p))
    wide = pl.BlockSpec((ext, PAIR), lambda p: (0, p))
    both = lambda n: pl.BlockSpec((2, n, PAIR), lambda p: (0, 0, p))
    return pl.pallas_call(
        functools.partial(attend_back_kernel, chunk),
        grid=(pairs,),
        in_specs=[
            pl.BlockSpec((2, rows), lambda p: (0, 0)),
            own,
            wide,
            wide,
            own,
            own,
            pl.BlockSpec((1, 2, rows), lambda p: (p, 0, 0)),
        ],
        out_specs=[own, both(rows), both(reach), both(reach)],
        out_shape=[
            shape((rows, width), full),
            shape((2, rows, width), full),
            shape((2, reach, width), low),
            shape((2, reach, width), low),
        ],
        scratch_shapes=[
            pltpu.VMEM((blocks, span, QUERY_BLOCK), full),
            pltpu.VMEM((PAIR, ext), low),
            pltpu.VMEM((ext, PAIR), full),
            pltpu.VMEM((ext, PAIR), full),
        ],
        compiler_params=params(),
        cost_estimate=pl.CostEstimate(
            flops=40 * rows * span * width,
            bytes_accessed=20 * rows * width,
            transcendentals=rows * span * width // HEAD,
        ),
        name="attend_back",
    )(bounds, q, k, v, o, do, lse)


def mean(x):
    return jnp.mean(x, axis=-1, keepdims=True)


def norm(x):
    centred = x - mean(x)
    inverse = lax.rsqrt(mean(centred * centred) + epsilon)
    return centred * inverse, inverse


def norm_back(scaled, normed, inverse):
    return inverse * (scaled - mean(scaled) - normed * mean(scaled * normed))


def middle_kernel(plan, sources, ids, at_ref, tok_ref, cot_ref, vec_ref, *refs):
    srcs = refs[:sources]
    (
        out_ref,
        dz1_ref,
        da_ref,
        hidden_ref,
        product_ref,
        dfeed_ref,
        dgate_ref,
        dlift_ref,
        dbranch_ref,
        gains_ref,
        out_w,
        gate_w,
        up_w,
        down_w,
        lift_factor,
        gate_factor,
        sems,
    ) = refs[sources:]
    step = pl.program_id(0)
    copies = plan(ids, srcs, (out_w, gate_w, up_w, down_w), sems)

    @pl.when(step == 0)
    def _():
        for group in copies:
            for copy in group:
                copy.start()
        gains_ref[...] = jnp.zeros_like(gains_ref)

    def ready(*groups):
        @pl.when(step == 0)
        def _():
            for group in groups:
                for copy in copies[group]:
                    copy.wait()

    parts, _, width = gate_w.shape
    gain1, bias1, gain2, bias2 = (vec_ref[i : i + 1] for i in range(4))
    ready(0)
    normed1, inverse1 = norm(tok_ref[...].astype(full) + dot_nn(at_ref[...], out_w[...]))
    hidden = normed1 * gain1 + bias1
    hidden_low = hidden.astype(low)
    hidden_ref[...] = hidden_low
    ready(1, 2, 3)
    feed = None
    for part in range(parts):
        at = slice(part * width, (part + 1) * width)
        gate = dot_nn(hidden_low, gate_w[part])
        lift = dot_nn(hidden_low, up_w[part])
        sigma = jax.nn.sigmoid(gate)
        opened = gate * sigma
        product = (opened * lift).astype(low)
        product_ref[:, at] = product
        lift_factor[:, at] = opened
        gate_factor[:, at] = lift * sigma * (1.0 + gate * (1.0 - sigma))
        term = dot_nn(product, down_w[at, :])
        feed = term if feed is None else feed + term
    normed2, inverse2 = norm(hidden + feed)
    out_ref[...] = (normed2 * gain2 + bias2).astype(low)
    cot = cot_ref[...].astype(full)
    gains_ref[2:3] += jnp.sum(cot * normed2, axis=0, keepdims=True)
    gains_ref[3:4] += jnp.sum(cot, axis=0, keepdims=True)
    grad = norm_back(cot * gain2, normed2, inverse2)
    dfeed = grad.astype(low)
    dfeed_ref[...] = dfeed
    for part in range(parts):
        at = slice(part * width, (part + 1) * width)
        dproduct = dot_nt(dfeed, down_w[at, :])
        dgate = (dproduct * gate_factor[:, at]).astype(low)
        dlift = (dproduct * lift_factor[:, at]).astype(low)
        dgate_ref[:, at] = dgate
        dlift_ref[:, at] = dlift
        grad = grad + dot_nt(dgate, gate_w[part]) + dot_nt(dlift, up_w[part])
    gains_ref[0:1] += jnp.sum(grad * normed1, axis=0, keepdims=True)
    gains_ref[1:2] += jnp.sum(grad, axis=0, keepdims=True)
    grad = norm_back(grad * gain1, normed1, inverse1)
    dz1_ref[...] = grad
    dbranch = grad.astype(low)
    dbranch_ref[...] = dbranch
    da_ref[...] = dot_nt(dbranch, out_w[...]).astype(low)


def middle(plan, ids, attended, tokens, cot, vectors, sources, hidden):
    rows, width = tokens.shape
    block = TOKEN_BLOCK
    tile = lambda w: pl.BlockSpec((block, w), lambda i, *_: (i, 0))
    whole = pl.BlockSpec((8, width), lambda i, *_: (0, 0))
    return pl.pallas_call(
        functools.partial(middle_kernel, plan, len(sources)),
        grid_spec=pltpu.PrefetchScalarGridSpec(
            num_scalar_prefetch=1,
            grid=(rows // block,),
            in_specs=[tile(width), tile(width), tile(width), whole]
            + [pl.BlockSpec(memory_space=pl.ANY)] * len(sources),
            out_specs=[
                tile(width),
                tile(width),
                tile(width),
                tile(width),
                tile(hidden),
                tile(width),
                tile(hidden),
                tile(hidden),
                tile(width),
                whole,
            ],
            scratch_shapes=[
                pltpu.VMEM((width, width), low),
                pltpu.VMEM((hidden // width, width, width), low),
                pltpu.VMEM((hidden // width, width, width), low),
                pltpu.VMEM((hidden, width), low),
                pltpu.VMEM((block, hidden), full),
                pltpu.VMEM((block, hidden), full),
                pltpu.SemaphoreType.DMA((4,)),
            ],
        ),
        out_shape=[
            shape((rows, width), low),
            shape((rows, width), full),
            shape((rows, width), low),
            shape((rows, width), low),
            shape((rows, hidden), low),
            shape((rows, width), low),
            shape((rows, hidden), low),
            shape((rows, hidden), low),
            shape((rows, width), low),
            shape((8, width), full),
        ],
        compiler_params=params(),
        cost_estimate=pl.CostEstimate(
            flops=2 * rows * width * (2 * width + 6 * hidden),
            bytes_accessed=40 << 20,
            transcendentals=rows * hidden,
        ),
        name="middle",
    )(ids, attended, tokens, cot, vectors, *sources)


def weight_grad_kernel(a_ref, b_ref, o_ref):
    o_ref[...] = dot_tn(a_ref[...], b_ref[...]).astype(o_ref.dtype)


def weight_grad(a, b, tile_a=768, tile_b=768):
    rows, size_a = a.shape
    size_b = b.shape[1]
    return pl.pallas_call(
        weight_grad_kernel,
        grid=(size_a // tile_a, size_b // tile_b),
        in_specs=[
            pl.BlockSpec((rows, tile_a), lambda i, j: (0, i)),
            pl.BlockSpec((rows, tile_b), lambda i, j: (0, j)),
        ],
        out_specs=pl.BlockSpec((tile_a, tile_b), lambda i, j: (i, j)),
        out_shape=shape((size_a, size_b), low),
        compiler_params=params(),
        cost_estimate=pl.CostEstimate(
            flops=2 * rows * size_a * size_b,
            bytes_accessed=2 * (rows * (size_a + size_b) + size_a * size_b),
            transcendentals=0,
        ),
        name="weight_grad",
    )(a, b)


def joint_kernel(reach, dq_ref, own_ref, prior_ref, next_ref, cos_ref, sin_ref, dj_ref):
    block, width = dq_ref.shape
    step = pl.program_id(0)
    early = step < pl.num_programs(0) // 2
    cosine = cos_ref[...]
    sine = sin_ref[...]
    for at in range(0, width, PAIR):
        lanes = slice(at, at + PAIR)
        near = [
            jnp.where(early, prior_ref[i, :, lanes], next_ref[i, :, lanes]).astype(full)
            for i in range(2)
        ]
        dj_ref[:, lanes] = turn_back(dq_ref[:, lanes], cosine, sine).astype(low)
        dj_ref[:, width + at : width + at + PAIR] = turn_back(
            own_ref[0, :, lanes] + near[0], cosine, sine
        ).astype(low)
        dj_ref[:, 2 * width + at : 2 * width + at + PAIR] = (
            own_ref[1, :, lanes] + near[1]
        ).astype(low)


def joint(dq, own, prior, following, cosine, sine):
    rows, width = dq.shape
    reach = prior.shape[1]
    block = TOKEN_BLOCK
    half = reach // block
    tile = lambda w: pl.BlockSpec((block, w), lambda i: (i, 0))
    inner = pl.BlockSpec((block, PAIR), lambda i: (i + half, 0))
    return pl.pallas_call(
        functools.partial(joint_kernel, reach),
        grid=(rows // block,),
        in_specs=[
            tile(width),
            pl.BlockSpec((2, block, width), lambda i: (0, i, 0)),
            pl.BlockSpec((2, block, width), lambda i: (0, jnp.minimum(i, half - 1), 0)),
            pl.BlockSpec((2, block, width), lambda i: (0, jnp.maximum(i - half, 0), 0)),
            inner,
            inner,
        ],
        out_specs=tile(3 * width),
        out_shape=shape((rows, 3 * width), low),
        compiler_params=params(),
        cost_estimate=pl.CostEstimate(
            flops=12 * rows * width, bytes_accessed=24 * rows * width, transcendentals=0
        ),
        name="joint",
    )(dq, own, prior, following, cosine, sine)


def input_grad_kernel(plan, sources, ids, dj_ref, dz1_ref, *refs):
    srcs = refs[:sources]
    out_ref, weight, sems = refs[sources:]
    copies = plan(ids, srcs, weight, sems)

    @pl.when(pl.program_id(0) == 0)
    def _():
        for copy in copies:
            copy.start()
        for copy in copies:
            copy.wait()

    width = dz1_ref.shape[1]
    out = dz1_ref[...]
    for i in range(3):
        out = out + dot_nt(dj_ref[:, i * width : (i + 1) * width], weight[i])
    out_ref[...] = out


def input_grad(plan, ids, dj, dz1, sources):
    rows, width = dz1.shape
    block = TOKEN_BLOCK
    tile = lambda w: pl.BlockSpec((block, w), lambda i, *_: (i, 0))
    return pl.pallas_call(
        functools.partial(input_grad_kernel, plan, len(sources)),
        grid_spec=pltpu.PrefetchScalarGridSpec(
            num_scalar_prefetch=1,
            grid=(rows // block,),
            in_specs=[tile(3 * width), tile(width)]
            + [pl.BlockSpec(memory_space=pl.ANY)] * len(sources),
            out_specs=tile(width),
            scratch_shapes=[
                pltpu.VMEM((3, width, width), low),
                pltpu.SemaphoreType.DMA((1,)),
            ],
        ),
        out_shape=shape((rows, width), full),
        compiler_params=params(),
        cost_estimate=pl.CostEstimate(
            flops=6 * rows * width * width, bytes_accessed=14 * rows * width, transcendentals=0
        ),
        name="input_grad",
    )(ids, dj, dz1, *sources)


def whole_joint_plan(ids, srcs, weight, sems):
    width = weight.shape[1]
    return [
        pltpu.make_async_copy(srcs[0].at[:, i * width : (i + 1) * width], weight.at[i], sems.at[0])
        for i in range(3)
    ]


def whole_middle_plan(ids, srcs, weights, sems):
    out_w, gate_w, up_w, down_w = weights
    parts, _, width = gate_w.shape
    columns = lambda src, dst, sem: [
        pltpu.make_async_copy(src.at[:, i * width : (i + 1) * width], dst.at[i], sem)
        for i in range(parts)
    ]
    return [
        [pltpu.make_async_copy(srcs[0], out_w, sems.at[0])],
        columns(srcs[1], gate_w, sems.at[1]),
        columns(srcs[2], up_w, sems.at[2]),
        [pltpu.make_async_copy(srcs[3], down_w, sems.at[3])],
    ]


def shards(
    tokens,
    lengths,
    qkv_weight,
    out_weight,
    gate_weight,
    up_weight,
    down_weight,
    norm1_gain,
    norm1_bias,
    norm2_gain,
    norm2_bias,
    cotangent,
):
    rows, width = tokens.shape
    hidden = gate_weight.shape[1]
    size = lax.axis_size("fsdp")
    me = lax.axis_index("fsdp")
    up = [(i, i + 1) for i in range(size - 1)]
    down = [(i + 1, i) for i in range(size - 1)]
    tokens_ext = jnp.concatenate(
        [
            lax.ppermute(tokens[rows - REACH :], "fsdp", up),
            tokens,
            lax.ppermute(tokens[:REACH], "fsdp", down),
        ],
        axis=0,
    )

    doc_lengths = lengths[0]
    ends = jnp.cumsum(doc_lengths)
    index = me * rows - REACH + jnp.arange(rows + 2 * REACH, dtype=jnp.int32)
    after = (index[:, None] >= ends[None, :]).astype(jnp.int32)
    starts = jnp.sum(after * doc_lengths[None, :], axis=1)
    cosine, sine = tables(index - starts)
    own_starts = starts[REACH : REACH + rows]
    own_index = index[REACH : REACH + rows]
    stops = jnp.min(
        jnp.where(ends[None, :] > own_index[:, None], ends[None, :], size * rows), axis=1
    )
    base = me * rows - REACH
    bounds = jnp.stack(
        [
            jnp.maximum(own_starts, own_index - REACH) - base,
            jnp.minimum(stops, own_index + REACH + 1) - base,
        ]
    ).astype(jnp.int32)

    ids = jnp.zeros((8,), jnp.int32)
    gather = lambda w: lax.all_gather(w.astype(low), "fsdp", axis=0, tiled=True)
    qkv_full = gather(qkv_weight)
    weights = [gather(w) for w in (out_weight, gate_weight, up_weight, down_weight)]
    vectors = jnp.stack([norm1_gain, norm1_bias, norm2_gain, norm2_bias])
    vectors = lax.all_gather(vectors.astype(low), "fsdp", axis=1, tiled=True).astype(full)
    vectors = jnp.concatenate([vectors, vectors], axis=0)

    queries, keys, values = project(
        whole_joint_plan, ids, tokens_ext, cosine, sine, [qkv_full], rows
    )
    attended, lse = attend(bounds, queries, keys, values)
    result, dz1, dattended, hidden_low, product, dfeed, dgate, dlift, dbranch, gains = middle(
        whole_middle_plan, ids, attended, tokens, cotangent, vectors, weights, hidden
    )
    spread = lambda g: lax.psum_scatter(g, "fsdp", scatter_dimension=0, tiled=True)
    share_down = spread(weight_grad(product, dfeed))
    share_gate = spread(weight_grad(hidden_low, dgate))
    share_up = spread(weight_grad(hidden_low, dlift))
    share_out = spread(weight_grad(attended, dbranch))
    share_gains = lax.psum_scatter(gains[:4], "fsdp", scatter_dimension=1, tiled=True)

    dq, dkv, to_prior, to_next = attend_back(
        bounds, queries, keys, values, attended, dattended, lse
    )
    from_prior = lax.ppermute(to_next, "fsdp", up)
    from_next = lax.ppermute(to_prior, "fsdp", down)
    djoint = joint(dq, dkv, from_prior, from_next, cosine, sine)
    share_qkv = spread(weight_grad(tokens, djoint))
    grad_tokens = input_grad(whole_joint_plan, ids, djoint, dz1, [qkv_full])
    summed = lax.psum(
        tuple(
            s.astype(full)
            for s in (share_qkv, share_out, share_gate, share_up, share_down, share_gains)
        ),
        "rep",
    )
    return (result, grad_tokens, *summed[:5], *(summed[5][i] for i in range(4)))


def solution(mesh):
    rows = P(("rep", "fsdp"), None)
    matrix = P("fsdp", None)
    vector = P("fsdp")
    return jax.shard_map(
        shards,
        mesh=mesh,
        in_specs=(rows, P("rep", None)) + (matrix,) * 5 + (vector,) * 4 + (rows,),
        out_specs=(rows, rows) + (matrix,) * 5 + (vector,) * 4,
        check_vma=False,
    )
```

```python
import functools
import math

import jax
import jax.numpy as jnp
from jax import lax
from jax.experimental import pallas as pl
from jax.experimental.pallas import tpu as pltpu
from jax.sharding import PartitionSpec as P

HEADS = 12
WINDOW = 1024
REACH = WINDOW // 2
HEAD = 64
PAIR = 2 * HEAD
QUERY_BLOCK = 256
TOKEN_BLOCK = 256
FORCE_WHOLE = False
VMEM = 56 * 1024 * 1024

epsilon = 1e-06
rope_base = 1000.0
masked_score = -1e30
low = jnp.bfloat16
full = jnp.float32


def dot_nn(a, b):
    return lax.dot_general(a, b, (((1,), (0,)), ((), ())), preferred_element_type=full)


def dot_nt(a, b):
    return lax.dot_general(a, b, (((1,), (1,)), ((), ())), preferred_element_type=full)


def dot_tn(a, b):
    return lax.dot_general(a, b, (((0,), (0,)), ((), ())), preferred_element_type=full)


def params():
    return pltpu.CompilerParams(vmem_limit_bytes=VMEM)


def shape(dims, dtype):
    return jax.ShapeDtypeStruct(dims, dtype)


def cost(micros):
    return pl.CostEstimate(flops=int(micros * 1.15e9), bytes_accessed=1 << 20, transcendentals=0)


def tables(position):
    lane = jnp.arange(PAIR, dtype=jnp.int32) % HEAD
    half = HEAD // 2
    frequency = rope_base ** (-2.0 * (lane % half).astype(full) / HEAD)
    angle = position.astype(full)[:, None] * frequency[None, :]
    sign = jnp.where(lane < half, -1.0, 1.0).astype(full)
    return jnp.cos(angle), jnp.sin(angle) * sign[None, :]


def partner(x):
    half = HEAD // 2
    lane = lax.broadcasted_iota(jnp.int32, x.shape, 1) % HEAD
    return jnp.where(lane < half, pltpu.roll(x, PAIR - half, 1), pltpu.roll(x, half, 1))


def turn(x, cosine, sine):
    return x * cosine + partner(x) * sine


def turn_back(x, cosine, sine):
    return x * cosine - partner(x) * sine


def project_kernel(plan, sources, first, count, ids, tok_ref, cos_ref, sin_ref, *refs):
    srcs = refs[:sources]
    q_ref, k_ref, v_ref, weight, sems = refs[sources:]
    step = pl.program_id(0)

    @pl.when(step == 0)
    def _():
        for copy in plan(ids, srcs, weight, sems.at[0]):
            copy.start()
        pltpu.make_async_copy(weight, weight, sems.at[0]).wait()

    width = tok_ref.shape[1]
    rows = tok_ref[...]
    cosine = cos_ref[...]
    sine = sin_ref[...]
    keys = dot_nn(rows, weight[1])
    for at in range(0, width, PAIR):
        k_ref[:, at : at + PAIR] = turn(keys[:, at : at + PAIR], cosine, sine).astype(low)
    v_ref[...] = dot_nn(rows, weight[2]).astype(low)

    @pl.when((step >= first) & (step < first + count))
    def _():
        queries = dot_nn(rows, weight[0])
        for at in range(0, width, PAIR):
            turned = turn(queries[:, at : at + PAIR], cosine, sine).astype(low)
            q_ref[:, at : at + PAIR] = (turned.astype(full) * (1.0 / math.sqrt(HEAD))).astype(low)


def project(plan, ids, tokens, cosine, sine, sources, rows):
    ext, width = tokens.shape
    block = TOKEN_BLOCK
    first, count = (ext - rows) // 2 // block, rows // block
    tile = lambda w: pl.BlockSpec((block, w), lambda i, *_: (i, 0))
    inner = pl.BlockSpec((block, width), lambda i, *_: (jnp.clip(i - first, 0, count - 1), 0))
    return pl.pallas_call(
        functools.partial(project_kernel, plan, len(sources), first, count),
        grid_spec=pltpu.PrefetchScalarGridSpec(
            num_scalar_prefetch=1,
            grid=(ext // block,),
            in_specs=[tile(width), tile(PAIR), tile(PAIR)]
            + [pl.BlockSpec(memory_space=pl.ANY)] * len(sources),
            out_specs=[
                inner,
                tile(width),
                tile(width),
                pl.BlockSpec((4, width, width), lambda i, *_: (0, 0, 0)),
            ],
            scratch_shapes=[pltpu.SemaphoreType.DMA((1,))],
        ),
        out_shape=[
            shape((rows, width), low),
            shape((ext, width), low),
            shape((ext, width), low),
            shape((4, width, width), low),
        ],
        compiler_params=params(),
        cost_estimate=cost(15),
        name="project",
    )(ids, tokens, cosine, sine, *sources)


def fill_bias(bounds_ref, bias_ref, blocks, span):
    for b in range(blocks):
        lo = bounds_ref[0:1, b * QUERY_BLOCK : (b + 1) * QUERY_BLOCK] - b * QUERY_BLOCK
        hi = bounds_ref[1:2, b * QUERY_BLOCK : (b + 1) * QUERY_BLOCK] - b * QUERY_BLOCK
        at = lax.broadcasted_iota(jnp.int32, (span, QUERY_BLOCK), 0)
        bias_ref[b] = jnp.where((at >= lo) & (at < hi), 0.0, masked_score)


def only(x, head):
    lane = lax.broadcasted_iota(jnp.int32, x.shape, 1)
    return jnp.where((lane >= HEAD) if head else (lane < HEAD), x, jnp.zeros_like(x))


def attend_kernel(chunk, bounds_ref, q_ref, k_ref, v_ref, *refs):
    o_ref, lse_ref, bias_ref, vt_ref, s_ref = refs[-5:]
    rows = q_ref.shape[0]
    block = QUERY_BLOCK
    blocks = rows // block
    span = k_ref.shape[0] - rows + block

    @pl.when(pl.program_id(0) == 0)
    def _():
        fill_bias(bounds_ref, bias_ref, blocks, span)

    vt_ref[...] = v_ref[...].T
    chunks = [(c, min(chunk, span - c)) for c in range(0, span, chunk)]
    for b in range(blocks):
        out = []
        for h in range(2):
            query = only(q_ref[b * block : (b + 1) * block, :], h)
            slot = s_ref.at[(2 * b + h) % 2]
            top = None
            for c, n in chunks:
                s = dot_nt(k_ref[b * block + c : b * block + c + n, :], query)
                s = s + bias_ref[b, c : c + n, :]
                slot[c : c + n, :] = s
                t = jnp.max(s.reshape(n // 8, 8, block), axis=0)
                top = t if top is None else jnp.maximum(top, t)
            peak = jnp.max(top, axis=0, keepdims=True)
            total = None
            mixed = None
            for c, n in chunks:
                e = jnp.exp(slot[c : c + n, :] - peak)
                t = jnp.sum(e.reshape(n // 8, 8, block), axis=0)
                total = t if total is None else total + t
                o = dot_nn(
                    vt_ref[h * HEAD : (h + 1) * HEAD, b * block + c : b * block + c + n],
                    e.astype(low),
                )
                mixed = o if mixed is None else mixed + o
            total = jnp.sum(total, axis=0, keepdims=True)
            out.append(mixed / total)
            lse_ref[0, h : h + 1, b * block : (b + 1) * block] = peak + jnp.log(total)
        o_ref[b * block : (b + 1) * block, :] = jnp.concatenate(out, axis=0).T.astype(low)


def attend(bounds, q, k, v, first, pairs, before=None, chunk=640):
    rows, width = q.shape
    ext = k.shape[0]
    blocks = rows // QUERY_BLOCK
    span = ext - rows + QUERY_BLOCK
    own = pl.BlockSpec((rows, PAIR), lambda p: (0, p + first))
    wide = pl.BlockSpec((ext, PAIR), lambda p: (0, p + first))
    before = () if before is None else tuple(before)
    return pl.pallas_call(
        functools.partial(attend_kernel, chunk),
        grid=(pairs,),
        in_specs=[pl.BlockSpec((2, rows), lambda p: (0, 0)), own, wide, wide]
        + [pl.BlockSpec(memory_space=pl.ANY)] * len(before),
        out_specs=[own, pl.BlockSpec((1, 2, rows), lambda p: (p + first, 0, 0))],
        out_shape=[shape((rows, width), low), shape((width // PAIR, 2, rows), full)],
        input_output_aliases={4 + i: i for i in range(len(before))},
        scratch_shapes=[
            pltpu.VMEM((blocks, span, QUERY_BLOCK), full),
            pltpu.VMEM((PAIR, ext), low),
            pltpu.VMEM((2, span, QUERY_BLOCK), full),
        ],
        compiler_params=params(),
        cost_estimate=cost(6 * pairs),
        name="attend",
    )(bounds, q, k, v, *before)


def attend_back_kernel(
    chunk,
    bounds_ref,
    q_ref,
    k_ref,
    v_ref,
    o_ref,
    do_ref,
    lse_ref,
    *refs,
):
    dq_ref, own_ref, prior_ref, next_ref, bias_ref, kt_ref, dk_ref, dv_ref = refs[-8:]
    rows = q_ref.shape[0]
    ext = k_ref.shape[0]
    block = QUERY_BLOCK
    blocks = rows // block
    reach = (ext - rows) // 2
    span = ext - rows + block

    @pl.when(pl.program_id(0) == 0)
    def _():
        fill_bias(bounds_ref, bias_ref, blocks, span)

    kt_ref[...] = k_ref[...].T
    dk_ref[...] = jnp.zeros_like(dk_ref)
    dv_ref[...] = jnp.zeros_like(dv_ref)
    chunks = [(c, min(chunk, span - c)) for c in range(0, span, chunk)]
    for b in range(blocks):
        at = slice(b * block, (b + 1) * block)
        q = q_ref[at, :]
        do = do_ref[at, :]
        product = (do.astype(full) * o_ref[at, :].astype(full)).T
        query = [only(q, h) for h in range(2)]
        grad = [only(do, h) for h in range(2)]
        delta = [
            jnp.sum(product[h * HEAD : (h + 1) * HEAD], axis=0, keepdims=True) for h in range(2)
        ]
        lse = [lse_ref[0, h : h + 1, at] for h in range(2)]
        dq = [None, None]
        queries = jnp.concatenate(query, axis=0)
        grads = jnp.concatenate(grad, axis=0)
        for c, n in chunks:
            lo = b * block + c
            keys = k_ref[lo : lo + n, :]
            values = v_ref[lo : lo + n, :]
            chances = []
            grad_scores = []
            for h in range(2):
                s = dot_nt(keys, query[h]) + bias_ref[b, c : c + n, :]
                p = jnp.exp(s - lse[h])
                dp = dot_nt(values, grad[h])
                ds = (p * (dp - delta[h])).astype(low)
                chances.append(p.astype(low))
                grad_scores.append(ds)
                t = dot_nn(kt_ref[h * HEAD : (h + 1) * HEAD, lo : lo + n], ds)
                dq[h] = t if dq[h] is None else dq[h] + t
            dv_ref[lo : lo + n, :] += dot_nn(jnp.concatenate(chances, axis=1), grads)
            dk_ref[lo : lo + n, :] += dot_nn(jnp.concatenate(grad_scores, axis=1), queries)
        dq_ref[at, :] = jnp.concatenate(dq, axis=0).T * (1.0 / math.sqrt(HEAD))
    for i, ref in enumerate((dk_ref, dv_ref)):
        prior_ref[i] = ref[:reach, :].astype(low)
        own_ref[i] = ref[reach : reach + rows, :]
        next_ref[i] = ref[reach + rows :, :].astype(low)


def attend_back(bounds, q, k, v, o, do, lse, first, pairs, halo, before=None, chunk=1280):
    rows, width = q.shape
    ext = k.shape[0]
    blocks = rows // QUERY_BLOCK
    reach = (ext - rows) // 2
    span = ext - rows + QUERY_BLOCK
    halo_first, halo_pairs = halo
    before = () if before is None else tuple(before)
    own = pl.BlockSpec((rows, PAIR), lambda p: (0, p + first))
    wide = pl.BlockSpec((ext, PAIR), lambda p: (0, p + first))
    edge = pl.BlockSpec((2, reach, PAIR), lambda p: (0, 0, p + first - halo_first))
    return pl.pallas_call(
        functools.partial(attend_back_kernel, chunk),
        grid=(pairs,),
        in_specs=[
            pl.BlockSpec((2, rows), lambda p: (0, 0)),
            own,
            wide,
            wide,
            own,
            own,
            pl.BlockSpec((1, 2, rows), lambda p: (p + first, 0, 0)),
        ]
        + [pl.BlockSpec(memory_space=pl.ANY)] * len(before),
        out_specs=[
            own,
            pl.BlockSpec((2, rows, PAIR), lambda p: (0, 0, p + first)),
            edge,
            edge,
        ],
        out_shape=[
            shape((rows, width), full),
            shape((2, rows, width), full),
            shape((2, reach, halo_pairs * PAIR), low),
            shape((2, reach, halo_pairs * PAIR), low),
        ],
        input_output_aliases={7 + i: i for i in range(len(before))},
        scratch_shapes=[
            pltpu.VMEM((blocks, span, QUERY_BLOCK), full),
            pltpu.VMEM((PAIR, ext), low),
            pltpu.VMEM((ext, PAIR), full),
            pltpu.VMEM((ext, PAIR), full),
        ],
        compiler_params=params(),
        cost_estimate=cost(8 * pairs),
        name="attend_back",
    )(bounds, q, k, v, o, do, lse, *before)


def mean(x):
    return jnp.mean(x, axis=-1, keepdims=True)


def norm(x):
    centred = x - mean(x)
    inverse = lax.rsqrt(mean(centred * centred) + epsilon)
    return centred * inverse, inverse


def norm_back(scaled, normed, inverse):
    return inverse * (scaled - mean(scaled) - normed * mean(scaled * normed))


def middle_kernel(plan, sources, ids, at_ref, tok_ref, cot_ref, vec_ref, *refs):
    srcs = refs[:sources]
    (
        out_ref,
        dz1_ref,
        da_ref,
        hidden_ref,
        product_ref,
        dfeed_ref,
        dgate_ref,
        dlift_ref,
        dbranch_ref,
        gains_ref,
        out_w,
        gate_w,
        up_w,
        down_w,
        lift_factor,
        gate_factor,
        sems,
    ) = refs[sources:]
    step = pl.program_id(0)
    weights = (out_w, gate_w, up_w, down_w)

    @pl.when(step == 0)
    def _():
        for copy in plan(ids, srcs, weights, sems):
            copy.start()
        gains_ref[...] = jnp.zeros_like(gains_ref)

    def ready(*which):
        @pl.when(step == 0)
        def _():
            for i in which:
                pltpu.make_async_copy(weights[i], weights[i], sems.at[i]).wait()

    parts, _, width = gate_w.shape
    gain1, bias1, gain2, bias2 = (vec_ref[i : i + 1] for i in range(4))
    ready(0)
    normed1, inverse1 = norm(tok_ref[...].astype(full) + dot_nn(at_ref[...], out_w[...]))
    hidden = normed1 * gain1 + bias1
    hidden_low = hidden.astype(low)
    hidden_ref[...] = hidden_low
    ready(1, 2, 3)
    feed = None
    for part in range(parts):
        at = slice(part * width, (part + 1) * width)
        gate = dot_nn(hidden_low, gate_w[part])
        lift = dot_nn(hidden_low, up_w[part])
        sigma = jax.nn.sigmoid(gate)
        opened = gate * sigma
        product = (opened * lift).astype(low)
        product_ref[:, at] = product
        lift_factor[:, at] = opened
        gate_factor[:, at] = lift * sigma * (1.0 + gate * (1.0 - sigma))
        term = dot_nn(product, down_w[at, :])
        feed = term if feed is None else feed + term
    normed2, inverse2 = norm(hidden + feed)
    out_ref[...] = (normed2 * gain2 + bias2).astype(low)
    cot = cot_ref[...].astype(full)
    gains_ref[2:3] += jnp.sum(cot * normed2, axis=0, keepdims=True)
    gains_ref[3:4] += jnp.sum(cot, axis=0, keepdims=True)
    grad = norm_back(cot * gain2, normed2, inverse2)
    dfeed = grad.astype(low)
    dfeed_ref[...] = dfeed
    for part in range(parts):
        at = slice(part * width, (part + 1) * width)
        dproduct = dot_nt(dfeed, down_w[at, :])
        dgate = (dproduct * gate_factor[:, at]).astype(low)
        dlift = (dproduct * lift_factor[:, at]).astype(low)
        dgate_ref[:, at] = dgate
        dlift_ref[:, at] = dlift
        grad = grad + dot_nt(dgate, gate_w[part]) + dot_nt(dlift, up_w[part])
    gains_ref[0:1] += jnp.sum(grad * normed1, axis=0, keepdims=True)
    gains_ref[1:2] += jnp.sum(grad, axis=0, keepdims=True)
    grad = norm_back(grad * gain1, normed1, inverse1)
    dz1_ref[...] = grad
    dbranch = grad.astype(low)
    dbranch_ref[...] = dbranch
    da_ref[...] = dot_nt(dbranch, out_w[...]).astype(low)


def middle(plan, ids, attended, tokens, cot, vectors, sources, hidden):
    rows, width = tokens.shape
    block = TOKEN_BLOCK
    tile = lambda w: pl.BlockSpec((block, w), lambda i, *_: (i, 0))
    whole = pl.BlockSpec((8, width), lambda i, *_: (0, 0))
    return pl.pallas_call(
        functools.partial(middle_kernel, plan, len(sources)),
        grid_spec=pltpu.PrefetchScalarGridSpec(
            num_scalar_prefetch=1,
            grid=(rows // block,),
            in_specs=[tile(width), tile(width), tile(width), whole]
            + [pl.BlockSpec(memory_space=pl.ANY)] * len(sources),
            out_specs=[
                tile(width),
                tile(width),
                tile(width),
                tile(width),
                tile(hidden),
                tile(width),
                tile(hidden),
                tile(hidden),
                tile(width),
                whole,
            ],
            scratch_shapes=[
                pltpu.VMEM((width, width), low),
                pltpu.VMEM((hidden // width, width, width), low),
                pltpu.VMEM((hidden // width, width, width), low),
                pltpu.VMEM((hidden, width), low),
                pltpu.VMEM((block, hidden), full),
                pltpu.VMEM((block, hidden), full),
                pltpu.SemaphoreType.DMA((4,)),
            ],
        ),
        out_shape=[
            shape((rows, width), low),
            shape((rows, width), full),
            shape((rows, width), low),
            shape((rows, width), low),
            shape((rows, hidden), low),
            shape((rows, width), low),
            shape((rows, hidden), low),
            shape((rows, hidden), low),
            shape((rows, width), low),
            shape((8, width), full),
        ],
        compiler_params=params(),
        cost_estimate=cost(53),
        name="middle",
    )(ids, attended, tokens, cot, vectors, *sources)


def weight_grad_kernel(a_ref, b_ref, o_ref):
    o_ref[...] = dot_tn(a_ref[...], b_ref[...]).astype(o_ref.dtype)


def weight_grad(a, b, tile_a=768, tile_b=768):
    rows, size_a = a.shape
    size_b = b.shape[1]
    return pl.pallas_call(
        weight_grad_kernel,
        grid=(size_a // tile_a, size_b // tile_b),
        in_specs=[
            pl.BlockSpec((rows, tile_a), lambda i, j: (0, i)),
            pl.BlockSpec((rows, tile_b), lambda i, j: (0, j)),
        ],
        out_specs=pl.BlockSpec((tile_a, tile_b), lambda i, j: (i, j)),
        out_shape=shape((size_a, size_b), low),
        compiler_params=params(),
        cost_estimate=cost(9),
        name="weight_grad",
    )(a, b)


def joint_kernel(halos, dq_ref, own_ref, *refs):
    priors = refs[:halos]
    nexts = refs[halos : 2 * halos]
    cos_ref, sin_ref, dj_ref = refs[2 * halos :]
    block, width = dq_ref.shape
    early = pl.program_id(0) < pl.num_programs(0) // 2
    cosine = cos_ref[...]
    sine = sin_ref[...]
    start = 0
    for prior_ref, next_ref in zip(priors, nexts):
        for at in range(0, prior_ref.shape[2], PAIR):
            near = [
                jnp.where(
                    early, prior_ref[i, :, at : at + PAIR], next_ref[i, :, at : at + PAIR]
                ).astype(full)
                for i in range(2)
            ]
            lanes = slice(start + at, start + at + PAIR)
            keys = turn_back(own_ref[0, :, lanes] + near[0], cosine, sine)
            dj_ref[0, :, lanes] = turn_back(dq_ref[:, lanes], cosine, sine).astype(low)
            dj_ref[1, :, lanes] = keys.astype(low)
            dj_ref[2, :, lanes] = (own_ref[1, :, lanes] + near[1]).astype(low)
        start += prior_ref.shape[2]


def joint(dq, own, priors, nexts, cosine, sine):
    rows, width = dq.shape
    block = TOKEN_BLOCK
    half = priors[0].shape[1] // block
    inner = pl.BlockSpec((block, PAIR), lambda i: (i + half, 0))
    edges = [
        pl.BlockSpec((2, block, p.shape[2]), lambda i: (0, jnp.minimum(i, half - 1), 0))
        for p in priors
    ] + [
        pl.BlockSpec((2, block, p.shape[2]), lambda i: (0, jnp.maximum(i - half, 0), 0))
        for p in nexts
    ]
    return pl.pallas_call(
        functools.partial(joint_kernel, len(priors)),
        grid=(rows // block,),
        in_specs=[
            pl.BlockSpec((block, width), lambda i: (i, 0)),
            pl.BlockSpec((2, block, width), lambda i: (0, i, 0)),
        ]
        + edges
        + [inner, inner],
        out_specs=pl.BlockSpec((3, block, width), lambda i: (0, i, 0)),
        out_shape=shape((3, rows, width), low),
        compiler_params=params(),
        cost_estimate=cost(9),
        name="joint",
    )(dq, own, *priors, *nexts, cosine, sine)


def input_grad_kernel(dj_ref, dz1_ref, weight_ref, out_ref):
    out = dz1_ref[...]
    for i in range(3):
        out = out + dot_nt(dj_ref[i], weight_ref[i])
    out_ref[...] = out


def input_grad(dj, dz1, weights):
    rows, width = dz1.shape
    block = TOKEN_BLOCK
    tile = pl.BlockSpec((block, width), lambda i: (i, 0))
    return pl.pallas_call(
        input_grad_kernel,
        grid=(rows // block,),
        in_specs=[
            pl.BlockSpec((3, block, width), lambda i: (0, i, 0)),
            tile,
            pl.BlockSpec((3, width, width), lambda i: (0, 0, 0)),
        ],
        out_specs=tile,
        out_shape=shape((rows, width), full),
        compiler_params=params(),
        cost_estimate=cost(10),
        name="input_grad",
    )(dj, dz1, weights)


def whole_joint_plan(ids, srcs, weight, sem):
    width = weight.shape[1]
    return [
        pltpu.make_async_copy(srcs[0].at[:, i * width : (i + 1) * width], weight.at[i], sem)
        for i in range(3)
    ] + [pltpu.make_async_copy(srcs[1], weight.at[3], sem)]


def whole_middle_plan(ids, srcs, weights, sems):
    out_w, gate_w, up_w, down_w = weights
    parts, _, width = gate_w.shape
    columns = lambda src, dst, sem: [
        pltpu.make_async_copy(src.at[:, i * width : (i + 1) * width], dst.at[i], sem)
        for i in range(parts)
    ]
    return (
        [pltpu.make_async_copy(srcs[0].at[3], out_w, sems.at[0])]
        + columns(srcs[1], gate_w, sems.at[1])
        + columns(srcs[2], up_w, sems.at[2])
        + [pltpu.make_async_copy(srcs[3], down_w, sems.at[3])]
    )


def swap_with(value, place):
    pairs = []
    for r in range(4):
        for z in range(4):
            for c in range(2):
                to_r, to_z, to_c = place(r, z, c)
                pairs.append(((r * 4 + z) * 2 + c, (to_r * 4 + to_z) * 2 + to_c))
    return lax.ppermute(value, ("rep", "fsdp"), pairs)


def over_core(value):
    return swap_with(value, lambda r, z, c: (r, z, 1 - c))


def over_z(value, k):
    return swap_with(value, lambda r, z, c: (r, z ^ k, c))


def over_square_1(value):
    return swap_with(value, lambda r, z, c: (r ^ (1 + c), z, c))


def over_square_2(value):
    return swap_with(value, lambda r, z, c: (r ^ (2 - c), z, c))


def pieces(ids, srcs):
    r, z, c = ids[0], ids[1], ids[2]
    found = []
    for core, (shard, near, far) in ((c, srcs[:3]), (1 - c, srcs[3:6])):
        bit1, bit2 = 1 + core, 2 - core
        for quarter in range(4):
            found.append((shard.at[quarter], quarter, z, core))
        for ref, base in ((near, r), (far, r ^ bit2)):
            for j in range(2):
                for k in range(1, 4):
                    found.append((ref.at[j, k - 1], base ^ bit1 if j else base, z ^ k, core))
    return found


def piece_joint_plan(ids, srcs, weight, sem):
    size = srcs[0].shape[1]
    copies = []
    for ref, quarter, z, core in pieces(ids, srcs):
        at = pl.multiple_of((2 * z + core) * size, size)
        copies.append(pltpu.make_async_copy(ref, weight.at[quarter, pl.ds(at, size)], sem))
    return copies


def piece_middle_plan(ids, srcs, weights, sems):
    out_w, gate_w, up_w, down_w = weights
    size = srcs[1].shape[1] // 3
    copies = [pltpu.make_async_copy(srcs[0].at[3], out_w, sems.at[0])]
    found = pieces(ids, srcs[1:])
    for i, target in enumerate((gate_w, up_w)):
        for ref, quarter, z, core in found:
            at = pl.multiple_of((2 * z + core) * size, size)
            copies.append(
                pltpu.make_async_copy(
                    ref.at[i * size : (i + 1) * size],
                    target.at[quarter, pl.ds(at, size)],
                    sems.at[1 + i],
                )
            )
    for ref, quarter, z, core in found:
        at = pl.multiple_of(((2 * z + core) * 4 + quarter) * size, size)
        copies.append(
            pltpu.make_async_copy(
                ref.at[2 * size : 3 * size], down_w.at[pl.ds(at, size)], sems.at[3]
            )
        )
    return copies


def gather_quarters(shard, mine, extra):
    n, width = shard.shape[1:]
    arrived = [over_z(mine, k) for k in (1, 2, 3)]
    mate_shard = over_core(shard)
    own = jnp.stack([a[:n] for a in arrived])
    other = over_square_1(own)
    near = jnp.stack([own, other])
    far = over_square_2(near)
    mate_near = over_core(near)
    mate_far = over_core(far)
    return [shard, near, far, mate_shard, mate_near, mate_far], arrived


def flip(value, axis, bit):
    return jnp.where(bit == 1, jnp.flip(value, axis), value)


def position(j, core):
    return jnp.where(core == 0, j, (j & 1) * 2 + (j >> 1))


def put_pieces(ids, block_ref, own_ref, other_ref, first, size):
    z, c = ids[1], ids[2]
    for ref, core in ((own_ref, c), (other_ref, 1 - c)):
        for k in range(4):
            at = pl.multiple_of((2 * (z ^ k) + core) * size, 8)
            ref[0, k, first : first + size, :] = block_ref[pl.ds(at, size), :].astype(low)


def gate_up_grad_kernel(ids, hidden_ref, dgate_ref, dlift_ref, gains_ref, own_ref, other_ref, block_ref):
    size = block_ref.shape[0] // 8
    z, c = ids[1], ids[2]
    quarter = ids[0] ^ pl.program_id(0)
    for i, ref in enumerate((dgate_ref, dlift_ref)):
        block_ref[...] = dot_tn(hidden_ref[...], ref[...])
        put_pieces(ids, block_ref, own_ref, other_ref, i * size, size)
    for ref, core in ((own_ref, c), (other_ref, 1 - c)):
        for k in range(4):
            ref[0, k, 2 * size :, :] = jnp.zeros((16, ref.shape[3]), low)
            row = gains_ref[quarter * 8 + 2 * (z ^ k) + core]
            ref[0, k, 2 * size :, : row.shape[1]] = row.astype(low)


def grad_specs(size, width):
    own = pl.BlockSpec((1, 4, size, width), lambda j, ids: (position(j, ids[2]), 0, 0, 0))
    other = pl.BlockSpec((1, 4, size, width), lambda j, ids: (position(j, 1 - ids[2]), 0, 0, 0))
    return [own, other], [shape((4, 4, size, width), low)] * 2


def gate_up_grad(ids, hidden_low, dgate, dlift, gains):
    rows, width = hidden_low.shape
    size = width // 8
    out_specs, out_shape = grad_specs(2 * size + 16, width)
    column = pl.BlockSpec((rows, width), lambda j, ids: (0, ids[0] ^ j))
    return pl.pallas_call(
        gate_up_grad_kernel,
        grid_spec=pltpu.PrefetchScalarGridSpec(
            num_scalar_prefetch=1,
            grid=(4,),
            in_specs=[
                pl.BlockSpec((rows, width), lambda j, ids: (0, 0)),
                column,
                column,
                pl.BlockSpec(gains.shape, lambda j, ids: (0, 0, 0)),
            ],
            out_specs=out_specs,
            scratch_shapes=[pltpu.VMEM((width, width), full)],
        ),
        out_shape=out_shape,
        compiler_params=params(),
        cost_estimate=cost(18),
        name="gate_up_grad",
    )(ids, hidden_low, dgate, dlift, gains)


def joint_grad_kernel(ids, tok_ref, dj_ref, at_ref, db_ref, own_ref, other_ref, block_ref):
    size = block_ref.shape[0] // 8
    quarter = ids[0] ^ pl.program_id(0)

    @pl.when(quarter < 3)
    def _():
        block_ref[...] = dot_tn(tok_ref[...], dj_ref[0])

    @pl.when(quarter == 3)
    def _():
        block_ref[...] = dot_tn(at_ref[...], db_ref[...])

    put_pieces(ids, block_ref, own_ref, other_ref, 0, size)


def joint_grad(ids, tokens, djoint, attended, dbranch):
    rows, width = tokens.shape
    size = width // 8
    out_specs, out_shape = grad_specs(size, width)
    whole = pl.BlockSpec((rows, width), lambda j, ids: (0, 0))
    return pl.pallas_call(
        joint_grad_kernel,
        grid_spec=pltpu.PrefetchScalarGridSpec(
            num_scalar_prefetch=1,
            grid=(4,),
            in_specs=[
                whole,
                pl.BlockSpec(
                    (1, rows, width), lambda j, ids: (jnp.minimum(ids[0] ^ j, 2), 0, 0)
                ),
                whole,
                whole,
            ],
            out_specs=out_specs,
            scratch_shapes=[pltpu.VMEM((width, width), full)],
        ),
        out_shape=out_shape,
        compiler_params=params(),
        cost_estimate=cost(9),
        name="joint_grad",
    )(ids, tokens, djoint, attended, dbranch)


def reduce_pieces(own, other, r, c):
    wide = lambda v: v.astype(full)
    a = over_core(other)
    b = over_square_2((wide(own[2:]) + wide(a[2:])).astype(low))
    d = over_square_1((wide(own[1]) + wide(a[1]) + wide(b[1])).astype(low))
    kept = wide(own[0]) + wide(a[0]) + wide(b[0]) + wide(d)
    e = over_z(kept[2:].astype(low), 2)
    f = over_z((kept[1] + wide(e[1])).astype(low), 1)
    mine = (kept[0] + wide(e[0]) + wide(f)).astype(low)
    pair = jnp.stack([mine, over_square_1(mine)])
    four = jnp.stack([pair, over_square_2(pair)])
    four = jnp.where(c == 1, jnp.swapaxes(four, 0, 1), four)
    four = flip(flip(four, 1, r & 1), 0, r >> 1)
    return four.reshape(4, *mine.shape).astype(full)


def shards(
    custom,
    tokens,
    lengths,
    qkv_weight,
    out_weight,
    gate_weight,
    up_weight,
    down_weight,
    norm1_gain,
    norm1_bias,
    norm2_gain,
    norm2_bias,
    cotangent,
):
    rows, width = tokens.shape
    hidden = gate_weight.shape[1]
    size = lax.axis_size("fsdp")
    me = lax.axis_index("fsdp")
    up = [(i, i + 1) for i in range(size - 1)]
    down = [(i + 1, i) for i in range(size - 1)]
    r = lax.axis_index("rep")
    z, c = me // 2, me % 2
    ids = jnp.stack([r, z, c]).astype(jnp.int32)
    vectors = jnp.stack([norm1_gain, norm1_bias, norm2_gain, norm2_bias]).astype(low)

    if custom:
        part = qkv_weight.shape[0]
        columns = lambda w: jnp.swapaxes(w.astype(low).reshape(part, -1, width), 0, 1)
        first_shard = jnp.concatenate([columns(qkv_weight), out_weight.astype(low)[None]])
        mine = lax.dynamic_index_in_dim(first_shard, r, 0, keepdims=False)
        joint_sources, arrived = gather_quarters(first_shard, mine, 0)
        joint_plan = piece_joint_plan
    else:
        gather = lambda w: lax.all_gather(w.astype(low), "fsdp", axis=0, tiled=True)
        joint_sources = [gather(qkv_weight), gather(out_weight)]
        joint_plan = whole_joint_plan

    tokens_ext = jnp.concatenate(
        [
            lax.ppermute(tokens[rows - REACH :], "fsdp", up),
            tokens,
            lax.ppermute(tokens[:REACH], "fsdp", down),
        ],
        axis=0,
    )

    if custom:
        second_shard = jnp.concatenate(
            [
                columns(gate_weight),
                columns(up_weight),
                down_weight.astype(low).reshape(4, part, width),
            ],
            axis=1,
        )
        second_shard = lax.optimization_barrier((second_shard, *arrived))[0]
        rows_of = jnp.pad(vectors, ((0, 12), (0, width - part)))
        mine = jnp.concatenate(
            [lax.dynamic_index_in_dim(second_shard, r, 0, keepdims=False), rows_of]
        )
        middle_sources, arrived = gather_quarters(second_shard, mine, 16)
        found = jnp.stack([rows_of] + [a[3 * part :] for a in arrived])
        found = jnp.stack([found, over_core(found)])[:, :, :4, :part].reshape(2, 2, 2, 4, part)
        found = flip(flip(flip(found, 0, c), 1, z >> 1), 2, z & 1)
        vectors = jnp.transpose(found, (3, 1, 2, 0, 4)).reshape(4, width)
        middle_plan = piece_middle_plan
    else:
        middle_sources = [gather(w) for w in (gate_weight, up_weight, down_weight)]
        vectors = lax.all_gather(vectors, "fsdp", axis=1, tiled=True)
        middle_plan = whole_middle_plan
    vectors = jnp.concatenate([vectors, vectors], axis=0).astype(full)

    doc_lengths = lengths[0]
    ends = jnp.cumsum(doc_lengths)
    index = me * rows - REACH + jnp.arange(rows + 2 * REACH, dtype=jnp.int32)
    after = (index[:, None] >= ends[None, :]).astype(jnp.int32)
    starts = jnp.sum(after * doc_lengths[None, :], axis=1)
    cosine, sine = tables(index - starts)
    own_starts = starts[REACH : REACH + rows]
    own_index = index[REACH : REACH + rows]
    stops = jnp.min(
        jnp.where(ends[None, :] > own_index[:, None], ends[None, :], size * rows), axis=1
    )
    base = me * rows - REACH
    bounds = jnp.stack(
        [
            jnp.maximum(own_starts, own_index - REACH) - base,
            jnp.minimum(stops, own_index + REACH + 1) - base,
        ]
    ).astype(jnp.int32)

    queries, keys, values, joint_weights = project(
        joint_plan, ids, tokens_ext, cosine, sine, joint_sources, rows
    )
    done = None
    for first in (0, 2, 4):
        done = attend(bounds, queries, keys, values, first, 2, done)
    attended, lse = done
    result, dz1, dattended, hidden_low, product, dfeed, dgate, dlift, dbranch, gains = middle(
        middle_plan,
        ids,
        attended,
        tokens,
        cotangent,
        vectors,
        [joint_weights, *middle_sources],
        hidden,
    )
    gains = gains[:4]
    spread = lambda g: lax.psum_scatter(g, "fsdp", scatter_dimension=0, tiled=True)
    share_down = spread(weight_grad(product, dfeed))
    if custom:
        gains = jnp.pad(gains.reshape(32, 1, part), ((0, 0), (0, 15), (0, PAIR - part)))
        gate_up = gate_up_grad(ids, hidden_low, dgate, dlift, gains)
    else:
        share_gate = spread(weight_grad(hidden_low, dgate))
        share_up = spread(weight_grad(hidden_low, dlift))
        share_out = spread(weight_grad(attended, dbranch))
        share_gains = lax.psum_scatter(gains, "fsdp", scatter_dimension=1, tiled=True)

    given = (bounds, queries, keys, values, attended, dattended, lse)
    done = attend_back(*given, 0, 2, (0, 4))
    dq, dkv, to_prior, to_next = attend_back(*given, 2, 2, (0, 4), done)
    from_prior = [lax.ppermute(to_next, "fsdp", up)]
    from_next = [lax.ppermute(to_prior, "fsdp", down)]
    dq, dkv, to_prior, to_next = attend_back(*given, 4, 2, (4, 2), (dq, dkv))
    from_prior.append(lax.ppermute(to_next, "fsdp", up))
    from_next.append(lax.ppermute(to_prior, "fsdp", down))
    djoint = joint(dq, dkv, from_prior, from_next, cosine, sine)
    if custom:
        joint_pieces = joint_grad(ids, tokens, djoint, attended, dbranch)
    else:
        share_qkv = jnp.concatenate([spread(weight_grad(tokens, djoint[i])) for i in range(3)], 1)
    grad_tokens = input_grad(djoint, dz1, joint_weights)

    if custom:
        down_sum = share_down
        for over in (over_square_1, over_square_2):
            down_sum = (down_sum.astype(full) + over(down_sum).astype(full)).astype(low)
        natural = lambda v: jnp.swapaxes(v, 0, 1).reshape(part, -1)
        gate_up = reduce_pieces(*gate_up, r, c)
        joint_sum = reduce_pieces(*joint_pieces, r, c)
        summed = (
            natural(joint_sum[:3]),
            joint_sum[3],
            natural(gate_up[:, :part]),
            natural(gate_up[:, part : 2 * part]),
            down_sum.astype(full),
            gate_up[:, 2 * part, :part],
        )
    else:
        summed = lax.psum(
            tuple(
                s.astype(full)
                for s in (share_qkv, share_out, share_gate, share_up, share_down, share_gains)
            ),
            "rep",
        )
    return (result, grad_tokens, *summed[:5], *(summed[5][i] for i in range(4)))


def solution(mesh):
    rows = P(("rep", "fsdp"), None)
    matrix = P("fsdp", None)
    vector = P("fsdp")
    custom = (mesh.shape["rep"], mesh.shape["fsdp"]) == (4, 8)
    return jax.shard_map(
        functools.partial(shards, custom and not FORCE_WHOLE),
        mesh=mesh,
        in_specs=(rows, P("rep", None)) + (matrix,) * 5 + (vector,) * 4 + (rows,),
        out_specs=(rows, rows) + (matrix,) * 5 + (vector,) * 4,
        check_vma=False,
    )
```

```python
import functools
import math

import jax
import jax.numpy as jnp
from jax import lax
from jax.experimental import pallas as pl
from jax.experimental.pallas import tpu as pltpu
from jax.sharding import PartitionSpec as P

HEADS = 12
WINDOW = 1024
REACH = WINDOW // 2
HEAD = 64
PAIR = 2 * HEAD
QUERY_BLOCK = 256
TOKEN_BLOCK = 256
FORCE_WHOLE = False
VMEM = 56 * 1024 * 1024

epsilon = 1e-06
rope_base = 1000.0
masked_score = -1e30
low = jnp.bfloat16
full = jnp.float32


def dot_nn(a, b):
    return lax.dot_general(a, b, (((1,), (0,)), ((), ())), preferred_element_type=full)


def dot_nt(a, b):
    return lax.dot_general(a, b, (((1,), (1,)), ((), ())), preferred_element_type=full)


def dot_tn(a, b):
    return lax.dot_general(a, b, (((0,), (0,)), ((), ())), preferred_element_type=full)


def params():
    return pltpu.CompilerParams(vmem_limit_bytes=VMEM)


def after(value, *others):
    return lax.optimization_barrier((value, *others))[0]


def shape(dims, dtype):
    return jax.ShapeDtypeStruct(dims, dtype)


def cost(micros):
    return pl.CostEstimate(flops=int(micros * 1.15e9), bytes_accessed=1 << 20, transcendentals=0)


def tables(position):
    lane = jnp.arange(PAIR, dtype=jnp.int32) % HEAD
    half = HEAD // 2
    frequency = rope_base ** (-2.0 * (lane % half).astype(full) / HEAD)
    angle = position.astype(full)[:, None] * frequency[None, :]
    sign = jnp.where(lane < half, -1.0, 1.0).astype(full)
    return jnp.cos(angle), jnp.sin(angle) * sign[None, :]


def partner(x):
    half = HEAD // 2
    lane = lax.broadcasted_iota(jnp.int32, x.shape, 1) % HEAD
    return jnp.where(lane < half, pltpu.roll(x, PAIR - half, 1), pltpu.roll(x, half, 1))


def turn(x, cosine, sine):
    return x * cosine + partner(x) * sine


def turn_back(x, cosine, sine):
    return x * cosine - partner(x) * sine


def project_kernel(plan, sources, first, count, ids, tok_ref, cos_ref, sin_ref, *refs):
    srcs = refs[:sources]
    q_ref, k_ref, v_ref, weight, sems = refs[sources:]
    step = pl.program_id(0)

    @pl.when(step == 0)
    def _():
        for copy in plan(ids, srcs, weight, sems.at[0]):
            copy.start()
        pltpu.make_async_copy(weight, weight, sems.at[0]).wait()

    width = tok_ref.shape[1]
    rows = tok_ref[...]
    cosine = cos_ref[...]
    sine = sin_ref[...]
    keys = dot_nn(rows, weight[1])
    for at in range(0, width, PAIR):
        k_ref[:, at : at + PAIR] = turn(keys[:, at : at + PAIR], cosine, sine).astype(low)
    v_ref[...] = dot_nn(rows, weight[2]).astype(low)

    @pl.when((step >= first) & (step < first + count))
    def _():
        queries = dot_nn(rows, weight[0])
        for at in range(0, width, PAIR):
            turned = turn(queries[:, at : at + PAIR], cosine, sine).astype(low)
            q_ref[:, at : at + PAIR] = (turned.astype(full) * (1.0 / math.sqrt(HEAD))).astype(low)


def project(plan, ids, tokens, cosine, sine, sources, rows):
    ext, width = tokens.shape
    block = TOKEN_BLOCK
    first, count = (ext - rows) // 2 // block, rows // block
    tile = lambda w: pl.BlockSpec((block, w), lambda i, *_: (i, 0))
    inner = pl.BlockSpec((block, width), lambda i, *_: (jnp.clip(i - first, 0, count - 1), 0))
    return pl.pallas_call(
        functools.partial(project_kernel, plan, len(sources), first, count),
        grid_spec=pltpu.PrefetchScalarGridSpec(
            num_scalar_prefetch=1,
            grid=(ext // block,),
            in_specs=[tile(width), tile(PAIR), tile(PAIR)]
            + [pl.BlockSpec(memory_space=pl.ANY)] * len(sources),
            out_specs=[
                inner,
                tile(width),
                tile(width),
                pl.BlockSpec((4, width, width), lambda i, *_: (0, 0, 0)),
            ],
            scratch_shapes=[pltpu.SemaphoreType.DMA((1,))],
        ),
        out_shape=[
            shape((rows, width), low),
            shape((ext, width), low),
            shape((ext, width), low),
            shape((4, width, width), low),
        ],
        compiler_params=params(),
        cost_estimate=cost(15),
        name="project",
    )(ids, tokens, cosine, sine, *sources)


def fill_bias(bounds_ref, bias_ref, blocks, span):
    for b in range(blocks):
        lo = bounds_ref[0:1, b * QUERY_BLOCK : (b + 1) * QUERY_BLOCK] - b * QUERY_BLOCK
        hi = bounds_ref[1:2, b * QUERY_BLOCK : (b + 1) * QUERY_BLOCK] - b * QUERY_BLOCK
        at = lax.broadcasted_iota(jnp.int32, (span, QUERY_BLOCK), 0)
        bias_ref[b] = jnp.where((at >= lo) & (at < hi), 0.0, masked_score)


def only(x, head):
    lane = lax.broadcasted_iota(jnp.int32, x.shape, 1)
    return jnp.where((lane >= HEAD) if head else (lane < HEAD), x, jnp.zeros_like(x))


def attend_kernel(chunk, bounds_ref, q_ref, k_ref, v_ref, *refs):
    o_ref, lse_ref, bias_ref, vt_ref, s_ref = refs[-5:]
    rows = q_ref.shape[0]
    block = QUERY_BLOCK
    blocks = rows // block
    span = k_ref.shape[0] - rows + block

    @pl.when(pl.program_id(0) == 0)
    def _():
        fill_bias(bounds_ref, bias_ref, blocks, span)

    vt_ref[...] = v_ref[...].T
    chunks = [(c, min(chunk, span - c)) for c in range(0, span, chunk)]
    for b in range(blocks):
        out = []
        for h in range(2):
            query = only(q_ref[b * block : (b + 1) * block, :], h)
            slot = s_ref.at[(2 * b + h) % 2]
            top = None
            for c, n in chunks:
                s = dot_nt(k_ref[b * block + c : b * block + c + n, :], query)
                s = s + bias_ref[b, c : c + n, :]
                slot[c : c + n, :] = s
                t = jnp.max(s.reshape(n // 8, 8, block), axis=0)
                top = t if top is None else jnp.maximum(top, t)
            peak = jnp.max(top, axis=0, keepdims=True)
            total = None
            mixed = None
            for c, n in chunks:
                e = jnp.exp(slot[c : c + n, :] - peak)
                t = jnp.sum(e.reshape(n // 8, 8, block), axis=0)
                total = t if total is None else total + t
                o = dot_nn(
                    vt_ref[h * HEAD : (h + 1) * HEAD, b * block + c : b * block + c + n],
                    e.astype(low),
                )
                mixed = o if mixed is None else mixed + o
            total = jnp.sum(total, axis=0, keepdims=True)
            out.append(mixed / total)
            lse_ref[0, h : h + 1, b * block : (b + 1) * block] = peak + jnp.log(total)
        o_ref[b * block : (b + 1) * block, :] = jnp.concatenate(out, axis=0).T.astype(low)


def attend(bounds, q, k, v, first, pairs, before=None, chunk=640):
    rows, width = q.shape
    ext = k.shape[0]
    blocks = rows // QUERY_BLOCK
    span = ext - rows + QUERY_BLOCK
    own = pl.BlockSpec((rows, PAIR), lambda p: (0, p + first))
    wide = pl.BlockSpec((ext, PAIR), lambda p: (0, p + first))
    before = () if before is None else tuple(before)
    return pl.pallas_call(
        functools.partial(attend_kernel, chunk),
        grid=(pairs,),
        in_specs=[pl.BlockSpec((2, rows), lambda p: (0, 0)), own, wide, wide]
        + [pl.BlockSpec(memory_space=pl.ANY)] * len(before),
        out_specs=[own, pl.BlockSpec((1, 2, rows), lambda p: (p + first, 0, 0))],
        out_shape=[shape((rows, width), low), shape((width // PAIR, 2, rows), full)],
        input_output_aliases={4 + i: i for i in range(len(before))},
        scratch_shapes=[
            pltpu.VMEM((blocks, span, QUERY_BLOCK), full),
            pltpu.VMEM((PAIR, ext), low),
            pltpu.VMEM((2, span, QUERY_BLOCK), full),
        ],
        compiler_params=params(),
        cost_estimate=cost(6 * pairs),
        name="attend",
    )(bounds, q, k, v, *before)


def attend_back_kernel(
    chunk,
    bounds_ref,
    q_ref,
    k_ref,
    v_ref,
    o_ref,
    do_ref,
    lse_ref,
    *refs,
):
    dq_ref, own_ref, prior_ref, next_ref, bias_ref, kt_ref, dk_ref, dv_ref = refs[-8:]
    rows = q_ref.shape[0]
    ext = k_ref.shape[0]
    block = QUERY_BLOCK
    blocks = rows // block
    reach = (ext - rows) // 2
    span = ext - rows + block

    @pl.when(pl.program_id(0) == 0)
    def _():
        fill_bias(bounds_ref, bias_ref, blocks, span)

    kt_ref[...] = k_ref[...].T
    dk_ref[...] = jnp.zeros_like(dk_ref)
    dv_ref[...] = jnp.zeros_like(dv_ref)
    chunks = [(c, min(chunk, span - c)) for c in range(0, span, chunk)]
    for b in range(blocks):
        at = slice(b * block, (b + 1) * block)
        q = q_ref[at, :]
        do = do_ref[at, :]
        product = (do.astype(full) * o_ref[at, :].astype(full)).T
        query = [only(q, h) for h in range(2)]
        grad = [only(do, h) for h in range(2)]
        delta = [
            jnp.sum(product[h * HEAD : (h + 1) * HEAD], axis=0, keepdims=True) for h in range(2)
        ]
        lse = [lse_ref[0, h : h + 1, at] for h in range(2)]
        dq = [None, None]
        queries = jnp.concatenate(query, axis=0)
        grads = jnp.concatenate(grad, axis=0)
        for c, n in chunks:
            lo = b * block + c
            keys = k_ref[lo : lo + n, :]
            values = v_ref[lo : lo + n, :]
            chances = []
            grad_scores = []
            for h in range(2):
                s = dot_nt(keys, query[h]) + bias_ref[b, c : c + n, :]
                p = jnp.exp(s - lse[h])
                dp = dot_nt(values, grad[h])
                ds = (p * (dp - delta[h])).astype(low)
                chances.append(p.astype(low))
                grad_scores.append(ds)
                t = dot_nn(kt_ref[h * HEAD : (h + 1) * HEAD, lo : lo + n], ds)
                dq[h] = t if dq[h] is None else dq[h] + t
            dv_ref[lo : lo + n, :] += dot_nn(jnp.concatenate(chances, axis=1), grads)
            dk_ref[lo : lo + n, :] += dot_nn(jnp.concatenate(grad_scores, axis=1), queries)
        dq_ref[at, :] = jnp.concatenate(dq, axis=0).T * (1.0 / math.sqrt(HEAD))
    for i, ref in enumerate((dk_ref, dv_ref)):
        prior_ref[i] = ref[:reach, :].astype(low)
        own_ref[i] = ref[reach : reach + rows, :]
        next_ref[i] = ref[reach + rows :, :].astype(low)


def attend_back(bounds, q, k, v, o, do, lse, first, pairs, halo, before=None, chunk=1280):
    rows, width = q.shape
    ext = k.shape[0]
    blocks = rows // QUERY_BLOCK
    reach = (ext - rows) // 2
    span = ext - rows + QUERY_BLOCK
    halo_first, halo_pairs = halo
    before = () if before is None else tuple(before)
    own = pl.BlockSpec((rows, PAIR), lambda p: (0, p + first))
    wide = pl.BlockSpec((ext, PAIR), lambda p: (0, p + first))
    edge = pl.BlockSpec((2, reach, PAIR), lambda p: (0, 0, p + first - halo_first))
    return pl.pallas_call(
        functools.partial(attend_back_kernel, chunk),
        grid=(pairs,),
        in_specs=[
            pl.BlockSpec((2, rows), lambda p: (0, 0)),
            own,
            wide,
            wide,
            own,
            own,
            pl.BlockSpec((1, 2, rows), lambda p: (p + first, 0, 0)),
        ]
        + [pl.BlockSpec(memory_space=pl.ANY)] * len(before),
        out_specs=[
            own,
            pl.BlockSpec((2, rows, PAIR), lambda p: (0, 0, p + first)),
            edge,
            edge,
        ],
        out_shape=[
            shape((rows, width), full),
            shape((2, rows, width), full),
            shape((2, reach, halo_pairs * PAIR), low),
            shape((2, reach, halo_pairs * PAIR), low),
        ],
        input_output_aliases={7 + i: i for i in range(len(before))},
        scratch_shapes=[
            pltpu.VMEM((blocks, span, QUERY_BLOCK), full),
            pltpu.VMEM((PAIR, ext), low),
            pltpu.VMEM((ext, PAIR), full),
            pltpu.VMEM((ext, PAIR), full),
        ],
        compiler_params=params(),
        cost_estimate=cost(8 * pairs),
        name="attend_back",
    )(bounds, q, k, v, o, do, lse, *before)


def mean(x):
    return jnp.mean(x, axis=-1, keepdims=True)


def norm(x):
    centred = x - mean(x)
    inverse = lax.rsqrt(mean(centred * centred) + epsilon)
    return centred * inverse, inverse


def norm_back(scaled, normed, inverse):
    return inverse * (scaled - mean(scaled) - normed * mean(scaled * normed))


def gather_vectors(ids, vec_refs, width):
    count = vec_refs[0].shape[0]
    if count == 1:
        return vec_refs[0][0].astype(full)
    size = width // (2 * count)
    row = lax.broadcasted_iota(jnp.int32, (PAIR, width), 0)
    column = lax.broadcasted_iota(jnp.int32, (PAIR, width), 1)
    out = jnp.zeros((16, width), full)
    for i, ref in enumerate(vec_refs):
        for at in range(count):
            f = 2 * at + (ids[2] ^ i)
            place = ((column - f * size == row) & (row < size)).astype(full).astype(low)
            out = out + dot_nn(ref[at], place)
    return out


def middle_kernel(plan, sources, ids, at_ref, tok_ref, cot_ref, *refs):
    vec_refs, refs = refs[:2], refs[2:]
    srcs = refs[:sources]
    (
        out_ref,
        dz1_ref,
        da_ref,
        hidden_ref,
        product_ref,
        dfeed_ref,
        dgate_ref,
        dlift_ref,
        dbranch_ref,
        gains_ref,
        out_w,
        gate_w,
        up_w,
        down_w,
        lift_factor,
        gate_factor,
        vectors,
        sems,
    ) = refs[sources:]
    step = pl.program_id(0)
    weights = (out_w, gate_w, up_w, down_w)

    @pl.when(step == 0)
    def _():
        for copy in plan(ids, srcs, weights, sems):
            copy.start()
        gains_ref[...] = jnp.zeros_like(gains_ref)

    def ready(*which):
        @pl.when(step == 0)
        def _():
            for i in which:
                pltpu.make_async_copy(weights[i], weights[i], sems.at[i]).wait()

    parts, _, width = gate_w.shape

    @pl.when(step == 0)
    def _():
        vectors[...] = gather_vectors(ids, vec_refs, width)

    gain1, bias1, gain2, bias2 = (vectors[i : i + 1] for i in range(4))
    ready(0)
    normed1, inverse1 = norm(tok_ref[...].astype(full) + dot_nn(at_ref[...], out_w[...]))
    hidden = normed1 * gain1 + bias1
    hidden_low = hidden.astype(low)
    hidden_ref[...] = hidden_low
    ready(1, 2, 3)
    feed = None
    for part in range(parts):
        at = slice(part * width, (part + 1) * width)
        gate = dot_nn(hidden_low, gate_w[part])
        lift = dot_nn(hidden_low, up_w[part])
        sigma = jax.nn.sigmoid(gate)
        opened = gate * sigma
        product = (opened * lift).astype(low)
        product_ref[:, at] = product
        lift_factor[:, at] = opened
        gate_factor[:, at] = lift * sigma * (1.0 + gate * (1.0 - sigma))
        term = dot_nn(product, down_w[at, :])
        feed = term if feed is None else feed + term
    normed2, inverse2 = norm(hidden + feed)
    out_ref[...] = (normed2 * gain2 + bias2).astype(low)
    cot = cot_ref[...].astype(full)
    gains_ref[2:3] += jnp.sum(cot * normed2, axis=0, keepdims=True)
    gains_ref[3:4] += jnp.sum(cot, axis=0, keepdims=True)
    grad = norm_back(cot * gain2, normed2, inverse2)
    dfeed = grad.astype(low)
    dfeed_ref[...] = dfeed
    for part in range(parts):
        at = slice(part * width, (part + 1) * width)
        dproduct = dot_nt(dfeed, down_w[at, :])
        dgate = (dproduct * gate_factor[:, at]).astype(low)
        dlift = (dproduct * lift_factor[:, at]).astype(low)
        dgate_ref[:, at] = dgate
        dlift_ref[:, at] = dlift
        grad = grad + dot_nt(dgate, gate_w[part]) + dot_nt(dlift, up_w[part])
    gains_ref[0:1] += jnp.sum(grad * normed1, axis=0, keepdims=True)
    gains_ref[1:2] += jnp.sum(grad, axis=0, keepdims=True)
    grad = norm_back(grad * gain1, normed1, inverse1)
    dz1_ref[...] = grad
    dbranch = grad.astype(low)
    dbranch_ref[...] = dbranch
    da_ref[...] = dot_nt(dbranch, out_w[...]).astype(low)


def middle(plan, ids, attended, tokens, cot, vectors, sources, hidden):
    rows, width = tokens.shape
    block = TOKEN_BLOCK
    tile = lambda w: pl.BlockSpec((block, w), lambda i, *_: (i, 0))
    whole = pl.BlockSpec((8, width), lambda i, *_: (0, 0))
    return pl.pallas_call(
        functools.partial(middle_kernel, plan, len(sources)),
        grid_spec=pltpu.PrefetchScalarGridSpec(
            num_scalar_prefetch=1,
            grid=(rows // block,),
            in_specs=[
                tile(width),
                tile(width),
                tile(width),
            ]
            + [pl.BlockSpec(vectors[0].shape, lambda i, *_: (0, 0, 0))] * 2
            + [pl.BlockSpec(memory_space=pl.ANY)] * len(sources),
            out_specs=[
                tile(width),
                tile(width),
                tile(width),
                tile(width),
                tile(hidden),
                tile(width),
                tile(hidden),
                tile(hidden),
                tile(width),
                whole,
            ],
            scratch_shapes=[
                pltpu.VMEM((width, width), low),
                pltpu.VMEM((hidden // width, width, width), low),
                pltpu.VMEM((hidden // width, width, width), low),
                pltpu.VMEM((hidden, width), low),
                pltpu.VMEM((block, hidden), full),
                pltpu.VMEM((block, hidden), full),
                pltpu.VMEM((16, width), full),
                pltpu.SemaphoreType.DMA((4,)),
            ],
        ),
        out_shape=[
            shape((rows, width), low),
            shape((rows, width), full),
            shape((rows, width), low),
            shape((rows, width), low),
            shape((rows, hidden), low),
            shape((rows, width), low),
            shape((rows, hidden), low),
            shape((rows, hidden), low),
            shape((rows, width), low),
            shape((8, width), full),
        ],
        compiler_params=params(),
        cost_estimate=cost(53),
        name="middle",
    )(ids, attended, tokens, cot, *vectors, *sources)


def weight_grad_kernel(a_ref, b_ref, o_ref):
    o_ref[...] = dot_tn(a_ref[...], b_ref[...]).astype(o_ref.dtype)


def weight_grad(a, b, tile_a=768, tile_b=768):
    rows, size_a = a.shape
    size_b = b.shape[1]
    return pl.pallas_call(
        weight_grad_kernel,
        grid=(size_a // tile_a, size_b // tile_b),
        in_specs=[
            pl.BlockSpec((rows, tile_a), lambda i, j: (0, i)),
            pl.BlockSpec((rows, tile_b), lambda i, j: (0, j)),
        ],
        out_specs=pl.BlockSpec((tile_a, tile_b), lambda i, j: (i, j)),
        out_shape=shape((size_a, size_b), low),
        compiler_params=params(),
        cost_estimate=cost(9),
        name="weight_grad",
    )(a, b)


def joint_kernel(dq_ref, own_ref, prior_ref, next_ref, cos_ref, sin_ref, *refs):
    dj_ref = refs[-1]
    width = dq_ref.shape[1]
    early = pl.program_id(0) < pl.num_programs(0) // 2
    cosine = cos_ref[...]
    sine = sin_ref[...]
    for at in range(0, width, PAIR):
        lanes = slice(at, at + PAIR)
        near = [
            jnp.where(early, prior_ref[i, :, lanes], next_ref[i, :, lanes]).astype(full)
            for i in range(2)
        ]
        keys = turn_back(own_ref[0, :, lanes] + near[0], cosine, sine)
        dj_ref[0, :, lanes] = turn_back(dq_ref[:, lanes], cosine, sine).astype(low)
        dj_ref[1, :, lanes] = keys.astype(low)
        dj_ref[2, :, lanes] = (own_ref[1, :, lanes] + near[1]).astype(low)


def joint(dq, own, prior, following, cosine, sine, at, before=()):
    rows, width = dq.shape
    part = prior.shape[2]
    block = TOKEN_BLOCK
    half = prior.shape[1] // block
    inner = pl.BlockSpec((block, PAIR), lambda i: (i + half, 0))
    return pl.pallas_call(
        joint_kernel,
        grid=(rows // block,),
        in_specs=[
            pl.BlockSpec((block, part), lambda i: (i, at)),
            pl.BlockSpec((2, block, part), lambda i: (0, i, at)),
            pl.BlockSpec((2, block, part), lambda i: (0, jnp.minimum(i, half - 1), 0)),
            pl.BlockSpec((2, block, part), lambda i: (0, jnp.maximum(i - half, 0), 0)),
            inner,
            inner,
        ]
        + [pl.BlockSpec(memory_space=pl.ANY)] * len(before),
        out_specs=pl.BlockSpec((3, block, part), lambda i: (0, i, at)),
        out_shape=shape((3, rows, width), low),
        input_output_aliases={6 + i: i for i in range(len(before))},
        compiler_params=params(),
        cost_estimate=cost(part // PAIR),
        name="joint",
    )(dq, own, prior, following, cosine, sine, *before)


def input_grad_kernel(dj_ref, dz1_ref, weight_ref, out_ref):
    out = dz1_ref[...]
    for i in range(3):
        out = out + dot_nt(dj_ref[i], weight_ref[i])
    out_ref[...] = out


def input_grad(dj, dz1, weights):
    rows, width = dz1.shape
    block = TOKEN_BLOCK
    tile = pl.BlockSpec((block, width), lambda i: (i, 0))
    return pl.pallas_call(
        input_grad_kernel,
        grid=(rows // block,),
        in_specs=[
            pl.BlockSpec((3, block, width), lambda i: (0, i, 0)),
            tile,
            pl.BlockSpec((3, width, width), lambda i: (0, 0, 0)),
        ],
        out_specs=tile,
        out_shape=shape((rows, width), full),
        compiler_params=params(),
        cost_estimate=cost(10),
        name="input_grad",
    )(dj, dz1, weights)


def whole_joint_plan(ids, srcs, weight, sem):
    width = weight.shape[1]
    return [
        pltpu.make_async_copy(srcs[0].at[:, i * width : (i + 1) * width], weight.at[i], sem)
        for i in range(3)
    ] + [pltpu.make_async_copy(srcs[1], weight.at[3], sem)]


def whole_middle_plan(ids, srcs, weights, sems):
    out_w, gate_w, up_w, down_w = weights
    parts, _, width = gate_w.shape
    columns = lambda src, dst, sem: [
        pltpu.make_async_copy(src.at[:, i * width : (i + 1) * width], dst.at[i], sem)
        for i in range(parts)
    ]
    return (
        [pltpu.make_async_copy(srcs[0].at[3], out_w, sems.at[0])]
        + columns(srcs[1], gate_w, sems.at[1])
        + columns(srcs[2], up_w, sems.at[2])
        + [pltpu.make_async_copy(srcs[3], down_w, sems.at[3])]
    )


def swap_with(value, place):
    pairs = []
    for r in range(4):
        for z in range(4):
            for c in range(2):
                to_r, to_z, to_c = place(r, z, c)
                pairs.append(((r * 4 + z) * 2 + c, (to_r * 4 + to_z) * 2 + to_c))
    return lax.ppermute(value, ("rep", "fsdp"), pairs)


def over_core(value):
    return swap_with(value, lambda r, z, c: (r, z, 1 - c))


def over_z(value, k):
    return swap_with(value, lambda r, z, c: (r, z ^ k, c))


def over_square_1(value):
    return swap_with(value, lambda r, z, c: (r ^ (1 + c), z, c))


def over_square_2(value):
    return swap_with(value, lambda r, z, c: (r ^ (2 - c), z, c))


def pieces(ids, srcs):
    r, z, c = ids[0], ids[1], ids[2]
    found = []
    for core, (shard, near, far) in ((c, srcs[:3]), (1 - c, srcs[3:6])):
        bit1, bit2 = 1 + core, 2 - core
        for quarter in range(4):
            found.append((shard.at[quarter], quarter, z, core))
        for ref, base in ((near, r), (far, r ^ bit2)):
            for j in range(2):
                for k in range(1, 4):
                    found.append((ref.at[j, k - 1], base ^ bit1 if j else base, z ^ k, core))
    return found


def piece_joint_plan(ids, srcs, weight, sem):
    size = srcs[0].shape[1]
    copies = []
    for ref, quarter, z, core in pieces(ids, srcs):
        at = pl.multiple_of((2 * z + core) * size, size)
        copies.append(pltpu.make_async_copy(ref, weight.at[quarter, pl.ds(at, size)], sem))
    return copies


def piece_middle_plan(ids, srcs, weights, sems):
    out_w, gate_w, up_w, down_w = weights
    size = srcs[1].shape[1] // 3
    copies = [pltpu.make_async_copy(srcs[0].at[3], out_w, sems.at[0])]
    found = pieces(ids, srcs[1:])
    for i, target in enumerate((gate_w, up_w)):
        for ref, quarter, z, core in found:
            at = pl.multiple_of((2 * z + core) * size, size)
            copies.append(
                pltpu.make_async_copy(
                    ref.at[i * size : (i + 1) * size],
                    target.at[quarter, pl.ds(at, size)],
                    sems.at[1 + i],
                )
            )
    for ref, quarter, z, core in found:
        at = pl.multiple_of(((2 * z + core) * 4 + quarter) * size, size)
        copies.append(
            pltpu.make_async_copy(
                ref.at[2 * size : 3 * size], down_w.at[pl.ds(at, size)], sems.at[3]
            )
        )
    return copies


def position(j, core):
    return jnp.where(core == 0, j, (j & 1) * 2 + (j >> 1))


def put_pieces(ids, block_ref, own_ref, other_ref, first, size):
    z, c = ids[1], ids[2]
    for ref, core in ((own_ref, c), (other_ref, 1 - c)):
        for k in range(4):
            at = pl.multiple_of((2 * (z ^ k) + core) * size, 8)
            ref[0, k, first : first + size, :] = block_ref[pl.ds(at, size), :].astype(low)


def gate_up_grad_kernel(
    ids, hidden_ref, dgate_ref, dlift_ref, gains_ref, own_ref, other_ref, block_ref
):
    size = block_ref.shape[0] // 8
    z, c = ids[1], ids[2]
    quarter = ids[0] ^ pl.program_id(0)
    for i, ref in enumerate((dgate_ref, dlift_ref)):
        block_ref[...] = dot_tn(hidden_ref[...], ref[...])
        put_pieces(ids, block_ref, own_ref, other_ref, i * size, size)
    for ref, core in ((own_ref, c), (other_ref, 1 - c)):
        for k in range(4):
            ref[0, k, 2 * size :, :] = jnp.zeros((16, ref.shape[3]), low)
            row = gains_ref[quarter * 8 + 2 * (z ^ k) + core]
            ref[0, k, 2 * size :, : row.shape[1]] = row.astype(low)


def grad_specs(size, width):
    own = pl.BlockSpec((1, 4, size, width), lambda j, ids: (position(j, ids[2]), 0, 0, 0))
    other = pl.BlockSpec((1, 4, size, width), lambda j, ids: (position(j, 1 - ids[2]), 0, 0, 0))
    return [own, other], [shape((4, 4, size, width), low)] * 2


def gate_up_grad(ids, hidden_low, dgate, dlift, gains):
    rows, width = hidden_low.shape
    size = width // 8
    out_specs, out_shape = grad_specs(2 * size + 16, width)
    column = pl.BlockSpec((rows, width), lambda j, ids: (0, ids[0] ^ j))
    return pl.pallas_call(
        gate_up_grad_kernel,
        grid_spec=pltpu.PrefetchScalarGridSpec(
            num_scalar_prefetch=1,
            grid=(4,),
            in_specs=[
                pl.BlockSpec((rows, width), lambda j, ids: (0, 0)),
                column,
                column,
                pl.BlockSpec(gains.shape, lambda j, ids: (0, 0, 0)),
            ],
            out_specs=out_specs,
            scratch_shapes=[pltpu.VMEM((width, width), full)],
        ),
        out_shape=out_shape,
        compiler_params=params(),
        cost_estimate=cost(17),
        name="gate_up_grad",
    )(ids, hidden_low, dgate, dlift, gains)


def joint_grad_kernel(ids, tok_ref, dj_ref, at_ref, db_ref, own_ref, other_ref, block_ref):
    size = block_ref.shape[0] // 8
    quarter = ids[0] ^ pl.program_id(0)

    @pl.when(quarter < 3)
    def _():
        block_ref[...] = dot_tn(tok_ref[...], dj_ref[0])

    @pl.when(quarter == 3)
    def _():
        block_ref[...] = dot_tn(at_ref[...], db_ref[...])

    put_pieces(ids, block_ref, own_ref, other_ref, 0, size)


def joint_grad(ids, tokens, djoint, attended, dbranch):
    rows, width = tokens.shape
    size = width // 8
    out_specs, out_shape = grad_specs(size, width)
    whole = pl.BlockSpec((rows, width), lambda j, ids: (0, 0))
    return pl.pallas_call(
        joint_grad_kernel,
        grid_spec=pltpu.PrefetchScalarGridSpec(
            num_scalar_prefetch=1,
            grid=(4,),
            in_specs=[
                whole,
                pl.BlockSpec(
                    (1, rows, width), lambda j, ids: (jnp.minimum(ids[0] ^ j, 2), 0, 0)
                ),
                whole,
                whole,
            ],
            out_specs=out_specs,
            scratch_shapes=[pltpu.VMEM((width, width), full)],
        ),
        out_shape=out_shape,
        compiler_params=params(),
        cost_estimate=cost(9),
        name="joint_grad",
    )(ids, tokens, djoint, attended, dbranch)


def wide(v):
    return v.astype(full)


def sum_core(own, mate):
    return (wide(own[2:]) + wide(mate[2:])).astype(low)


def sum_square(own, mate, b):
    return (wide(own[1]) + wide(mate[1]) + wide(b[1])).astype(low)


def sum_rest(own, mate, b, d):
    return wide(own[0]) + wide(mate[0]) + wide(b[0]) + wide(d)


def send_z(kept):
    return [over_z(kept[k].astype(low), k) for k in (1, 2, 3)]


def sum_z(kept, arrived):
    return (kept[0] + wide(arrived[0]) + wide(arrived[1]) + wide(arrived[2])).astype(low)


def place(ids, quarter):
    return position(quarter ^ ids[0], ids[2])


def finish_kernel(ids, pair_ref, others_ref, gate_ref, up_ref, vec_ref):
    size, width = gate_ref.shape
    quarter = pl.program_id(0)
    at = place(ids, quarter)

    def put(ref):
        piece = ref[at & 1].astype(full)
        gate_ref[...] = piece[:size]
        up_ref[...] = piece[size : 2 * size]
        vec_ref[0] = piece[2 * size : 2 * size + 8, :PAIR]

    pl.when(at < 2)(lambda: put(pair_ref))
    pl.when(at >= 2)(lambda: put(others_ref))


def finish(ids, pair, others, size):
    width = pair.shape[2]
    whole = pl.BlockSpec(pair.shape, lambda j, ids: (0, 0, 0))
    column = pl.BlockSpec((size, width), lambda j, ids: (0, j))
    gate, up, vectors = pl.pallas_call(
        finish_kernel,
        grid_spec=pltpu.PrefetchScalarGridSpec(
            num_scalar_prefetch=1,
            grid=(4,),
            in_specs=[whole, whole],
            out_specs=[column, column, pl.BlockSpec((1, 8, PAIR), lambda j, ids: (j, 0, 0))],
        ),
        out_shape=[shape((size, 4 * width), full)] * 2 + [shape((4, 8, PAIR), full)],
        compiler_params=params(),
        cost_estimate=cost(3),
        name="finish",
    )(ids, pair, others)
    return gate, up, vectors[:, 0, :size]


def finish_joint_kernel(ids, pair_ref, others_ref, joint_ref, out_ref):
    quarter = pl.program_id(0)
    at = place(ids, quarter)

    def put(ref):
        piece = ref[at & 1].astype(full)

        @pl.when(quarter < 3)
        def _():
            joint_ref[...] = piece

        @pl.when(quarter == 3)
        def _():
            out_ref[...] = piece

    pl.when(at < 2)(lambda: put(pair_ref))
    pl.when(at >= 2)(lambda: put(others_ref))


def finish_joint(ids, pair, others):
    size, width = pair.shape[1:]
    whole = pl.BlockSpec(pair.shape, lambda j, ids: (0, 0, 0))
    return pl.pallas_call(
        finish_joint_kernel,
        grid_spec=pltpu.PrefetchScalarGridSpec(
            num_scalar_prefetch=1,
            grid=(4,),
            in_specs=[whole, whole],
            out_specs=[
                pl.BlockSpec((size, width), lambda j, ids: (0, jnp.minimum(j, 2))),
                pl.BlockSpec((size, width), lambda j, ids: (0, 0)),
            ],
        ),
        out_shape=[shape((size, 3 * width), full), shape((size, width), full)],
        compiler_params=params(),
        cost_estimate=cost(2),
        name="finish_joint",
    )(ids, pair, others)


def shards(
    custom,
    tokens,
    lengths,
    qkv_weight,
    out_weight,
    gate_weight,
    up_weight,
    down_weight,
    norm1_gain,
    norm1_bias,
    norm2_gain,
    norm2_bias,
    cotangent,
):
    rows, width = tokens.shape
    hidden = gate_weight.shape[1]
    size = lax.axis_size("fsdp")
    me = lax.axis_index("fsdp")
    up = [(i, i + 1) for i in range(size - 1)]
    down = [(i + 1, i) for i in range(size - 1)]
    r = lax.axis_index("rep")
    z, c = me // 2, me % 2
    ids = jnp.stack([r, z, c]).astype(jnp.int32)
    vectors = jnp.stack([norm1_gain, norm1_bias, norm2_gain, norm2_bias]).astype(low)

    before = tokens[rows - REACH :]
    behind = tokens[:REACH]
    swap_edges = lambda last, first: (
        lax.ppermute(last, "fsdp", up),
        lax.ppermute(first, "fsdp", down),
    )
    if custom:
        part = qkv_weight.shape[0]
        columns = lambda w: jnp.swapaxes(w.astype(low).reshape(part, -1, width), 0, 1)
        column = lambda w, i: lax.dynamic_slice_in_dim(w, i * width, width, 1).astype(low)
        mine = jnp.where(
            r == 3, out_weight.astype(low), column(qkv_weight, jnp.minimum(r, 2))
        )
        arrived = [over_z(mine, k) for k in (1, 2, 3)]
        mine = jnp.concatenate(
            [
                column(gate_weight, r),
                column(up_weight, r),
                lax.dynamic_slice_in_dim(down_weight, r * part, part, 0).astype(low),
                jnp.pad(vectors, ((0, 12), (0, width - part))),
            ]
        )
        shard_1 = jnp.concatenate([columns(qkv_weight), out_weight.astype(low)[None]])
        mate_shard_1 = over_core(shard_1)
        own_1 = jnp.stack(after(tuple(arrived), mine))
        before, behind = after((before, behind), own_1)
        before, behind = swap_edges(before, behind)
        along_z = [[2 * i + j for i in range(size // 2)] for j in range(2)]
        arrived_2 = lax.all_gather(
            after(mine, before, behind), "fsdp", axis=0, axis_index_groups=along_z
        )
        other_1 = over_square_1(own_1)
        near_1 = jnp.stack([own_1, other_1])
        far_1 = over_square_2(near_1)
        mate_near_1 = over_core(near_1)
        mate_far_1 = over_core(far_1)
        joint_sources = [shard_1, near_1, far_1, mate_shard_1, mate_near_1, mate_far_1]
        joint_plan = piece_joint_plan
        shard_2 = jnp.concatenate(
            [
                columns(gate_weight),
                columns(up_weight),
                down_weight.astype(low).reshape(4, part, width),
            ],
            axis=1,
        )
        mate_shard_2 = over_core(after(shard_2, far_1))
    else:
        before, behind = swap_edges(before, behind)
        gather = lambda w: lax.all_gather(w.astype(low), "fsdp", axis=0, tiled=True)
        joint_sources = [gather(qkv_weight), gather(out_weight)]
        joint_plan = whole_joint_plan
        middle_sources = [gather(w) for w in (gate_weight, up_weight, down_weight)]
        vectors = lax.all_gather(vectors, "fsdp", axis=1, tiled=True)
        found = [jnp.pad(vectors, ((0, 12), (0, 0)))[None]] * 2
        middle_plan = whole_middle_plan

    tokens_ext = jnp.concatenate([before, tokens, behind], axis=0)

    doc_lengths = lengths[0]
    ends = jnp.cumsum(doc_lengths)
    index = me * rows - REACH + jnp.arange(rows + 2 * REACH, dtype=jnp.int32)
    passed = (index[:, None] >= ends[None, :]).astype(jnp.int32)
    starts = jnp.sum(passed * doc_lengths[None, :], axis=1)
    cosine, sine = tables(index - starts)
    own_starts = starts[REACH : REACH + rows]
    own_index = index[REACH : REACH + rows]
    stops = jnp.min(
        jnp.where(ends[None, :] > own_index[:, None], ends[None, :], size * rows), axis=1
    )
    base = me * rows - REACH
    bounds = jnp.stack(
        [
            jnp.maximum(own_starts, own_index - REACH) - base,
            jnp.minimum(stops, own_index + REACH + 1) - base,
        ]
    ).astype(jnp.int32)

    queries, keys, values, joint_weights = project(
        joint_plan, ids, tokens_ext, cosine, sine, joint_sources, rows
    )
    given = (queries, keys, values)
    if custom:
        arrived_2 = after(arrived_2, queries)
        own_2 = jnp.stack(
            [
                lax.dynamic_slice(arrived_2, (z ^ k, 0, 0), (1, 3 * part, width))[0]
                for k in (1, 2, 3)
            ]
        )
        found = arrived_2[:, 3 * part :, :PAIR]
        other_2 = over_square_1(own_2)
        mate_found = over_core(found)
        done = attend(after(bounds, own_2, found), *given, 0, 2)
        near_2 = jnp.stack([own_2, after(other_2, done[1], mate_shard_2, mate_found)])
        far_2 = over_square_2(near_2)
        mate_near_2 = over_core(near_2)
        done = attend(after(bounds, near_2), *given, 2, 2, done)
        attended, lse = attend(bounds, *given, 4, 2, done)
        mate_far_2 = over_core(after(far_2, lse, mate_near_2))
        middle_sources = [shard_2, near_2, far_2, mate_shard_2, mate_near_2, mate_far_2]
        middle_plan = piece_middle_plan
        found = [found, mate_found]
    else:
        done = None
        for first in (0, 2, 4):
            done = attend(bounds, *given, first, 2, done)
        attended, lse = done
    result, dz1, dattended, hidden_low, product, dfeed, dgate, dlift, dbranch, gains = middle(
        middle_plan,
        ids,
        attended,
        tokens,
        cotangent,
        found,
        [joint_weights, *middle_sources],
        hidden,
    )
    gains = gains[:4]
    given = (queries, keys, values, attended, dattended, lse)
    spread = lambda g: lax.psum_scatter(g, "fsdp", scatter_dimension=0, tiled=True)
    if custom:
        gains = jnp.pad(gains.reshape(32, 1, part), ((0, 0), (0, 15), (0, PAIR - part)))
        own, other = gate_up_grad(ids, hidden_low, dgate, dlift, gains)
        mate = over_core(other)
        grad_down = weight_grad(after(product, own), dfeed)
        share_down = spread(grad_down)
        sent = sum_core(own, after(mate, grad_down))
        b = over_square_2(sent)
        done = attend_back(after(bounds, sent), *given, 0, 2, (0, 4))
        dq, dkv, to_prior, to_next = attend_back(
            after(bounds, done[0]), *given, 2, 2, (0, 4), done
        )
        edges_1 = swap_edges(to_next, to_prior)
        sent = sum_square(own, mate, after(b, dq))
        d = over_square_1(sent)
        dq, dkv, to_prior, to_next = attend_back(
            after(bounds, sent), *given, 4, 2, (4, 2), (dq, dkv)
        )
        edges_2 = swap_edges(to_next, to_prior)
        djoint = joint(dq, dkv, *edges_1, cosine, sine, 0)
        kept = sum_rest(own, mate, b, after(d, djoint))
        arrived = send_z(kept)
        share_down = after(share_down, djoint)
        down_1 = over_square_1(share_down)
        djoint = joint(after(dq, kept), dkv, *edges_2, cosine, sine, 2, (djoint,))
        own, other = joint_grad(ids, tokens, djoint, attended, dbranch)
        mate = over_core(other)
        share_down = (wide(share_down) + wide(after(down_1, own))).astype(low)
        down_2 = over_square_2(share_down)
        grad_tokens = input_grad(after(djoint, own, share_down), dz1, joint_weights)
        down_sum = (wide(share_down) + wide(after(down_2, grad_tokens))).astype(low)
        b = over_square_2(sum_core(own, after(mate, grad_tokens)))
        mine = sum_z(kept, after(tuple(arrived), grad_tokens))
        gate_1 = over_square_1(mine)
        d = over_square_1(sum_square(own, mate, after(b, mine)))
        pair = jnp.stack([mine, after(gate_1, d)])
        others = over_square_2(pair)
        kept = sum_rest(own, mate, b, after(d, pair))
        mine = sum_z(kept, send_z(kept))
        joint_pair = jnp.stack([mine, over_square_1(mine)])
        joint_others = over_square_2(joint_pair)
        gate_sum, up_sum, vector_sum = finish(ids, after(pair, joint_pair), others, part)
        joint_sum, out_sum = finish_joint(ids, joint_pair, joint_others)
        summed = (joint_sum, out_sum, gate_sum, up_sum, wide(down_sum), vector_sum)
    else:
        share_down = spread(weight_grad(product, dfeed))
        share_gate = spread(weight_grad(hidden_low, dgate))
        share_up = spread(weight_grad(hidden_low, dlift))
        share_out = spread(weight_grad(attended, dbranch))
        share_gains = lax.psum_scatter(gains, "fsdp", scatter_dimension=1, tiled=True)
        done = attend_back(bounds, *given, 0, 2, (0, 4))
        dq, dkv, to_prior, to_next = attend_back(bounds, *given, 2, 2, (0, 4), done)
        edges_1 = swap_edges(to_next, to_prior)
        dq, dkv, to_prior, to_next = attend_back(bounds, *given, 4, 2, (4, 2), (dq, dkv))
        edges_2 = swap_edges(to_next, to_prior)
        djoint = joint(dq, dkv, *edges_1, cosine, sine, 0)
        djoint = joint(dq, dkv, *edges_2, cosine, sine, 2, (djoint,))
        share_qkv = jnp.concatenate([spread(weight_grad(tokens, djoint[i])) for i in range(3)], 1)
        grad_tokens = input_grad(djoint, dz1, joint_weights)
        summed = lax.psum(
            tuple(
                s.astype(full)
                for s in (share_qkv, share_out, share_gate, share_up, share_down, share_gains)
            ),
            "rep",
        )
    return (result, grad_tokens, *summed[:5], *(summed[5][i] for i in range(4)))


def solution(mesh):
    rows = P(("rep", "fsdp"), None)
    matrix = P("fsdp", None)
    vector = P("fsdp")
    custom = (mesh.shape["rep"], mesh.shape["fsdp"]) == (4, 8)
    return jax.shard_map(
        functools.partial(shards, custom and not FORCE_WHOLE),
        mesh=mesh,
        in_specs=(rows, P("rep", None)) + (matrix,) * 5 + (vector,) * 4 + (rows,),
        out_specs=(rows, rows) + (matrix,) * 5 + (vector,) * 4,
        check_vma=False,
    )
```

```python
import functools
import math

import jax
import jax.numpy as jnp
from jax import lax
from jax.experimental import pallas as pl
from jax.experimental.pallas import tpu as pltpu
from jax.sharding import PartitionSpec as P

HEADS = 12
WINDOW = 1024
REACH = WINDOW // 2
HEAD = 64
PAIR = 2 * HEAD
QUERY_BLOCK = 256
TOKEN_BLOCK = 256
FORCE_WHOLE = False
VMEM = 56 * 1024 * 1024

epsilon = 1e-06
rope_base = 1000.0
masked_score = -1e30
low = jnp.bfloat16
full = jnp.float32


def dot_nn(a, b):
    return lax.dot_general(a, b, (((1,), (0,)), ((), ())), preferred_element_type=full)


def dot_nt(a, b):
    return lax.dot_general(a, b, (((1,), (1,)), ((), ())), preferred_element_type=full)


def dot_tn(a, b):
    return lax.dot_general(a, b, (((0,), (0,)), ((), ())), preferred_element_type=full)


def params():
    return pltpu.CompilerParams(vmem_limit_bytes=VMEM)


def after(value, *others):
    return lax.optimization_barrier((value, *others))[0]


def shape(dims, dtype):
    return jax.ShapeDtypeStruct(dims, dtype)


def cost(micros):
    return pl.CostEstimate(flops=int(micros * 1.15e9), bytes_accessed=1, transcendentals=0)


def tables(position):
    lane = jnp.arange(PAIR, dtype=jnp.int32) % HEAD
    half = HEAD // 2
    frequency = rope_base ** (-2.0 * (lane % half).astype(full) / HEAD)
    angle = position.astype(full)[:, None] * frequency[None, :]
    sign = jnp.where(lane < half, -1.0, 1.0).astype(full)
    return jnp.cos(angle), jnp.sin(angle) * sign[None, :]


def partner(x):
    half = HEAD // 2
    lane = lax.broadcasted_iota(jnp.int32, x.shape, 1) % HEAD
    return jnp.where(lane < half, pltpu.roll(x, PAIR - half, 1), pltpu.roll(x, half, 1))


def turn(x, cosine, sine):
    return x * cosine + partner(x) * sine


def turn_back(x, cosine, sine):
    return x * cosine - partner(x) * sine


def project_kernel(
    plan, sources, first, count, ids, before_ref, tok_ref, behind_ref, cos_ref, sin_ref, *refs
):
    srcs = refs[:sources]
    q_ref, k_ref, v_ref, weight, sems = refs[sources:]
    step = pl.program_id(0)

    @pl.when(step == 0)
    def _():
        for copy in plan(ids, srcs, weight, sems.at[0]):
            copy.start()
        pltpu.make_async_copy(weight, weight, sems.at[0]).wait()

    width = tok_ref.shape[1]
    rows = jnp.where(
        step < first,
        before_ref[...],
        jnp.where(step < first + count, tok_ref[...], behind_ref[...]),
    )
    cosine = cos_ref[...]
    sine = sin_ref[...]
    keys = dot_nn(rows, weight[1])
    for at in range(0, width, PAIR):
        k_ref[:, at : at + PAIR] = turn(keys[:, at : at + PAIR], cosine, sine).astype(low)
    v_ref[...] = dot_nn(rows, weight[2]).astype(low)

    @pl.when((step >= first) & (step < first + count))
    def _():
        queries = dot_nn(rows, weight[0])
        for at in range(0, width, PAIR):
            turned = turn(queries[:, at : at + PAIR], cosine, sine).astype(low)
            q_ref[:, at : at + PAIR] = (turned.astype(full) * (1.0 / math.sqrt(HEAD))).astype(low)


def project(plan, ids, before, tokens, behind, cosine, sine, sources):
    rows, width = tokens.shape
    ext = rows + 2 * before.shape[0]
    block = TOKEN_BLOCK
    first, count = before.shape[0] // block, rows // block
    tile = lambda w: pl.BlockSpec((block, w), lambda i, *_: (i, 0))
    inner = pl.BlockSpec((block, width), lambda i, *_: (jnp.clip(i - first, 0, count - 1), 0))
    return pl.pallas_call(
        functools.partial(project_kernel, plan, len(sources), first, count),
        grid_spec=pltpu.PrefetchScalarGridSpec(
            num_scalar_prefetch=1,
            grid=(ext // block,),
            in_specs=[
                pl.BlockSpec((block, width), lambda i, *_: (jnp.minimum(i, first - 1), 0)),
                inner,
                pl.BlockSpec(
                    (block, width), lambda i, *_: (jnp.maximum(i - first - count, 0), 0)
                ),
                tile(PAIR),
                tile(PAIR),
            ]
            + [pl.BlockSpec(memory_space=pl.ANY)] * len(sources),
            out_specs=[
                inner,
                tile(width),
                tile(width),
                pl.BlockSpec((4, width, width), lambda i, *_: (0, 0, 0)),
            ],
            scratch_shapes=[pltpu.SemaphoreType.DMA((1,))],
        ),
        out_shape=[
            shape((rows, width), low),
            shape((ext, width), low),
            shape((ext, width), low),
            shape((4, width, width), low),
        ],
        compiler_params=params(),
        cost_estimate=cost(1),
        name="project",
    )(ids, before, tokens, behind, cosine, sine, *sources)


def fill_bias(bounds_ref, bias_ref, blocks, span):
    for b in range(blocks):
        lo = bounds_ref[0:1, b * QUERY_BLOCK : (b + 1) * QUERY_BLOCK] - b * QUERY_BLOCK
        hi = bounds_ref[1:2, b * QUERY_BLOCK : (b + 1) * QUERY_BLOCK] - b * QUERY_BLOCK
        at = lax.broadcasted_iota(jnp.int32, (span, QUERY_BLOCK), 0)
        bias_ref[b] = jnp.where((at >= lo) & (at < hi), 0.0, masked_score)


def only(x, head):
    lane = lax.broadcasted_iota(jnp.int32, x.shape, 1)
    return jnp.where((lane >= HEAD) if head else (lane < HEAD), x, jnp.zeros_like(x))


def attend_kernel(chunk, bounds_ref, q_ref, k_ref, v_ref, *refs):
    o_ref, lse_ref, bias_ref, vt_ref, s_ref = refs[-5:]
    rows = q_ref.shape[0]
    block = QUERY_BLOCK
    blocks = rows // block
    span = k_ref.shape[0] - rows + block

    @pl.when(pl.program_id(0) == 0)
    def _():
        fill_bias(bounds_ref, bias_ref, blocks, span)

    vt_ref[...] = v_ref[...].T
    chunks = [(c, min(chunk, span - c)) for c in range(0, span, chunk)]
    for b in range(blocks):
        out = []
        for h in range(2):
            query = only(q_ref[b * block : (b + 1) * block, :], h)
            slot = s_ref.at[(2 * b + h) % 2]
            top = None
            for c, n in chunks:
                s = dot_nt(k_ref[b * block + c : b * block + c + n, :], query)
                s = s + bias_ref[b, c : c + n, :]
                slot[c : c + n, :] = s
                t = jnp.max(s.reshape(n // 8, 8, block), axis=0)
                top = t if top is None else jnp.maximum(top, t)
            peak = jnp.max(top, axis=0, keepdims=True)
            total = None
            mixed = None
            for c, n in chunks:
                e = jnp.exp(slot[c : c + n, :] - peak)
                t = jnp.sum(e.reshape(n // 8, 8, block), axis=0)
                total = t if total is None else total + t
                o = dot_nn(
                    vt_ref[h * HEAD : (h + 1) * HEAD, b * block + c : b * block + c + n],
                    e.astype(low),
                )
                mixed = o if mixed is None else mixed + o
            total = jnp.sum(total, axis=0, keepdims=True)
            out.append(mixed / total)
            lse_ref[0, h : h + 1, b * block : (b + 1) * block] = peak + jnp.log(total)
        o_ref[b * block : (b + 1) * block, :] = jnp.concatenate(out, axis=0).T.astype(low)


def attend(bounds, q, k, v, first, pairs, before=None, chunk=640):
    rows, width = q.shape
    ext = k.shape[0]
    blocks = rows // QUERY_BLOCK
    span = ext - rows + QUERY_BLOCK
    own = pl.BlockSpec((rows, PAIR), lambda p: (0, p + first))
    wide = pl.BlockSpec((ext, PAIR), lambda p: (0, p + first))
    before = () if before is None else tuple(before)
    return pl.pallas_call(
        functools.partial(attend_kernel, chunk),
        grid=(pairs,),
        in_specs=[pl.BlockSpec((2, rows), lambda p: (0, 0)), own, wide, wide]
        + [pl.BlockSpec(memory_space=pl.ANY)] * len(before),
        out_specs=[own, pl.BlockSpec((1, 2, rows), lambda p: (p + first, 0, 0))],
        out_shape=[shape((rows, width), low), shape((width // PAIR, 2, rows), full)],
        input_output_aliases={4 + i: i for i in range(len(before))},
        scratch_shapes=[
            pltpu.VMEM((blocks, span, QUERY_BLOCK), full),
            pltpu.VMEM((PAIR, ext), low),
            pltpu.VMEM((2, span, QUERY_BLOCK), full),
        ],
        compiler_params=params(),
        cost_estimate=cost(pairs),
        name="attend",
    )(bounds, q, k, v, *before)


def attend_back_kernel(
    chunk,
    bounds_ref,
    q_ref,
    k_ref,
    v_ref,
    o_ref,
    do_ref,
    lse_ref,
    *refs,
):
    cos_ref, sin_ref = refs[:2]
    dq_ref, own_ref, prior_ref, next_ref, bias_ref, kt_ref, dk_ref, dv_ref = refs[-8:]
    rows = q_ref.shape[0]
    ext = k_ref.shape[0]
    block = QUERY_BLOCK
    blocks = rows // block
    reach = (ext - rows) // 2
    span = ext - rows + block

    @pl.when(pl.program_id(0) == 0)
    def _():
        fill_bias(bounds_ref, bias_ref, blocks, span)

    kt_ref[...] = k_ref[...].T
    dk_ref[...] = jnp.zeros_like(dk_ref)
    dv_ref[...] = jnp.zeros_like(dv_ref)
    chunks = [(c, min(chunk, span - c)) for c in range(0, span, chunk)]
    for b in range(blocks):
        at = slice(b * block, (b + 1) * block)
        q = q_ref[at, :]
        do = do_ref[at, :]
        product = (do.astype(full) * o_ref[at, :].astype(full)).T
        query = [only(q, h) for h in range(2)]
        grad = [only(do, h) for h in range(2)]
        delta = [
            jnp.sum(product[h * HEAD : (h + 1) * HEAD], axis=0, keepdims=True) for h in range(2)
        ]
        lse = [lse_ref[0, h : h + 1, at] for h in range(2)]
        dq = [None, None]
        queries = jnp.concatenate(query, axis=0)
        grads = jnp.concatenate(grad, axis=0)
        for c, n in chunks:
            lo = b * block + c
            keys = k_ref[lo : lo + n, :]
            values = v_ref[lo : lo + n, :]
            chances = []
            grad_scores = []
            for h in range(2):
                s = dot_nt(keys, query[h]) + bias_ref[b, c : c + n, :]
                p = jnp.exp(s - lse[h])
                dp = dot_nt(values, grad[h])
                ds = (p * (dp - delta[h])).astype(low)
                chances.append(p.astype(low))
                grad_scores.append(ds)
                t = dot_nn(kt_ref[h * HEAD : (h + 1) * HEAD, lo : lo + n], ds)
                dq[h] = t if dq[h] is None else dq[h] + t
            dv_ref[lo : lo + n, :] += dot_nn(jnp.concatenate(chances, axis=1), grads)
            dk_ref[lo : lo + n, :] += dot_nn(jnp.concatenate(grad_scores, axis=1), queries)
        turned = turn_back(jnp.concatenate(dq, axis=0).T, cos_ref[at, :], sin_ref[at, :])
        dq_ref[at, :] = (turned * (1.0 / math.sqrt(HEAD))).astype(low)
    for i, ref in enumerate((dk_ref, dv_ref)):
        prior_ref[i] = ref[:reach, :].astype(low)
        own_ref[i] = ref[reach : reach + rows, :]
        next_ref[i] = ref[reach + rows :, :].astype(low)


def attend_back(bounds, q, k, v, o, do, lse, cosine, sine, first, pairs, halo, before=None, chunk=1280):
    rows, width = q.shape
    ext = k.shape[0]
    blocks = rows // QUERY_BLOCK
    reach = (ext - rows) // 2
    span = ext - rows + QUERY_BLOCK
    halo_first, halo_pairs = halo
    before = () if before is None else tuple(before)
    own = pl.BlockSpec((rows, PAIR), lambda p: (0, p + first))
    wide = pl.BlockSpec((ext, PAIR), lambda p: (0, p + first))
    edge = pl.BlockSpec((2, reach, PAIR), lambda p: (0, 0, p + first - halo_first))
    return pl.pallas_call(
        functools.partial(attend_back_kernel, chunk),
        grid=(pairs,),
        in_specs=[
            pl.BlockSpec((2, rows), lambda p: (0, 0)),
            own,
            wide,
            wide,
            own,
            own,
            pl.BlockSpec((1, 2, rows), lambda p: (p + first, 0, 0)),
            pl.BlockSpec((rows, PAIR), lambda p: (0, 0)),
            pl.BlockSpec((rows, PAIR), lambda p: (0, 0)),
        ]
        + [pl.BlockSpec(memory_space=pl.ANY)] * len(before),
        out_specs=[
            own,
            pl.BlockSpec((2, rows, PAIR), lambda p: (0, 0, p + first)),
            edge,
            edge,
        ],
        out_shape=[
            shape((rows, width), low),
            shape((2, rows, width), full),
            shape((2, reach, halo_pairs * PAIR), low),
            shape((2, reach, halo_pairs * PAIR), low),
        ],
        input_output_aliases={9 + i: i for i in range(len(before))},
        scratch_shapes=[
            pltpu.VMEM((blocks, span, QUERY_BLOCK), full),
            pltpu.VMEM((PAIR, ext), low),
            pltpu.VMEM((ext, PAIR), full),
            pltpu.VMEM((ext, PAIR), full),
        ],
        compiler_params=params(),
        cost_estimate=cost(24 * pairs),
        name="attend_back",
    )(bounds, q, k, v, o, do, lse, cosine, sine, *before)


def mean(x):
    return jnp.mean(x, axis=-1, keepdims=True)


def norm(x):
    centred = x - mean(x)
    inverse = lax.rsqrt(mean(centred * centred) + epsilon)
    return centred * inverse, inverse


def norm_back(scaled, normed, inverse):
    return inverse * (scaled - mean(scaled) - normed * mean(scaled * normed))


def gather_vectors(ids, vec_refs, width):
    count = vec_refs[0].shape[0]
    if count == 1:
        return vec_refs[0][0].astype(full)
    size = width // (2 * count)
    row = lax.broadcasted_iota(jnp.int32, (PAIR, width), 0)
    column = lax.broadcasted_iota(jnp.int32, (PAIR, width), 1)
    out = jnp.zeros((16, width), full)
    for i, ref in enumerate(vec_refs):
        for at in range(count):
            f = 2 * at + (ids[2] ^ i)
            place = ((column - f * size == row) & (row < size)).astype(full).astype(low)
            out = out + dot_nn(ref[at], place)
    return out


def middle_kernel(plan, sources, ids, at_ref, tok_ref, cot_ref, *refs):
    vec_refs, refs = refs[:2], refs[2:]
    srcs = refs[:sources]
    (
        out_ref,
        dz1_ref,
        da_ref,
        hidden_ref,
        product_ref,
        dfeed_ref,
        dgate_ref,
        dlift_ref,
        dbranch_ref,
        gains_ref,
        out_w,
        gate_w,
        up_w,
        down_w,
        lift_factor,
        gate_factor,
        vectors,
        sems,
    ) = refs[sources:]
    step = pl.program_id(0)
    weights = (out_w, gate_w, up_w, down_w)

    @pl.when(step == 0)
    def _():
        for copy in plan(ids, srcs, weights, sems):
            copy.start()
        gains_ref[...] = jnp.zeros_like(gains_ref)

    def ready(*which):
        @pl.when(step == 0)
        def _():
            for i in which:
                pltpu.make_async_copy(weights[i], weights[i], sems.at[i]).wait()

    parts, _, width = gate_w.shape

    @pl.when(step == 0)
    def _():
        vectors[...] = gather_vectors(ids, vec_refs, width)

    gain1, bias1, gain2, bias2 = (vectors[i : i + 1] for i in range(4))
    ready(0)
    normed1, inverse1 = norm(tok_ref[...].astype(full) + dot_nn(at_ref[...], out_w[...]))
    hidden = normed1 * gain1 + bias1
    hidden_low = hidden.astype(low)
    hidden_ref[...] = hidden_low
    ready(1, 2, 3)
    feed = None
    for part in range(parts):
        at = slice(part * width, (part + 1) * width)
        gate = dot_nn(hidden_low, gate_w[part])
        lift = dot_nn(hidden_low, up_w[part])
        sigma = jax.nn.sigmoid(gate)
        opened = gate * sigma
        product = (opened * lift).astype(low)
        product_ref[:, at] = product
        lift_factor[:, at] = opened
        gate_factor[:, at] = lift * sigma * (1.0 + gate * (1.0 - sigma))
        term = dot_nn(product, down_w[at, :])
        feed = term if feed is None else feed + term
    normed2, inverse2 = norm(hidden + feed)
    out_ref[...] = (normed2 * gain2 + bias2).astype(low)
    cot = cot_ref[...].astype(full)
    gains_ref[2:3] += jnp.sum(cot * normed2, axis=0, keepdims=True)
    gains_ref[3:4] += jnp.sum(cot, axis=0, keepdims=True)
    grad = norm_back(cot * gain2, normed2, inverse2)
    dfeed = grad.astype(low)
    dfeed_ref[...] = dfeed
    for part in range(parts):
        at = slice(part * width, (part + 1) * width)
        dproduct = dot_nt(dfeed, down_w[at, :])
        dgate = (dproduct * gate_factor[:, at]).astype(low)
        dlift = (dproduct * lift_factor[:, at]).astype(low)
        dgate_ref[:, at] = dgate
        dlift_ref[:, at] = dlift
        grad = grad + dot_nt(dgate, gate_w[part]) + dot_nt(dlift, up_w[part])
    gains_ref[0:1] += jnp.sum(grad * normed1, axis=0, keepdims=True)
    gains_ref[1:2] += jnp.sum(grad, axis=0, keepdims=True)
    grad = norm_back(grad * gain1, normed1, inverse1)
    dz1_ref[...] = grad
    dbranch = grad.astype(low)
    dbranch_ref[...] = dbranch
    da_ref[...] = dot_nt(dbranch, out_w[...]).astype(low)


def middle(plan, ids, attended, tokens, cot, vectors, sources, hidden):
    rows, width = tokens.shape
    block = TOKEN_BLOCK
    tile = lambda w: pl.BlockSpec((block, w), lambda i, *_: (i, 0))
    whole = pl.BlockSpec((8, width), lambda i, *_: (0, 0))
    return pl.pallas_call(
        functools.partial(middle_kernel, plan, len(sources)),
        grid_spec=pltpu.PrefetchScalarGridSpec(
            num_scalar_prefetch=1,
            grid=(rows // block,),
            in_specs=[
                tile(width),
                tile(width),
                tile(width),
            ]
            + [pl.BlockSpec(vectors[0].shape, lambda i, *_: (0, 0, 0))] * 2
            + [pl.BlockSpec(memory_space=pl.ANY)] * len(sources),
            out_specs=[
                tile(width),
                tile(width),
                tile(width),
                tile(width),
                tile(hidden),
                tile(width),
                tile(hidden),
                tile(hidden),
                tile(width),
                whole,
            ],
            scratch_shapes=[
                pltpu.VMEM((width, width), low),
                pltpu.VMEM((hidden // width, width, width), low),
                pltpu.VMEM((hidden // width, width, width), low),
                pltpu.VMEM((hidden, width), low),
                pltpu.VMEM((block, hidden), full),
                pltpu.VMEM((block, hidden), full),
                pltpu.VMEM((16, width), full),
                pltpu.SemaphoreType.DMA((4,)),
            ],
        ),
        out_shape=[
            shape((rows, width), low),
            shape((rows, width), full),
            shape((rows, width), low),
            shape((rows, width), low),
            shape((rows, hidden), low),
            shape((rows, width), low),
            shape((rows, hidden), low),
            shape((rows, hidden), low),
            shape((rows, width), low),
            shape((8, width), full),
        ],
        compiler_params=params(),
        cost_estimate=cost(53),
        name="middle",
    )(ids, attended, tokens, cot, *vectors, *sources)


def weight_grad_kernel(a_ref, b_ref, o_ref):
    o_ref[...] = dot_tn(a_ref[...], b_ref[...]).astype(o_ref.dtype)


def weight_grad(a, b, tile_a=768, tile_b=768):
    rows, size_a = a.shape
    size_b = b.shape[1]
    return pl.pallas_call(
        weight_grad_kernel,
        grid=(size_a // tile_a, size_b // tile_b),
        in_specs=[
            pl.BlockSpec((rows, tile_a), lambda i, j: (0, i)),
            pl.BlockSpec((rows, tile_b), lambda i, j: (0, j)),
        ],
        out_specs=pl.BlockSpec((tile_a, tile_b), lambda i, j: (i, j)),
        out_shape=shape((size_a, size_b), low),
        compiler_params=params(),
        cost_estimate=cost(9),
        name="weight_grad",
    )(a, b)


def joint_kernel(dq_ref, own_ref, prior_ref, next_ref, cos_ref, sin_ref, dj_ref):
    width = dq_ref.shape[1]
    early = pl.program_id(0) < pl.num_programs(0) // 2
    cosine = cos_ref[...]
    sine = sin_ref[...]
    for at in range(0, width, PAIR):
        lanes = slice(at, at + PAIR)
        near = [
            jnp.where(early, prior_ref[i, :, lanes], next_ref[i, :, lanes]).astype(full)
            for i in range(2)
        ]
        keys = turn_back(own_ref[0, :, lanes] + near[0], cosine, sine)
        dj_ref[:, lanes] = dq_ref[:, lanes]
        dj_ref[:, width + at : width + at + PAIR] = keys.astype(low)
        dj_ref[:, 2 * width + at : 2 * width + at + PAIR] = (
            own_ref[1, :, lanes] + near[1]
        ).astype(low)


def joint(dq, own, prior, following, cosine, sine, at):
    rows, width = dq.shape
    part = prior.shape[2]
    block = TOKEN_BLOCK
    half = prior.shape[1] // block
    inner = pl.BlockSpec((block, PAIR), lambda i: (i + half, 0))
    return pl.pallas_call(
        joint_kernel,
        grid=(rows // block,),
        in_specs=[
            pl.BlockSpec((block, part), lambda i: (i, at)),
            pl.BlockSpec((2, block, part), lambda i: (0, i, at)),
            pl.BlockSpec((2, block, part), lambda i: (0, jnp.minimum(i, half - 1), 0)),
            pl.BlockSpec((2, block, part), lambda i: (0, jnp.maximum(i - half, 0), 0)),
            inner,
            inner,
        ],
        out_specs=pl.BlockSpec((block, 3 * part), lambda i: (i, 0)),
        out_shape=shape((rows, 3 * part), low),
        compiler_params=params(),
        cost_estimate=cost(0.001),
        name="joint",
    )(dq, own, prior, following, cosine, sine)


def input_grad_kernel(dj1_ref, dj2_ref, dz1_ref, weight_ref, out_ref):
    out = dz1_ref[...]
    at = 0
    for ref in (dj1_ref, dj2_ref):
        part = ref.shape[1] // 3
        for i in range(3):
            weight = weight_ref[i, :, at : at + part]
            out = out + dot_nt(ref[:, i * part : (i + 1) * part], weight)
        at += part
    out_ref[...] = out


def input_grad(dj1, dj2, dz1, weights):
    rows, width = dz1.shape
    block = TOKEN_BLOCK
    tile = lambda w: pl.BlockSpec((block, w), lambda i: (i, 0))
    return pl.pallas_call(
        input_grad_kernel,
        grid=(rows // block,),
        in_specs=[
            tile(dj1.shape[1]),
            tile(dj2.shape[1]),
            tile(width),
            pl.BlockSpec((3, width, width), lambda i: (0, 0, 0)),
        ],
        out_specs=tile(width),
        out_shape=shape((rows, width), full),
        compiler_params=params(),
        cost_estimate=cost(0.001),
        name="input_grad",
    )(dj1, dj2, dz1, weights)


def whole_joint_plan(ids, srcs, weight, sem):
    width = weight.shape[1]
    return [
        pltpu.make_async_copy(srcs[0].at[:, i * width : (i + 1) * width], weight.at[i], sem)
        for i in range(3)
    ] + [pltpu.make_async_copy(srcs[1], weight.at[3], sem)]


def whole_middle_plan(ids, srcs, weights, sems):
    out_w, gate_w, up_w, down_w = weights
    parts, _, width = gate_w.shape
    columns = lambda src, dst, sem: [
        pltpu.make_async_copy(src.at[:, i * width : (i + 1) * width], dst.at[i], sem)
        for i in range(parts)
    ]
    return (
        [pltpu.make_async_copy(srcs[0].at[3], out_w, sems.at[0])]
        + columns(srcs[1], gate_w, sems.at[1])
        + columns(srcs[2], up_w, sems.at[2])
        + [pltpu.make_async_copy(srcs[3], down_w, sems.at[3])]
    )


def swap_with(value, place):
    pairs = []
    for r in range(4):
        for z in range(4):
            for c in range(2):
                to_r, to_z, to_c = place(r, z, c)
                pairs.append(((r * 4 + z) * 2 + c, (to_r * 4 + to_z) * 2 + to_c))
    return lax.ppermute(value, ("rep", "fsdp"), pairs)


def over_core(value):
    return swap_with(value, lambda r, z, c: (r, z, 1 - c))


def over_z(value, k):
    return swap_with(value, lambda r, z, c: (r, z ^ k, c))


def over_square_1(value):
    return swap_with(value, lambda r, z, c: (r ^ (1 + c), z, c))


def over_square_2(value):
    return swap_with(value, lambda r, z, c: (r ^ (2 - c), z, c))


def over_z_1(value):
    return swap_with(value, lambda r, z, c: (r, z ^ (2 - c), c))


def over_z_2(value):
    return swap_with(value, lambda r, z, c: (r, z ^ (1 + c), c))


def pieces(ids, srcs):
    r, z, c = ids[0], ids[1], ids[2]
    found = []
    for i in range(2):
        core = (1 - c) if i else c
        bit1, bit2 = 1 + core, 2 - core
        shard, near, far = srcs[i], srcs[2 + i], srcs[4 + i]
        for quarter in range(4):
            found.append((shard.at[quarter], quarter, z, core))
        for ref, base in ((near, r), (far, r ^ bit2)):
            for j in range(2):
                for k in range(1, 4):
                    found.append((ref.at[j, k - 1], base ^ bit1 if j else base, z ^ k, core))
    return found


def piece_joint_plan(ids, srcs, weight, sem):
    size = srcs[0].shape[1]
    copies = []
    for ref, quarter, z, core in pieces(ids, srcs):
        at = pl.multiple_of((2 * z + core) * size, size)
        copies.append(pltpu.make_async_copy(ref, weight.at[quarter, pl.ds(at, size)], sem))
    return copies


def piece_middle_plan(ids, srcs, weights, sems):
    out_w, gate_w, up_w, down_w = weights
    size = srcs[1].shape[1] // 3
    copies = [pltpu.make_async_copy(srcs[0].at[3], out_w, sems.at[0])]
    found = pieces(ids, srcs[1:])
    for i, target in enumerate((gate_w, up_w)):
        for ref, quarter, z, core in found:
            at = pl.multiple_of((2 * z + core) * size, size)
            copies.append(
                pltpu.make_async_copy(
                    ref.at[i * size : (i + 1) * size],
                    target.at[quarter, pl.ds(at, size)],
                    sems.at[1 + i],
                )
            )
    for ref, quarter, z, core in found:
        at = pl.multiple_of(((2 * z + core) * 4 + quarter) * size, size)
        copies.append(
            pltpu.make_async_copy(
                ref.at[2 * size : 3 * size], down_w.at[pl.ds(at, size)], sems.at[3]
            )
        )
    return copies


def position(j, core):
    return jnp.where(core == 0, j, (j & 1) * 2 + (j >> 1))


def put_pieces(ids, block_ref, own_ref, other_ref, first, size):
    z, c = ids[1], ids[2]
    for ref, core in ((own_ref, c), (other_ref, 1 - c)):
        for k in range(4):
            at = pl.multiple_of((2 * (z ^ position(k, core)) + core) * size, 8)
            ref[0, k, first : first + size, :] = block_ref[pl.ds(at, size), :].astype(low)


def gate_up_grad_kernel(
    ids, hidden_ref, dgate_ref, dlift_ref, gains_ref, own_ref, other_ref, block_ref
):
    size = block_ref.shape[0] // 8
    z, c = ids[1], ids[2]
    quarter = ids[0] ^ pl.program_id(0)
    for i, ref in enumerate((dgate_ref, dlift_ref)):
        block_ref[...] = dot_tn(hidden_ref[...], ref[...])
        put_pieces(ids, block_ref, own_ref, other_ref, i * size, size)
    for ref, core in ((own_ref, c), (other_ref, 1 - c)):
        for k in range(4):
            ref[0, k, 2 * size :, :] = jnp.zeros((16, ref.shape[3]), low)
            row = gains_ref[quarter * 8 + 2 * (z ^ position(k, core)) + core]
            ref[0, k, 2 * size :, : row.shape[1]] = row.astype(low)


def grad_specs(size, width):
    own = pl.BlockSpec((1, 4, size, width), lambda j, ids: (position(j, ids[2]), 0, 0, 0))
    other = pl.BlockSpec((1, 4, size, width), lambda j, ids: (position(j, 1 - ids[2]), 0, 0, 0))
    return [own, other], [shape((4, 4, size, width), low)] * 2


def gate_up_grad(ids, hidden_low, dgate, dlift, gains):
    rows, width = hidden_low.shape
    size = width // 8
    out_specs, out_shape = grad_specs(2 * size + 16, width)
    column = pl.BlockSpec((rows, width), lambda j, ids: (0, ids[0] ^ j))
    return pl.pallas_call(
        gate_up_grad_kernel,
        grid_spec=pltpu.PrefetchScalarGridSpec(
            num_scalar_prefetch=1,
            grid=(4,),
            in_specs=[
                pl.BlockSpec((rows, width), lambda j, ids: (0, 0)),
                column,
                column,
                pl.BlockSpec(gains.shape, lambda j, ids: (0, 0, 0)),
            ],
            out_specs=out_specs,
            scratch_shapes=[pltpu.VMEM((width, width), full)],
        ),
        out_shape=out_shape,
        compiler_params=params(),
        cost_estimate=cost(1),
        name="gate_up_grad",
    )(ids, hidden_low, dgate, dlift, gains)


def joint_grad_1_kernel(ids, tok_ref, dj_ref, own_ref, other_ref, block_ref):
    block_ref[...] = dot_tn(tok_ref[...], dj_ref[...])
    put_pieces(ids, block_ref, own_ref, other_ref, 0, block_ref.shape[0] // 8)


def joint_grad_1(ids, tokens, djoint):
    rows, width = tokens.shape
    part = djoint.shape[1] // 4
    out_specs, out_shape = grad_specs(width // 8, part)
    return pl.pallas_call(
        joint_grad_1_kernel,
        grid_spec=pltpu.PrefetchScalarGridSpec(
            num_scalar_prefetch=1,
            grid=(4,),
            in_specs=[
                pl.BlockSpec((rows, width), lambda j, ids: (0, 0)),
                pl.BlockSpec((rows, part), lambda j, ids: (0, ids[0] ^ j)),
            ],
            out_specs=out_specs,
            scratch_shapes=[pltpu.VMEM((width, part), full)],
        ),
        out_shape=out_shape,
        compiler_params=params(),
        cost_estimate=cost(0.001),
        name="joint_grad",
    )(ids, tokens, djoint)


def joint_grad_2_kernel(ids, tok_ref, dj_ref, own_ref, other_ref, block_ref):
    size = block_ref.shape[0] // 8
    z, c = ids[1], ids[2]
    block_ref[...] = dot_tn(tok_ref[...], dj_ref[...])
    for ref, core in ((own_ref, c), (other_ref, 1 - c)):
        for k in range(4):
            at = pl.multiple_of((2 * (z ^ position(k, core)) + core) * size, 8)
            ref[k] = block_ref[pl.ds(at, size), :].astype(low)


def joint_grad_2(ids, tokens, djoint):
    rows, width = tokens.shape
    columns = djoint.shape[1]
    part = columns // 2
    out = pl.BlockSpec((4, width // 8, part), lambda j, ids: (0, 0, j))
    return pl.pallas_call(
        joint_grad_2_kernel,
        grid_spec=pltpu.PrefetchScalarGridSpec(
            num_scalar_prefetch=1,
            grid=(2,),
            in_specs=[
                pl.BlockSpec((rows, width), lambda j, ids: (0, 0)),
                pl.BlockSpec((rows, part), lambda j, ids: (0, j)),
            ],
            out_specs=[out, out],
            scratch_shapes=[pltpu.VMEM((width, part), full)],
        ),
        out_shape=[shape((4, width // 8, columns), low)] * 2,
        compiler_params=params(),
        cost_estimate=cost(0.001),
        name="joint_grad",
    )(ids, tokens, djoint)


def down_out_grad_kernel(product_ref, dfeed_ref, at_ref, db_ref, out_ref, block_ref):
    count, size, _ = out_ref.shape
    step = pl.program_id(0)

    @pl.when(step == 0)
    def _():
        block_ref[...] = dot_tn(at_ref[...], db_ref[...])

    down = dot_tn(product_ref[...], dfeed_ref[...]).astype(low)
    rows = down.shape[0] // count
    for i in range(count):
        at = pl.multiple_of((step * count + i) * (size - rows), 8)
        out_ref[i, :rows] = down[i * rows : (i + 1) * rows]
        out_ref[i, rows:] = block_ref[pl.ds(at, size - rows), :].astype(low)


def down_out_grad(product, dfeed, attended, dbranch, shards):
    rows, hidden = product.shape
    width = dfeed.shape[1]
    size = (hidden + width) // shards
    whole = pl.BlockSpec((rows, width), lambda j: (0, 0))
    steps = shards // 2
    return pl.pallas_call(
        down_out_grad_kernel,
        grid=(steps,),
        in_specs=[
            pl.BlockSpec((rows, hidden // steps), lambda j: (0, j)),
            whole,
            whole,
            whole,
        ],
        out_specs=pl.BlockSpec((2, size, width), lambda j: (j, 0, 0)),
        out_shape=shape((shards, size, width), low),
        scratch_shapes=[pltpu.VMEM((width, width), full)],
        compiler_params=params(),
        cost_estimate=cost(1),
        name="down_out_grad",
    )(product, dfeed, attended, dbranch)


def wide(v):
    return v.astype(full)


def sum_core(own, mate):
    return (wide(own[2:]) + wide(mate[2:])).astype(low)


def sum_square(own, mate, b):
    return (wide(own[1]) + wide(mate[1]) + wide(b[1])).astype(low)


def sum_rest(own, mate, b, d):
    return wide(own[0]) + wide(mate[0]) + wide(b[0]) + wide(d)


def send_z(kept):
    return over_z_1(kept[2:].astype(low))


def send_z_rest(kept, e):
    return over_z_2((kept[1] + wide(e[1])).astype(low))


def sum_z(kept, e, f):
    return (kept[0] + wide(e[0]) + wide(f)).astype(low)


def place(ids, quarter):
    return position(quarter ^ ids[0], ids[2])


def finish_kernel(ids, pair_ref, others_ref, gate_ref, up_ref, vec_ref):
    size, width = gate_ref.shape
    quarter = pl.program_id(0)
    at = place(ids, quarter)

    def put(ref):
        piece = ref[at & 1].astype(full)
        gate_ref[...] = piece[:size]
        up_ref[...] = piece[size : 2 * size]
        vec_ref[0] = piece[2 * size : 2 * size + 8, :PAIR]

    pl.when(at < 2)(lambda: put(pair_ref))
    pl.when(at >= 2)(lambda: put(others_ref))


def finish(ids, pair, others, size):
    width = pair.shape[2]
    whole = pl.BlockSpec(pair.shape, lambda j, ids: (0, 0, 0))
    column = pl.BlockSpec((size, width), lambda j, ids: (0, j))
    gate, up, vectors = pl.pallas_call(
        finish_kernel,
        grid_spec=pltpu.PrefetchScalarGridSpec(
            num_scalar_prefetch=1,
            grid=(4,),
            in_specs=[whole, whole],
            out_specs=[column, column, pl.BlockSpec((1, 8, PAIR), lambda j, ids: (j, 0, 0))],
        ),
        out_shape=[shape((size, 4 * width), full)] * 2 + [shape((4, 8, PAIR), full)],
        compiler_params=params(),
        cost_estimate=cost(3),
        name="finish",
    )(ids, pair, others)
    return gate, up, vectors[:, 0, :size]


def finish_joint_kernel(ids, near_ref, far_ref, out_ref):
    width = out_ref.shape[1] // 3
    part = (near_ref.shape[1] - width) // 2
    first = 4 * part // 3
    for quarter in range(4):
        at = place(ids, quarter)
        halves = [
            jnp.where(at < 2, near_ref[:, i : i + part], far_ref[:, i : i + part])
            for i in (width, width + part)
        ]
        piece = jnp.where((at & 1) == 0, *halves).astype(full)
        for start in range(0, part, PAIR):
            which, column = divmod(quarter * part + start, first)
            column += which * width
            out_ref[:, column : column + PAIR] = piece[:, start : start + PAIR]
    rest = near_ref[:, :width].astype(full) + far_ref[:, :width].astype(full)
    rest = rest.astype(low).astype(full)
    second = width - first
    for which in range(3):
        column = which * width + first
        out_ref[:, column : column + second] = rest[:, which * second : (which + 1) * second]


def finish_joint(ids, near, far):
    size, columns = near.shape
    width = columns // 2
    whole = pl.BlockSpec(near.shape, lambda j, ids: (0, 0))
    return pl.pallas_call(
        finish_joint_kernel,
        grid_spec=pltpu.PrefetchScalarGridSpec(
            num_scalar_prefetch=1,
            grid=(1,),
            in_specs=[whole, whole],
            out_specs=pl.BlockSpec((size, 3 * width), lambda j, ids: (0, 0)),
        ),
        out_shape=shape((size, 3 * width), full),
        compiler_params=params(),
        cost_estimate=cost(2),
        name="finish_joint",
    )(ids, near, far)


def shards(
    custom,
    tokens,
    lengths,
    qkv_weight,
    out_weight,
    gate_weight,
    up_weight,
    down_weight,
    norm1_gain,
    norm1_bias,
    norm2_gain,
    norm2_bias,
    cotangent,
):
    rows, width = tokens.shape
    hidden = gate_weight.shape[1]
    size = lax.axis_size("fsdp")
    me = lax.axis_index("fsdp")
    up = [(i, i + 1) for i in range(size - 1)]
    down = [(i + 1, i) for i in range(size - 1)]
    r = lax.axis_index("rep")
    z, c = me // 2, me % 2
    ids = jnp.stack([r, z, c]).astype(jnp.int32)
    vectors = jnp.stack([norm1_gain, norm1_bias, norm2_gain, norm2_bias]).astype(low)

    before = tokens[rows - REACH :]
    behind = tokens[:REACH]
    swap_edges = lambda last, first: (
        lax.ppermute(last, "fsdp", up),
        lax.ppermute(first, "fsdp", down),
    )
    if custom:
        part = qkv_weight.shape[0]
        columns = lambda w: jnp.swapaxes(w.astype(low).reshape(part, -1, width), 0, 1)
        column = lambda w, i: lax.dynamic_slice_in_dim(w, i * width, width, 1).astype(low)
        mine = jnp.where(
            r == 3, out_weight.astype(low), column(qkv_weight, jnp.minimum(r, 2))
        )
        arrived = [over_z(mine, k) for k in (1, 2, 3)]
        before, behind = swap_edges(before, behind)
        mine_2 = jnp.concatenate(
            [
                column(gate_weight, r),
                column(up_weight, r),
                lax.dynamic_slice_in_dim(down_weight, r * part, part, 0).astype(low),
                jnp.pad(vectors, ((0, 12), (0, width - part))),
            ]
        )
        shard_1 = jnp.concatenate([columns(qkv_weight), out_weight.astype(low)[None]])
        shard_2 = jnp.concatenate(
            [
                columns(gate_weight),
                columns(up_weight),
                down_weight.astype(low).reshape(4, part, width),
            ],
            axis=1,
        )
        own_1 = jnp.stack(after(tuple(arrived), mine_2, shard_1))
        mate_shard_1 = over_core(after(shard_1, own_1))
        along_z = [[2 * i + j for i in range(size // 2)] for j in range(2)]
        arrived_2 = lax.all_gather(
            after(mine_2, before, behind, own_1), "fsdp", axis=0, axis_index_groups=along_z
        )
        other_1 = over_square_1(own_1)
        near_1 = jnp.stack([own_1, other_1])
        far_1 = over_square_2(near_1)
        mate_near_1 = over_core(near_1)
        joint_sources = [shard_1, mate_shard_1, near_1, mate_near_1, far_1]
        joint_plan = piece_joint_plan
    else:
        before, behind = swap_edges(before, behind)
        gather = lambda w: lax.all_gather(w.astype(low), "fsdp", axis=0, tiled=True)
        joint_sources = [gather(qkv_weight), gather(out_weight)]
        joint_plan = whole_joint_plan
        middle_sources = [gather(w) for w in (gate_weight, up_weight, down_weight)]
        vectors = lax.all_gather(vectors, "fsdp", axis=1, tiled=True)
        found = [jnp.pad(vectors, ((0, 12), (0, 0)))[None]] * 2
        middle_plan = whole_middle_plan

    doc_lengths = lengths[0]
    ends = jnp.cumsum(doc_lengths)
    index = me * rows - REACH + jnp.arange(rows + 2 * REACH, dtype=jnp.int32)
    if custom:
        index = after(index, near_1)
    passed = (index[:, None] >= ends[None, :]).astype(jnp.int32)
    starts = jnp.sum(passed * doc_lengths[None, :], axis=1)
    cosine, sine = tables(index - starts)
    if custom:
        mate_far_1 = over_core(after(far_1, cosine))
        joint_sources.append(mate_far_1)
        mate_shard_2 = over_core(after(shard_2, far_1))
    own_starts = starts[REACH : REACH + rows]
    own_index = index[REACH : REACH + rows]
    stops = jnp.min(
        jnp.where(ends[None, :] > own_index[:, None], ends[None, :], size * rows), axis=1
    )
    base = me * rows - REACH
    bounds = jnp.stack(
        [
            jnp.maximum(own_starts, own_index - REACH) - base,
            jnp.minimum(stops, own_index + REACH + 1) - base,
        ]
    ).astype(jnp.int32)

    queries, keys, values, joint_weights = project(
        joint_plan, ids, before, tokens, behind, cosine, sine, joint_sources
    )
    given = (queries, keys, values)
    if custom:
        arrived_2 = after(arrived_2, queries)
        own_2 = jnp.stack(
            [
                lax.dynamic_slice(arrived_2, (z ^ k, 0, 0), (1, 3 * part, width))[0]
                for k in (1, 2, 3)
            ]
        )
        found = arrived_2[:, 3 * part :, :PAIR]
        other_2 = over_square_1(own_2)
        mate_found = over_core(found)
        done = attend(after(bounds, own_2, found, mate_shard_2), *given, 0, 2)
        near_2 = jnp.stack([own_2, after(other_2, done[1], mate_found)])
        far_2 = over_square_2(near_2)
        mate_near_2 = over_core(near_2)
        done = attend(after(bounds, near_2), *given, 2, 2, done)
        attended, lse = attend(bounds, *given, 4, 2, done)
        mate_far_2 = over_core(after(far_2, lse, mate_near_2))
        middle_sources = [shard_2, mate_shard_2, near_2, mate_near_2, far_2, mate_far_2]
        middle_plan = piece_middle_plan
        found = [found, mate_found]
    else:
        done = None
        for first in (0, 2, 4):
            done = attend(bounds, *given, first, 2, done)
        attended, lse = done
    result, dz1, dattended, hidden_low, product, dfeed, dgate, dlift, dbranch, gains = middle(
        middle_plan,
        ids,
        attended,
        tokens,
        cotangent,
        found,
        [joint_weights, *middle_sources],
        hidden,
    )
    gains = gains[:4]
    given = (queries, keys, values, attended, dattended, lse)
    given += (cosine[REACH : REACH + rows], sine[REACH : REACH + rows])
    spread = lambda g: lax.psum_scatter(g, "fsdp", scatter_dimension=0, tiled=True)
    if custom:
        gains = jnp.pad(gains.reshape(32, 1, part), ((0, 0), (0, 15), (0, PAIR - part)))
        grad_down = down_out_grad(product, dfeed, attended, dbranch, size)
        share_down = spread(grad_down)[0]
        own, other = gate_up_grad(ids, after(hidden_low, grad_down), dgate, dlift, gains)
        mate = over_core(other)
        done = attend_back(after(bounds, own), *given, 0, 2, (0, 4))
        sent = sum_core(own, after(mate, done[0]))
        b = over_square_2(sent)
        dq, dkv, to_prior, to_next = attend_back(
            after(bounds, sent), *given, 2, 2, (0, 4), done
        )
        edges_1 = swap_edges(to_next, to_prior)
        dq, dkv, to_prior, to_next = attend_back(
            after(bounds, dq), *given, 4, 2, (4, 2), (dq, dkv)
        )
        edges_1 = after(edges_1, dq)
        sent = sum_square(own, mate, after(b, *edges_1))
        d = over_square_1(sent)
        edges_2 = swap_edges(to_next, to_prior)
        dj1 = joint(after(dq, sent), dkv, *edges_1, cosine, sine, 0)
        kept = sum_rest(own, mate, b, after(d, dj1))
        sent = kept[2:].astype(low)
        e = over_z_1(sent)
        share_down = after(share_down, dj1)
        down_1 = over_square_1(share_down)
        edges_2 = after(edges_2, dj1)
        own_1, other_1 = joint_grad_1(ids, tokens, after(dj1, sent, share_down, *edges_2))
        mate_1 = over_core(other_1)
        share_down = (wide(share_down) + wide(after(down_1, own_1))).astype(low)
        dj2 = joint(after(dq, own_1, share_down), dkv, *edges_2, cosine, sine, 2)
        sent_1 = sum_core(own_1, after(mate_1, dj2, e))
        b_1 = over_square_2(sent_1)
        f = send_z_rest(kept, after(e, dj2))
        own_2, other_2 = joint_grad_2(ids, tokens, after(dj2, sent_1))
        mate_2 = over_core(other_2)
        sent_1 = sum_square(own_1, mate_1, after(b_1, own_2))
        d_1 = over_square_1(sent_1)
        rest = wide(own_2) + wide(after(mate_2, sent_1))
        kept_1 = jnp.concatenate(
            [rest, sum_rest(own_1, mate_1, b_1, after(d_1, rest))], axis=2
        )
        e_1 = send_z(kept_1)
        mine = sum_z(kept, e, after(f, kept_1))
        gate_1 = over_square_1(mine)
        down_2 = over_square_2(after(share_down, kept_1))
        grad_tokens = input_grad(after(dj1, kept_1, mine), dj2, dz1, joint_weights)
        f_1 = send_z_rest(kept_1, after(e_1, grad_tokens))
        pair = jnp.stack([mine, after(gate_1, f_1)])
        others = over_square_2(pair)
        down_sum = (wide(share_down) + wide(after(down_2, pair))).astype(low)
        mine = sum_z(kept_1, e_1, after(f_1, down_sum))
        got = over_square_1(mine)
        gate_sum, up_sum, vector_sum = finish(ids, after(pair, mine), others, part)
        got = after(got, gate_sum)
        pair = jnp.concatenate(
            [
                (wide(mine[:, :width]) + wide(got[:, :width])).astype(low),
                mine[:, width:],
                got[:, width:],
            ],
            axis=1,
        )
        joint_sum = finish_joint(ids, pair, over_square_2(pair))
        down_sum = wide(down_sum)
        down_rows = down_weight.shape[0]
        summed = (
            joint_sum,
            down_sum[down_rows:],
            gate_sum,
            up_sum,
            down_sum[:down_rows],
            vector_sum,
        )
    else:
        share_down = spread(weight_grad(product, dfeed))
        share_gate = spread(weight_grad(hidden_low, dgate))
        share_up = spread(weight_grad(hidden_low, dlift))
        share_out = spread(weight_grad(attended, dbranch))
        share_gains = lax.psum_scatter(gains, "fsdp", scatter_dimension=1, tiled=True)
        dq, dkv, to_prior, to_next = attend_back(bounds, *given, 0, 4, (0, 4))
        edges_1 = swap_edges(to_next, to_prior)
        dq, dkv, to_prior, to_next = attend_back(bounds, *given, 4, 2, (4, 2), (dq, dkv))
        edges_2 = swap_edges(to_next, to_prior)
        dj1 = joint(dq, dkv, *edges_1, cosine, sine, 0)
        dj2 = joint(dq, dkv, *edges_2, cosine, sine, 2)
        share_1 = spread(weight_grad(tokens, dj1)).reshape(-1, 3, dj1.shape[1] // 3)
        share_2 = spread(weight_grad(tokens, dj2)).reshape(-1, 3, dj2.shape[1] // 3)
        share_qkv = jnp.concatenate([share_1, share_2], axis=2).reshape(-1, 3 * width)
        grad_tokens = input_grad(dj1, dj2, dz1, joint_weights)
        summed = lax.psum(
            tuple(
                s.astype(full)
                for s in (share_qkv, share_out, share_gate, share_up, share_down, share_gains)
            ),
            "rep",
        )
    return (result, grad_tokens, *summed[:5], *(summed[5][i] for i in range(4)))


def solution(mesh):
    rows = P(("rep", "fsdp"), None)
    matrix = P("fsdp", None)
    vector = P("fsdp")
    custom = (mesh.shape["rep"], mesh.shape["fsdp"]) == (4, 8)
    return jax.shard_map(
        functools.partial(shards, custom and not FORCE_WHOLE),
        mesh=mesh,
        in_specs=(rows, P("rep", None)) + (matrix,) * 5 + (vector,) * 4 + (rows,),
        out_specs=(rows, rows) + (matrix,) * 5 + (vector,) * 4,
        check_vma=False,
    )
```

```python
import functools
import math

import jax
import jax.numpy as jnp
from jax import lax
from jax.experimental import pallas as pl
from jax.experimental.pallas import tpu as pltpu
from jax.sharding import PartitionSpec as P

HEADS = 12
WINDOW = 1024
REACH = WINDOW // 2
HEAD = 64
PAIR = 2 * HEAD
QUERY_BLOCK = 256
TOKEN_BLOCK = 256
FORCE_WHOLE = False
VMEM = 56 * 1024 * 1024

epsilon = 1e-06
rope_base = 1000.0
masked_score = -1e30
low = jnp.bfloat16
full = jnp.float32


def dot_nn(a, b):
    return lax.dot_general(a, b, (((1,), (0,)), ((), ())), preferred_element_type=full)


def dot_nt(a, b):
    return lax.dot_general(a, b, (((1,), (1,)), ((), ())), preferred_element_type=full)


def dot_tn(a, b):
    return lax.dot_general(a, b, (((0,), (0,)), ((), ())), preferred_element_type=full)


def params():
    return pltpu.CompilerParams(vmem_limit_bytes=VMEM)


def after(value, *others):
    return lax.optimization_barrier((value, *others))[0]


def shape(dims, dtype):
    return jax.ShapeDtypeStruct(dims, dtype)


def cost(micros):
    return pl.CostEstimate(flops=int(micros * 0.575e9), bytes_accessed=1, transcendentals=0)


def tables(position):
    lane = jnp.arange(PAIR, dtype=jnp.int32) % HEAD
    half = HEAD // 2
    frequency = rope_base ** (-2.0 * (lane % half).astype(full) / HEAD)
    angle = position.astype(full)[:, None] * frequency[None, :]
    sign = jnp.where(lane < half, -1.0, 1.0).astype(full)
    return jnp.cos(angle), jnp.sin(angle) * sign[None, :]


def partner(x):
    half = HEAD // 2
    lane = lax.broadcasted_iota(jnp.int32, x.shape, 1) % HEAD
    return jnp.where(lane < half, pltpu.roll(x, PAIR - half, 1), pltpu.roll(x, half, 1))


def turn(x, cosine, sine):
    return x * cosine + partner(x) * sine


def turn_back(x, cosine, sine):
    return x * cosine - partner(x) * sine


def project_kernel(
    plan, sources, first, count, ids, before_ref, tok_ref, behind_ref, cos_ref, sin_ref, *refs
):
    srcs = refs[:sources]
    q_ref, k_ref, v_ref, weight, sems = refs[sources:]
    step = pl.program_id(0)

    @pl.when(step == 0)
    def _():
        for copy in plan(ids, srcs, weight, sems.at[0]):
            copy.start()
        pltpu.make_async_copy(weight, weight, sems.at[0]).wait()

    width = tok_ref.shape[1]
    rows = jnp.where(
        step < first,
        before_ref[...],
        jnp.where(step < first + count, tok_ref[...], behind_ref[...]),
    )
    cosine = cos_ref[...]
    sine = sin_ref[...]
    keys = dot_nn(rows, weight[1])
    for at in range(0, width, PAIR):
        k_ref[:, at : at + PAIR] = turn(keys[:, at : at + PAIR], cosine, sine).astype(low)
    v_ref[...] = dot_nn(rows, weight[2]).astype(low)

    @pl.when((step >= first) & (step < first + count))
    def _():
        queries = dot_nn(rows, weight[0])
        for at in range(0, width, PAIR):
            turned = turn(queries[:, at : at + PAIR], cosine, sine).astype(low)
            q_ref[:, at : at + PAIR] = (turned.astype(full) * (1.0 / math.sqrt(HEAD))).astype(low)


def project(plan, ids, before, tokens, behind, cosine, sine, sources):
    rows, width = tokens.shape
    ext = rows + 2 * before.shape[0]
    block = 2 * TOKEN_BLOCK
    first, count = before.shape[0] // block, rows // block
    tile = lambda w: pl.BlockSpec((block, w), lambda i, *_: (i, 0))
    inner = pl.BlockSpec((block, width), lambda i, *_: (jnp.clip(i - first, 0, count - 1), 0))
    return pl.pallas_call(
        functools.partial(project_kernel, plan, len(sources), first, count),
        grid_spec=pltpu.PrefetchScalarGridSpec(
            num_scalar_prefetch=1,
            grid=(ext // block,),
            in_specs=[
                pl.BlockSpec((block, width), lambda i, *_: (jnp.minimum(i, first - 1), 0)),
                inner,
                pl.BlockSpec(
                    (block, width), lambda i, *_: (jnp.maximum(i - first - count, 0), 0)
                ),
                tile(PAIR),
                tile(PAIR),
            ]
            + [pl.BlockSpec(memory_space=pl.ANY)] * len(sources),
            out_specs=[
                inner,
                tile(width),
                tile(width),
                pl.BlockSpec((4, width, width), lambda i, *_: (0, 0, 0)),
            ],
            scratch_shapes=[pltpu.SemaphoreType.DMA((1,))],
        ),
        out_shape=[
            shape((rows, width), low),
            shape((ext, width), low),
            shape((ext, width), low),
            shape((4, width, width), low),
        ],
        compiler_params=params(),
        cost_estimate=cost(2),
        name="project",
    )(ids, before, tokens, behind, cosine, sine, *sources)


def fill_bias(bounds_ref, bias_ref, blocks, span):
    for b in range(blocks):
        lo = bounds_ref[0:1, b * QUERY_BLOCK : (b + 1) * QUERY_BLOCK] - b * QUERY_BLOCK
        hi = bounds_ref[1:2, b * QUERY_BLOCK : (b + 1) * QUERY_BLOCK] - b * QUERY_BLOCK
        at = lax.broadcasted_iota(jnp.int32, (span, QUERY_BLOCK), 0)
        bias_ref[b] = jnp.where((at >= lo) & (at < hi), 0.0, masked_score)


def only(x, head):
    lane = lax.broadcasted_iota(jnp.int32, x.shape, 1)
    return jnp.where((lane >= HEAD) if head else (lane < HEAD), x, jnp.zeros_like(x))


def attend_kernel(chunk, bounds_ref, q_ref, k_ref, v_ref, *refs):
    o_ref, lse_ref, bias_ref, vt_ref, s_ref = refs[-5:]
    rows = q_ref.shape[0]
    block = QUERY_BLOCK
    blocks = rows // block
    span = k_ref.shape[0] - rows + block

    @pl.when(pl.program_id(0) == 0)
    def _():
        fill_bias(bounds_ref, bias_ref, blocks, span)

    vt_ref[...] = v_ref[...].T
    chunks = [(c, min(chunk, span - c)) for c in range(0, span, chunk)]
    steps = [(b, h) for b in range(blocks) for h in range(2)]
    fold = lambda x, by: by(x.reshape(x.shape[0] // 64, 64, block), axis=0)
    add = lambda old, new: new if old is None else old + new

    def begin(i):
        b, h = steps[i]
        return {"query": only(q_ref[b * block : (b + 1) * block, :], h), "top": None}

    def score(i, c, n, state):
        b, _ = steps[i]
        s = dot_nt(k_ref[b * block + c : b * block + c + n, :], state["query"])
        s = s + bias_ref[b, c : c + n, :]
        s_ref[i % 2, c : c + n, :] = s
        top = fold(s, jnp.max)
        state["top"] = top if state["top"] is None else jnp.maximum(state["top"], top)

    def weigh(i, c, n, state):
        b, h = steps[i]
        e = jnp.exp(s_ref[i % 2, c : c + n, :] - state["peak"])
        state["total"] = add(state.get("total"), fold(e, jnp.sum))
        lanes = slice(b * block + c, b * block + c + n)
        mixed = dot_nn(vt_ref[h * HEAD : (h + 1) * HEAD, lanes], e.astype(low))
        state["mixed"] = add(state.get("mixed"), mixed)

    state = begin(0)
    for c, n in chunks:
        score(0, c, n, state)
    out = []
    for i, (b, h) in enumerate(steps):
        state["peak"] = jnp.max(state["top"], axis=0, keepdims=True)
        following = begin(i + 1) if i + 1 < len(steps) else None
        for c, n in chunks:
            if following is not None:
                score(i + 1, c, n, following)
            weigh(i, c, n, state)
        total = jnp.sum(state["total"], axis=0, keepdims=True)
        out.append(state["mixed"] / total)
        at = slice(b * block, (b + 1) * block)
        lse_ref[0, h : h + 1, at] = state["peak"] + jnp.log(total)
        if h == 1:
            o_ref[at, :] = jnp.concatenate(out, axis=0).T.astype(low)
            out = []
        state = following


def attend(bounds, q, k, v, first, pairs, before=None, chunk=640):
    rows, width = q.shape
    ext = k.shape[0]
    blocks = rows // QUERY_BLOCK
    span = ext - rows + QUERY_BLOCK
    own = pl.BlockSpec((rows, PAIR), lambda p: (0, p + first))
    wide = pl.BlockSpec((ext, PAIR), lambda p: (0, p + first))
    before = () if before is None else tuple(before)
    return pl.pallas_call(
        functools.partial(attend_kernel, chunk),
        grid=(pairs,),
        in_specs=[pl.BlockSpec((2, rows), lambda p: (0, 0)), own, wide, wide]
        + [pl.BlockSpec(memory_space=pl.ANY)] * len(before),
        out_specs=[own, pl.BlockSpec((1, 2, rows), lambda p: (p + first, 0, 0))],
        out_shape=[shape((rows, width), low), shape((width // PAIR, 2, rows), full)],
        input_output_aliases={4 + i: i for i in range(len(before))},
        scratch_shapes=[
            pltpu.VMEM((blocks, span, QUERY_BLOCK), full),
            pltpu.VMEM((PAIR, ext), low),
            pltpu.VMEM((2, span, QUERY_BLOCK), full),
        ],
        compiler_params=params(),
        cost_estimate=cost(2 * pairs),
        name="attend",
    )(bounds, q, k, v, *before)


def attend_back_kernel(
    chunk,
    bounds_ref,
    q_ref,
    k_ref,
    v_ref,
    o_ref,
    do_ref,
    lse_ref,
    *refs,
):
    cos_ref, sin_ref = refs[:2]
    dq_ref, own_ref, prior_ref, next_ref = refs[-10:-6]
    bias_ref, kt_ref, dk_ref, dv_ref, p_ref, ds_ref = refs[-6:]
    rows = q_ref.shape[0]
    ext = k_ref.shape[0]
    block = QUERY_BLOCK
    blocks = rows // block
    reach = (ext - rows) // 2
    span = ext - rows + block

    @pl.when(pl.program_id(0) == 0)
    def _():
        fill_bias(bounds_ref, bias_ref, blocks, span)

    kt_ref[...] = k_ref[...].T
    dk_ref[...] = jnp.zeros_like(dk_ref)
    dv_ref[...] = jnp.zeros_like(dv_ref)
    chunks = [(c, min(chunk, span - c)) for c in range(0, span, chunk)]

    def begin(b):
        at = slice(b * block, (b + 1) * block)
        q = q_ref[at, :]
        do = do_ref[at, :]
        product = (do.astype(full) * o_ref[at, :].astype(full)).T
        heads = range(2)
        return {
            "query": [only(q, h) for h in heads],
            "grad": [only(do, h) for h in heads],
            "delta": [
                jnp.sum(product[h * HEAD : (h + 1) * HEAD], axis=0, keepdims=True) for h in heads
            ],
            "lse": [lse_ref[0, h : h + 1, at] for h in heads],
            "dq": [None, None],
        }

    def score(b, h, c, n, state):
        rows_of = slice(b * block + c, b * block + c + n)
        lanes = slice(h * block, (h + 1) * block)
        s = dot_nt(k_ref[rows_of, :], state["query"][h]) + bias_ref[b, c : c + n, :]
        p = jnp.exp(s - state["lse"][h])
        dp = dot_nt(v_ref[rows_of, :], state["grad"][h])
        p_ref[b % 2, c : c + n, lanes] = p.astype(low)
        ds_ref[b % 2, c : c + n, lanes] = (p * (dp - state["delta"][h])).astype(low)

    def spread(b, h, c, n, state):
        rows_of = slice(b * block + c, b * block + c + n)
        if h == 0:
            both = jnp.concatenate(state["grad"], axis=0)
            dv_ref[rows_of, :] += dot_nn(p_ref[b % 2, c : c + n, :], both)
        else:
            both = jnp.concatenate(state["query"], axis=0)
            dk_ref[rows_of, :] += dot_nn(ds_ref[b % 2, c : c + n, :], both)
        ds = ds_ref[b % 2, c : c + n, h * block : (h + 1) * block]
        t = dot_nn(kt_ref[h * HEAD : (h + 1) * HEAD, rows_of], ds)
        state["dq"][h] = t if state["dq"][h] is None else state["dq"][h] + t

    state = begin(0)
    for h in range(2):
        for c, n in chunks:
            score(0, h, c, n, state)
    for b in range(blocks):
        following = begin(b + 1) if b + 1 < blocks else None
        for h in range(2):
            for c, n in chunks:
                if following is not None:
                    score(b + 1, h, c, n, following)
                spread(b, h, c, n, state)
        at = slice(b * block, (b + 1) * block)
        turned = turn_back(jnp.concatenate(state["dq"], axis=0).T, cos_ref[at, :], sin_ref[at, :])
        dq_ref[at, :] = (turned * (1.0 / math.sqrt(HEAD))).astype(low)
        state = following
    for i, ref in enumerate((dk_ref, dv_ref)):
        prior_ref[i] = ref[:reach, :].astype(low)
        own_ref[i] = ref[reach : reach + rows, :]
        next_ref[i] = ref[reach + rows :, :].astype(low)


def attend_back(bounds, q, k, v, o, do, lse, cosine, sine, first, pairs, halo, before=None, chunk=256):
    rows, width = q.shape
    ext = k.shape[0]
    blocks = rows // QUERY_BLOCK
    reach = (ext - rows) // 2
    span = ext - rows + QUERY_BLOCK
    halo_first, halo_pairs = halo
    before = () if before is None else tuple(before)
    own = pl.BlockSpec((rows, PAIR), lambda p: (0, p + first))
    wide = pl.BlockSpec((ext, PAIR), lambda p: (0, p + first))
    edge = pl.BlockSpec((2, reach, PAIR), lambda p: (0, 0, p + first - halo_first))
    return pl.pallas_call(
        functools.partial(attend_back_kernel, chunk),
        grid=(pairs,),
        in_specs=[
            pl.BlockSpec((2, rows), lambda p: (0, 0)),
            own,
            wide,
            wide,
            own,
            own,
            pl.BlockSpec((1, 2, rows), lambda p: (p + first, 0, 0)),
            pl.BlockSpec((rows, PAIR), lambda p: (0, 0)),
            pl.BlockSpec((rows, PAIR), lambda p: (0, 0)),
        ]
        + [pl.BlockSpec(memory_space=pl.ANY)] * len(before),
        out_specs=[
            own,
            pl.BlockSpec((2, rows, PAIR), lambda p: (0, 0, p + first)),
            edge,
            edge,
        ],
        out_shape=[
            shape((rows, width), low),
            shape((2, rows, width), full),
            shape((2, reach, halo_pairs * PAIR), low),
            shape((2, reach, halo_pairs * PAIR), low),
        ],
        input_output_aliases={9 + i: i for i in range(len(before))},
        scratch_shapes=[
            pltpu.VMEM((blocks, span, QUERY_BLOCK), full),
            pltpu.VMEM((PAIR, ext), low),
            pltpu.VMEM((ext, PAIR), full),
            pltpu.VMEM((ext, PAIR), full),
            pltpu.VMEM((2, span, 2 * QUERY_BLOCK), low),
            pltpu.VMEM((2, span, 2 * QUERY_BLOCK), low),
        ],
        compiler_params=params(),
        cost_estimate=cost(9 * pairs),
        name="attend_back",
    )(bounds, q, k, v, o, do, lse, cosine, sine, *before)


def mean(x):
    return jnp.mean(x, axis=-1, keepdims=True)


def norm(x):
    centred = x - mean(x)
    inverse = lax.rsqrt(mean(centred * centred) + epsilon)
    return centred * inverse, inverse


def norm_back(scaled, normed, inverse):
    return inverse * (scaled - mean(scaled) - normed * mean(scaled * normed))


def gather_vectors(ids, vec_ref, width):
    count = vec_ref.shape[0]
    if count == 1:
        return vec_ref[0].astype(full)[:8]
    size = width // (2 * count)
    row = lax.broadcasted_iota(jnp.int32, (PAIR, width), 0)
    column = lax.broadcasted_iota(jnp.int32, (PAIR, width), 1)
    half = lax.broadcasted_iota(jnp.int32, (16, PAIR), 0) // 8
    out = jnp.zeros((16, width), full)
    for at in range(count):
        found = vec_ref[at].astype(full)
        for i in range(2):
            f = 2 * at + (ids[2] ^ i)
            place = ((column - f * size == row) & (row < size)).astype(full).astype(low)
            out = out + dot_nn(jnp.where(half == i, found, 0.0).astype(low), place)
    return out[:8] + out[8:]


def middle_kernel(plan, sources, ids, at_ref, tok_ref, cot_ref, *refs):
    vec_ref, refs = refs[0], refs[1:]
    srcs = refs[:sources]
    (
        out_ref,
        dz1_ref,
        da_ref,
        hidden_ref,
        product_ref,
        dfeed_ref,
        dgate_ref,
        dlift_ref,
        dbranch_ref,
        gains_ref,
        out_w,
        gate_w,
        up_w,
        down_w,
        lift_factor,
        gate_factor,
        vectors,
        sems,
    ) = refs[sources:]
    step = pl.program_id(0)
    weights = (out_w, gate_w, up_w, down_w)

    @pl.when(step == 0)
    def _():
        for copy in plan(ids, srcs, weights, sems):
            copy.start()
        gains_ref[...] = jnp.zeros_like(gains_ref)

    def ready(*which):
        @pl.when(step == 0)
        def _():
            for i in which:
                pltpu.make_async_copy(weights[i], weights[i], sems.at[i]).wait()

    parts, _, width = gate_w.shape

    @pl.when(step == 0)
    def _():
        vectors[...] = gather_vectors(ids, vec_ref, width)

    gain1, bias1, gain2, bias2 = (vectors[i : i + 1] for i in range(4))
    ready(0)
    normed1, inverse1 = norm(tok_ref[...].astype(full) + dot_nn(at_ref[...], out_w[...]))
    hidden = normed1 * gain1 + bias1
    hidden_low = hidden.astype(low)
    hidden_ref[...] = hidden_low
    ready(1, 2, 3)
    feed = None
    for part in range(parts):
        at = slice(part * width, (part + 1) * width)
        gate = dot_nn(hidden_low, gate_w[part])
        lift = dot_nn(hidden_low, up_w[part])
        sigma = jax.nn.sigmoid(gate)
        opened = gate * sigma
        product = (opened * lift).astype(low)
        product_ref[:, at] = product
        lift_factor[:, at] = opened
        gate_factor[:, at] = lift * sigma * (1.0 + gate * (1.0 - sigma))
        term = dot_nn(product, down_w[at, :])
        feed = term if feed is None else feed + term
    normed2, inverse2 = norm(hidden + feed)
    out_ref[...] = (normed2 * gain2 + bias2).astype(low)
    cot = cot_ref[...].astype(full)
    gains_ref[2:3] += jnp.sum(cot * normed2, axis=0, keepdims=True)
    gains_ref[3:4] += jnp.sum(cot, axis=0, keepdims=True)
    grad = norm_back(cot * gain2, normed2, inverse2)
    dfeed = grad.astype(low)
    dfeed_ref[...] = dfeed
    for part in range(parts):
        at = slice(part * width, (part + 1) * width)
        dproduct = dot_nt(dfeed, down_w[at, :])
        dgate = (dproduct * gate_factor[:, at]).astype(low)
        dlift = (dproduct * lift_factor[:, at]).astype(low)
        dgate_ref[:, at] = dgate
        dlift_ref[:, at] = dlift
        grad = grad + dot_nt(dgate, gate_w[part]) + dot_nt(dlift, up_w[part])
    gains_ref[0:1] += jnp.sum(grad * normed1, axis=0, keepdims=True)
    gains_ref[1:2] += jnp.sum(grad, axis=0, keepdims=True)
    grad = norm_back(grad * gain1, normed1, inverse1)
    dz1_ref[...] = grad
    dbranch = grad.astype(low)
    dbranch_ref[...] = dbranch
    da_ref[...] = dot_nt(dbranch, out_w[...]).astype(low)


def middle(plan, ids, attended, tokens, cot, vectors, sources, hidden):
    rows, width = tokens.shape
    block = TOKEN_BLOCK
    tile = lambda w: pl.BlockSpec((block, w), lambda i, *_: (i, 0))
    whole = pl.BlockSpec((8, width), lambda i, *_: (0, 0))
    return pl.pallas_call(
        functools.partial(middle_kernel, plan, len(sources)),
        grid_spec=pltpu.PrefetchScalarGridSpec(
            num_scalar_prefetch=1,
            grid=(rows // block,),
            in_specs=[
                tile(width),
                tile(width),
                tile(width),
            ]
            + [pl.BlockSpec(vectors.shape, lambda i, *_: (0, 0, 0))]
            + [pl.BlockSpec(memory_space=pl.ANY)] * len(sources),
            out_specs=[
                tile(width),
                tile(width),
                tile(width),
                tile(width),
                tile(hidden),
                tile(width),
                tile(hidden),
                tile(hidden),
                tile(width),
                whole,
            ],
            scratch_shapes=[
                pltpu.VMEM((width, width), low),
                pltpu.VMEM((hidden // width, width, width), low),
                pltpu.VMEM((hidden // width, width, width), low),
                pltpu.VMEM((hidden, width), low),
                pltpu.VMEM((block, hidden), full),
                pltpu.VMEM((block, hidden), full),
                pltpu.VMEM((8, width), full),
                pltpu.SemaphoreType.DMA((4,)),
            ],
        ),
        out_shape=[
            shape((rows, width), low),
            shape((rows, width), full),
            shape((rows, width), low),
            shape((rows, width), low),
            shape((rows, hidden), low),
            shape((rows, width), low),
            shape((rows, hidden), low),
            shape((rows, hidden), low),
            shape((rows, width), low),
            shape((8, width), full),
        ],
        compiler_params=params(),
        cost_estimate=cost(53),
        name="middle",
    )(ids, attended, tokens, cot, vectors, *sources)


def weight_grad_kernel(a_ref, b_ref, o_ref):
    o_ref[...] = dot_tn(a_ref[...], b_ref[...]).astype(o_ref.dtype)


def weight_grad(a, b, tile_a=768, tile_b=768):
    rows, size_a = a.shape
    size_b = b.shape[1]
    return pl.pallas_call(
        weight_grad_kernel,
        grid=(size_a // tile_a, size_b // tile_b),
        in_specs=[
            pl.BlockSpec((rows, tile_a), lambda i, j: (0, i)),
            pl.BlockSpec((rows, tile_b), lambda i, j: (0, j)),
        ],
        out_specs=pl.BlockSpec((tile_a, tile_b), lambda i, j: (i, j)),
        out_shape=shape((size_a, size_b), low),
        compiler_params=params(),
        cost_estimate=cost(9),
        name="weight_grad",
    )(a, b)


def joint_kernel(halos, dq_ref, own_ref, cos_ref, sin_ref, *refs):
    dj_ref = refs[-1]
    width = dq_ref.shape[1]
    early = pl.program_id(0) < pl.num_programs(0) // 2
    cosine = cos_ref[...]
    sine = sin_ref[...]
    start = 0
    for prior_ref, next_ref in zip(refs[:halos], refs[halos : 2 * halos]):
        for at in range(0, prior_ref.shape[2], PAIR):
            near = [
                jnp.where(
                    early, prior_ref[i, :, at : at + PAIR], next_ref[i, :, at : at + PAIR]
                ).astype(full)
                for i in range(2)
            ]
            lanes = slice(start, start + PAIR)
            keys = turn_back(own_ref[0, :, lanes] + near[0], cosine, sine)
            dj_ref[:, lanes] = dq_ref[:, lanes]
            dj_ref[:, width + start : width + start + PAIR] = keys.astype(low)
            dj_ref[:, 2 * width + start : 2 * width + start + PAIR] = (
                own_ref[1, :, lanes] + near[1]
            ).astype(low)
            start += PAIR


def joint(dq, own, edges, cosine, sine, at):
    rows, width = dq.shape
    priors, nexts = zip(*edges)
    part = sum(p.shape[2] for p in priors)
    block = TOKEN_BLOCK
    half = priors[0].shape[1] // block
    inner = pl.BlockSpec((block, PAIR), lambda i: (i + half, 0))
    return pl.pallas_call(
        functools.partial(joint_kernel, len(edges)),
        grid=(rows // block,),
        in_specs=[
            pl.BlockSpec((block, part), lambda i: (i, at)),
            pl.BlockSpec((2, block, part), lambda i: (0, i, at)),
            inner,
            inner,
        ]
        + [
            pl.BlockSpec((2, block, p.shape[2]), lambda i: (0, jnp.minimum(i, half - 1), 0))
            for p in priors
        ]
        + [
            pl.BlockSpec((2, block, p.shape[2]), lambda i: (0, jnp.maximum(i - half, 0), 0))
            for p in nexts
        ],
        out_specs=pl.BlockSpec((block, 3 * part), lambda i: (i, 0)),
        out_shape=shape((rows, 3 * part), low),
        compiler_params=params(),
        cost_estimate=cost(2 + part // PAIR),
        name="joint",
    )(dq, own, cosine, sine, *priors, *nexts)


def input_grad_kernel(dj1_ref, dj2_ref, dz1_ref, weight_ref, out_ref):
    out = dz1_ref[...]
    at = 0
    for ref in (dj1_ref, dj2_ref):
        part = ref.shape[1] // 3
        for i in range(3):
            weight = weight_ref[i, :, at : at + part]
            out = out + dot_nt(ref[:, i * part : (i + 1) * part], weight)
        at += part
    out_ref[...] = out


def input_grad(dj1, dj2, dz1, weights):
    rows, width = dz1.shape
    block = 2 * TOKEN_BLOCK
    tile = lambda w: pl.BlockSpec((block, w), lambda i: (i, 0))
    return pl.pallas_call(
        input_grad_kernel,
        grid=(rows // block,),
        in_specs=[
            tile(dj1.shape[1]),
            tile(dj2.shape[1]),
            tile(width),
            pl.BlockSpec((3, width, width), lambda i: (0, 0, 0)),
        ],
        out_specs=tile(width),
        out_shape=shape((rows, width), full),
        compiler_params=params(),
        cost_estimate=cost(9),
        name="input_grad",
    )(dj1, dj2, dz1, weights)


def whole_joint_plan(ids, srcs, weight, sem):
    width = weight.shape[1]
    return [
        pltpu.make_async_copy(srcs[0].at[:, i * width : (i + 1) * width], weight.at[i], sem)
        for i in range(3)
    ] + [pltpu.make_async_copy(srcs[1], weight.at[3], sem)]


def whole_middle_plan(ids, srcs, weights, sems):
    out_w, gate_w, up_w, down_w = weights
    parts, _, width = gate_w.shape
    columns = lambda src, dst, sem: [
        pltpu.make_async_copy(src.at[:, i * width : (i + 1) * width], dst.at[i], sem)
        for i in range(parts)
    ]
    return (
        [pltpu.make_async_copy(srcs[0].at[3], out_w, sems.at[0])]
        + columns(srcs[1], gate_w, sems.at[1])
        + columns(srcs[2], up_w, sems.at[2])
        + [pltpu.make_async_copy(srcs[3], down_w, sems.at[3])]
    )


def swap_with(value, place):
    pairs = []
    for r in range(4):
        for z in range(4):
            for c in range(2):
                to_r, to_z, to_c = place(r, z, c)
                pairs.append(((r * 4 + z) * 2 + c, (to_r * 4 + to_z) * 2 + to_c))
    return lax.ppermute(value, ("rep", "fsdp"), pairs)


def over_core(value):
    return swap_with(value, lambda r, z, c: (r, z, 1 - c))


def over_z(value, k):
    return swap_with(value, lambda r, z, c: (r, z ^ k, c))


def over_square_1(value):
    return swap_with(value, lambda r, z, c: (r ^ (1 + c), z, c))


def over_square_2(value):
    return swap_with(value, lambda r, z, c: (r ^ (2 - c), z, c))


def over_z_1(value):
    return swap_with(value, lambda r, z, c: (r, z ^ (2 - c), c))


def over_z_2(value):
    return swap_with(value, lambda r, z, c: (r, z ^ (1 + c), c))


def pieces(ids, shards, nears, fars):
    r, z, c = ids[0], ids[1], ids[2]
    found = []
    for i in range(2):
        core = (1 - c) if i else c
        bit1, bit2 = 1 + core, 2 - core
        for quarter in range(4):
            found.append((shards[i].at[quarter], True, quarter, z, core))
        for ref, base in ((nears[i], r), (fars[i], r ^ bit2)):
            for j in range(2):
                for k in range(1, 4):
                    quarter = base ^ bit1 if j else base
                    found.append((ref.at[j, k - 1], False, quarter, z ^ k, core))
    return found


def piece_joint_plan(ids, srcs, weight, sem):
    size = srcs[0].shape[1]
    copies = []
    for ref, _, quarter, z, core in pieces(ids, srcs[0:2], srcs[2:4], srcs[4:6]):
        at = pl.multiple_of((2 * z + core) * size, size)
        copies.append(pltpu.make_async_copy(ref, weight.at[quarter, pl.ds(at, size)], sem))
    return copies


def piece_middle_plan(ids, srcs, weights, sems):
    out_w, gate_w, up_w, down_w = weights
    size = srcs[1].shape[1] // 3
    copies = [pltpu.make_async_copy(srcs[0].at[3], out_w, sems.at[0])]
    for i, target in enumerate((gate_w, up_w)):
        for ref, _, quarter, z, core in pieces(ids, srcs[1:3], srcs[3:5], srcs[5:7]):
            at = pl.multiple_of((2 * z + core) * size, size)
            copies.append(
                pltpu.make_async_copy(
                    ref.at[i * size : (i + 1) * size],
                    target.at[quarter, pl.ds(at, size)],
                    sems.at[1 + i],
                )
            )
    for ref, own, quarter, z, core in pieces(ids, srcs[1:3], srcs[7:9], srcs[9:11]):
        at = pl.multiple_of(((2 * z + core) * 4 + quarter) * size, size)
        source = ref.at[2 * size : 3 * size] if own else ref
        copies.append(pltpu.make_async_copy(source, down_w.at[pl.ds(at, size)], sems.at[3]))
    return copies


def position(j, core):
    return jnp.where(core == 0, j, (j & 1) * 2 + (j >> 1))


def put_pieces(ids, block_ref, own_ref, other_ref, first, size):
    z, c = ids[1], ids[2]
    for ref, core in ((own_ref, c), (other_ref, 1 - c)):
        for k in range(4):
            at = pl.multiple_of((2 * (z ^ position(k, core)) + core) * size, 8)
            ref[0, k, first : first + size, :] = block_ref[pl.ds(at, size), :].astype(low)


def gate_up_grad_kernel(
    ids, hidden_ref, dgate_ref, dlift_ref, gains_ref, own_ref, other_ref, block_ref
):
    size = block_ref.shape[0] // 8
    z, c = ids[1], ids[2]
    quarter = ids[0] ^ pl.program_id(0)
    for i, ref in enumerate((dgate_ref, dlift_ref)):
        block_ref[...] = dot_tn(hidden_ref[...], ref[...])
        put_pieces(ids, block_ref, own_ref, other_ref, i * size, size)
    for ref, core in ((own_ref, c), (other_ref, 1 - c)):
        for k in range(4):
            ref[0, k, 2 * size :, :] = jnp.zeros((16, ref.shape[3]), low)
            row = gains_ref[quarter * 8 + 2 * (z ^ position(k, core)) + core]
            ref[0, k, 2 * size :, : row.shape[1]] = row.astype(low)


def grad_specs(size, width):
    own = pl.BlockSpec((1, 4, size, width), lambda j, ids: (position(j, ids[2]), 0, 0, 0))
    other = pl.BlockSpec((1, 4, size, width), lambda j, ids: (position(j, 1 - ids[2]), 0, 0, 0))
    return [own, other], [shape((4, 4, size, width), low)] * 2


def gate_up_grad(ids, hidden_low, dgate, dlift, gains):
    rows, width = hidden_low.shape
    size = width // 8
    out_specs, out_shape = grad_specs(2 * size + 16, width)
    column = pl.BlockSpec((rows, width), lambda j, ids: (0, ids[0] ^ j))
    return pl.pallas_call(
        gate_up_grad_kernel,
        grid_spec=pltpu.PrefetchScalarGridSpec(
            num_scalar_prefetch=1,
            grid=(4,),
            in_specs=[
                pl.BlockSpec((rows, width), lambda j, ids: (0, 0)),
                column,
                column,
                pl.BlockSpec(gains.shape, lambda j, ids: (0, 0, 0)),
            ],
            out_specs=out_specs,
            scratch_shapes=[pltpu.VMEM((width, width), full)],
        ),
        out_shape=out_shape,
        compiler_params=params(),
        cost_estimate=cost(16),
        name="gate_up_grad",
    )(ids, hidden_low, dgate, dlift, gains)


def joint_grad_1_kernel(ids, tok_ref, dj_ref, own_ref, other_ref, block_ref):
    block_ref[...] = dot_tn(tok_ref[...], dj_ref[...])
    put_pieces(ids, block_ref, own_ref, other_ref, 0, block_ref.shape[0] // 8)


def joint_grad_1(ids, tokens, djoint):
    rows, width = tokens.shape
    part = djoint.shape[1] // 4
    out_specs, out_shape = grad_specs(width // 8, part)
    return pl.pallas_call(
        joint_grad_1_kernel,
        grid_spec=pltpu.PrefetchScalarGridSpec(
            num_scalar_prefetch=1,
            grid=(4,),
            in_specs=[
                pl.BlockSpec((rows, width), lambda j, ids: (0, 0)),
                pl.BlockSpec((rows, part), lambda j, ids: (0, ids[0] ^ j)),
            ],
            out_specs=out_specs,
            scratch_shapes=[pltpu.VMEM((width, part), full)],
        ),
        out_shape=out_shape,
        compiler_params=params(),
        cost_estimate=cost(8),
        name="joint_grad",
    )(ids, tokens, djoint)


def joint_grad_2_kernel(ids, tok_ref, dj_ref, own_ref, other_ref, block_ref):
    size = block_ref.shape[0] // 8
    z, c = ids[1], ids[2]
    block_ref[...] = dot_tn(tok_ref[...], dj_ref[...])
    for ref, core in ((own_ref, c), (other_ref, 1 - c)):
        for k in range(4):
            at = pl.multiple_of((2 * (z ^ position(k, core)) + core) * size, 8)
            ref[k] = block_ref[pl.ds(at, size), :].astype(low)


def joint_grad_2(ids, tokens, djoint):
    rows, width = tokens.shape
    columns = djoint.shape[1]
    part = columns // 2
    out = pl.BlockSpec((4, width // 8, part), lambda j, ids: (0, 0, j))
    return pl.pallas_call(
        joint_grad_2_kernel,
        grid_spec=pltpu.PrefetchScalarGridSpec(
            num_scalar_prefetch=1,
            grid=(2,),
            in_specs=[
                pl.BlockSpec((rows, width), lambda j, ids: (0, 0)),
                pl.BlockSpec((rows, part), lambda j, ids: (0, j)),
            ],
            out_specs=[out, out],
            scratch_shapes=[pltpu.VMEM((width, part), full)],
        ),
        out_shape=[shape((4, width // 8, columns), low)] * 2,
        compiler_params=params(),
        cost_estimate=cost(5),
        name="joint_grad",
    )(ids, tokens, djoint)


def down_out_grad_kernel(product_ref, dfeed_ref, at_ref, db_ref, out_ref, block_ref):
    count, size, _ = out_ref.shape
    step = pl.program_id(0)

    @pl.when(step == 0)
    def _():
        block_ref[...] = dot_tn(at_ref[...], db_ref[...])

    down = dot_tn(product_ref[...], dfeed_ref[...]).astype(low)
    rows = down.shape[0] // count
    for i in range(count):
        at = pl.multiple_of((step * count + i) * (size - rows), 8)
        out_ref[i, :rows] = down[i * rows : (i + 1) * rows]
        out_ref[i, rows:] = block_ref[pl.ds(at, size - rows), :].astype(low)


def down_out_grad(product, dfeed, attended, dbranch, shards):
    rows, hidden = product.shape
    width = dfeed.shape[1]
    size = (hidden + width) // shards
    whole = pl.BlockSpec((rows, width), lambda j: (0, 0))
    steps = shards // 2
    return pl.pallas_call(
        down_out_grad_kernel,
        grid=(steps,),
        in_specs=[
            pl.BlockSpec((rows, hidden // steps), lambda j: (0, j)),
            whole,
            whole,
            whole,
        ],
        out_specs=pl.BlockSpec((2, size, width), lambda j: (j, 0, 0)),
        out_shape=shape((shards, size, width), low),
        scratch_shapes=[pltpu.VMEM((width, width), full)],
        compiler_params=params(),
        cost_estimate=cost(12),
        name="down_out_grad",
    )(product, dfeed, attended, dbranch)


def wide(v):
    return v.astype(full)


def sum_core(own, mate):
    return (wide(own[2:]) + wide(mate[2:])).astype(low)


def sum_square(own, mate, b):
    return (wide(own[1]) + wide(mate[1]) + wide(b[1])).astype(low)


def sum_rest(own, mate, b, d):
    return wide(own[0]) + wide(mate[0]) + wide(b[0]) + wide(d)


def sum_z(kept, e, f):
    return (kept[0] + wide(e[0]) + wide(f)).astype(low)


def place(ids, quarter):
    return position(quarter ^ ids[0], ids[2])


def finish_kernel(ids, near_ref, far_ref, gate_ref, up_ref, vec_ref, down_ref, out_ref):
    size, width = gate_ref.shape
    step = pl.program_id(0)
    rows = 2 * size + 16
    at = place(ids, step)
    first = pl.multiple_of((at & 1) * rows, 16)

    def put(ref):
        gate_ref[...] = ref[pl.ds(first, size), :].astype(full)
        up_ref[...] = ref[pl.ds(pl.multiple_of(first + size, 16), size), :].astype(full)
        vectors = ref[pl.ds(pl.multiple_of(first + 2 * size, 16), 16), :PAIR]
        vec_ref[0] = vectors.astype(full)[:8]

    pl.when(at < 2)(lambda: put(near_ref))
    pl.when(at >= 2)(lambda: put(far_ref))

    def total(start):
        parts = [ref[pl.ds(start, size), :].astype(full) for ref in (near_ref, far_ref)]
        return (parts[0] + parts[1]).astype(low).astype(full)

    down_ref[...] = total(pl.multiple_of(2 * rows + step * size, 16))

    @pl.when(step == 0)
    def _():
        out_ref[...] = total(2 * rows + 4 * size)


def finish(ids, near, far, size):
    width = near.shape[1]
    whole = pl.BlockSpec(near.shape, lambda j, ids: (0, 0))
    column = pl.BlockSpec((size, width), lambda j, ids: (0, j))
    gate, up, vectors, down, out = pl.pallas_call(
        finish_kernel,
        grid_spec=pltpu.PrefetchScalarGridSpec(
            num_scalar_prefetch=1,
            grid=(4,),
            in_specs=[whole, whole],
            out_specs=[
                column,
                column,
                pl.BlockSpec((1, 8, PAIR), lambda j, ids: (j, 0, 0)),
                pl.BlockSpec((size, width), lambda j, ids: (j, 0)),
                pl.BlockSpec((size, width), lambda j, ids: (0, 0)),
            ],
        ),
        out_shape=[shape((size, 4 * width), full)] * 2
        + [
            shape((4, 8, PAIR), full),
            shape((4 * size, width), full),
            shape((size, width), full),
        ],
        compiler_params=params(),
        cost_estimate=cost(5),
        name="finish",
    )(ids, near, far)
    return gate, up, vectors[:, 0, :size], down, out


def finish_joint_kernel(ids, near_ref, far_ref, out_ref):
    width = out_ref.shape[1] // 3
    part = (near_ref.shape[1] - width) // 2
    first = 4 * part // 3
    for quarter in range(4):
        at = place(ids, quarter)
        halves = [
            jnp.where(at < 2, near_ref[:, i : i + part], far_ref[:, i : i + part])
            for i in (width, width + part)
        ]
        piece = jnp.where((at & 1) == 0, *halves).astype(full)
        for start in range(0, part, PAIR):
            which, column = divmod(quarter * part + start, first)
            column += which * width
            out_ref[:, column : column + PAIR] = piece[:, start : start + PAIR]
    rest = near_ref[:, :width].astype(full) + far_ref[:, :width].astype(full)
    rest = rest.astype(low).astype(full)
    second = width - first
    for which in range(3):
        column = which * width + first
        out_ref[:, column : column + second] = rest[:, which * second : (which + 1) * second]


def finish_joint(ids, near, far):
    size, columns = near.shape
    width = columns // 2
    whole = pl.BlockSpec(near.shape, lambda j, ids: (0, 0))
    return pl.pallas_call(
        finish_joint_kernel,
        grid_spec=pltpu.PrefetchScalarGridSpec(
            num_scalar_prefetch=1,
            grid=(1,),
            in_specs=[whole, whole],
            out_specs=pl.BlockSpec((size, 3 * width), lambda j, ids: (0, 0)),
        ),
        out_shape=shape((size, 3 * width), full),
        compiler_params=params(),
        cost_estimate=cost(3),
        name="finish_joint",
    )(ids, near, far)


def shards(
    custom,
    tokens,
    lengths,
    qkv_weight,
    out_weight,
    gate_weight,
    up_weight,
    down_weight,
    norm1_gain,
    norm1_bias,
    norm2_gain,
    norm2_bias,
    cotangent,
):
    rows, width = tokens.shape
    hidden = gate_weight.shape[1]
    size = lax.axis_size("fsdp")
    me = lax.axis_index("fsdp")
    up = [(i, i + 1) for i in range(size - 1)]
    down = [(i + 1, i) for i in range(size - 1)]
    r = lax.axis_index("rep")
    z, c = me // 2, me % 2
    ids = jnp.stack([r, z, c]).astype(jnp.int32)
    vectors = jnp.stack([norm1_gain, norm1_bias, norm2_gain, norm2_bias]).astype(low)

    before = tokens[rows - REACH :]
    behind = tokens[:REACH]
    swap_edges = lambda last, first: (
        lax.ppermute(last, "fsdp", up),
        lax.ppermute(first, "fsdp", down),
    )
    if custom:
        part = qkv_weight.shape[0]
        columns = lambda w: jnp.swapaxes(w.astype(low).reshape(part, -1, width), 0, 1)
        column = lambda w, i: lax.dynamic_slice_in_dim(w, i * width, width, 1).astype(low)
        mine = jnp.where(
            r == 3, out_weight.astype(low), column(qkv_weight, jnp.minimum(r, 2))
        )
        arrived = [over_z(mine, k) for k in (1, 2, 3)]
        before, behind = swap_edges(before, behind)
        rows_of = jnp.pad(vectors, ((0, 4), (0, width - part)))
        mine_2 = jnp.concatenate(
            [column(gate_weight, r), column(up_weight, r), rows_of, over_core(rows_of)]
        )
        mine_3 = lax.dynamic_slice_in_dim(down_weight, r * part, part, 0).astype(low)
        shard_1 = jnp.concatenate([columns(qkv_weight), out_weight.astype(low)[None]])
        shard_2 = jnp.concatenate(
            [
                columns(gate_weight),
                columns(up_weight),
                down_weight.astype(low).reshape(4, part, width),
            ],
            axis=1,
        )
        own_1 = jnp.stack(after(tuple(arrived), mine_2, mine_3, shard_1, shard_2))
        mate_shard_1 = over_core(after(shard_1, own_1))
        other_1 = over_square_1(own_1)
        near_1 = jnp.stack([own_1, after(other_1, mate_shard_1)])
        along_z = [[2 * i + j for i in range(size // 2)] for j in range(2)]
        arrived_2 = lax.all_gather(
            after(mine_2, before, behind, near_1), "fsdp", axis=0, axis_index_groups=along_z
        )
        far_1 = over_square_2(near_1)
        mate_near_1 = over_core(near_1)
        joint_sources = [shard_1, mate_shard_1, near_1, mate_near_1, far_1]
        joint_plan = piece_joint_plan
    else:
        before, behind = swap_edges(before, behind)
        gather = lambda w: lax.all_gather(w.astype(low), "fsdp", axis=0, tiled=True)
        joint_sources = [gather(qkv_weight), gather(out_weight)]
        joint_plan = whole_joint_plan
        middle_sources = [gather(w) for w in (gate_weight, up_weight, down_weight)]
        vectors = lax.all_gather(vectors, "fsdp", axis=1, tiled=True)
        found = jnp.pad(vectors, ((0, 12), (0, 0)))[None]
        middle_plan = whole_middle_plan

    doc_lengths = lengths[0]
    ends = jnp.cumsum(doc_lengths)
    index = me * rows - REACH + jnp.arange(rows + 2 * REACH, dtype=jnp.int32)
    if custom:
        index = after(index, near_1)
    passed = (index[:, None] >= ends[None, :]).astype(jnp.int32)
    starts = jnp.sum(passed * doc_lengths[None, :], axis=1)
    cosine, sine = tables(index - starts)
    if custom:
        mate_far_1 = over_core(after(far_1, cosine))
        joint_sources.append(mate_far_1)
        mate_shard_2 = over_core(after(shard_2, near_1))
    own_starts = starts[REACH : REACH + rows]
    own_index = index[REACH : REACH + rows]
    stops = jnp.min(
        jnp.where(ends[None, :] > own_index[:, None], ends[None, :], size * rows), axis=1
    )
    base = me * rows - REACH
    bounds = jnp.stack(
        [
            jnp.maximum(own_starts, own_index - REACH) - base,
            jnp.minimum(stops, own_index + REACH + 1) - base,
        ]
    ).astype(jnp.int32)

    queries, keys, values, joint_weights = project(
        joint_plan, ids, before, tokens, behind, cosine, sine, joint_sources
    )
    given = (queries, keys, values)
    if custom:
        arrived_2 = after(arrived_2, queries)
        own_2 = jnp.stack(
            [
                lax.dynamic_slice(arrived_2, (z ^ k, 0, 0), (1, 2 * part, width))[0]
                for k in (1, 2, 3)
            ]
        )
        found = arrived_2[:, 2 * part :, :PAIR]
        other_2 = over_square_1(own_2)
        mine_3 = after(mine_3, own_2)
        arrived_3 = [over_z(mine_3, k) for k in (1, 2, 3)]
        done = attend(after(bounds, own_2, mate_shard_2, mine_3), *given, 0, 2)
        own_3 = jnp.stack(after(tuple(arrived_3), done[1]))
        near_2 = jnp.stack([own_2, after(other_2, done[1], own_3)])
        far_2 = over_square_2(near_2)
        mate_near_2 = over_core(near_2)
        other_3 = over_square_1(own_3)
        done = attend(after(bounds, near_2, own_3), *given, 2, 2, done)
        near_3 = jnp.stack([own_3, after(other_3, done[1], mate_near_2)])
        far_3 = over_square_2(near_3)
        mate_near_3 = over_core(near_3)
        attended, lse = attend(after(bounds, near_3), *given, 4, 2, done)
        mate_far_2 = over_core(after(far_2, lse, mate_near_3))
        mate_far_3 = over_core(after(far_3, lse))
        middle_sources = [shard_2, mate_shard_2, near_2, mate_near_2, far_2, mate_far_2]
        middle_sources += [near_3, mate_near_3, far_3, mate_far_3]
        middle_plan = piece_middle_plan
    else:
        done = None
        for first in (0, 2, 4):
            done = attend(bounds, *given, first, 2, done)
        attended, lse = done
    result, dz1, dattended, hidden_low, product, dfeed, dgate, dlift, dbranch, gains = middle(
        middle_plan,
        ids,
        attended,
        tokens,
        cotangent,
        found,
        [joint_weights, *middle_sources],
        hidden,
    )
    gains = gains[:4]
    given = (queries, keys, values, attended, dattended, lse)
    given += (cosine[REACH : REACH + rows], sine[REACH : REACH + rows])
    spread = lambda g: lax.psum_scatter(g, "fsdp", scatter_dimension=0, tiled=True)
    if custom:
        gains = jnp.pad(gains.reshape(32, 1, part), ((0, 0), (0, 15), (0, PAIR - part)))
        own, other = gate_up_grad(ids, hidden_low, dgate, dlift, gains)
        mate = over_core(other)
        grad_down = down_out_grad(after(product, own), dfeed, attended, dbranch, size)
        share_down = spread(grad_down)[0]
        sent = sum_core(own, after(mate, grad_down))
        b = over_square_2(sent)
        dq, dkv, to_prior, to_next = attend_back(after(bounds, sent), *given, 0, 2, (0, 2))
        edges = [swap_edges(to_next, to_prior)]
        dq, dkv, to_prior, to_next = attend_back(
            after(bounds, dq), *given, 2, 2, (2, 2), (dq, dkv)
        )
        edges.append(swap_edges(to_next, to_prior))
        sent = sum_square(own, mate, after(b, dq, *edges[0]))
        d = over_square_1(sent)
        dq, dkv, to_prior, to_next = attend_back(
            after(bounds, sent), *given, 4, 2, (4, 2), (dq, dkv)
        )
        edges_2 = [swap_edges(to_next, to_prior)]
        kept = sum_rest(own, mate, b, after(d, dq, *edges[1]))
        sent = kept[2:].astype(low)
        e = over_z_1(sent)
        dj1 = joint(after(dq, sent), dkv, edges, cosine, sine, 0)
        own_1, other_1 = joint_grad_1(ids, tokens, dj1)
        mate_1 = over_core(after(other_1, e, *edges_2[0]))
        sent = (kept[1] + wide(after(e, own_1)[1])).astype(low)
        f = over_z_2(sent)
        dj2 = joint(after(dq, own_1, sent), dkv, edges_2, cosine, sine, 2)
        sent = sum_core(own_1, after(mate_1, dj2))
        b_1 = over_square_2(sent)
        own_2, other_2 = joint_grad_2(ids, tokens, after(dj2, sent))
        mate_2 = over_core(other_2)
        sent = sum_square(own_1, mate_1, after(b_1, own_2))
        d_1 = over_square_1(sent)
        mine = jnp.concatenate([sum_z(kept, e, after(f, own_2)), share_down])
        got = over_square_1(after(mine, sent))
        rest = wide(own_2) + wide(after(mate_2, mine))
        kept_1 = jnp.concatenate(
            [rest, sum_rest(own_1, mate_1, b_1, after(d_1, mine))], axis=2
        )
        sent = kept_1[2:].astype(low)
        e_1 = over_z_1(sent)
        grad_tokens = input_grad(after(dj1, sent), dj2, dz1, joint_weights)
        sent = (kept_1[1] + wide(after(e_1, grad_tokens)[1])).astype(low)
        f_1 = over_z_2(sent)
        got = after(got, sent)
        rows_of = 2 * part + 16
        near = jnp.concatenate(
            [
                mine[:rows_of],
                got[:rows_of],
                (wide(mine[rows_of:]) + wide(got[rows_of:])).astype(low),
            ]
        )
        far = over_square_2(near)
        mine = sum_z(kept_1, e_1, after(f_1, near))
        got = over_square_1(mine)
        pair = jnp.concatenate(
            [
                (wide(mine[:, :width]) + wide(got[:, :width])).astype(low),
                mine[:, width:],
                got[:, width:],
            ],
            axis=1,
        )
        others = over_square_2(pair)
        gate_sum, up_sum, vector_sum, down_sum, out_sum = finish(
            ids, near, after(far, pair), part
        )
        joint_sum = finish_joint(ids, pair, after(others, gate_sum))
        summed = (joint_sum, out_sum, gate_sum, up_sum, down_sum, vector_sum)
    else:
        share_down = spread(weight_grad(product, dfeed))
        share_gate = spread(weight_grad(hidden_low, dgate))
        share_up = spread(weight_grad(hidden_low, dlift))
        share_out = spread(weight_grad(attended, dbranch))
        share_gains = lax.psum_scatter(gains, "fsdp", scatter_dimension=1, tiled=True)
        dq, dkv, to_prior, to_next = attend_back(bounds, *given, 0, 4, (0, 4))
        edges_1 = swap_edges(to_next, to_prior)
        dq, dkv, to_prior, to_next = attend_back(bounds, *given, 4, 2, (4, 2), (dq, dkv))
        edges_2 = swap_edges(to_next, to_prior)
        dj1 = joint(dq, dkv, [edges_1], cosine, sine, 0)
        dj2 = joint(dq, dkv, [edges_2], cosine, sine, 2)
        share_1 = spread(weight_grad(tokens, dj1)).reshape(-1, 3, dj1.shape[1] // 3)
        share_2 = spread(weight_grad(tokens, dj2)).reshape(-1, 3, dj2.shape[1] // 3)
        share_qkv = jnp.concatenate([share_1, share_2], axis=2).reshape(-1, 3 * width)
        grad_tokens = input_grad(dj1, dj2, dz1, joint_weights)
        summed = lax.psum(
            tuple(
                s.astype(full)
                for s in (share_qkv, share_out, share_gate, share_up, share_down, share_gains)
            ),
            "rep",
        )
    return (result, grad_tokens, *summed[:5], *(summed[5][i] for i in range(4)))


def solution(mesh):
    rows = P(("rep", "fsdp"), None)
    matrix = P("fsdp", None)
    vector = P("fsdp")
    custom = (mesh.shape["rep"], mesh.shape["fsdp"]) == (4, 8)
    return jax.shard_map(
        functools.partial(shards, custom and not FORCE_WHOLE),
        mesh=mesh,
        in_specs=(rows, P("rep", None)) + (matrix,) * 5 + (vector,) * 4 + (rows,),
        out_specs=(rows, rows) + (matrix,) * 5 + (vector,) * 4,
        check_vma=False,
    )
```

```python
import functools
import math

import jax
import jax.numpy as jnp
from jax import lax
from jax.experimental import pallas as pl
from jax.experimental.pallas import tpu as pltpu
from jax.sharding import PartitionSpec as P

HEADS = 12
WINDOW = 1024
REACH = WINDOW // 2
HEAD = 64
PAIR = 2 * HEAD
QUERY_BLOCK = 256
TOKEN_BLOCK = 256
FORCE_WHOLE = False
VMEM = 56 * 1024 * 1024

epsilon = 1e-06
rope_base = 1000.0
masked_score = -1e30
low = jnp.bfloat16
full = jnp.float32


def dot_nn(a, b):
    return lax.dot_general(a, b, (((1,), (0,)), ((), ())), preferred_element_type=full)


def dot_nt(a, b):
    return lax.dot_general(a, b, (((1,), (1,)), ((), ())), preferred_element_type=full)


def dot_tn(a, b):
    return lax.dot_general(a, b, (((0,), (0,)), ((), ())), preferred_element_type=full)


def params():
    return pltpu.CompilerParams(vmem_limit_bytes=VMEM)


def after(value, *others):
    return lax.optimization_barrier((value, *others))[0]


def shape(dims, dtype):
    return jax.ShapeDtypeStruct(dims, dtype)


def cost(micros):
    return pl.CostEstimate(flops=int(micros * 0.575e9), bytes_accessed=1, transcendentals=0)


def tables(position):
    lane = jnp.arange(PAIR, dtype=jnp.int32) % HEAD
    half = HEAD // 2
    frequency = rope_base ** (-2.0 * (lane % half).astype(full) / HEAD)
    angle = position.astype(full)[:, None] * frequency[None, :]
    sign = jnp.where(lane < half, -1.0, 1.0).astype(full)
    return jnp.cos(angle), jnp.sin(angle) * sign[None, :]


def partner(x):
    half = HEAD // 2
    lane = lax.broadcasted_iota(jnp.int32, x.shape, 1) % HEAD
    return jnp.where(lane < half, pltpu.roll(x, PAIR - half, 1), pltpu.roll(x, half, 1))


def turn(x, cosine, sine):
    return x * cosine + partner(x) * sine


def turn_back(x, cosine, sine):
    return x * cosine - partner(x) * sine


def project_kernel(
    plan, sources, first, count, ids, mate_ref, tok_ref, cross_ref, cos_ref, sin_ref, *refs
):
    srcs = refs[:sources]
    q_ref, k_ref, v_ref, weight, sems = refs[sources:]
    step = pl.program_id(0)

    @pl.when(step == 0)
    def _():
        for copy in plan(ids, srcs, weight, sems.at[0]):
            copy.start()
        pltpu.make_async_copy(weight, weight, sems.at[0]).wait()

    width = tok_ref.shape[1]
    inside = (step >= first) & (step < first + count)
    by_mate = (step < first) == (ids[2] == 1)
    rows = jnp.where(
        inside, tok_ref[...], jnp.where(by_mate, mate_ref[...], cross_ref[...])
    )
    cosine = cos_ref[...]
    sine = sin_ref[...]
    keys = dot_nn(rows, weight[1])
    for at in range(0, width, PAIR):
        k_ref[:, at : at + PAIR] = turn(keys[:, at : at + PAIR], cosine, sine).astype(low)
    v_ref[...] = dot_nn(rows, weight[2]).astype(low)

    @pl.when((step >= first) & (step < first + count))
    def _():
        queries = dot_nn(rows, weight[0])
        for at in range(0, width, PAIR):
            turned = turn(queries[:, at : at + PAIR], cosine, sine).astype(low)
            q_ref[:, at : at + PAIR] = (turned.astype(full) * (1.0 / math.sqrt(HEAD))).astype(low)


def project(plan, ids, edges, tokens, cosine, sine, sources):
    rows, width = tokens.shape
    mate, cross = edges
    ext = rows + 2 * mate.shape[0]
    block = 2 * TOKEN_BLOCK
    first, count = mate.shape[0] // block, rows // block
    tile = lambda w: pl.BlockSpec((block, w), lambda i, *_: (i, 0))
    inner = pl.BlockSpec((block, width), lambda i, *_: (jnp.clip(i - first, 0, count - 1), 0))
    edge = lambda core: pl.BlockSpec(
        (block, width),
        lambda i, ids: (
            jnp.where(
                ids[2] == core, jnp.minimum(i, first - 1), jnp.maximum(i - first - count, 0)
            ),
            0,
        ),
    )
    return pl.pallas_call(
        functools.partial(project_kernel, plan, len(sources), first, count),
        grid_spec=pltpu.PrefetchScalarGridSpec(
            num_scalar_prefetch=1,
            grid=(ext // block,),
            in_specs=[
                edge(1),
                inner,
                edge(0),
                tile(PAIR),
                tile(PAIR),
            ]
            + [pl.BlockSpec(memory_space=pl.ANY)] * len(sources),
            out_specs=[
                inner,
                tile(width),
                tile(width),
                pl.BlockSpec((4, width, width), lambda i, *_: (0, 0, 0)),
            ],
            scratch_shapes=[pltpu.SemaphoreType.DMA((1,))],
        ),
        out_shape=[
            shape((rows, width), low),
            shape((ext, width), low),
            shape((ext, width), low),
            shape((4, width, width), low),
        ],
        compiler_params=params(),
        cost_estimate=cost(0.1),
        name="project",
    )(ids, mate, tokens, cross, cosine, sine, *sources)


def fill_bias(bounds_ref, bias_ref, blocks, span):
    for b in range(blocks):
        lo = bounds_ref[0:1, b * QUERY_BLOCK : (b + 1) * QUERY_BLOCK] - b * QUERY_BLOCK
        hi = bounds_ref[1:2, b * QUERY_BLOCK : (b + 1) * QUERY_BLOCK] - b * QUERY_BLOCK
        at = lax.broadcasted_iota(jnp.int32, (span, QUERY_BLOCK), 0)
        bias_ref[b] = jnp.where((at >= lo) & (at < hi), 0.0, masked_score)


def only(x, head):
    lane = lax.broadcasted_iota(jnp.int32, x.shape, 1)
    return jnp.where((lane >= HEAD) if head else (lane < HEAD), x, jnp.zeros_like(x))


def attend_kernel(chunk, bounds_ref, q_ref, k_ref, v_ref, *refs):
    o_ref, lse_ref, bias_ref, vt_ref, s_ref = refs[-5:]
    rows = q_ref.shape[0]
    block = QUERY_BLOCK
    blocks = rows // block
    span = k_ref.shape[0] - rows + block

    @pl.when(pl.program_id(0) == 0)
    def _():
        fill_bias(bounds_ref, bias_ref, blocks, span)

    vt_ref[...] = v_ref[...].T
    chunks = [(c, min(chunk, span - c)) for c in range(0, span, chunk)]
    steps = [(b, h) for b in range(blocks) for h in range(2)]
    fold = lambda x, by: by(x.reshape(x.shape[0] // 64, 64, block), axis=0)
    add = lambda old, new: new if old is None else old + new

    def begin(i):
        b, h = steps[i]
        return {"query": only(q_ref[b * block : (b + 1) * block, :], h), "top": None}

    def score(i, c, n, state):
        b, _ = steps[i]
        s = dot_nt(k_ref[b * block + c : b * block + c + n, :], state["query"])
        s = s + bias_ref[b, c : c + n, :]
        s_ref[i % 2, c : c + n, :] = s
        top = fold(s, jnp.max)
        state["top"] = top if state["top"] is None else jnp.maximum(state["top"], top)

    def weigh(i, c, n, state):
        b, h = steps[i]
        e = jnp.exp(s_ref[i % 2, c : c + n, :] - state["peak"])
        state["total"] = add(state.get("total"), fold(e, jnp.sum))
        lanes = slice(b * block + c, b * block + c + n)
        mixed = dot_nn(vt_ref[h * HEAD : (h + 1) * HEAD, lanes], e.astype(low))
        state["mixed"] = add(state.get("mixed"), mixed)

    state = begin(0)
    for c, n in chunks:
        score(0, c, n, state)
    out = []
    for i, (b, h) in enumerate(steps):
        state["peak"] = jnp.max(state["top"], axis=0, keepdims=True)
        following = begin(i + 1) if i + 1 < len(steps) else None
        for c, n in chunks:
            if following is not None:
                score(i + 1, c, n, following)
            weigh(i, c, n, state)
        total = jnp.sum(state["total"], axis=0, keepdims=True)
        out.append(state["mixed"] / total)
        at = slice(b * block, (b + 1) * block)
        lse_ref[0, h : h + 1, at] = state["peak"] + jnp.log(total)
        if h == 1:
            o_ref[at, :] = jnp.concatenate(out, axis=0).T.astype(low)
            out = []
        state = following


def attend(bounds, q, k, v, first, pairs, before=None, chunk=640):
    rows, width = q.shape
    ext = k.shape[0]
    blocks = rows // QUERY_BLOCK
    span = ext - rows + QUERY_BLOCK
    own = pl.BlockSpec((rows, PAIR), lambda p: (0, p + first))
    wide = pl.BlockSpec((ext, PAIR), lambda p: (0, p + first))
    before = () if before is None else tuple(before)
    return pl.pallas_call(
        functools.partial(attend_kernel, chunk),
        grid=(pairs,),
        in_specs=[pl.BlockSpec((2, rows), lambda p: (0, 0)), own, wide, wide]
        + [pl.BlockSpec(memory_space=pl.ANY)] * len(before),
        out_specs=[own, pl.BlockSpec((1, 2, rows), lambda p: (p + first, 0, 0))],
        out_shape=[shape((rows, width), low), shape((width // PAIR, 2, rows), full)],
        input_output_aliases={4 + i: i for i in range(len(before))},
        scratch_shapes=[
            pltpu.VMEM((blocks, span, QUERY_BLOCK), full),
            pltpu.VMEM((PAIR, ext), low),
            pltpu.VMEM((2, span, QUERY_BLOCK), full),
        ],
        compiler_params=params(),
        cost_estimate=cost(2 * pairs),
        name="attend",
    )(bounds, q, k, v, *before)


def attend_back_kernel(
    chunk,
    ids,
    bounds_ref,
    q_ref,
    k_ref,
    v_ref,
    o_ref,
    do_ref,
    lse_ref,
    *refs,
):
    cos_ref, sin_ref = refs[:2]
    dq_ref, own_ref, mate_ref, cross_ref = refs[-10:-6]
    bias_ref, kt_ref, dk_ref, dv_ref, p_ref, ds_ref = refs[-6:]
    rows = q_ref.shape[0]
    ext = k_ref.shape[0]
    block = QUERY_BLOCK
    blocks = rows // block
    reach = (ext - rows) // 2
    span = ext - rows + block

    @pl.when(pl.program_id(0) == 0)
    def _():
        fill_bias(bounds_ref, bias_ref, blocks, span)

    kt_ref[...] = k_ref[...].T
    dk_ref[...] = jnp.zeros_like(dk_ref)
    dv_ref[...] = jnp.zeros_like(dv_ref)
    chunks = [(c, min(chunk, span - c)) for c in range(0, span, chunk)]

    def begin(b):
        at = slice(b * block, (b + 1) * block)
        q = q_ref[at, :]
        do = do_ref[at, :]
        product = (do.astype(full) * o_ref[at, :].astype(full)).T
        heads = range(2)
        return {
            "query": [only(q, h) for h in heads],
            "grad": [only(do, h) for h in heads],
            "delta": [
                jnp.sum(product[h * HEAD : (h + 1) * HEAD], axis=0, keepdims=True) for h in heads
            ],
            "lse": [lse_ref[0, h : h + 1, at] for h in heads],
            "dq": [None, None],
        }

    def score(b, h, c, n, state):
        rows_of = slice(b * block + c, b * block + c + n)
        lanes = slice(h * block, (h + 1) * block)
        s = dot_nt(k_ref[rows_of, :], state["query"][h]) + bias_ref[b, c : c + n, :]
        p = jnp.exp(s - state["lse"][h])
        dp = dot_nt(v_ref[rows_of, :], state["grad"][h])
        p_ref[b % 2, c : c + n, lanes] = p.astype(low)
        ds_ref[b % 2, c : c + n, lanes] = (p * (dp - state["delta"][h])).astype(low)

    def spread(b, h, c, n, state):
        rows_of = slice(b * block + c, b * block + c + n)
        if h == 0:
            both = jnp.concatenate(state["grad"], axis=0)
            dv_ref[rows_of, :] += dot_nn(p_ref[b % 2, c : c + n, :], both)
        else:
            both = jnp.concatenate(state["query"], axis=0)
            dk_ref[rows_of, :] += dot_nn(ds_ref[b % 2, c : c + n, :], both)
        ds = ds_ref[b % 2, c : c + n, h * block : (h + 1) * block]
        t = dot_nn(kt_ref[h * HEAD : (h + 1) * HEAD, rows_of], ds)
        state["dq"][h] = t if state["dq"][h] is None else state["dq"][h] + t

    state = begin(0)
    for h in range(2):
        for c, n in chunks:
            score(0, h, c, n, state)
    for b in range(blocks):
        following = begin(b + 1) if b + 1 < blocks else None
        for h in range(2):
            for c, n in chunks:
                if following is not None:
                    score(b + 1, h, c, n, following)
                spread(b, h, c, n, state)
        at = slice(b * block, (b + 1) * block)
        turned = turn_back(jnp.concatenate(state["dq"], axis=0).T, cos_ref[at, :], sin_ref[at, :])
        dq_ref[at, :] = (turned * (1.0 / math.sqrt(HEAD))).astype(low)
        state = following
    first = ids[2] == 0
    for i, ref in enumerate((dk_ref, dv_ref)):
        prior = ref[:reach, :].astype(low)
        following = ref[reach + rows :, :].astype(low)
        own_ref[i] = ref[reach : reach + rows, :]
        mate_ref[i] = jnp.where(first, following, prior)
        cross_ref[i] = jnp.where(first, prior, following)


def attend_back(ids, bounds, q, k, v, o, do, lse, cosine, sine, first, pairs, halo, before=None, chunk=256):
    rows, width = q.shape
    ext = k.shape[0]
    blocks = rows // QUERY_BLOCK
    reach = (ext - rows) // 2
    span = ext - rows + QUERY_BLOCK
    halo_first, halo_pairs = halo
    before = () if before is None else tuple(before)
    own = pl.BlockSpec((rows, PAIR), lambda p, ids: (0, p + first))
    wide = pl.BlockSpec((ext, PAIR), lambda p, ids: (0, p + first))
    edge = pl.BlockSpec((2, reach, PAIR), lambda p, ids: (0, 0, p + first - halo_first))
    return pl.pallas_call(
        functools.partial(attend_back_kernel, chunk),
        grid_spec=pltpu.PrefetchScalarGridSpec(
            num_scalar_prefetch=1,
            grid=(pairs,),
            in_specs=[
            pl.BlockSpec((2, rows), lambda p, ids: (0, 0)),
            own,
            wide,
            wide,
            own,
            own,
            pl.BlockSpec((1, 2, rows), lambda p, ids: (p + first, 0, 0)),
            pl.BlockSpec((rows, PAIR), lambda p, ids: (0, 0)),
            pl.BlockSpec((rows, PAIR), lambda p, ids: (0, 0)),
        ]
        + [pl.BlockSpec(memory_space=pl.ANY)] * len(before),
        out_specs=[
            own,
            pl.BlockSpec((2, rows, PAIR), lambda p, ids: (0, 0, p + first)),
            edge,
            edge,
        ],
        scratch_shapes=[
            pltpu.VMEM((blocks, span, QUERY_BLOCK), full),
            pltpu.VMEM((PAIR, ext), low),
            pltpu.VMEM((ext, PAIR), full),
            pltpu.VMEM((ext, PAIR), full),
            pltpu.VMEM((2, span, 2 * QUERY_BLOCK), low),
            pltpu.VMEM((2, span, 2 * QUERY_BLOCK), low),
        ],
        ),
        out_shape=[
            shape((rows, width), low),
            shape((2, rows, width), full),
            shape((2, reach, halo_pairs * PAIR), low),
            shape((2, reach, halo_pairs * PAIR), low),
        ],
        input_output_aliases={10 + i: i for i in range(len(before))},
        compiler_params=params(),
        cost_estimate=cost(9 * pairs),
        name="attend_back",
    )(ids, bounds, q, k, v, o, do, lse, cosine, sine, *before)


def mean(x):
    return jnp.mean(x, axis=-1, keepdims=True)


def norm(x):
    centred = x - mean(x)
    inverse = lax.rsqrt(mean(centred * centred) + epsilon)
    return centred * inverse, inverse


def norm_back(scaled, normed, inverse):
    return inverse * (scaled - mean(scaled) - normed * mean(scaled * normed))


def position(j, core):
    return jnp.where(core == 0, j, (j & 1) * 2 + (j >> 1))


def gather_vectors(ids, vec_ref, width):
    count = vec_ref.shape[0]
    if count == 1:
        return vec_ref[0].astype(full)[:8]
    size = width // (2 * count)
    row = lax.broadcasted_iota(jnp.int32, (PAIR, width), 0)
    column = lax.broadcasted_iota(jnp.int32, (PAIR, width), 1)
    half = lax.broadcasted_iota(jnp.int32, (16, PAIR), 0) // 8
    out = jnp.zeros((16, width), full)
    for at in range(count):
        found = vec_ref[at].astype(full)
        for i in range(2):
            f = 2 * (ids[1] ^ position(at, ids[2])) + (ids[2] ^ i)
            place = ((column - f * size == row) & (row < size)).astype(full).astype(low)
            out = out + dot_nn(jnp.where(half == i, found, 0.0).astype(low), place)
    return out[:8] + out[8:]


def middle_kernel(plan, sources, ids, at_ref, tok_ref, cot_ref, *refs):
    vec_ref, refs = refs[0], refs[1:]
    srcs = refs[:sources]
    (
        out_ref,
        dz1_ref,
        da_ref,
        hidden_ref,
        product_ref,
        dfeed_ref,
        dgate_ref,
        dlift_ref,
        dbranch_ref,
        gains_ref,
        out_w,
        gate_w,
        up_w,
        down_w,
        lift_factor,
        gate_factor,
        vectors,
        sems,
    ) = refs[sources:]
    step = pl.program_id(0)
    weights = (out_w, gate_w, up_w, down_w)

    @pl.when(step == 0)
    def _():
        for copy in plan(ids, srcs, weights, sems):
            copy.start()
        gains_ref[...] = jnp.zeros_like(gains_ref)

    def ready(*which):
        @pl.when(step == 0)
        def _():
            for i in which:
                pltpu.make_async_copy(weights[i], weights[i], sems.at[i]).wait()

    parts, _, width = gate_w.shape

    @pl.when(step == 0)
    def _():
        vectors[...] = gather_vectors(ids, vec_ref, width)

    gain1, bias1, gain2, bias2 = (vectors[i : i + 1] for i in range(4))
    ready(0)
    normed1, inverse1 = norm(tok_ref[...].astype(full) + dot_nn(at_ref[...], out_w[...]))
    hidden = normed1 * gain1 + bias1
    hidden_low = hidden.astype(low)
    hidden_ref[...] = hidden_low
    ready(1, 2, 3)
    feed = None
    for part in range(parts):
        at = slice(part * width, (part + 1) * width)
        gate = dot_nn(hidden_low, gate_w[part])
        lift = dot_nn(hidden_low, up_w[part])
        sigma = jax.nn.sigmoid(gate)
        opened = gate * sigma
        product = (opened * lift).astype(low)
        product_ref[:, at] = product
        lift_factor[:, at] = opened
        gate_factor[:, at] = lift * sigma * (1.0 + gate * (1.0 - sigma))
        term = dot_nn(product, down_w[at, :])
        feed = term if feed is None else feed + term
    normed2, inverse2 = norm(hidden + feed)
    out_ref[...] = (normed2 * gain2 + bias2).astype(low)
    cot = cot_ref[...].astype(full)
    gains_ref[2:3] += jnp.sum(cot * normed2, axis=0, keepdims=True)
    gains_ref[3:4] += jnp.sum(cot, axis=0, keepdims=True)
    grad = norm_back(cot * gain2, normed2, inverse2)
    dfeed = grad.astype(low)
    dfeed_ref[...] = dfeed
    for part in range(parts):
        at = slice(part * width, (part + 1) * width)
        dproduct = dot_nt(dfeed, down_w[at, :])
        dgate = (dproduct * gate_factor[:, at]).astype(low)
        dlift = (dproduct * lift_factor[:, at]).astype(low)
        dgate_ref[:, at] = dgate
        dlift_ref[:, at] = dlift
        grad = grad + dot_nt(dgate, gate_w[part]) + dot_nt(dlift, up_w[part])
    gains_ref[0:1] += jnp.sum(grad * normed1, axis=0, keepdims=True)
    gains_ref[1:2] += jnp.sum(grad, axis=0, keepdims=True)
    grad = norm_back(grad * gain1, normed1, inverse1)
    dz1_ref[...] = grad
    dbranch = grad.astype(low)
    dbranch_ref[...] = dbranch
    da_ref[...] = dot_nt(dbranch, out_w[...]).astype(low)


def middle(plan, ids, attended, tokens, cot, vectors, sources, hidden):
    rows, width = tokens.shape
    block = TOKEN_BLOCK
    tile = lambda w: pl.BlockSpec((block, w), lambda i, *_: (i, 0))
    whole = pl.BlockSpec((8, width), lambda i, *_: (0, 0))
    return pl.pallas_call(
        functools.partial(middle_kernel, plan, len(sources)),
        grid_spec=pltpu.PrefetchScalarGridSpec(
            num_scalar_prefetch=1,
            grid=(rows // block,),
            in_specs=[
                tile(width),
                tile(width),
                tile(width),
            ]
            + [pl.BlockSpec(vectors.shape, lambda i, *_: (0, 0, 0))]
            + [pl.BlockSpec(memory_space=pl.ANY)] * len(sources),
            out_specs=[
                tile(width),
                tile(width),
                tile(width),
                tile(width),
                tile(hidden),
                tile(width),
                tile(hidden),
                tile(hidden),
                tile(width),
                whole,
            ],
            scratch_shapes=[
                pltpu.VMEM((width, width), low),
                pltpu.VMEM((hidden // width, width, width), low),
                pltpu.VMEM((hidden // width, width, width), low),
                pltpu.VMEM((hidden, width), low),
                pltpu.VMEM((block, hidden), full),
                pltpu.VMEM((block, hidden), full),
                pltpu.VMEM((8, width), full),
                pltpu.SemaphoreType.DMA((4,)),
            ],
        ),
        out_shape=[
            shape((rows, width), low),
            shape((rows, width), full),
            shape((rows, width), low),
            shape((rows, width), low),
            shape((rows, hidden), low),
            shape((rows, width), low),
            shape((rows, hidden), low),
            shape((rows, hidden), low),
            shape((rows, width), low),
            shape((8, width), full),
        ],
        compiler_params=params(),
        cost_estimate=cost(53),
        name="middle",
    )(ids, attended, tokens, cot, vectors, *sources)


def weight_grad_kernel(a_ref, b_ref, o_ref):
    o_ref[...] = dot_tn(a_ref[...], b_ref[...]).astype(o_ref.dtype)


def weight_grad(a, b, tile_a=768, tile_b=768):
    rows, size_a = a.shape
    size_b = b.shape[1]
    return pl.pallas_call(
        weight_grad_kernel,
        grid=(size_a // tile_a, size_b // tile_b),
        in_specs=[
            pl.BlockSpec((rows, tile_a), lambda i, j: (0, i)),
            pl.BlockSpec((rows, tile_b), lambda i, j: (0, j)),
        ],
        out_specs=pl.BlockSpec((tile_a, tile_b), lambda i, j: (i, j)),
        out_shape=shape((size_a, size_b), low),
        compiler_params=params(),
        cost_estimate=cost(9),
        name="weight_grad",
    )(a, b)


def joint_kernel(halos, ids, dq_ref, own_ref, cos_ref, sin_ref, *refs):
    dj_ref = refs[-1]
    width = dq_ref.shape[1]
    by_mate = (pl.program_id(0) < pl.num_programs(0) // 2) == (ids[2] == 1)
    cosine = cos_ref[...]
    sine = sin_ref[...]
    start = 0
    for mate_ref, cross_ref in zip(refs[:halos], refs[halos : 2 * halos]):
        for at in range(0, mate_ref.shape[2], PAIR):
            near = [
                jnp.where(
                    by_mate, mate_ref[i, :, at : at + PAIR], cross_ref[i, :, at : at + PAIR]
                ).astype(full)
                for i in range(2)
            ]
            lanes = slice(start, start + PAIR)
            keys = turn_back(own_ref[0, :, lanes] + near[0], cosine, sine)
            dj_ref[:, lanes] = dq_ref[:, lanes]
            dj_ref[:, width + start : width + start + PAIR] = keys.astype(low)
            dj_ref[:, 2 * width + start : 2 * width + start + PAIR] = (
                own_ref[1, :, lanes] + near[1]
            ).astype(low)
            start += PAIR


def joint(ids, dq, own, edges, cosine, sine, at):
    rows, width = dq.shape
    mates, crosses = zip(*edges)
    part = sum(m.shape[2] for m in mates)
    block = TOKEN_BLOCK
    half = mates[0].shape[1] // block
    inner = pl.BlockSpec((block, PAIR), lambda i, ids: (i + half, 0))
    edge = lambda size, core: pl.BlockSpec(
        (2, block, size),
        lambda i, ids: (
            0,
            jnp.where(ids[2] == core, jnp.minimum(i, half - 1), jnp.maximum(i - half, 0)),
            0,
        ),
    )
    return pl.pallas_call(
        functools.partial(joint_kernel, len(edges)),
        grid_spec=pltpu.PrefetchScalarGridSpec(
            num_scalar_prefetch=1,
            grid=(rows // block,),
            in_specs=[
                pl.BlockSpec((block, part), lambda i, ids: (i, at)),
                pl.BlockSpec((2, block, part), lambda i, ids: (0, i, at)),
                inner,
                inner,
            ]
            + [edge(m.shape[2], 1) for m in mates]
            + [edge(m.shape[2], 0) for m in crosses],
            out_specs=pl.BlockSpec((block, 3 * part), lambda i, ids: (i, 0)),
        ),
        out_shape=shape((rows, 3 * part), low),
        compiler_params=params(),
        cost_estimate=cost(1),
        name="joint",
    )(ids, dq, own, cosine, sine, *mates, *crosses)


def input_grad_kernel(dj1_ref, dj2_ref, dz1_ref, weight_ref, out_ref):
    out = dz1_ref[...]
    at = 0
    for ref in (dj1_ref, dj2_ref):
        part = ref.shape[1] // 3
        for i in range(3):
            weight = weight_ref[i, :, at : at + part]
            out = out + dot_nt(ref[:, i * part : (i + 1) * part], weight)
        at += part
    out_ref[...] = out


def input_grad(dj1, dj2, dz1, weights):
    rows, width = dz1.shape
    block = 2 * TOKEN_BLOCK
    tile = lambda w: pl.BlockSpec((block, w), lambda i: (i, 0))
    return pl.pallas_call(
        input_grad_kernel,
        grid=(rows // block,),
        in_specs=[
            tile(dj1.shape[1]),
            tile(dj2.shape[1]),
            tile(width),
            pl.BlockSpec((3, width, width), lambda i: (0, 0, 0)),
        ],
        out_specs=tile(width),
        out_shape=shape((rows, width), full),
        compiler_params=params(),
        cost_estimate=cost(9),
        name="input_grad",
    )(dj1, dj2, dz1, weights)


def whole_joint_plan(ids, srcs, weight, sem):
    width = weight.shape[1]
    return [
        pltpu.make_async_copy(srcs[0].at[:, i * width : (i + 1) * width], weight.at[i], sem)
        for i in range(3)
    ] + [pltpu.make_async_copy(srcs[1], weight.at[3], sem)]


def whole_middle_plan(ids, srcs, weights, sems):
    out_w, gate_w, up_w, down_w = weights
    parts, _, width = gate_w.shape
    columns = lambda src, dst, sem: [
        pltpu.make_async_copy(src.at[:, i * width : (i + 1) * width], dst.at[i], sem)
        for i in range(parts)
    ]
    return (
        [pltpu.make_async_copy(srcs[0].at[3], out_w, sems.at[0])]
        + columns(srcs[1], gate_w, sems.at[1])
        + columns(srcs[2], up_w, sems.at[2])
        + [pltpu.make_async_copy(srcs[3], down_w, sems.at[3])]
    )


def swap_with(value, place):
    pairs = []
    for r in range(4):
        for z in range(4):
            for c in range(2):
                to_r, to_z, to_c = place(r, z, c)
                pairs.append(((r * 4 + z) * 2 + c, (to_r * 4 + to_z) * 2 + to_c))
    return lax.ppermute(value, ("rep", "fsdp"), pairs)


def over_core(value):
    return swap_with(value, lambda r, z, c: (r, z, 1 - c))


def over_square_1(value):
    return swap_with(value, lambda r, z, c: (r ^ (1 + c), z, c))


def over_square_2(value):
    return swap_with(value, lambda r, z, c: (r ^ (2 - c), z, c))


def over_z_1(value):
    return swap_with(value, lambda r, z, c: (r, z ^ (2 - c), c))


def over_z_2(value):
    return swap_with(value, lambda r, z, c: (r, z ^ (1 + c), c))


def pieces(ids, srcs):
    r, z, c = ids[0], ids[1], ids[2]
    found = []
    for i in range(2):
        core = (1 - c) if i else c
        bit1, bit2 = 1 + core, 2 - core
        shard, near, far = srcs[i], srcs[2 + i], srcs[4 + i]
        for quarter in range(4):
            found.append((shard.at[quarter], quarter, z, core))
        for ref, base in ((near, r), (far, r ^ bit2)):
            for j in range(2):
                for k in range(1, 4):
                    where = z ^ position(k, core)
                    found.append((ref.at[j, k - 1], base ^ bit1 if j else base, where, core))
    return found


def piece_joint_plan(ids, srcs, weight, sem):
    size = srcs[0].shape[1]
    copies = []
    for ref, quarter, z, core in pieces(ids, srcs):
        at = pl.multiple_of((2 * z + core) * size, size)
        copies.append(pltpu.make_async_copy(ref, weight.at[quarter, pl.ds(at, size)], sem))
    return copies


def piece_middle_plan(ids, srcs, weights, sems):
    out_w, gate_w, up_w, down_w = weights
    size = srcs[1].shape[1] // 3
    copies = [pltpu.make_async_copy(srcs[0].at[3], out_w, sems.at[0])]
    found = pieces(ids, srcs[1:])
    for i, target in enumerate((gate_w, up_w)):
        for ref, quarter, z, core in found:
            at = pl.multiple_of((2 * z + core) * size, size)
            copies.append(
                pltpu.make_async_copy(
                    ref.at[i * size : (i + 1) * size],
                    target.at[quarter, pl.ds(at, size)],
                    sems.at[1 + i],
                )
            )
    for ref, quarter, z, core in found:
        at = pl.multiple_of(((2 * z + core) * 4 + quarter) * size, size)
        copies.append(
            pltpu.make_async_copy(
                ref.at[2 * size : 3 * size], down_w.at[pl.ds(at, size)], sems.at[3]
            )
        )
    return copies


def put_pieces(ids, block_ref, own_ref, other_ref, first, size):
    z, c = ids[1], ids[2]
    for ref, core in ((own_ref, c), (other_ref, 1 - c)):
        for k in range(4):
            at = pl.multiple_of((2 * (z ^ position(k, core)) + core) * size, 8)
            ref[0, k, first : first + size, :] = block_ref[pl.ds(at, size), :].astype(low)


def gate_up_grad_kernel(
    ids, hidden_ref, dgate_ref, dlift_ref, at_ref, db_ref, gains_ref, own_ref, other_ref, block_ref, out_ref
):
    size = block_ref.shape[0] // 8
    slim = size // 4
    z, c = ids[1], ids[2]
    quarter = ids[0] ^ pl.program_id(0)

    @pl.when(pl.program_id(0) == 0)
    def _():
        out_ref[...] = dot_tn(at_ref[...], db_ref[...])

    for i, ref in enumerate((dgate_ref, dlift_ref)):
        block_ref[...] = dot_tn(hidden_ref[...], ref[...])
        put_pieces(ids, block_ref, own_ref, other_ref, i * size, size)
    for ref, core in ((own_ref, c), (other_ref, 1 - c)):
        for k in range(4):
            f = 2 * (z ^ position(k, core)) + core
            at = pl.multiple_of(f * size + quarter * slim, 8)
            row = jnp.pad(gains_ref[quarter * 8 + f][:8], ((0, 0), (0, ref.shape[3] - PAIR)))
            rest = jnp.concatenate([out_ref[pl.ds(at, slim), :], row])
            ref[0, k, 2 * size :, :] = rest.astype(low)


def grad_specs(size, width):
    own = pl.BlockSpec((1, 4, size, width), lambda j, ids: (position(j, ids[2]), 0, 0, 0))
    other = pl.BlockSpec((1, 4, size, width), lambda j, ids: (position(j, 1 - ids[2]), 0, 0, 0))
    return [own, other], [shape((4, 4, size, width), low)] * 2


def gate_up_grad(ids, hidden_low, dgate, dlift, attended, dbranch, gains):
    rows, width = hidden_low.shape
    size = width // 8
    out_specs, out_shape = grad_specs(2 * size + size // 4 + 8, width)
    column = pl.BlockSpec((rows, width), lambda j, ids: (0, ids[0] ^ j))
    whole = pl.BlockSpec((rows, width), lambda j, ids: (0, 0))
    return pl.pallas_call(
        gate_up_grad_kernel,
        grid_spec=pltpu.PrefetchScalarGridSpec(
            num_scalar_prefetch=1,
            grid=(4,),
            in_specs=[
                whole,
                column,
                column,
                whole,
                whole,
                pl.BlockSpec(gains.shape, lambda j, ids: (0, 0, 0)),
            ],
            out_specs=out_specs,
            scratch_shapes=[pltpu.VMEM((width, width), full), pltpu.VMEM((width, width), full)],
        ),
        out_shape=out_shape,
        compiler_params=params(),
        cost_estimate=cost(18),
        name="gate_up_grad",
    )(ids, hidden_low, dgate, dlift, attended, dbranch, gains)


def down_grad_kernel(ids, product_ref, dfeed_ref, own_ref, other_ref, block_ref):
    size = own_ref.shape[2]
    r, z, c = ids[0], ids[1], ids[2]
    step = pl.program_id(0)
    block_ref[...] = dot_tn(product_ref[...], dfeed_ref[...])
    for ref, core in ((own_ref, c), (other_ref, 1 - c)):
        for j in range(4):
            at = pl.multiple_of((core * 4 + (r ^ position(j, core))) * size, 8)
            ref[j, 0] = block_ref[pl.ds(at, size), :].astype(low)


def down_grad(ids, product, dfeed):
    rows, hidden = product.shape
    width = dfeed.shape[1]
    size = hidden // 32
    out = lambda core: pl.BlockSpec(
        (4, 1, size, width),
        lambda j, ids: (0, position(ids[1] ^ j, (1 - ids[2]) if core else ids[2]), 0, 0),
    )
    return pl.pallas_call(
        down_grad_kernel,
        grid_spec=pltpu.PrefetchScalarGridSpec(
            num_scalar_prefetch=1,
            grid=(4,),
            in_specs=[
                pl.BlockSpec((rows, hidden // 4), lambda j, ids: (0, j)),
                pl.BlockSpec((rows, width), lambda j, ids: (0, 0)),
            ],
            out_specs=[out(0), out(1)],
            scratch_shapes=[pltpu.VMEM((hidden // 4, width), full)],
        ),
        out_shape=[shape((4, 4, size, width), low)] * 2,
        compiler_params=params(),
        cost_estimate=cost(10),
        name="down_grad",
    )(ids, product, dfeed)


def joint_grad_1_kernel(ids, tok_ref, dj_ref, own_ref, other_ref, block_ref):
    block_ref[...] = dot_tn(tok_ref[...], dj_ref[...])
    put_pieces(ids, block_ref, own_ref, other_ref, 0, block_ref.shape[0] // 8)


def joint_grad_1(ids, tokens, djoint):
    rows, width = tokens.shape
    part = djoint.shape[1] // 4
    out_specs, out_shape = grad_specs(width // 8, part)
    return pl.pallas_call(
        joint_grad_1_kernel,
        grid_spec=pltpu.PrefetchScalarGridSpec(
            num_scalar_prefetch=1,
            grid=(4,),
            in_specs=[
                pl.BlockSpec((rows, width), lambda j, ids: (0, 0)),
                pl.BlockSpec((rows, part), lambda j, ids: (0, ids[0] ^ j)),
            ],
            out_specs=out_specs,
            scratch_shapes=[pltpu.VMEM((width, part), full)],
        ),
        out_shape=out_shape,
        compiler_params=params(),
        cost_estimate=cost(4),
        name="joint_grad",
    )(ids, tokens, djoint)


def joint_grad_2_kernel(ids, tok_ref, dj_ref, own_ref, other_ref, block_ref):
    size = block_ref.shape[0] // 8
    z, c = ids[1], ids[2]
    block_ref[...] = dot_tn(tok_ref[...], dj_ref[...])
    for ref, core in ((own_ref, c), (other_ref, 1 - c)):
        for k in range(4):
            at = pl.multiple_of((2 * (z ^ position(k, core)) + core) * size, 8)
            ref[k] = block_ref[pl.ds(at, size), :].astype(low)


def joint_grad_2(ids, tokens, djoint):
    rows, width = tokens.shape
    columns = djoint.shape[1]
    part = columns // 2
    out = pl.BlockSpec((4, width // 8, part), lambda j, ids: (0, 0, j))
    return pl.pallas_call(
        joint_grad_2_kernel,
        grid_spec=pltpu.PrefetchScalarGridSpec(
            num_scalar_prefetch=1,
            grid=(2,),
            in_specs=[
                pl.BlockSpec((rows, width), lambda j, ids: (0, 0)),
                pl.BlockSpec((rows, part), lambda j, ids: (0, j)),
            ],
            out_specs=[out, out],
            scratch_shapes=[pltpu.VMEM((width, part), full)],
        ),
        out_shape=[shape((4, width // 8, columns), low)] * 2,
        compiler_params=params(),
        cost_estimate=cost(5),
        name="joint_grad",
    )(ids, tokens, djoint)


def wide(v):
    return v.astype(full)


def sum_core(own, mate):
    return (wide(own[2:]) + wide(mate[2:])).astype(low)


def sum_square(own, mate, b):
    return (wide(own[1]) + wide(mate[1]) + wide(b[1])).astype(low)


def sum_rest(own, mate, b, d):
    return wide(own[0]) + wide(mate[0]) + wide(b[0]) + wide(d)


def sum_z(kept, e, f):
    return (kept[0] + wide(e[0]) + wide(f)).astype(low)


def place(ids, quarter):
    return position(quarter ^ ids[0], ids[2])


def finish_kernel(ids, near_ref, far_ref, gate_ref, up_ref, down_ref, out_ref, vec_ref):
    size, width = gate_ref.shape
    slim = out_ref.shape[0]
    at = place(ids, pl.program_id(0))

    def put(ref):
        piece = ref[at & 1].astype(full)
        gate_ref[...] = piece[:size]
        up_ref[...] = piece[size : 2 * size]
        out_ref[...] = piece[2 * size : 2 * size + slim]
        vec_ref[0] = piece[2 * size + slim : 2 * size + slim + 8, :PAIR]
        down_ref[...] = piece[2 * size + slim + 8 :]

    pl.when(at < 2)(lambda: put(near_ref))
    pl.when(at >= 2)(lambda: put(far_ref))


def finish(ids, near, far, size):
    width = near.shape[2]
    whole = pl.BlockSpec(near.shape, lambda j, ids: (0, 0, 0))
    column = pl.BlockSpec((size, width), lambda j, ids: (0, j))
    gate, up, down, out, vectors = pl.pallas_call(
        finish_kernel,
        grid_spec=pltpu.PrefetchScalarGridSpec(
            num_scalar_prefetch=1,
            grid=(4,),
            in_specs=[whole, whole],
            out_specs=[
                column,
                column,
                pl.BlockSpec((size, width), lambda j, ids: (j, 0)),
                pl.BlockSpec((size // 4, width), lambda j, ids: (j, 0)),
                pl.BlockSpec((1, 8, PAIR), lambda j, ids: (j, 0, 0)),
            ],
        ),
        out_shape=[shape((size, 4 * width), full)] * 2
        + [
            shape((4 * size, width), full),
            shape((size, width), full),
            shape((4, 8, PAIR), full),
        ],
        compiler_params=params(),
        cost_estimate=cost(5),
        name="finish",
    )(ids, near, far)
    return gate, up, down, out, vectors[:, 0, :size]


def finish_joint_kernel(ids, near_ref, far_ref, out_ref):
    width = out_ref.shape[1] // 3
    part = (near_ref.shape[1] - width) // 2
    first = 4 * part // 3
    for quarter in range(4):
        at = place(ids, quarter)
        halves = [
            jnp.where(at < 2, near_ref[:, i : i + part], far_ref[:, i : i + part])
            for i in (width, width + part)
        ]
        piece = jnp.where((at & 1) == 0, *halves).astype(full)
        for start in range(0, part, PAIR):
            which, column = divmod(quarter * part + start, first)
            column += which * width
            out_ref[:, column : column + PAIR] = piece[:, start : start + PAIR]
    rest = near_ref[:, :width].astype(full) + far_ref[:, :width].astype(full)
    rest = rest.astype(low).astype(full)
    second = width - first
    for which in range(3):
        column = which * width + first
        out_ref[:, column : column + second] = rest[:, which * second : (which + 1) * second]


def finish_joint(ids, near, far):
    size, columns = near.shape
    width = columns // 2
    whole = pl.BlockSpec(near.shape, lambda j, ids: (0, 0))
    return pl.pallas_call(
        finish_joint_kernel,
        grid_spec=pltpu.PrefetchScalarGridSpec(
            num_scalar_prefetch=1,
            grid=(1,),
            in_specs=[whole, whole],
            out_specs=pl.BlockSpec((size, 3 * width), lambda j, ids: (0, 0)),
        ),
        out_shape=shape((size, 3 * width), full),
        compiler_params=params(),
        cost_estimate=cost(3),
        name="finish_joint",
    )(ids, near, far)


def shards(
    custom,
    tokens,
    lengths,
    qkv_weight,
    out_weight,
    gate_weight,
    up_weight,
    down_weight,
    norm1_gain,
    norm1_bias,
    norm2_gain,
    norm2_bias,
    cotangent,
):
    rows, width = tokens.shape
    hidden = gate_weight.shape[1]
    size = lax.axis_size("fsdp")
    me = lax.axis_index("fsdp")
    r = lax.axis_index("rep")
    z, c = me // 2, me % 2
    ids = jnp.stack([r, z, c]).astype(jnp.int32)
    vectors = jnp.stack([norm1_gain, norm1_bias, norm2_gain, norm2_bias]).astype(low)

    mates = [(i, i ^ 1) for i in range(size)]
    crossed = [(i, i + 1 if i % 2 else i - 1) for i in range(1, size - 1)]
    swap_edges = lambda to_mate, to_cross: (
        lax.ppermute(to_mate, "fsdp", mates),
        lax.ppermute(to_cross, "fsdp", crossed),
    )
    edges = (tokens[rows - REACH :], tokens[:REACH])
    edges = (jnp.where(c == 0, *edges), jnp.where(c == 0, *edges[::-1]))
    if custom:
        part = qkv_weight.shape[0]
        columns = lambda w: jnp.swapaxes(w.astype(low).reshape(part, -1, width), 0, 1)
        column = lambda w, i: lax.dynamic_slice_in_dim(w, i * width, width, 1).astype(low)
        mine = jnp.where(
            r == 3, out_weight.astype(low), column(qkv_weight, jnp.minimum(r, 2))
        )
        first = over_z_2(mine)
        second = over_z_1(jnp.stack([mine, first]))
        rows_of = jnp.pad(vectors, ((0, 4), (0, width - part)))
        mine_2 = jnp.concatenate(
            [
                column(gate_weight, r),
                column(up_weight, r),
                lax.dynamic_slice_in_dim(down_weight, r * part, part, 0).astype(low),
                rows_of,
                over_core(rows_of),
            ]
        )
        shard_1 = jnp.concatenate([columns(qkv_weight), out_weight.astype(low)[None]])
        shard_2 = jnp.concatenate(
            [
                columns(gate_weight),
                columns(up_weight),
                down_weight.astype(low).reshape(4, part, width),
            ],
            axis=1,
        )
        mate_shard_1 = over_core(shard_1)
        own_1 = jnp.concatenate([first[None], after(second, mine_2, mate_shard_1)])
        first_2 = over_z_2(after(mine_2, own_1))
        other_1 = over_square_1(own_1)
        edges = swap_edges(*after(edges, first))
        mate_shard_2 = over_core(after(shard_2, own_1))
        near_1 = jnp.stack([own_1, after(other_1, shard_2, *edges)])
        far_1 = over_square_2(near_1)
        mate_near_1 = over_core(near_1)
        joint_sources = [shard_1, mate_shard_1, near_1, mate_near_1, far_1]
        joint_plan = piece_joint_plan
    else:
        edges = swap_edges(*edges)
        gather = lambda w: lax.all_gather(w.astype(low), "fsdp", axis=0, tiled=True)
        joint_sources = [gather(qkv_weight), gather(out_weight)]
        joint_plan = whole_joint_plan
        middle_sources = [gather(w) for w in (gate_weight, up_weight, down_weight)]
        vectors = lax.all_gather(vectors, "fsdp", axis=1, tiled=True)
        found = jnp.pad(vectors, ((0, 12), (0, 0)))[None]
        middle_plan = whole_middle_plan

    doc_lengths = lengths[0]
    ends = jnp.cumsum(doc_lengths)
    index = me * rows - REACH + jnp.arange(rows + 2 * REACH, dtype=jnp.int32)
    if custom:
        index = after(index, near_1)
    passed = (index[:, None] >= ends[None, :]).astype(jnp.int32)
    starts = jnp.sum(passed * doc_lengths[None, :], axis=1)
    cosine, sine = tables(index - starts)
    if custom:
        pair_2 = jnp.stack([mine_2, after(first_2, cosine)])
        second_2 = over_z_1(pair_2)
        mate_far_1 = over_core(after(far_1, pair_2))
        joint_sources.append(mate_far_1)
    own_starts = starts[REACH : REACH + rows]
    own_index = index[REACH : REACH + rows]
    stops = jnp.min(
        jnp.where(ends[None, :] > own_index[:, None], ends[None, :], size * rows), axis=1
    )
    base = me * rows - REACH
    bounds = jnp.stack(
        [
            jnp.maximum(own_starts, own_index - REACH) - base,
            jnp.minimum(stops, own_index + REACH + 1) - base,
        ]
    ).astype(jnp.int32)

    queries, keys, values, joint_weights = project(
        joint_plan, ids, edges, tokens, cosine, sine, joint_sources
    )
    given = (queries, keys, values)
    if custom:
        second_2 = after(second_2, queries)
        own_2 = jnp.concatenate([first_2[None, : 3 * part], second_2[:, : 3 * part]])
        found = jnp.concatenate([pair_2[:, 3 * part :, :PAIR], second_2[:, 3 * part :, :PAIR]])
        other_2 = over_square_1(own_2)
        done = attend(after(bounds, own_2, mate_shard_2), *given, 0, 2)
        near_2 = jnp.stack([own_2, after(other_2, done[1])])
        far_2 = over_square_2(near_2)
        mate_near_2 = over_core(near_2)
        done = attend(after(bounds, near_2), *given, 2, 2, done)
        attended, lse = attend(bounds, *given, 4, 2, done)
        mate_far_2 = over_core(after(far_2, lse, mate_near_2))
        middle_sources = [shard_2, mate_shard_2, near_2, mate_near_2, far_2, mate_far_2]
        middle_plan = piece_middle_plan
    else:
        done = None
        for first in (0, 2, 4):
            done = attend(bounds, *given, first, 2, done)
        attended, lse = done
    result, dz1, dattended, hidden_low, product, dfeed, dgate, dlift, dbranch, gains = middle(
        middle_plan,
        ids,
        attended,
        tokens,
        cotangent,
        found,
        [joint_weights, *middle_sources],
        hidden,
    )
    gains = gains[:4]
    given = (queries, keys, values, attended, dattended, lse)
    given += (cosine[REACH : REACH + rows], sine[REACH : REACH + rows])
    spread = lambda g: lax.psum_scatter(g, "fsdp", scatter_dimension=0, tiled=True)
    if custom:
        gains = jnp.pad(gains.reshape(32, 1, part), ((0, 0), (0, 7), (0, PAIR - part)))
        own, other = gate_up_grad(ids, hidden_low, dgate, dlift, attended, dbranch, gains)
        mate = over_core(other)
        own_d, other_d = down_grad(ids, after(product, own), dfeed)
        sent = sum_core(own, after(mate, own_d))
        b = over_square_2(sent)
        mate_d = over_core(after(other_d, sent))
        dq, dkv, to_mate, to_cross = attend_back(ids, after(bounds, sent), *given, 0, 2, (0, 2))
        edges = [swap_edges(to_mate, to_cross)]
        sent = sum_core(own_d, after(mate_d, dq))
        b_d = over_square_2(sent)
        dq, dkv, to_mate, to_cross = attend_back(
            ids, after(bounds, sent), *given, 2, 2, (2, 2), (dq, dkv)
        )
        edges.append(swap_edges(to_mate, to_cross))
        sent = sum_square(own, mate, after(b, dq, *edges[0]))
        d = over_square_1(sent)
        sent_d = sum_square(own_d, mate_d, after(b_d, sent))
        d_d = over_square_1(sent_d)
        dq, dkv, to_mate, to_cross = attend_back(
            ids, after(bounds, sent_d), *given, 4, 2, (4, 2), (dq, dkv)
        )
        edges_2 = [swap_edges(to_mate, to_cross)]
        kept = jnp.concatenate(
            [
                sum_rest(own, mate, b, after(d, dq, *edges[1])),
                sum_rest(own_d, mate_d, b_d, after(d_d, dq)),
            ],
            axis=1,
        )
        sent = kept[2:].astype(low)
        edges_2 = [after(edges_2[0], sent)]
        sent = after(sent, *edges_2[0])
        e = over_z_1(sent)
        dj1 = joint(ids, after(dq, sent), dkv, edges, cosine, sine, 0)
        dj2 = joint(ids, after(dq, dj1), dkv, edges_2, cosine, sine, 2)
        own_1, other_1 = joint_grad_1(ids, tokens, after(dj1, dj2))
        mate_1 = over_core(after(other_1, e))
        sent = (kept[1] + wide(after(e, own_1)[1])).astype(low)
        f = over_z_2(sent)
        own_2, other_2 = joint_grad_2(ids, tokens, after(dj2, own_1, sent))
        mate_2 = over_core(other_2)
        sent = sum_core(own_1, after(mate_1, own_2))
        b_1 = over_square_2(sent)
        mine = sum_z(kept, e, after(f, sent))
        got = over_square_1(mine)
        sent = sum_square(own_1, mate_1, after(b_1, mine))
        d_1 = over_square_1(sent)
        rest = wide(own_2) + wide(after(mate_2, sent))
        kept_1 = jnp.concatenate(
            [rest, sum_rest(own_1, mate_1, b_1, after(d_1, sent))], axis=2
        )
        sent = kept_1[2:].astype(low)
        e_1 = over_z_1(sent)
        grad_tokens = input_grad(after(dj1, sent), dj2, dz1, joint_weights)
        near = jnp.stack([mine, after(got, grad_tokens)])
        far = over_square_2(near)
        f_1 = over_z_2((kept_1[1] + wide(after(e_1, near)[1])).astype(low))
        mine = sum_z(kept_1, e_1, f_1)
        got = over_square_1(mine)
        gate_sum, up_sum, down_sum, out_sum, vector_sum = finish(
            ids, near, after(far, mine), part
        )
        got = after(got, gate_sum)
        pair = jnp.concatenate(
            [
                (wide(mine[:, :width]) + wide(got[:, :width])).astype(low),
                mine[:, width:],
                got[:, width:],
            ],
            axis=1,
        )
        joint_sum = finish_joint(ids, pair, over_square_2(pair))
        summed = (joint_sum, out_sum, gate_sum, up_sum, down_sum, vector_sum)
    else:
        share_down = spread(weight_grad(product, dfeed))
        share_gate = spread(weight_grad(hidden_low, dgate))
        share_up = spread(weight_grad(hidden_low, dlift))
        share_out = spread(weight_grad(attended, dbranch))
        share_gains = lax.psum_scatter(gains, "fsdp", scatter_dimension=1, tiled=True)
        dq, dkv, to_mate, to_cross = attend_back(ids, bounds, *given, 0, 4, (0, 4))
        edges_1 = swap_edges(to_mate, to_cross)
        dq, dkv, to_mate, to_cross = attend_back(ids, bounds, *given, 4, 2, (4, 2), (dq, dkv))
        edges_2 = swap_edges(to_mate, to_cross)
        dj1 = joint(ids, dq, dkv, [edges_1], cosine, sine, 0)
        dj2 = joint(ids, dq, dkv, [edges_2], cosine, sine, 2)
        share_1 = spread(weight_grad(tokens, dj1)).reshape(-1, 3, dj1.shape[1] // 3)
        share_2 = spread(weight_grad(tokens, dj2)).reshape(-1, 3, dj2.shape[1] // 3)
        share_qkv = jnp.concatenate([share_1, share_2], axis=2).reshape(-1, 3 * width)
        grad_tokens = input_grad(dj1, dj2, dz1, joint_weights)
        summed = lax.psum(
            tuple(
                s.astype(full)
                for s in (share_qkv, share_out, share_gate, share_up, share_down, share_gains)
            ),
            "rep",
        )
    return (result, grad_tokens, *summed[:5], *(summed[5][i] for i in range(4)))


def solution(mesh):
    rows = P(("rep", "fsdp"), None)
    matrix = P("fsdp", None)
    vector = P("fsdp")
    custom = (mesh.shape["rep"], mesh.shape["fsdp"]) == (4, 8)
    return jax.shard_map(
        functools.partial(shards, custom and not FORCE_WHOLE),
        mesh=mesh,
        in_specs=(rows, P("rep", None)) + (matrix,) * 5 + (vector,) * 4 + (rows,),
        out_specs=(rows, rows) + (matrix,) * 5 + (vector,) * 4,
        check_vma=False,
    )
```

```python
import functools
import math

import jax
import jax.numpy as jnp
from jax import lax
from jax.experimental import pallas as pl
from jax.experimental.pallas import tpu as pltpu
from jax.sharding import PartitionSpec as P

HEADS = 12
WINDOW = 1024
REACH = WINDOW // 2
HEAD = 64
PAIR = 2 * HEAD
QUERY_BLOCK = 256
TOKEN_BLOCK = 256
FORCE_WHOLE = False
VMEM = 56 * 1024 * 1024

epsilon = 1e-06
rope_base = 1000.0
masked_score = -1e30
low = jnp.bfloat16
full = jnp.float32


def dot_nn(a, b):
    return lax.dot_general(a, b, (((1,), (0,)), ((), ())), preferred_element_type=full)


def dot_nt(a, b):
    return lax.dot_general(a, b, (((1,), (1,)), ((), ())), preferred_element_type=full)


def dot_tn(a, b):
    return lax.dot_general(a, b, (((0,), (0,)), ((), ())), preferred_element_type=full)


def params():
    return pltpu.CompilerParams(vmem_limit_bytes=VMEM)


def after(value, *others):
    return lax.optimization_barrier((value, *others))[0]


def shape(dims, dtype):
    return jax.ShapeDtypeStruct(dims, dtype)


def cost(micros):
    return pl.CostEstimate(flops=int(micros * 0.575e9), bytes_accessed=1, transcendentals=0)


def tables(position):
    lane = jnp.arange(PAIR, dtype=jnp.int32) % HEAD
    half = HEAD // 2
    frequency = rope_base ** (-2.0 * (lane % half).astype(full) / HEAD)
    angle = position.astype(full)[:, None] * frequency[None, :]
    sign = jnp.where(lane < half, -1.0, 1.0).astype(full)
    return jnp.cos(angle), jnp.sin(angle) * sign[None, :]


def partner(x):
    half = HEAD // 2
    lane = lax.broadcasted_iota(jnp.int32, x.shape, 1) % HEAD
    return jnp.where(lane < half, pltpu.roll(x, PAIR - half, 1), pltpu.roll(x, half, 1))


def turn(x, cosine, sine):
    return x * cosine + partner(x) * sine


def turn_back(x, cosine, sine):
    return x * cosine - partner(x) * sine


def project_kernel(
    plan, sources, first, count, ids, mate_ref, tok_ref, cross_ref, cos_ref, sin_ref, *refs
):
    srcs = refs[:sources]
    q_ref, k_ref, v_ref, weight, sems = refs[sources:]
    step = pl.program_id(0)

    @pl.when(step == 0)
    def _():
        for copy in plan(ids, srcs, weight, sems.at[0]):
            copy.start()
        pltpu.make_async_copy(weight, weight, sems.at[0]).wait()

    width = tok_ref.shape[1]
    inside = (step >= first) & (step < first + count)
    by_mate = (step < first) == (ids[2] == 1)
    rows = jnp.where(
        inside, tok_ref[...], jnp.where(by_mate, mate_ref[...], cross_ref[...])
    )
    cosine = cos_ref[...]
    sine = sin_ref[...]
    keys = dot_nn(rows, weight[1])
    for at in range(0, width, PAIR):
        k_ref[:, at : at + PAIR] = turn(keys[:, at : at + PAIR], cosine, sine).astype(low)
    v_ref[...] = dot_nn(rows, weight[2]).astype(low)

    @pl.when((step >= first) & (step < first + count))
    def _():
        queries = dot_nn(rows, weight[0])
        for at in range(0, width, PAIR):
            turned = turn(queries[:, at : at + PAIR], cosine, sine).astype(low)
            q_ref[:, at : at + PAIR] = (turned.astype(full) * (1.0 / math.sqrt(HEAD))).astype(low)


def project(plan, ids, edges, tokens, cosine, sine, sources):
    rows, width = tokens.shape
    mate, cross = edges
    ext = rows + 2 * mate.shape[0]
    block = 2 * TOKEN_BLOCK
    first, count = mate.shape[0] // block, rows // block
    tile = lambda w: pl.BlockSpec((block, w), lambda i, *_: (i, 0))
    inner = pl.BlockSpec((block, width), lambda i, *_: (jnp.clip(i - first, 0, count - 1), 0))
    edge = lambda core: pl.BlockSpec(
        (block, width),
        lambda i, ids: (
            jnp.where(
                ids[2] == core, jnp.minimum(i, first - 1), jnp.maximum(i - first - count, 0)
            ),
            0,
        ),
    )
    return pl.pallas_call(
        functools.partial(project_kernel, plan, len(sources), first, count),
        grid_spec=pltpu.PrefetchScalarGridSpec(
            num_scalar_prefetch=1,
            grid=(ext // block,),
            in_specs=[
                edge(1),
                inner,
                edge(0),
                tile(PAIR),
                tile(PAIR),
            ]
            + [pl.BlockSpec(memory_space=pl.ANY)] * len(sources),
            out_specs=[
                inner,
                tile(width),
                tile(width),
                pl.BlockSpec((4, width, width), lambda i, *_: (0, 0, 0)),
            ],
            scratch_shapes=[pltpu.SemaphoreType.DMA((1,))],
        ),
        out_shape=[
            shape((rows, width), low),
            shape((ext, width), low),
            shape((ext, width), low),
            shape((4, width, width), low),
        ],
        compiler_params=params(),
        cost_estimate=cost(0.1),
        name="project",
    )(ids, mate, tokens, cross, cosine, sine, *sources)


def fill_bias(bounds_ref, bias_ref, blocks, span):
    for b in range(blocks):
        lo = bounds_ref[0:1, b * QUERY_BLOCK : (b + 1) * QUERY_BLOCK] - b * QUERY_BLOCK
        hi = bounds_ref[1:2, b * QUERY_BLOCK : (b + 1) * QUERY_BLOCK] - b * QUERY_BLOCK
        at = lax.broadcasted_iota(jnp.int32, (span, QUERY_BLOCK), 0)
        bias_ref[b] = jnp.where((at >= lo) & (at < hi), 0.0, masked_score)


def only(x, head):
    lane = lax.broadcasted_iota(jnp.int32, x.shape, 1)
    return jnp.where((lane >= HEAD) if head else (lane < HEAD), x, jnp.zeros_like(x))


def attend_kernel(chunk, bounds_ref, q_ref, k_ref, v_ref, *refs):
    o_ref, lse_ref, bias_ref, vt_ref, s_ref = refs[-5:]
    rows = q_ref.shape[0]
    block = QUERY_BLOCK
    blocks = rows // block
    span = k_ref.shape[0] - rows + block

    @pl.when(pl.program_id(0) == 0)
    def _():
        fill_bias(bounds_ref, bias_ref, blocks, span)

    vt_ref[...] = v_ref[...].T
    chunks = [(c, min(chunk, span - c)) for c in range(0, span, chunk)]
    steps = [(b, h) for b in range(blocks) for h in range(2)]
    fold = lambda x, by: by(x.reshape(x.shape[0] // 64, 64, block), axis=0)
    add = lambda old, new: new if old is None else old + new

    def begin(i):
        b, h = steps[i]
        return {"query": only(q_ref[b * block : (b + 1) * block, :], h), "top": None}

    def score(i, c, n, state):
        b, _ = steps[i]
        s = dot_nt(k_ref[b * block + c : b * block + c + n, :], state["query"])
        s = s + bias_ref[b, c : c + n, :]
        s_ref[i % 2, c : c + n, :] = s
        top = fold(s, jnp.max)
        state["top"] = top if state["top"] is None else jnp.maximum(state["top"], top)

    def weigh(i, c, n, state):
        b, h = steps[i]
        e = jnp.exp(s_ref[i % 2, c : c + n, :] - state["peak"])
        state["total"] = add(state.get("total"), fold(e, jnp.sum))
        lanes = slice(b * block + c, b * block + c + n)
        mixed = dot_nn(vt_ref[h * HEAD : (h + 1) * HEAD, lanes], e.astype(low))
        state["mixed"] = add(state.get("mixed"), mixed)

    state = begin(0)
    for c, n in chunks:
        score(0, c, n, state)
    out = []
    for i, (b, h) in enumerate(steps):
        state["peak"] = jnp.max(state["top"], axis=0, keepdims=True)
        following = begin(i + 1) if i + 1 < len(steps) else None
        for c, n in chunks:
            if following is not None:
                score(i + 1, c, n, following)
            weigh(i, c, n, state)
        total = jnp.sum(state["total"], axis=0, keepdims=True)
        out.append(state["mixed"] / total)
        at = slice(b * block, (b + 1) * block)
        lse_ref[0, h : h + 1, at] = state["peak"] + jnp.log(total)
        if h == 1:
            o_ref[at, :] = jnp.concatenate(out, axis=0).T.astype(low)
            out = []
        state = following


def attend(bounds, q, k, v, first, pairs, before=None, chunk=640):
    rows, width = q.shape
    ext = k.shape[0]
    blocks = rows // QUERY_BLOCK
    span = ext - rows + QUERY_BLOCK
    own = pl.BlockSpec((rows, PAIR), lambda p: (0, p + first))
    wide = pl.BlockSpec((ext, PAIR), lambda p: (0, p + first))
    before = () if before is None else tuple(before)
    return pl.pallas_call(
        functools.partial(attend_kernel, chunk),
        grid=(pairs,),
        in_specs=[pl.BlockSpec((2, rows), lambda p: (0, 0)), own, wide, wide]
        + [pl.BlockSpec(memory_space=pl.ANY)] * len(before),
        out_specs=[own, pl.BlockSpec((1, 2, rows), lambda p: (p + first, 0, 0))],
        out_shape=[shape((rows, width), low), shape((width // PAIR, 2, rows), full)],
        input_output_aliases={4 + i: i for i in range(len(before))},
        scratch_shapes=[
            pltpu.VMEM((blocks, span, QUERY_BLOCK), full),
            pltpu.VMEM((PAIR, ext), low),
            pltpu.VMEM((2, span, QUERY_BLOCK), full),
        ],
        compiler_params=params(),
        cost_estimate=cost(2 * pairs),
        name="attend",
    )(bounds, q, k, v, *before)


def attend_back_kernel(
    chunk,
    ids,
    bounds_ref,
    q_ref,
    k_ref,
    v_ref,
    o_ref,
    do_ref,
    lse_ref,
    *refs,
):
    cos_ref, sin_ref = refs[:2]
    dq_ref, own_ref, mate_ref, cross_ref = refs[-10:-6]
    bias_ref, kt_ref, dk_ref, dv_ref, p_ref, ds_ref = refs[-6:]
    rows = q_ref.shape[0]
    ext = k_ref.shape[0]
    block = QUERY_BLOCK
    blocks = rows // block
    reach = (ext - rows) // 2
    span = ext - rows + block

    @pl.when(pl.program_id(0) == 0)
    def _():
        fill_bias(bounds_ref, bias_ref, blocks, span)

    kt_ref[...] = k_ref[...].T
    dk_ref[...] = jnp.zeros_like(dk_ref)
    dv_ref[...] = jnp.zeros_like(dv_ref)
    chunks = [(c, min(chunk, span - c)) for c in range(0, span, chunk)]

    def begin(b):
        at = slice(b * block, (b + 1) * block)
        q = q_ref[at, :]
        do = do_ref[at, :]
        product = (do.astype(full) * o_ref[at, :].astype(full)).T
        heads = range(2)
        return {
            "query": [only(q, h) for h in heads],
            "grad": [only(do, h) for h in heads],
            "delta": [
                jnp.sum(product[h * HEAD : (h + 1) * HEAD], axis=0, keepdims=True) for h in heads
            ],
            "lse": [lse_ref[0, h : h + 1, at] for h in heads],
            "dq": [None, None],
        }

    def score(b, h, c, n, state):
        rows_of = slice(b * block + c, b * block + c + n)
        lanes = slice(h * block, (h + 1) * block)
        s = dot_nt(k_ref[rows_of, :], state["query"][h]) + bias_ref[b, c : c + n, :]
        p = jnp.exp(s - state["lse"][h])
        dp = dot_nt(v_ref[rows_of, :], state["grad"][h])
        p_ref[b % 2, c : c + n, lanes] = p.astype(low)
        ds_ref[b % 2, c : c + n, lanes] = (p * (dp - state["delta"][h])).astype(low)

    def spread(b, h, c, n, state):
        rows_of = slice(b * block + c, b * block + c + n)
        if h == 0:
            both = jnp.concatenate(state["grad"], axis=0)
            dv_ref[rows_of, :] += dot_nn(p_ref[b % 2, c : c + n, :], both)
        else:
            both = jnp.concatenate(state["query"], axis=0)
            dk_ref[rows_of, :] += dot_nn(ds_ref[b % 2, c : c + n, :], both)
        ds = ds_ref[b % 2, c : c + n, h * block : (h + 1) * block]
        t = dot_nn(kt_ref[h * HEAD : (h + 1) * HEAD, rows_of], ds)
        state["dq"][h] = t if state["dq"][h] is None else state["dq"][h] + t

    state = begin(0)
    for h in range(2):
        for c, n in chunks:
            score(0, h, c, n, state)
    for b in range(blocks):
        following = begin(b + 1) if b + 1 < blocks else None
        for h in range(2):
            for c, n in chunks:
                if following is not None:
                    score(b + 1, h, c, n, following)
                spread(b, h, c, n, state)
        at = slice(b * block, (b + 1) * block)
        turned = turn_back(jnp.concatenate(state["dq"], axis=0).T, cos_ref[at, :], sin_ref[at, :])
        dq_ref[at, :] = (turned * (1.0 / math.sqrt(HEAD))).astype(low)
        state = following
    first = ids[2] == 0
    for i, ref in enumerate((dk_ref, dv_ref)):
        prior = ref[:reach, :].astype(low)
        following = ref[reach + rows :, :].astype(low)
        own_ref[i] = ref[reach : reach + rows, :]
        mate_ref[i] = jnp.where(first, following, prior)
        cross_ref[i] = jnp.where(first, prior, following)


def attend_back(ids, bounds, q, k, v, o, do, lse, cosine, sine, first, pairs, halo, before=None, chunk=256):
    rows, width = q.shape
    ext = k.shape[0]
    blocks = rows // QUERY_BLOCK
    reach = (ext - rows) // 2
    span = ext - rows + QUERY_BLOCK
    halo_first, halo_pairs = halo
    before = () if before is None else tuple(before)
    own = pl.BlockSpec((rows, PAIR), lambda p, ids: (0, p + first))
    wide = pl.BlockSpec((ext, PAIR), lambda p, ids: (0, p + first))
    edge = pl.BlockSpec((2, reach, PAIR), lambda p, ids: (0, 0, p + first - halo_first))
    return pl.pallas_call(
        functools.partial(attend_back_kernel, chunk),
        grid_spec=pltpu.PrefetchScalarGridSpec(
            num_scalar_prefetch=1,
            grid=(pairs,),
            in_specs=[
            pl.BlockSpec((2, rows), lambda p, ids: (0, 0)),
            own,
            wide,
            wide,
            own,
            own,
            pl.BlockSpec((1, 2, rows), lambda p, ids: (p + first, 0, 0)),
            pl.BlockSpec((rows, PAIR), lambda p, ids: (0, 0)),
            pl.BlockSpec((rows, PAIR), lambda p, ids: (0, 0)),
        ]
        + [pl.BlockSpec(memory_space=pl.ANY)] * len(before),
        out_specs=[
            own,
            pl.BlockSpec((2, rows, PAIR), lambda p, ids: (0, 0, p + first)),
            edge,
            edge,
        ],
        scratch_shapes=[
            pltpu.VMEM((blocks, span, QUERY_BLOCK), full),
            pltpu.VMEM((PAIR, ext), low),
            pltpu.VMEM((ext, PAIR), full),
            pltpu.VMEM((ext, PAIR), full),
            pltpu.VMEM((2, span, 2 * QUERY_BLOCK), low),
            pltpu.VMEM((2, span, 2 * QUERY_BLOCK), low),
        ],
        ),
        out_shape=[
            shape((rows, width), low),
            shape((2, rows, width), full),
            shape((2, reach, halo_pairs * PAIR), low),
            shape((2, reach, halo_pairs * PAIR), low),
        ],
        input_output_aliases={10 + i: i for i in range(len(before))},
        compiler_params=params(),
        cost_estimate=cost(9 * pairs),
        name="attend_back",
    )(ids, bounds, q, k, v, o, do, lse, cosine, sine, *before)


def mean(x):
    return jnp.mean(x, axis=-1, keepdims=True)


def norm(x):
    centred = x - mean(x)
    inverse = lax.rsqrt(mean(centred * centred) + epsilon)
    return centred * inverse, inverse


def norm_back(scaled, normed, inverse):
    return inverse * (scaled - mean(scaled) - normed * mean(scaled * normed))


def position(j, core):
    return jnp.where(core == 0, j, (j & 1) * 2 + (j >> 1))


def gather_vectors(ids, vec_ref, width):
    count = vec_ref.shape[0]
    if count == 1:
        return vec_ref[0].astype(full)[:8]
    size = width // (2 * count)
    row = lax.broadcasted_iota(jnp.int32, (PAIR, width), 0)
    column = lax.broadcasted_iota(jnp.int32, (PAIR, width), 1)
    half = lax.broadcasted_iota(jnp.int32, (16, PAIR), 0) // 8
    out = jnp.zeros((16, width), full)
    for at in range(count):
        found = vec_ref[at].astype(full)
        for i in range(2):
            f = 2 * (ids[1] ^ position(at, ids[2])) + (ids[2] ^ i)
            place = ((column - f * size == row) & (row < size)).astype(full).astype(low)
            out = out + dot_nn(jnp.where(half == i, found, 0.0).astype(low), place)
    return out[:8] + out[8:]


def middle_kernel(plan, sources, ids, at_ref, tok_ref, cot_ref, *refs):
    vec_ref, refs = refs[0], refs[1:]
    srcs = refs[:sources]
    (
        out_ref,
        dz1_ref,
        da_ref,
        hidden_ref,
        product_ref,
        dfeed_ref,
        dgate_ref,
        dlift_ref,
        dbranch_ref,
        gains_ref,
        out_w,
        gate_w,
        up_w,
        down_w,
        lift_factor,
        gate_factor,
        vectors,
        sems,
    ) = refs[sources:]
    step = pl.program_id(0)
    weights = (out_w, gate_w, up_w, down_w)

    @pl.when(step == 0)
    def _():
        for copy in plan(ids, srcs, weights, sems):
            copy.start()
        gains_ref[...] = jnp.zeros_like(gains_ref)

    def ready(*which):
        @pl.when(step == 0)
        def _():
            for i in which:
                pltpu.make_async_copy(weights[i], weights[i], sems.at[i]).wait()

    parts, _, width = gate_w.shape

    @pl.when(step == 0)
    def _():
        vectors[...] = gather_vectors(ids, vec_ref, width)

    gain1, bias1, gain2, bias2 = (vectors[i : i + 1] for i in range(4))
    ready(0)
    normed1, inverse1 = norm(tok_ref[...].astype(full) + dot_nn(at_ref[...], out_w[...]))
    hidden = normed1 * gain1 + bias1
    hidden_low = hidden.astype(low)
    hidden_ref[...] = hidden_low
    ready(1, 2, 3)
    feed = None
    for part in range(parts):
        at = slice(part * width, (part + 1) * width)
        gate = dot_nn(hidden_low, gate_w[part])
        lift = dot_nn(hidden_low, up_w[part])
        sigma = jax.nn.sigmoid(gate)
        opened = gate * sigma
        product = (opened * lift).astype(low)
        product_ref[:, at] = product
        lift_factor[:, at] = opened
        gate_factor[:, at] = lift * sigma * (1.0 + gate * (1.0 - sigma))
        term = dot_nn(product, down_w[at, :])
        feed = term if feed is None else feed + term
    normed2, inverse2 = norm(hidden + feed)
    out_ref[...] = (normed2 * gain2 + bias2).astype(low)
    cot = cot_ref[...].astype(full)
    gains_ref[2:3] += jnp.sum(cot * normed2, axis=0, keepdims=True)
    gains_ref[3:4] += jnp.sum(cot, axis=0, keepdims=True)
    grad = norm_back(cot * gain2, normed2, inverse2)
    dfeed = grad.astype(low)
    dfeed_ref[...] = dfeed
    for part in range(parts):
        at = slice(part * width, (part + 1) * width)
        dproduct = dot_nt(dfeed, down_w[at, :])
        dgate = (dproduct * gate_factor[:, at]).astype(low)
        dlift = (dproduct * lift_factor[:, at]).astype(low)
        dgate_ref[:, at] = dgate
        dlift_ref[:, at] = dlift
        grad = grad + dot_nt(dgate, gate_w[part]) + dot_nt(dlift, up_w[part])
    gains_ref[0:1] += jnp.sum(grad * normed1, axis=0, keepdims=True)
    gains_ref[1:2] += jnp.sum(grad, axis=0, keepdims=True)
    grad = norm_back(grad * gain1, normed1, inverse1)
    dz1_ref[...] = grad
    dbranch = grad.astype(low)
    dbranch_ref[...] = dbranch
    da_ref[...] = dot_nt(dbranch, out_w[...]).astype(low)


def middle(plan, ids, attended, tokens, cot, vectors, sources, hidden):
    rows, width = tokens.shape
    block = TOKEN_BLOCK
    tile = lambda w: pl.BlockSpec((block, w), lambda i, *_: (i, 0))
    whole = pl.BlockSpec((8, width), lambda i, *_: (0, 0))
    return pl.pallas_call(
        functools.partial(middle_kernel, plan, len(sources)),
        grid_spec=pltpu.PrefetchScalarGridSpec(
            num_scalar_prefetch=1,
            grid=(rows // block,),
            in_specs=[
                tile(width),
                tile(width),
                tile(width),
            ]
            + [pl.BlockSpec(vectors.shape, lambda i, *_: (0, 0, 0))]
            + [pl.BlockSpec(memory_space=pl.ANY)] * len(sources),
            out_specs=[
                tile(width),
                tile(width),
                tile(width),
                tile(width),
                tile(hidden),
                tile(width),
                tile(hidden),
                tile(hidden),
                tile(width),
                whole,
            ],
            scratch_shapes=[
                pltpu.VMEM((width, width), low),
                pltpu.VMEM((hidden // width, width, width), low),
                pltpu.VMEM((hidden // width, width, width), low),
                pltpu.VMEM((hidden, width), low),
                pltpu.VMEM((block, hidden), full),
                pltpu.VMEM((block, hidden), full),
                pltpu.VMEM((8, width), full),
                pltpu.SemaphoreType.DMA((4,)),
            ],
        ),
        out_shape=[
            shape((rows, width), low),
            shape((rows, width), full),
            shape((rows, width), low),
            shape((rows, width), low),
            shape((rows, hidden), low),
            shape((rows, width), low),
            shape((rows, hidden), low),
            shape((rows, hidden), low),
            shape((rows, width), low),
            shape((8, width), full),
        ],
        compiler_params=params(),
        cost_estimate=cost(53),
        name="middle",
    )(ids, attended, tokens, cot, vectors, *sources)


def weight_grad_kernel(a_ref, b_ref, o_ref):
    o_ref[...] = dot_tn(a_ref[...], b_ref[...]).astype(o_ref.dtype)


def weight_grad(a, b, tile_a=768, tile_b=768):
    rows, size_a = a.shape
    size_b = b.shape[1]
    return pl.pallas_call(
        weight_grad_kernel,
        grid=(size_a // tile_a, size_b // tile_b),
        in_specs=[
            pl.BlockSpec((rows, tile_a), lambda i, j: (0, i)),
            pl.BlockSpec((rows, tile_b), lambda i, j: (0, j)),
        ],
        out_specs=pl.BlockSpec((tile_a, tile_b), lambda i, j: (i, j)),
        out_shape=shape((size_a, size_b), low),
        compiler_params=params(),
        cost_estimate=cost(9),
        name="weight_grad",
    )(a, b)


def joint_kernel(halos, ids, dq_ref, own_ref, cos_ref, sin_ref, *refs):
    by_mate = (pl.program_id(0) < pl.num_programs(0) // 2) == (ids[2] == 1)
    cosine = cos_ref[...]
    sine = sin_ref[...]
    dj_ref = refs[-1]
    width = dq_ref.shape[1]
    start = 0
    for mate_ref, cross_ref in zip(refs[:halos], refs[halos : 2 * halos]):
        for at in range(0, mate_ref.shape[2], PAIR):
            near = [
                jnp.where(
                    by_mate, mate_ref[i, :, at : at + PAIR], cross_ref[i, :, at : at + PAIR]
                ).astype(full)
                for i in range(2)
            ]
            lanes = slice(start, start + PAIR)
            keys = turn_back(own_ref[0, :, lanes] + near[0], cosine, sine)
            values = own_ref[1, :, lanes] + near[1]
            for i, x in enumerate((dq_ref[:, lanes], keys, values)):
                dj_ref[:, i * width + start : i * width + start + PAIR] = x.astype(low)
            start += PAIR


def joint(ids, dq, own, edges, cosine, sine):
    rows, width = dq.shape
    mates, crosses = zip(*edges)
    block = TOKEN_BLOCK
    half = mates[0].shape[1] // block
    inner = pl.BlockSpec((block, PAIR), lambda i, ids: (i + half, 0))
    tile = lambda w: pl.BlockSpec((block, w), lambda i, ids: (i, 0))
    edge = lambda size, core: pl.BlockSpec(
        (2, block, size),
        lambda i, ids: (
            0,
            jnp.where(ids[2] == core, jnp.minimum(i, half - 1), jnp.maximum(i - half, 0)),
            0,
        ),
    )
    return pl.pallas_call(
        functools.partial(joint_kernel, len(edges)),
        grid_spec=pltpu.PrefetchScalarGridSpec(
            num_scalar_prefetch=1,
            grid=(rows // block,),
            in_specs=[
                tile(width),
                pl.BlockSpec((2, block, width), lambda i, ids: (0, i, 0)),
                inner,
                inner,
            ]
            + [edge(m.shape[2], 1) for m in mates]
            + [edge(m.shape[2], 0) for m in crosses],
            out_specs=tile(3 * width),
        ),
        out_shape=shape((rows, 3 * width), low),
        compiler_params=params(),
        cost_estimate=cost(2),
        name="joint",
    )(ids, dq, own, cosine, sine, *mates, *crosses)


def input_grad_kernel(dj_ref, dz1_ref, weight_ref, out_ref):
    width = dz1_ref.shape[1]
    out = dz1_ref[...]
    for i in range(3):
        out = out + dot_nt(dj_ref[:, i * width : (i + 1) * width], weight_ref[i])
    out_ref[...] = out


def input_grad(djoint, dz1, weights):
    rows, width = dz1.shape
    block = 2 * TOKEN_BLOCK
    tile = lambda w: pl.BlockSpec((block, w), lambda i: (i, 0))
    return pl.pallas_call(
        input_grad_kernel,
        grid=(rows // block,),
        in_specs=[
            tile(3 * width),
            tile(width),
            pl.BlockSpec((3, width, width), lambda i: (0, 0, 0)),
        ],
        out_specs=tile(width),
        out_shape=shape((rows, width), full),
        compiler_params=params(),
        cost_estimate=cost(9),
        name="input_grad",
    )(djoint, dz1, weights)


def whole_joint_plan(ids, srcs, weight, sem):
    width = weight.shape[1]
    return [
        pltpu.make_async_copy(srcs[0].at[:, i * width : (i + 1) * width], weight.at[i], sem)
        for i in range(3)
    ] + [pltpu.make_async_copy(srcs[1], weight.at[3], sem)]


def whole_middle_plan(ids, srcs, weights, sems):
    out_w, gate_w, up_w, down_w = weights
    parts, _, width = gate_w.shape
    columns = lambda src, dst, sem: [
        pltpu.make_async_copy(src.at[:, i * width : (i + 1) * width], dst.at[i], sem)
        for i in range(parts)
    ]
    return (
        [pltpu.make_async_copy(srcs[0].at[3], out_w, sems.at[0])]
        + columns(srcs[1], gate_w, sems.at[1])
        + columns(srcs[2], up_w, sems.at[2])
        + [pltpu.make_async_copy(srcs[3], down_w, sems.at[3])]
    )


def swap_with(value, place):
    pairs = []
    for r in range(4):
        for z in range(4):
            for c in range(2):
                to_r, to_z, to_c = place(r, z, c)
                pairs.append(((r * 4 + z) * 2 + c, (to_r * 4 + to_z) * 2 + to_c))
    return lax.ppermute(value, ("rep", "fsdp"), pairs)


def over_core(value):
    return swap_with(value, lambda r, z, c: (r, z, 1 - c))


def over_square_1(value):
    return swap_with(value, lambda r, z, c: (r ^ (1 + c), z, c))


def over_square_2(value):
    return swap_with(value, lambda r, z, c: (r ^ (2 - c), z, c))


def over_z_1(value):
    return swap_with(value, lambda r, z, c: (r, z ^ (2 - c), c))


def over_z_2(value):
    return swap_with(value, lambda r, z, c: (r, z ^ (1 + c), c))


def pieces(ids, srcs):
    r, z, c = ids[0], ids[1], ids[2]
    found = []
    for i in range(2):
        core = (1 - c) if i else c
        bit1, bit2 = 1 + core, 2 - core
        shard, near, far = srcs[i], srcs[2 + i], srcs[4 + i]
        for quarter in range(4):
            found.append((shard.at[quarter], quarter, z, core))
        for ref, base in ((near, r), (far, r ^ bit2)):
            for j in range(2):
                for k in range(1, 4):
                    where = z ^ position(k, core)
                    found.append((ref.at[j, k - 1], base ^ bit1 if j else base, where, core))
    return found


def piece_joint_plan(ids, srcs, weight, sem):
    size = srcs[0].shape[1]
    copies = []
    for ref, quarter, z, core in pieces(ids, srcs):
        at = pl.multiple_of((2 * z + core) * size, size)
        copies.append(pltpu.make_async_copy(ref, weight.at[quarter, pl.ds(at, size)], sem))
    return copies


def piece_middle_plan(ids, srcs, weights, sems):
    out_w, gate_w, up_w, down_w = weights
    size = srcs[1].shape[1] // 3
    copies = [pltpu.make_async_copy(srcs[0].at[3], out_w, sems.at[0])]
    found = pieces(ids, srcs[1:])
    for i, target in enumerate((gate_w, up_w)):
        for ref, quarter, z, core in found:
            at = pl.multiple_of((2 * z + core) * size, size)
            copies.append(
                pltpu.make_async_copy(
                    ref.at[i * size : (i + 1) * size],
                    target.at[quarter, pl.ds(at, size)],
                    sems.at[1 + i],
                )
            )
    for ref, quarter, z, core in found:
        at = pl.multiple_of(((2 * z + core) * 4 + quarter) * size, size)
        copies.append(
            pltpu.make_async_copy(
                ref.at[2 * size : 3 * size], down_w.at[pl.ds(at, size)], sems.at[3]
            )
        )
    return copies


def put_pieces(ids, block_ref, own_ref, other_ref, first, size):
    z, c = ids[1], ids[2]
    for ref, core in ((own_ref, c), (other_ref, 1 - c)):
        for k in range(4):
            at = pl.multiple_of((2 * (z ^ position(k, core)) + core) * size, 8)
            ref[0, k, first : first + size, :] = block_ref[pl.ds(at, size), :].astype(low)


def gate_up_grad_kernel(
    ids, hidden_ref, dgate_ref, dlift_ref, at_ref, db_ref, gains_ref, own_ref, other_ref, block_ref, out_ref
):
    size = block_ref.shape[0] // 8
    slim = size // 4
    z, c = ids[1], ids[2]
    quarter = ids[0] ^ pl.program_id(0)

    @pl.when(pl.program_id(0) == 0)
    def _():
        out_ref[...] = dot_tn(at_ref[...], db_ref[...])

    for i, ref in enumerate((dgate_ref, dlift_ref)):
        block_ref[...] = dot_tn(hidden_ref[...], ref[...])
        put_pieces(ids, block_ref, own_ref, other_ref, i * size, size)
    for ref, core in ((own_ref, c), (other_ref, 1 - c)):
        for k in range(4):
            f = 2 * (z ^ position(k, core)) + core
            at = pl.multiple_of(f * size + quarter * slim, 8)
            row = jnp.pad(gains_ref[quarter * 8 + f][:8], ((0, 0), (0, ref.shape[3] - PAIR)))
            rest = jnp.concatenate([out_ref[pl.ds(at, slim), :], row])
            ref[0, k, 2 * size :, :] = rest.astype(low)


def grad_specs(size, width):
    own = pl.BlockSpec((1, 4, size, width), lambda j, ids: (position(j, ids[2]), 0, 0, 0))
    other = pl.BlockSpec((1, 4, size, width), lambda j, ids: (position(j, 1 - ids[2]), 0, 0, 0))
    return [own, other], [shape((4, 4, size, width), low)] * 2


def gate_up_grad(ids, hidden_low, dgate, dlift, attended, dbranch, gains):
    rows, width = hidden_low.shape
    size = width // 8
    out_specs, out_shape = grad_specs(2 * size + size // 4 + 8, width)
    column = pl.BlockSpec((rows, width), lambda j, ids: (0, ids[0] ^ j))
    whole = pl.BlockSpec((rows, width), lambda j, ids: (0, 0))
    return pl.pallas_call(
        gate_up_grad_kernel,
        grid_spec=pltpu.PrefetchScalarGridSpec(
            num_scalar_prefetch=1,
            grid=(4,),
            in_specs=[
                whole,
                column,
                column,
                whole,
                whole,
                pl.BlockSpec(gains.shape, lambda j, ids: (0, 0, 0)),
            ],
            out_specs=out_specs,
            scratch_shapes=[pltpu.VMEM((width, width), full), pltpu.VMEM((width, width), full)],
        ),
        out_shape=out_shape,
        compiler_params=params(),
        cost_estimate=cost(18),
        name="gate_up_grad",
    )(ids, hidden_low, dgate, dlift, attended, dbranch, gains)


def down_grad_kernel(ids, product_ref, dfeed_ref, own_ref, other_ref, block_ref):
    size = own_ref.shape[2]
    r, z, c = ids[0], ids[1], ids[2]
    step = pl.program_id(0)
    block_ref[...] = dot_tn(product_ref[...], dfeed_ref[...])
    for ref, core in ((own_ref, c), (other_ref, 1 - c)):
        for j in range(4):
            at = pl.multiple_of((core * 4 + (r ^ position(j, core))) * size, 8)
            ref[j, 0] = block_ref[pl.ds(at, size), :].astype(low)


def down_grad(ids, product, dfeed):
    rows, hidden = product.shape
    width = dfeed.shape[1]
    size = hidden // 32
    out = lambda core: pl.BlockSpec(
        (4, 1, size, width),
        lambda j, ids: (0, position(ids[1] ^ j, (1 - ids[2]) if core else ids[2]), 0, 0),
    )
    return pl.pallas_call(
        down_grad_kernel,
        grid_spec=pltpu.PrefetchScalarGridSpec(
            num_scalar_prefetch=1,
            grid=(4,),
            in_specs=[
                pl.BlockSpec((rows, hidden // 4), lambda j, ids: (0, j)),
                pl.BlockSpec((rows, width), lambda j, ids: (0, 0)),
            ],
            out_specs=[out(0), out(1)],
            scratch_shapes=[pltpu.VMEM((hidden // 4, width), full)],
        ),
        out_shape=[shape((4, 4, size, width), low)] * 2,
        compiler_params=params(),
        cost_estimate=cost(10),
        name="down_grad",
    )(ids, product, dfeed)


def joint_grad_kernel(ids, tok_ref, dj_ref, own_ref, other_ref, block_ref):
    block_ref[...] = dot_tn(tok_ref[...], dj_ref[...])
    put_pieces(ids, block_ref, own_ref, other_ref, 0, block_ref.shape[0] // 8)


def half(r, core):
    return jnp.where(core == 0, r >> 1, r & 1)


def joint_grad(ids, tokens, djoint):
    rows, width = tokens.shape
    part = djoint.shape[1] // 2
    size = width // 8
    out = lambda other: pl.BlockSpec(
        (1, 4, size, part),
        lambda j, ids: (j ^ half(ids[0], (1 - ids[2]) if other else ids[2]), 0, 0, 0),
    )
    return pl.pallas_call(
        joint_grad_kernel,
        grid_spec=pltpu.PrefetchScalarGridSpec(
            num_scalar_prefetch=1,
            grid=(2,),
            in_specs=[
                pl.BlockSpec((rows, width), lambda j, ids: (0, 0)),
                pl.BlockSpec((rows, part), lambda j, ids: (0, j)),
            ],
            out_specs=[out(0), out(1)],
            scratch_shapes=[pltpu.VMEM((width, part), full)],
        ),
        out_shape=[shape((2, 4, size, part), low)] * 2,
        compiler_params=params(),
        cost_estimate=cost(4),
        name="joint_grad",
    )(ids, tokens, djoint)


def wide(v):
    return v.astype(full)


def sum_core(own, mate):
    return (wide(own[2:]) + wide(mate[2:])).astype(low)


def sum_square(own, mate, b):
    return (wide(own[1]) + wide(mate[1]) + wide(b[1])).astype(low)


def sum_rest(own, mate, b, d):
    return wide(own[0]) + wide(mate[0]) + wide(b[0]) + wide(d)


def sum_z(kept, e, f):
    return (kept[0] + wide(e[0]) + wide(f)).astype(low)


def place(ids, quarter):
    return position(quarter ^ ids[0], ids[2])


def finish_kernel(ids, near_ref, far_ref, gate_ref, up_ref, down_ref, out_ref, vec_ref):
    size, width = gate_ref.shape
    slim = out_ref.shape[0]
    at = place(ids, pl.program_id(0))

    def put(ref):
        piece = ref[at & 1].astype(full)
        gate_ref[...] = piece[:size]
        up_ref[...] = piece[size : 2 * size]
        out_ref[...] = piece[2 * size : 2 * size + slim]
        vec_ref[0] = piece[2 * size + slim : 2 * size + slim + 8, :PAIR]
        down_ref[...] = piece[2 * size + slim + 8 :]

    pl.when(at < 2)(lambda: put(near_ref))
    pl.when(at >= 2)(lambda: put(far_ref))


def finish(ids, near, far, size):
    width = near.shape[2]
    whole = pl.BlockSpec(near.shape, lambda j, ids: (0, 0, 0))
    column = pl.BlockSpec((size, width), lambda j, ids: (0, j))
    gate, up, down, out, vectors = pl.pallas_call(
        finish_kernel,
        grid_spec=pltpu.PrefetchScalarGridSpec(
            num_scalar_prefetch=1,
            grid=(4,),
            in_specs=[whole, whole],
            out_specs=[
                column,
                column,
                pl.BlockSpec((size, width), lambda j, ids: (j, 0)),
                pl.BlockSpec((size // 4, width), lambda j, ids: (j, 0)),
                pl.BlockSpec((1, 8, PAIR), lambda j, ids: (j, 0, 0)),
            ],
        ),
        out_shape=[shape((size, 4 * width), full)] * 2
        + [
            shape((4 * size, width), full),
            shape((size, width), full),
            shape((4, 8, PAIR), full),
        ],
        compiler_params=params(),
        cost_estimate=cost(5),
        name="finish",
    )(ids, near, far)
    return gate, up, down, out, vectors[:, 0, :size]


def shards(
    custom,
    tokens,
    lengths,
    qkv_weight,
    out_weight,
    gate_weight,
    up_weight,
    down_weight,
    norm1_gain,
    norm1_bias,
    norm2_gain,
    norm2_bias,
    cotangent,
):
    rows, width = tokens.shape
    hidden = gate_weight.shape[1]
    size = lax.axis_size("fsdp")
    me = lax.axis_index("fsdp")
    r = lax.axis_index("rep")
    z, c = me // 2, me % 2
    ids = jnp.stack([r, z, c]).astype(jnp.int32)
    vectors = jnp.stack([norm1_gain, norm1_bias, norm2_gain, norm2_bias]).astype(low)

    mates = [(i, i ^ 1) for i in range(size)]
    crossed = [(i, i + 1 if i % 2 else i - 1) for i in range(1, size - 1)]
    swap_edges = lambda to_mate, to_cross: (
        lax.ppermute(to_mate, "fsdp", mates),
        lax.ppermute(to_cross, "fsdp", crossed),
    )
    edges = (tokens[rows - REACH :], tokens[:REACH])
    edges = (jnp.where(c == 0, *edges), jnp.where(c == 0, *edges[::-1]))
    if custom:
        part = qkv_weight.shape[0]
        columns = lambda w: jnp.swapaxes(w.astype(low).reshape(part, -1, width), 0, 1)
        column = lambda w, i: lax.dynamic_slice_in_dim(w, i * width, width, 1).astype(low)
        mine = jnp.where(
            r == 3, out_weight.astype(low), column(qkv_weight, jnp.minimum(r, 2))
        )
        first = over_z_2(mine)
        second = over_z_1(jnp.stack([mine, first]))
        rows_of = jnp.pad(vectors, ((0, 4), (0, width - part)))
        mine_2 = jnp.concatenate(
            [
                column(gate_weight, r),
                column(up_weight, r),
                lax.dynamic_slice_in_dim(down_weight, r * part, part, 0).astype(low),
                rows_of,
                over_core(rows_of),
            ]
        )
        shard_1 = jnp.concatenate([columns(qkv_weight), out_weight.astype(low)[None]])
        shard_2 = jnp.concatenate(
            [
                columns(gate_weight),
                columns(up_weight),
                down_weight.astype(low).reshape(4, part, width),
            ],
            axis=1,
        )
        mate_shard_1 = over_core(shard_1)
        own_1 = jnp.concatenate([first[None], after(second, mine_2, mate_shard_1)])
        first_2 = over_z_2(after(mine_2, own_1))
        other_1 = over_square_1(own_1)
        edges = swap_edges(*after(edges, first))
        mate_shard_2 = over_core(after(shard_2, own_1))
        near_1 = jnp.stack([own_1, after(other_1, shard_2, *edges)])
        far_1 = over_square_2(near_1)
        mate_near_1 = over_core(near_1)
        joint_sources = [shard_1, mate_shard_1, near_1, mate_near_1, far_1]
        joint_plan = piece_joint_plan
    else:
        edges = swap_edges(*edges)
        gather = lambda w: lax.all_gather(w.astype(low), "fsdp", axis=0, tiled=True)
        joint_sources = [gather(qkv_weight), gather(out_weight)]
        joint_plan = whole_joint_plan
        middle_sources = [gather(w) for w in (gate_weight, up_weight, down_weight)]
        vectors = lax.all_gather(vectors, "fsdp", axis=1, tiled=True)
        found = jnp.pad(vectors, ((0, 12), (0, 0)))[None]
        middle_plan = whole_middle_plan

    doc_lengths = lengths[0]
    ends = jnp.cumsum(doc_lengths)
    index = me * rows - REACH + jnp.arange(rows + 2 * REACH, dtype=jnp.int32)
    if custom:
        index = after(index, near_1)
    passed = (index[:, None] >= ends[None, :]).astype(jnp.int32)
    starts = jnp.sum(passed * doc_lengths[None, :], axis=1)
    cosine, sine = tables(index - starts)
    if custom:
        pair_2 = jnp.stack([mine_2, after(first_2, cosine)])
        second_2 = over_z_1(pair_2)
        mate_far_1 = over_core(after(far_1, pair_2))
        joint_sources.append(mate_far_1)
    own_starts = starts[REACH : REACH + rows]
    own_index = index[REACH : REACH + rows]
    stops = jnp.min(
        jnp.where(ends[None, :] > own_index[:, None], ends[None, :], size * rows), axis=1
    )
    base = me * rows - REACH
    bounds = jnp.stack(
        [
            jnp.maximum(own_starts, own_index - REACH) - base,
            jnp.minimum(stops, own_index + REACH + 1) - base,
        ]
    ).astype(jnp.int32)

    queries, keys, values, joint_weights = project(
        joint_plan, ids, edges, tokens, cosine, sine, joint_sources
    )
    given = (queries, keys, values)
    if custom:
        second_2 = after(second_2, queries)
        own_2 = jnp.concatenate([first_2[None, : 3 * part], second_2[:, : 3 * part]])
        found = jnp.concatenate([pair_2[:, 3 * part :, :PAIR], second_2[:, 3 * part :, :PAIR]])
        other_2 = over_square_1(own_2)
        done = attend(after(bounds, own_2, mate_shard_2), *given, 0, 2)
        tables_own = after((cosine, sine), done[1])
        tables_own = tuple(t[REACH : REACH + rows] for t in tables_own)
        near_2 = jnp.stack([own_2, after(other_2, done[1], *tables_own)])
        far_2 = over_square_2(near_2)
        mate_near_2 = over_core(near_2)
        done = attend(after(bounds, near_2), *given, 2, 2, done)
        attended, lse = attend(bounds, *given, 4, 2, done)
        mate_far_2 = over_core(after(far_2, lse, mate_near_2))
        middle_sources = [shard_2, mate_shard_2, near_2, mate_near_2, far_2, mate_far_2]
        middle_plan = piece_middle_plan
    else:
        done = None
        for first in (0, 2, 4):
            done = attend(bounds, *given, first, 2, done)
        attended, lse = done
        tables_own = tuple(t[REACH : REACH + rows] for t in (cosine, sine))
    result, dz1, dattended, hidden_low, product, dfeed, dgate, dlift, dbranch, gains = middle(
        middle_plan,
        ids,
        attended,
        tokens,
        cotangent,
        found,
        [joint_weights, *middle_sources],
        hidden,
    )
    gains = gains[:4]
    given = (queries, keys, values, attended, dattended, lse)
    given += tables_own
    spread = lambda g: lax.psum_scatter(g, "fsdp", scatter_dimension=0, tiled=True)
    if custom:
        gains = jnp.pad(gains.reshape(32, 1, part), ((0, 0), (0, 7), (0, PAIR - part)))
        own, other = gate_up_grad(ids, hidden_low, dgate, dlift, attended, dbranch, gains)
        mate = over_core(other)
        own_d, other_d = down_grad(ids, after(product, own), dfeed)
        sent = sum_core(own, after(mate, own_d))
        b = over_square_2(sent)
        mate_d = over_core(after(other_d, sent))
        dq, dkv, to_mate, to_cross = attend_back(ids, after(bounds, sent), *given, 0, 2, (0, 2))
        edges = [swap_edges(to_mate, to_cross)]
        sent = sum_core(own_d, after(mate_d, dq))
        b_d = over_square_2(sent)
        dq, dkv, to_mate, to_cross = attend_back(
            ids, after(bounds, sent), *given, 2, 2, (2, 2), (dq, dkv)
        )
        edges.append(swap_edges(to_mate, to_cross))
        sent = sum_square(own, mate, after(b, dq, *edges[0]))
        d = over_square_1(sent)
        sent_d = sum_square(own_d, mate_d, after(b_d, sent))
        d_d = over_square_1(sent_d)
        dq, dkv, to_mate, to_cross = attend_back(
            ids, after(bounds, sent_d), *given, 4, 2, (4, 2), (dq, dkv)
        )
        edges_2 = [swap_edges(to_mate, to_cross)]
        kept = jnp.concatenate(
            [
                sum_rest(own, mate, b, after(d, dq, *edges[1])),
                sum_rest(own_d, mate_d, b_d, after(d_d, dq)),
            ],
            axis=1,
        )
        sent = kept[2:].astype(low)
        edges_2 = [after(edges_2[0], sent)]
        sent = after(sent, *edges_2[0])
        e = over_z_1(sent)
        djoint = joint(ids, after(dq, sent), dkv, edges + edges_2, cosine, sine)
        own_1, other_1 = joint_grad(ids, tokens, djoint)
        mate_1 = over_core(after(other_1, e))
        sent = (kept[1] + wide(after(e, own_1)[1])).astype(low)
        f = over_z_2(sent)
        sent = (wide(own_1[1]) + wide(after(mate_1, sent)[1])).astype(low)
        b_1 = over_square_2(sent)
        grad_tokens = input_grad(after(djoint, sent), dz1, joint_weights)
        kept_1 = wide(own_1[0]) + wide(mate_1[0]) + wide(after(b_1, grad_tokens))
        sent = kept_1[2:].astype(low)
        e_1 = over_z_1(sent)
        mine = sum_z(kept, e, after(f, sent))
        got = over_square_1(mine)
        near = jnp.stack([mine, after(got, sent)])
        far = over_square_2(near)
        f_1 = over_z_2((kept_1[1] + wide(after(e_1, near)[1])).astype(low))
        mine = sum_z(kept_1, e_1, f_1)
        got = over_square_1(mine)
        gate_sum, up_sum, down_sum, out_sum, vector_sum = finish(
            ids, near, after(far, mine), part
        )
        mine = (wide(mine) + wide(after(got, gate_sum))).astype(low)
        halves = (mine, over_square_2(mine))
        joint_sum = wide(
            jnp.where(
                half(r, c) == 0,
                jnp.concatenate(halves, axis=1),
                jnp.concatenate(halves[::-1], axis=1),
            )
        )
        summed = (joint_sum, out_sum, gate_sum, up_sum, down_sum, vector_sum)
    else:
        share_down = spread(weight_grad(product, dfeed))
        share_gate = spread(weight_grad(hidden_low, dgate))
        share_up = spread(weight_grad(hidden_low, dlift))
        share_out = spread(weight_grad(attended, dbranch))
        share_gains = lax.psum_scatter(gains, "fsdp", scatter_dimension=1, tiled=True)
        dq, dkv, to_mate, to_cross = attend_back(ids, bounds, *given, 0, 4, (0, 4))
        edges_1 = swap_edges(to_mate, to_cross)
        dq, dkv, to_mate, to_cross = attend_back(ids, bounds, *given, 4, 2, (4, 2), (dq, dkv))
        edges_2 = swap_edges(to_mate, to_cross)
        djoint = joint(ids, dq, dkv, [edges_1, edges_2], cosine, sine)
        share_qkv = spread(weight_grad(tokens, djoint))
        grad_tokens = input_grad(djoint, dz1, joint_weights)
        summed = lax.psum(
            tuple(
                s.astype(full)
                for s in (share_qkv, share_out, share_gate, share_up, share_down, share_gains)
            ),
            "rep",
        )
    return (result, grad_tokens, *summed[:5], *(summed[5][i] for i in range(4)))


def solution(mesh):
    rows = P(("rep", "fsdp"), None)
    matrix = P("fsdp", None)
    vector = P("fsdp")
    custom = (mesh.shape["rep"], mesh.shape["fsdp"]) == (4, 8)
    return jax.shard_map(
        functools.partial(shards, custom and not FORCE_WHOLE),
        mesh=mesh,
        in_specs=(rows, P("rep", None)) + (matrix,) * 5 + (vector,) * 4 + (rows,),
        out_specs=(rows, rows) + (matrix,) * 5 + (vector,) * 4,
        check_vma=False,
    )
```

```python
import functools
import math

import jax
import jax.numpy as jnp
from jax import lax
from jax.experimental import pallas as pl
from jax.experimental.pallas import tpu as pltpu
from jax.sharding import PartitionSpec as P

HEADS = 12
WINDOW = 1024
REACH = WINDOW // 2
HEAD = 64
PAIR = 2 * HEAD
QUERY_BLOCK = 256
TOKEN_BLOCK = 256
FORCE_WHOLE = False
VMEM = 56 * 1024 * 1024

epsilon = 1e-06
rope_base = 1000.0
masked_score = -1e30
low = jnp.bfloat16
full = jnp.float32


def dot_nn(a, b):
    return lax.dot_general(a, b, (((1,), (0,)), ((), ())), preferred_element_type=full)


def dot_nt(a, b):
    return lax.dot_general(a, b, (((1,), (1,)), ((), ())), preferred_element_type=full)


def dot_tn(a, b):
    return lax.dot_general(a, b, (((0,), (0,)), ((), ())), preferred_element_type=full)


def params():
    return pltpu.CompilerParams(vmem_limit_bytes=VMEM)


def after(value, *others):
    return lax.optimization_barrier((value, *others))[0]


def shape(dims, dtype):
    return jax.ShapeDtypeStruct(dims, dtype)


def cost(micros):
    return pl.CostEstimate(flops=int(micros * 0.575e9), bytes_accessed=1, transcendentals=0)


def tables(position):
    lane = jnp.arange(PAIR, dtype=jnp.int32) % HEAD
    half = HEAD // 2
    frequency = rope_base ** (-2.0 * (lane % half).astype(full) / HEAD)
    angle = position.astype(full)[:, None] * frequency[None, :]
    sign = jnp.where(lane < half, -1.0, 1.0).astype(full)
    return jnp.cos(angle), jnp.sin(angle) * sign[None, :]


def partner(x):
    half = HEAD // 2
    lane = lax.broadcasted_iota(jnp.int32, x.shape, 1) % HEAD
    return jnp.where(lane < half, pltpu.roll(x, PAIR - half, 1), pltpu.roll(x, half, 1))


def turn(x, cosine, sine):
    return x * cosine + partner(x) * sine


def turn_back(x, cosine, sine):
    return x * cosine - partner(x) * sine


def project_kernel(
    plan, sources, first, count, ids, mate_ref, tok_ref, cross_ref, cos_ref, sin_ref, *refs
):
    srcs = refs[:sources]
    q_ref, k_ref, v_ref, weight, sems = refs[sources:]
    step = pl.program_id(0)

    @pl.when(step == 0)
    def _():
        for copy in plan(ids, srcs, weight, sems.at[0]):
            copy.start()
        pltpu.make_async_copy(weight, weight, sems.at[0]).wait()

    width = tok_ref.shape[1]
    inside = (step >= first) & (step < first + count)
    by_mate = (step < first) == (ids[2] == 1)
    rows = jnp.where(
        inside, tok_ref[...], jnp.where(by_mate, mate_ref[...], cross_ref[...])
    )
    cosine = cos_ref[...]
    sine = sin_ref[...]
    keys = dot_nn(rows, weight[1])
    for at in range(0, width, PAIR):
        k_ref[:, at : at + PAIR] = turn(keys[:, at : at + PAIR], cosine, sine).astype(low)
    v_ref[...] = dot_nn(rows, weight[2]).astype(low)

    @pl.when((step >= first) & (step < first + count))
    def _():
        queries = dot_nn(rows, weight[0])
        for at in range(0, width, PAIR):
            turned = turn(queries[:, at : at + PAIR], cosine, sine).astype(low)
            q_ref[:, at : at + PAIR] = (turned.astype(full) * (1.0 / math.sqrt(HEAD))).astype(low)


def project(plan, ids, edges, tokens, cosine, sine, sources):
    rows, width = tokens.shape
    mate, cross = edges
    ext = rows + 2 * mate.shape[0]
    block = 2 * TOKEN_BLOCK
    first, count = mate.shape[0] // block, rows // block
    tile = lambda w: pl.BlockSpec((block, w), lambda i, *_: (i, 0))
    inner = pl.BlockSpec((block, width), lambda i, *_: (jnp.clip(i - first, 0, count - 1), 0))
    edge = lambda core: pl.BlockSpec(
        (block, width),
        lambda i, ids: (
            jnp.where(
                ids[2] == core, jnp.minimum(i, first - 1), jnp.maximum(i - first - count, 0)
            ),
            0,
        ),
    )
    return pl.pallas_call(
        functools.partial(project_kernel, plan, len(sources), first, count),
        grid_spec=pltpu.PrefetchScalarGridSpec(
            num_scalar_prefetch=1,
            grid=(ext // block,),
            in_specs=[
                edge(1),
                inner,
                edge(0),
                tile(PAIR),
                tile(PAIR),
            ]
            + [pl.BlockSpec(memory_space=pl.ANY)] * len(sources),
            out_specs=[
                inner,
                tile(width),
                tile(width),
                pl.BlockSpec((4, width, width), lambda i, *_: (0, 0, 0)),
            ],
            scratch_shapes=[pltpu.SemaphoreType.DMA((1,))],
        ),
        out_shape=[
            shape((rows, width), low),
            shape((ext, width), low),
            shape((ext, width), low),
            shape((4, width, width), low),
        ],
        compiler_params=params(),
        cost_estimate=cost(0.1),
        name="project",
    )(ids, mate, tokens, cross, cosine, sine, *sources)


def fill_bias(bounds_ref, bias_ref, blocks, span):
    for b in range(blocks):
        lo = bounds_ref[0:1, b * QUERY_BLOCK : (b + 1) * QUERY_BLOCK] - b * QUERY_BLOCK
        hi = bounds_ref[1:2, b * QUERY_BLOCK : (b + 1) * QUERY_BLOCK] - b * QUERY_BLOCK
        at = lax.broadcasted_iota(jnp.int32, (span, QUERY_BLOCK), 0)
        bias_ref[b] = jnp.where((at >= lo) & (at < hi), 0.0, masked_score)


def only(x, head):
    lane = lax.broadcasted_iota(jnp.int32, x.shape, 1)
    return jnp.where((lane >= HEAD) if head else (lane < HEAD), x, jnp.zeros_like(x))


def attend_kernel(chunk, bounds_ref, q_ref, k_ref, v_ref, *refs):
    o_ref, lse_ref, bias_ref, vt_ref, s_ref = refs[-5:]
    rows = q_ref.shape[0]
    block = QUERY_BLOCK
    blocks = rows // block
    span = k_ref.shape[0] - rows + block

    @pl.when(pl.program_id(0) == 0)
    def _():
        fill_bias(bounds_ref, bias_ref, blocks, span)

    vt_ref[...] = v_ref[...].T
    chunks = [(c, min(chunk, span - c)) for c in range(0, span, chunk)]
    steps = [(b, h) for b in range(blocks) for h in range(2)]
    fold = lambda x, by: by(x.reshape(x.shape[0] // 64, 64, block), axis=0)
    add = lambda old, new: new if old is None else old + new

    def begin(i):
        b, h = steps[i]
        return {"query": only(q_ref[b * block : (b + 1) * block, :], h), "top": None}

    def score(i, c, n, state):
        b, _ = steps[i]
        s = dot_nt(k_ref[b * block + c : b * block + c + n, :], state["query"])
        s = s + bias_ref[b, c : c + n, :]
        s_ref[i % 2, c : c + n, :] = s
        top = fold(s, jnp.max)
        state["top"] = top if state["top"] is None else jnp.maximum(state["top"], top)

    def weigh(i, c, n, state):
        b, h = steps[i]
        e = jnp.exp(s_ref[i % 2, c : c + n, :] - state["peak"])
        state["total"] = add(state.get("total"), fold(e, jnp.sum))
        lanes = slice(b * block + c, b * block + c + n)
        mixed = dot_nn(vt_ref[h * HEAD : (h + 1) * HEAD, lanes], e.astype(low))
        state["mixed"] = add(state.get("mixed"), mixed)

    state = begin(0)
    for c, n in chunks:
        score(0, c, n, state)
    out = []
    for i, (b, h) in enumerate(steps):
        state["peak"] = jnp.max(state["top"], axis=0, keepdims=True)
        following = begin(i + 1) if i + 1 < len(steps) else None
        for c, n in chunks:
            if following is not None:
                score(i + 1, c, n, following)
            weigh(i, c, n, state)
        total = jnp.sum(state["total"], axis=0, keepdims=True)
        out.append(state["mixed"] / total)
        at = slice(b * block, (b + 1) * block)
        lse_ref[0, h : h + 1, at] = state["peak"] + jnp.log(total)
        if h == 1:
            o_ref[at, :] = jnp.concatenate(out, axis=0).T.astype(low)
            out = []
        state = following


def attend(bounds, q, k, v, first, pairs, before=None, chunk=640):
    rows, width = q.shape
    ext = k.shape[0]
    blocks = rows // QUERY_BLOCK
    span = ext - rows + QUERY_BLOCK
    own = pl.BlockSpec((rows, PAIR), lambda p: (0, p + first))
    wide = pl.BlockSpec((ext, PAIR), lambda p: (0, p + first))
    before = () if before is None else tuple(before)
    return pl.pallas_call(
        functools.partial(attend_kernel, chunk),
        grid=(pairs,),
        in_specs=[pl.BlockSpec((2, rows), lambda p: (0, 0)), own, wide, wide]
        + [pl.BlockSpec(memory_space=pl.ANY)] * len(before),
        out_specs=[own, pl.BlockSpec((1, 2, rows), lambda p: (p + first, 0, 0))],
        out_shape=[shape((rows, width), low), shape((width // PAIR, 2, rows), full)],
        input_output_aliases={4 + i: i for i in range(len(before))},
        scratch_shapes=[
            pltpu.VMEM((blocks, span, QUERY_BLOCK), full),
            pltpu.VMEM((PAIR, ext), low),
            pltpu.VMEM((2, span, QUERY_BLOCK), full),
        ],
        compiler_params=params(),
        cost_estimate=cost(2 * pairs),
        name="attend",
    )(bounds, q, k, v, *before)


def attend_back_kernel(
    chunk,
    ids,
    bounds_ref,
    q_ref,
    k_ref,
    v_ref,
    o_ref,
    do_ref,
    lse_ref,
    *refs,
):
    cos_ref, sin_ref = refs[:2]
    dq_ref, own_ref, mate_ref, cross_ref = refs[-10:-6]
    bias_ref, kt_ref, dk_ref, dv_ref, p_ref, ds_ref = refs[-6:]
    rows = q_ref.shape[0]
    ext = k_ref.shape[0]
    block = QUERY_BLOCK
    blocks = rows // block
    reach = (ext - rows) // 2
    span = ext - rows + block

    @pl.when(pl.program_id(0) == 0)
    def _():
        fill_bias(bounds_ref, bias_ref, blocks, span)

    kt_ref[...] = k_ref[...].T
    dk_ref[...] = jnp.zeros_like(dk_ref)
    dv_ref[...] = jnp.zeros_like(dv_ref)
    chunks = [(c, min(chunk, span - c)) for c in range(0, span, chunk)]

    def begin(b):
        at = slice(b * block, (b + 1) * block)
        q = q_ref[at, :]
        do = do_ref[at, :]
        product = (do.astype(full) * o_ref[at, :].astype(full)).T
        heads = range(2)
        return {
            "query": [only(q, h) for h in heads],
            "grad": [only(do, h) for h in heads],
            "delta": [
                jnp.sum(product[h * HEAD : (h + 1) * HEAD], axis=0, keepdims=True) for h in heads
            ],
            "lse": [lse_ref[0, h : h + 1, at] for h in heads],
            "dq": [None, None],
        }

    def score(b, h, c, n, state):
        rows_of = slice(b * block + c, b * block + c + n)
        lanes = slice(h * block, (h + 1) * block)
        s = dot_nt(k_ref[rows_of, :], state["query"][h]) + bias_ref[b, c : c + n, :]
        p = jnp.exp(s - state["lse"][h])
        dp = dot_nt(v_ref[rows_of, :], state["grad"][h])
        p_ref[b % 2, c : c + n, lanes] = p.astype(low)
        ds_ref[b % 2, c : c + n, lanes] = (p * (dp - state["delta"][h])).astype(low)

    def spread(b, h, c, n, state):
        rows_of = slice(b * block + c, b * block + c + n)
        if h == 0:
            both = jnp.concatenate(state["grad"], axis=0)
            dv_ref[rows_of, :] += dot_nn(p_ref[b % 2, c : c + n, :], both)
        else:
            both = jnp.concatenate(state["query"], axis=0)
            dk_ref[rows_of, :] += dot_nn(ds_ref[b % 2, c : c + n, :], both)
        ds = ds_ref[b % 2, c : c + n, h * block : (h + 1) * block]
        t = dot_nn(kt_ref[h * HEAD : (h + 1) * HEAD, rows_of], ds)
        state["dq"][h] = t if state["dq"][h] is None else state["dq"][h] + t

    state = begin(0)
    for h in range(2):
        for c, n in chunks:
            score(0, h, c, n, state)
    for b in range(blocks):
        following = begin(b + 1) if b + 1 < blocks else None
        for h in range(2):
            for c, n in chunks:
                if following is not None:
                    score(b + 1, h, c, n, following)
                spread(b, h, c, n, state)
        at = slice(b * block, (b + 1) * block)
        turned = turn_back(jnp.concatenate(state["dq"], axis=0).T, cos_ref[at, :], sin_ref[at, :])
        dq_ref[at, :] = (turned * (1.0 / math.sqrt(HEAD))).astype(low)
        state = following
    first = ids[2] == 0
    for i, ref in enumerate((dk_ref, dv_ref)):
        prior = ref[:reach, :].astype(low)
        following = ref[reach + rows :, :].astype(low)
        own_ref[i] = ref[reach : reach + rows, :]
        mate_ref[i] = jnp.where(first, following, prior)
        cross_ref[i] = jnp.where(first, prior, following)


def attend_back(ids, bounds, q, k, v, o, do, lse, cosine, sine, first, pairs, halo, before=None, chunk=256):
    rows, width = q.shape
    ext = k.shape[0]
    blocks = rows // QUERY_BLOCK
    reach = (ext - rows) // 2
    span = ext - rows + QUERY_BLOCK
    halo_first, halo_pairs = halo
    before = () if before is None else tuple(before)
    own = pl.BlockSpec((rows, PAIR), lambda p, ids: (0, p + first))
    wide = pl.BlockSpec((ext, PAIR), lambda p, ids: (0, p + first))
    edge = pl.BlockSpec((2, reach, PAIR), lambda p, ids: (0, 0, p + first - halo_first))
    return pl.pallas_call(
        functools.partial(attend_back_kernel, chunk),
        grid_spec=pltpu.PrefetchScalarGridSpec(
            num_scalar_prefetch=1,
            grid=(pairs,),
            in_specs=[
            pl.BlockSpec((2, rows), lambda p, ids: (0, 0)),
            own,
            wide,
            wide,
            own,
            own,
            pl.BlockSpec((1, 2, rows), lambda p, ids: (p + first, 0, 0)),
            pl.BlockSpec((rows, PAIR), lambda p, ids: (0, 0)),
            pl.BlockSpec((rows, PAIR), lambda p, ids: (0, 0)),
        ]
        + [pl.BlockSpec(memory_space=pl.ANY)] * len(before),
        out_specs=[
            own,
            pl.BlockSpec((2, rows, PAIR), lambda p, ids: (0, 0, p + first)),
            edge,
            edge,
        ],
        scratch_shapes=[
            pltpu.VMEM((blocks, span, QUERY_BLOCK), full),
            pltpu.VMEM((PAIR, ext), low),
            pltpu.VMEM((ext, PAIR), full),
            pltpu.VMEM((ext, PAIR), full),
            pltpu.VMEM((2, span, 2 * QUERY_BLOCK), low),
            pltpu.VMEM((2, span, 2 * QUERY_BLOCK), low),
        ],
        ),
        out_shape=[
            shape((rows, width), low),
            shape((2, rows, width), full),
            shape((2, reach, halo_pairs * PAIR), low),
            shape((2, reach, halo_pairs * PAIR), low),
        ],
        input_output_aliases={10 + i: i for i in range(len(before))},
        compiler_params=params(),
        cost_estimate=cost(9 * pairs),
        name="attend_back",
    )(ids, bounds, q, k, v, o, do, lse, cosine, sine, *before)


def mean(x):
    return jnp.mean(x, axis=-1, keepdims=True)


def norm(x):
    centred = x - mean(x)
    inverse = lax.rsqrt(mean(centred * centred) + epsilon)
    return centred * inverse, inverse


def norm_back(scaled, normed, inverse):
    return inverse * (scaled - mean(scaled) - normed * mean(scaled * normed))


def position(j, core):
    return jnp.where(core == 0, j, (j & 1) * 2 + (j >> 1))


def gather_vectors(ids, vec_ref, width):
    count = vec_ref.shape[0]
    if count == 1:
        return vec_ref[0].astype(full)[:8]
    size = width // (2 * count)
    row = lax.broadcasted_iota(jnp.int32, (PAIR, width), 0)
    column = lax.broadcasted_iota(jnp.int32, (PAIR, width), 1)
    half = lax.broadcasted_iota(jnp.int32, (16, PAIR), 0) // 8
    out = jnp.zeros((16, width), full)
    for at in range(count):
        found = vec_ref[at].astype(full)
        for i in range(2):
            f = 2 * (ids[1] ^ position(at, ids[2])) + (ids[2] ^ i)
            place = ((column - f * size == row) & (row < size)).astype(full).astype(low)
            out = out + dot_nn(jnp.where(half == i, found, 0.0).astype(low), place)
    return out[:8] + out[8:]


def middle_kernel(plan, sources, ids, at_ref, tok_ref, cot_ref, *refs):
    vec_ref, refs = refs[0], refs[1:]
    srcs = refs[:sources]
    (
        out_ref,
        dz1_ref,
        da_ref,
        hidden_ref,
        product_ref,
        dfeed_ref,
        dgate_ref,
        dlift_ref,
        dbranch_ref,
        gains_ref,
        out_w,
        gate_w,
        up_w,
        down_w,
        lift_factor,
        gate_factor,
        vectors,
        sems,
    ) = refs[sources:]
    step = pl.program_id(0)
    weights = (out_w, gate_w, up_w, down_w)

    @pl.when(step == 0)
    def _():
        for copy in plan(ids, srcs, weights, sems):
            copy.start()
        gains_ref[...] = jnp.zeros_like(gains_ref)

    def ready(*which):
        @pl.when(step == 0)
        def _():
            for i in which:
                pltpu.make_async_copy(weights[i], weights[i], sems.at[i]).wait()

    parts, _, width = gate_w.shape

    @pl.when(step == 0)
    def _():
        vectors[...] = gather_vectors(ids, vec_ref, width)

    gain1, bias1, gain2, bias2 = (vectors[i : i + 1] for i in range(4))
    ready(0)
    normed1, inverse1 = norm(tok_ref[...].astype(full) + dot_nn(at_ref[...], out_w[...]))
    hidden = normed1 * gain1 + bias1
    hidden_low = hidden.astype(low)
    hidden_ref[...] = hidden_low
    ready(1, 2, 3)
    feed = None
    for part in range(parts):
        at = slice(part * width, (part + 1) * width)
        gate = dot_nn(hidden_low, gate_w[part])
        lift = dot_nn(hidden_low, up_w[part])
        sigma = jax.nn.sigmoid(gate)
        opened = gate * sigma
        product = (opened * lift).astype(low)
        product_ref[:, at] = product
        lift_factor[:, at] = opened
        gate_factor[:, at] = lift * sigma * (1.0 + gate * (1.0 - sigma))
        term = dot_nn(product, down_w[at, :])
        feed = term if feed is None else feed + term
    normed2, inverse2 = norm(hidden + feed)
    out_ref[...] = (normed2 * gain2 + bias2).astype(low)
    cot = cot_ref[...].astype(full)
    gains_ref[2:3] += jnp.sum(cot * normed2, axis=0, keepdims=True)
    gains_ref[3:4] += jnp.sum(cot, axis=0, keepdims=True)
    grad = norm_back(cot * gain2, normed2, inverse2)
    dfeed = grad.astype(low)
    dfeed_ref[...] = dfeed
    for part in range(parts):
        at = slice(part * width, (part + 1) * width)
        dproduct = dot_nt(dfeed, down_w[at, :])
        dgate = (dproduct * gate_factor[:, at]).astype(low)
        dlift = (dproduct * lift_factor[:, at]).astype(low)
        dgate_ref[:, at] = dgate
        dlift_ref[:, at] = dlift
        grad = grad + dot_nt(dgate, gate_w[part]) + dot_nt(dlift, up_w[part])
    gains_ref[0:1] += jnp.sum(grad * normed1, axis=0, keepdims=True)
    gains_ref[1:2] += jnp.sum(grad, axis=0, keepdims=True)
    grad = norm_back(grad * gain1, normed1, inverse1)
    dz1_ref[...] = grad
    dbranch = grad.astype(low)
    dbranch_ref[...] = dbranch
    da_ref[...] = dot_nt(dbranch, out_w[...]).astype(low)


def middle(plan, ids, attended, tokens, cot, vectors, sources, hidden):
    rows, width = tokens.shape
    block = TOKEN_BLOCK
    tile = lambda w: pl.BlockSpec((block, w), lambda i, *_: (i, 0))
    whole = pl.BlockSpec((8, width), lambda i, *_: (0, 0))
    return pl.pallas_call(
        functools.partial(middle_kernel, plan, len(sources)),
        grid_spec=pltpu.PrefetchScalarGridSpec(
            num_scalar_prefetch=1,
            grid=(rows // block,),
            in_specs=[
                tile(width),
                tile(width),
                tile(width),
            ]
            + [pl.BlockSpec(vectors.shape, lambda i, *_: (0, 0, 0))]
            + [pl.BlockSpec(memory_space=pl.ANY)] * len(sources),
            out_specs=[
                tile(width),
                tile(width),
                tile(width),
                tile(width),
                tile(hidden),
                tile(width),
                tile(hidden),
                tile(hidden),
                tile(width),
                whole,
            ],
            scratch_shapes=[
                pltpu.VMEM((width, width), low),
                pltpu.VMEM((hidden // width, width, width), low),
                pltpu.VMEM((hidden // width, width, width), low),
                pltpu.VMEM((hidden, width), low),
                pltpu.VMEM((block, hidden), full),
                pltpu.VMEM((block, hidden), full),
                pltpu.VMEM((8, width), full),
                pltpu.SemaphoreType.DMA((4,)),
            ],
        ),
        out_shape=[
            shape((rows, width), low),
            shape((rows, width), full),
            shape((rows, width), low),
            shape((rows, width), low),
            shape((rows, hidden), low),
            shape((rows, width), low),
            shape((rows, hidden), low),
            shape((rows, hidden), low),
            shape((rows, width), low),
            shape((8, width), full),
        ],
        compiler_params=params(),
        cost_estimate=cost(53),
        name="middle",
    )(ids, attended, tokens, cot, vectors, *sources)


def weight_grad_kernel(a_ref, b_ref, o_ref):
    o_ref[...] = dot_tn(a_ref[...], b_ref[...]).astype(o_ref.dtype)


def weight_grad(a, b, tile_a=768, tile_b=768):
    rows, size_a = a.shape
    size_b = b.shape[1]
    return pl.pallas_call(
        weight_grad_kernel,
        grid=(size_a // tile_a, size_b // tile_b),
        in_specs=[
            pl.BlockSpec((rows, tile_a), lambda i, j: (0, i)),
            pl.BlockSpec((rows, tile_b), lambda i, j: (0, j)),
        ],
        out_specs=pl.BlockSpec((tile_a, tile_b), lambda i, j: (i, j)),
        out_shape=shape((size_a, size_b), low),
        compiler_params=params(),
        cost_estimate=cost(9),
        name="weight_grad",
    )(a, b)


def joint_kernel(halos, ids, dq_ref, own_ref, cos_ref, sin_ref, *refs):
    by_mate = (pl.program_id(0) < pl.num_programs(0) // 2) == (ids[2] == 1)
    cosine = cos_ref[...]
    sine = sin_ref[...]
    dj_ref = refs[-1]
    width = dq_ref.shape[1]
    start = 0
    for mate_ref, cross_ref in zip(refs[:halos], refs[halos : 2 * halos]):
        for at in range(0, mate_ref.shape[2], PAIR):
            near = [
                jnp.where(
                    by_mate, mate_ref[i, :, at : at + PAIR], cross_ref[i, :, at : at + PAIR]
                ).astype(full)
                for i in range(2)
            ]
            lanes = slice(start, start + PAIR)
            keys = turn_back(own_ref[0, :, lanes] + near[0], cosine, sine)
            values = own_ref[1, :, lanes] + near[1]
            for i, x in enumerate((dq_ref[:, lanes], keys, values)):
                dj_ref[:, i * width + start : i * width + start + PAIR] = x.astype(low)
            start += PAIR


def joint(ids, dq, own, edges, cosine, sine):
    rows, width = dq.shape
    mates, crosses = zip(*edges)
    block = TOKEN_BLOCK
    half = mates[0].shape[1] // block
    inner = pl.BlockSpec((block, PAIR), lambda i, ids: (i + half, 0))
    tile = lambda w: pl.BlockSpec((block, w), lambda i, ids: (i, 0))
    edge = lambda size, core: pl.BlockSpec(
        (2, block, size),
        lambda i, ids: (
            0,
            jnp.where(ids[2] == core, jnp.minimum(i, half - 1), jnp.maximum(i - half, 0)),
            0,
        ),
    )
    return pl.pallas_call(
        functools.partial(joint_kernel, len(edges)),
        grid_spec=pltpu.PrefetchScalarGridSpec(
            num_scalar_prefetch=1,
            grid=(rows // block,),
            in_specs=[
                tile(width),
                pl.BlockSpec((2, block, width), lambda i, ids: (0, i, 0)),
                inner,
                inner,
            ]
            + [edge(m.shape[2], 1) for m in mates]
            + [edge(m.shape[2], 0) for m in crosses],
            out_specs=tile(3 * width),
        ),
        out_shape=shape((rows, 3 * width), low),
        compiler_params=params(),
        cost_estimate=cost(2),
        name="joint",
    )(ids, dq, own, cosine, sine, *mates, *crosses)


def input_grad_kernel(dj_ref, dz1_ref, weight_ref, out_ref):
    width = dz1_ref.shape[1]
    out = dz1_ref[...]
    for i in range(3):
        out = out + dot_nt(dj_ref[:, i * width : (i + 1) * width], weight_ref[i])
    out_ref[...] = out


def input_grad(djoint, dz1, weights):
    rows, width = dz1.shape
    block = 2 * TOKEN_BLOCK
    tile = lambda w: pl.BlockSpec((block, w), lambda i: (i, 0))
    return pl.pallas_call(
        input_grad_kernel,
        grid=(rows // block,),
        in_specs=[
            tile(3 * width),
            tile(width),
            pl.BlockSpec((3, width, width), lambda i: (0, 0, 0)),
        ],
        out_specs=tile(width),
        out_shape=shape((rows, width), full),
        compiler_params=params(),
        cost_estimate=cost(9),
        name="input_grad",
    )(djoint, dz1, weights)


def whole_joint_plan(ids, srcs, weight, sem):
    width = weight.shape[1]
    return [
        pltpu.make_async_copy(srcs[0].at[:, i * width : (i + 1) * width], weight.at[i], sem)
        for i in range(3)
    ] + [pltpu.make_async_copy(srcs[1], weight.at[3], sem)]


def whole_middle_plan(ids, srcs, weights, sems):
    out_w, gate_w, up_w, down_w = weights
    parts, _, width = gate_w.shape
    columns = lambda src, dst, sem: [
        pltpu.make_async_copy(src.at[:, i * width : (i + 1) * width], dst.at[i], sem)
        for i in range(parts)
    ]
    return (
        [pltpu.make_async_copy(srcs[0].at[3], out_w, sems.at[0])]
        + columns(srcs[1], gate_w, sems.at[1])
        + columns(srcs[2], up_w, sems.at[2])
        + [pltpu.make_async_copy(srcs[3], down_w, sems.at[3])]
    )


def swap_with(value, place):
    pairs = []
    for r in range(4):
        for z in range(4):
            for c in range(2):
                to_r, to_z, to_c = place(r, z, c)
                pairs.append(((r * 4 + z) * 2 + c, (to_r * 4 + to_z) * 2 + to_c))
    return lax.ppermute(value, ("rep", "fsdp"), pairs)


def over_core(value):
    return swap_with(value, lambda r, z, c: (r, z, 1 - c))


def over_square_1(value):
    return swap_with(value, lambda r, z, c: (r ^ (1 + c), z, c))


def over_square_2(value):
    return swap_with(value, lambda r, z, c: (r ^ (2 - c), z, c))


def over_z_1(value):
    return swap_with(value, lambda r, z, c: (r, z ^ (2 - c), c))


def over_z_2(value):
    return swap_with(value, lambda r, z, c: (r, z ^ (1 + c), c))


def pieces(ids, srcs):
    r, z, c = ids[0], ids[1], ids[2]
    found = []
    for i in range(2):
        core = (1 - c) if i else c
        bit1, bit2 = 1 + core, 2 - core
        for quarter in range(4):
            found.append((srcs[i][0].at[quarter], quarter, z, core))
        for ref, quarter in zip(srcs[i][1:], (r, r ^ bit1, r ^ bit2, r ^ 3)):
            for k in range(1, 4):
                found.append((ref.at[k - 1], quarter, z ^ position(k, core), core))
    return found


def piece_joint_plan(ids, srcs, weight, sem):
    size = srcs[0].shape[1]
    copies = []
    found = [
        [srcs[i]] + [srcs[k].at[j] for k in (2 + i, 4 + i) for j in range(2)] for i in range(2)
    ]
    for ref, quarter, z, core in pieces(ids, found):
        at = pl.multiple_of((2 * z + core) * size, size)
        copies.append(pltpu.make_async_copy(ref, weight.at[quarter, pl.ds(at, size)], sem))
    return copies


def piece_middle_plan(ids, srcs, weights, sems):
    out_w, gate_w, up_w, down_w = weights
    size = srcs[1].shape[1] // 3
    copies = [pltpu.make_async_copy(srcs[0].at[3], out_w, sems.at[0])]
    found = pieces(ids, [srcs[1::2], srcs[2::2]])
    for i, target in enumerate((gate_w, up_w)):
        for ref, quarter, z, core in found:
            at = pl.multiple_of((2 * z + core) * size, size)
            copies.append(
                pltpu.make_async_copy(
                    ref.at[i * size : (i + 1) * size],
                    target.at[quarter, pl.ds(at, size)],
                    sems.at[1 + i],
                )
            )
    for ref, quarter, z, core in found:
        at = pl.multiple_of(((2 * z + core) * 4 + quarter) * size, size)
        copies.append(
            pltpu.make_async_copy(
                ref.at[2 * size : 3 * size], down_w.at[pl.ds(at, size)], sems.at[3]
            )
        )
    return copies


def put_pieces(ids, block_ref, own_ref, other_ref, first, size):
    z, c = ids[1], ids[2]
    for ref, core in ((own_ref, c), (other_ref, 1 - c)):
        for k in range(4):
            at = pl.multiple_of((2 * (z ^ position(k, core)) + core) * size, 8)
            ref[0, k, first : first + size, :] = block_ref[pl.ds(at, size), :].astype(low)


def gate_up_grad_kernel(
    ids, hidden_ref, dgate_ref, dlift_ref, at_ref, db_ref, gains_ref, own_ref, other_ref, block_ref, out_ref
):
    size = block_ref.shape[0] // 8
    slim = size // 4
    z, c = ids[1], ids[2]
    quarter = ids[0] ^ pl.program_id(0)

    @pl.when(pl.program_id(0) == 0)
    def _():
        out_ref[...] = dot_tn(at_ref[...], db_ref[...])

    for i, ref in enumerate((dgate_ref, dlift_ref)):
        block_ref[...] = dot_tn(hidden_ref[...], ref[...])
        put_pieces(ids, block_ref, own_ref, other_ref, i * size, size)
    for ref, core in ((own_ref, c), (other_ref, 1 - c)):
        for k in range(4):
            f = 2 * (z ^ position(k, core)) + core
            at = pl.multiple_of(f * size + quarter * slim, 8)
            row = jnp.pad(gains_ref[quarter * 8 + f][:8], ((0, 0), (0, ref.shape[3] - PAIR)))
            rest = jnp.concatenate([out_ref[pl.ds(at, slim), :], row])
            ref[0, k, 2 * size :, :] = rest.astype(low)


def grad_specs(size, width):
    own = pl.BlockSpec((1, 4, size, width), lambda j, ids: (position(j, ids[2]), 0, 0, 0))
    other = pl.BlockSpec((1, 4, size, width), lambda j, ids: (position(j, 1 - ids[2]), 0, 0, 0))
    return [own, other], [shape((4, 4, size, width), low)] * 2


def gate_up_grad(ids, hidden_low, dgate, dlift, attended, dbranch, gains):
    rows, width = hidden_low.shape
    size = width // 8
    out_specs, out_shape = grad_specs(2 * size + size // 4 + 8, width)
    column = pl.BlockSpec((rows, width), lambda j, ids: (0, ids[0] ^ j))
    whole = pl.BlockSpec((rows, width), lambda j, ids: (0, 0))
    return pl.pallas_call(
        gate_up_grad_kernel,
        grid_spec=pltpu.PrefetchScalarGridSpec(
            num_scalar_prefetch=1,
            grid=(4,),
            in_specs=[
                whole,
                column,
                column,
                whole,
                whole,
                pl.BlockSpec(gains.shape, lambda j, ids: (0, 0, 0)),
            ],
            out_specs=out_specs,
            scratch_shapes=[pltpu.VMEM((width, width), full), pltpu.VMEM((width, width), full)],
        ),
        out_shape=out_shape,
        compiler_params=params(),
        cost_estimate=cost(18),
        name="gate_up_grad",
    )(ids, hidden_low, dgate, dlift, attended, dbranch, gains)


def down_grad_kernel(ids, product_ref, dfeed_ref, own_ref, other_ref, block_ref):
    size = own_ref.shape[2]
    r, z, c = ids[0], ids[1], ids[2]
    step = pl.program_id(0)
    block_ref[...] = dot_tn(product_ref[...], dfeed_ref[...])
    for ref, core in ((own_ref, c), (other_ref, 1 - c)):
        for j in range(4):
            at = pl.multiple_of((core * 4 + (r ^ position(j, core))) * size, 8)
            ref[j, 0] = block_ref[pl.ds(at, size), :].astype(low)


def down_grad(ids, product, dfeed):
    rows, hidden = product.shape
    width = dfeed.shape[1]
    size = hidden // 32
    out = lambda core: pl.BlockSpec(
        (4, 1, size, width),
        lambda j, ids: (0, position(ids[1] ^ j, (1 - ids[2]) if core else ids[2]), 0, 0),
    )
    return pl.pallas_call(
        down_grad_kernel,
        grid_spec=pltpu.PrefetchScalarGridSpec(
            num_scalar_prefetch=1,
            grid=(4,),
            in_specs=[
                pl.BlockSpec((rows, hidden // 4), lambda j, ids: (0, j)),
                pl.BlockSpec((rows, width), lambda j, ids: (0, 0)),
            ],
            out_specs=[out(0), out(1)],
            scratch_shapes=[pltpu.VMEM((hidden // 4, width), full)],
        ),
        out_shape=[shape((4, 4, size, width), low)] * 2,
        compiler_params=params(),
        cost_estimate=cost(10),
        name="down_grad",
    )(ids, product, dfeed)


def joint_grad_kernel(ids, tok_ref, dj_ref, own_ref, other_ref, block_ref):
    block_ref[...] = dot_tn(tok_ref[...], dj_ref[...])
    put_pieces(ids, block_ref, own_ref, other_ref, 0, block_ref.shape[0] // 8)


def half(r, core):
    return jnp.where(core == 0, r >> 1, r & 1)


def joint_grad(ids, tokens, djoint):
    rows, width = tokens.shape
    part = djoint.shape[1] // 2
    size = width // 8
    out = lambda other: pl.BlockSpec(
        (1, 4, size, part),
        lambda j, ids: (j ^ half(ids[0], (1 - ids[2]) if other else ids[2]), 0, 0, 0),
    )
    return pl.pallas_call(
        joint_grad_kernel,
        grid_spec=pltpu.PrefetchScalarGridSpec(
            num_scalar_prefetch=1,
            grid=(2,),
            in_specs=[
                pl.BlockSpec((rows, width), lambda j, ids: (0, 0)),
                pl.BlockSpec((rows, part), lambda j, ids: (0, j)),
            ],
            out_specs=[out(0), out(1)],
            scratch_shapes=[pltpu.VMEM((width, part), full)],
        ),
        out_shape=[shape((2, 4, size, part), low)] * 2,
        compiler_params=params(),
        cost_estimate=cost(4),
        name="joint_grad",
    )(ids, tokens, djoint)


def wide(v):
    return v.astype(full)


def sum_core(own, mate):
    return (wide(own[2:]) + wide(mate[2:])).astype(low)


def sum_square(own, mate, b):
    return (wide(own[1]) + wide(mate[1]) + wide(b[1])).astype(low)


def sum_rest(own, mate, b, d):
    return wide(own[0]) + wide(mate[0]) + wide(b[0]) + wide(d)


def sum_z(kept, e, f):
    return (kept[0] + wide(e[0]) + wide(f)).astype(low)


def place(ids, quarter):
    return position(quarter ^ ids[0], ids[2])


def finish_kernel(ids, near_ref, far_ref, gate_ref, up_ref, down_ref, out_ref, vec_ref):
    size, width = gate_ref.shape
    slim = out_ref.shape[0]
    at = place(ids, pl.program_id(0))

    def put(ref):
        piece = ref[at & 1].astype(full)
        gate_ref[...] = piece[:size]
        up_ref[...] = piece[size : 2 * size]
        out_ref[...] = piece[2 * size : 2 * size + slim]
        vec_ref[0] = piece[2 * size + slim : 2 * size + slim + 8, :PAIR]
        down_ref[...] = piece[2 * size + slim + 8 :]

    pl.when(at < 2)(lambda: put(near_ref))
    pl.when(at >= 2)(lambda: put(far_ref))


def finish(ids, near, far, size):
    width = near.shape[2]
    whole = pl.BlockSpec(near.shape, lambda j, ids: (0, 0, 0))
    column = pl.BlockSpec((size, width), lambda j, ids: (0, j))
    gate, up, down, out, vectors = pl.pallas_call(
        finish_kernel,
        grid_spec=pltpu.PrefetchScalarGridSpec(
            num_scalar_prefetch=1,
            grid=(4,),
            in_specs=[whole, whole],
            out_specs=[
                column,
                column,
                pl.BlockSpec((size, width), lambda j, ids: (j, 0)),
                pl.BlockSpec((size // 4, width), lambda j, ids: (j, 0)),
                pl.BlockSpec((1, 8, PAIR), lambda j, ids: (j, 0, 0)),
            ],
        ),
        out_shape=[shape((size, 4 * width), full)] * 2
        + [
            shape((4 * size, width), full),
            shape((size, width), full),
            shape((4, 8, PAIR), full),
        ],
        compiler_params=params(),
        cost_estimate=cost(5),
        name="finish",
    )(ids, near, far)
    return gate, up, down, out, vectors[:, 0, :size]


def shards(
    custom,
    tokens,
    lengths,
    qkv_weight,
    out_weight,
    gate_weight,
    up_weight,
    down_weight,
    norm1_gain,
    norm1_bias,
    norm2_gain,
    norm2_bias,
    cotangent,
):
    rows, width = tokens.shape
    hidden = gate_weight.shape[1]
    size = lax.axis_size("fsdp")
    me = lax.axis_index("fsdp")
    r = lax.axis_index("rep")
    z, c = me // 2, me % 2
    ids = jnp.stack([r, z, c]).astype(jnp.int32)
    vectors = jnp.stack([norm1_gain, norm1_bias, norm2_gain, norm2_bias]).astype(low)

    mates = [(i, i ^ 1) for i in range(size)]
    crossed = [(i, i + 1 if i % 2 else i - 1) for i in range(1, size - 1)]
    swap_edges = lambda to_mate, to_cross: (
        lax.ppermute(to_mate, "fsdp", mates),
        lax.ppermute(to_cross, "fsdp", crossed),
    )
    edges = (tokens[rows - REACH :], tokens[:REACH])
    edges = (jnp.where(c == 0, *edges), jnp.where(c == 0, *edges[::-1]))
    if custom:
        part = qkv_weight.shape[0]
        columns = lambda w: jnp.swapaxes(w.astype(low).reshape(part, -1, width), 0, 1)
        column = lambda w, i: lax.dynamic_slice_in_dim(w, i * width, width, 1).astype(low)
        mine = jnp.where(
            r == 3, out_weight.astype(low), column(qkv_weight, jnp.minimum(r, 2))
        )
        first = over_z_2(mine)
        second = over_z_1(jnp.stack([mine, first]))
        rows_of = jnp.pad(vectors, ((0, 4), (0, width - part)))
        mine_2 = jnp.concatenate(
            [
                column(gate_weight, r),
                column(up_weight, r),
                lax.dynamic_slice_in_dim(down_weight, r * part, part, 0).astype(low),
                rows_of,
                over_core(rows_of),
            ]
        )
        shard_1 = jnp.concatenate([columns(qkv_weight), out_weight.astype(low)[None]])
        shard_2 = jnp.concatenate(
            [
                columns(gate_weight),
                columns(up_weight),
                down_weight.astype(low).reshape(4, part, width),
            ],
            axis=1,
        )
        mate_shard_1 = over_core(shard_1)
        own_1 = jnp.concatenate([first[None], after(second, mine_2, mate_shard_1)])
        first_2 = over_z_2(after(mine_2, own_1))
        other_1 = over_square_1(own_1)
        edges = swap_edges(*after(edges, first))
        mate_shard_2 = over_core(after(shard_2, own_1))
        near_1 = jnp.stack([own_1, after(other_1, shard_2, *edges)])
        far_1 = over_square_2(near_1)
        mate_near_1 = over_core(near_1)
        joint_sources = [shard_1, mate_shard_1, near_1, mate_near_1, far_1]
        joint_plan = piece_joint_plan
    else:
        edges = swap_edges(*edges)
        gather = lambda w: lax.all_gather(w.astype(low), "fsdp", axis=0, tiled=True)
        joint_sources = [gather(qkv_weight), gather(out_weight)]
        joint_plan = whole_joint_plan
        middle_sources = [gather(w) for w in (gate_weight, up_weight, down_weight)]
        vectors = lax.all_gather(vectors, "fsdp", axis=1, tiled=True)
        found = jnp.pad(vectors, ((0, 12), (0, 0)))[None]
        middle_plan = whole_middle_plan

    doc_lengths = lengths[0]
    ends = jnp.cumsum(doc_lengths)
    index = me * rows - REACH + jnp.arange(rows + 2 * REACH, dtype=jnp.int32)
    if custom:
        index = after(index, near_1)
    passed = (index[:, None] >= ends[None, :]).astype(jnp.int32)
    starts = jnp.sum(passed * doc_lengths[None, :], axis=1)
    cosine, sine = tables(index - starts)
    if custom:
        pair_2 = jnp.stack([mine_2, after(first_2, cosine)])
        second_2 = over_z_1(pair_2)
        mate_far_1 = over_core(after(far_1, pair_2))
        joint_sources.append(mate_far_1)
    own_starts = starts[REACH : REACH + rows]
    own_index = index[REACH : REACH + rows]
    stops = jnp.min(
        jnp.where(ends[None, :] > own_index[:, None], ends[None, :], size * rows), axis=1
    )
    base = me * rows - REACH
    bounds = jnp.stack(
        [
            jnp.maximum(own_starts, own_index - REACH) - base,
            jnp.minimum(stops, own_index + REACH + 1) - base,
        ]
    ).astype(jnp.int32)

    queries, keys, values, joint_weights = project(
        joint_plan, ids, edges, tokens, cosine, sine, joint_sources
    )
    given = (queries, keys, values)
    if custom:
        second_2 = after(second_2, queries)
        own_2 = jnp.concatenate([first_2[None, : 3 * part], second_2[:, : 3 * part]])
        found = jnp.concatenate([pair_2[:, 3 * part :, :PAIR], second_2[:, 3 * part :, :PAIR]])
        other_2 = over_square_1(own_2)
        done = attend(after(bounds, own_2, mate_shard_2), *given, 0, 2)
        tables_own = after((cosine, sine), done[1])
        tables_own = tuple(t[REACH : REACH + rows] for t in tables_own)
        other_2 = after(other_2, done[1], *tables_own)
        far_2 = over_square_2(after(own_2, other_2))
        across_2 = over_square_2(other_2)
        mate_own_2 = over_core(own_2)
        mate_other_2 = over_core(other_2)
        done = attend(after(bounds, other_2), *given, 2, 2, done)
        far_2 = after(far_2, done[1], mate_other_2, mate_own_2)
        mate_far_2 = over_core(far_2)
        attended, lse = attend(after(bounds, far_2), *given, 4, 2, done)
        across_2 = after(across_2, lse, mate_far_2)
        mate_across_2 = over_core(across_2)
        middle_sources = [shard_2, mate_shard_2, own_2, mate_own_2, other_2, mate_other_2]
        middle_sources += [far_2, mate_far_2, across_2, mate_across_2]
        middle_plan = piece_middle_plan
    else:
        done = None
        for first in (0, 2, 4):
            done = attend(bounds, *given, first, 2, done)
        attended, lse = done
        tables_own = tuple(t[REACH : REACH + rows] for t in (cosine, sine))
    result, dz1, dattended, hidden_low, product, dfeed, dgate, dlift, dbranch, gains = middle(
        middle_plan,
        ids,
        attended,
        tokens,
        cotangent,
        found,
        [joint_weights, *middle_sources],
        hidden,
    )
    gains = gains[:4]
    given = (queries, keys, values, attended, dattended, lse)
    given += tables_own
    spread = lambda g: lax.psum_scatter(g, "fsdp", scatter_dimension=0, tiled=True)
    if custom:
        gains = jnp.pad(gains.reshape(32, 1, part), ((0, 0), (0, 7), (0, PAIR - part)))
        own, other = gate_up_grad(ids, hidden_low, dgate, dlift, attended, dbranch, gains)
        mate = over_core(other)
        own_d, other_d = down_grad(ids, after(product, own), dfeed)
        sent = sum_core(own, after(mate, own_d))
        b = over_square_2(sent)
        mate_d = over_core(other_d)
        sent = sum_core(own_d, after(mate_d, sent))
        b_d = over_square_2(sent)
        dq, dkv, to_mate, to_cross = attend_back(ids, after(bounds, sent), *given, 0, 4, (0, 4))
        edges = [swap_edges(to_mate, to_cross)]
        sent = sum_square(own, mate, after(b, dq))
        d = over_square_1(sent)
        sent_d = sum_square(own_d, mate_d, after(b_d, sent))
        d_d = over_square_1(sent_d)
        dq, dkv, to_mate, to_cross = attend_back(
            ids, after(bounds, sent_d), *given, 4, 2, (4, 2), (dq, dkv)
        )
        edges_2 = [swap_edges(to_mate, to_cross)]
        kept = jnp.concatenate(
            [
                sum_rest(own, mate, b, after(d, dq, *edges[0])),
                sum_rest(own_d, mate_d, b_d, after(d_d, dq)),
            ],
            axis=1,
        )
        sent = kept[2:].astype(low)
        edges_2 = [after(edges_2[0], sent)]
        sent = after(sent, *edges_2[0])
        e = over_z_1(sent)
        djoint = joint(ids, after(dq, sent), dkv, edges + edges_2, cosine, sine)
        own_1, other_1 = joint_grad(ids, tokens, djoint)
        mate_1 = over_core(after(other_1, e))
        sent = (kept[1] + wide(after(e, own_1)[1])).astype(low)
        f = over_z_2(sent)
        sent = (wide(own_1[1]) + wide(after(mate_1, sent)[1])).astype(low)
        b_1 = over_square_2(sent)
        grad_tokens = input_grad(after(djoint, sent), dz1, joint_weights)
        kept_1 = wide(own_1[0]) + wide(mate_1[0]) + wide(after(b_1, grad_tokens))
        sent = kept_1[2:].astype(low)
        e_1 = over_z_1(sent)
        mine = sum_z(kept, e, after(f, sent))
        got = over_square_1(mine)
        near = jnp.stack([mine, after(got, sent)])
        far = over_square_2(near)
        f_1 = over_z_2((kept_1[1] + wide(after(e_1, near)[1])).astype(low))
        mine = sum_z(kept_1, e_1, f_1)
        got = over_square_1(mine)
        gate_sum, up_sum, down_sum, out_sum, vector_sum = finish(
            ids, near, after(far, mine), part
        )
        mine = (wide(mine) + wide(after(got, gate_sum))).astype(low)
        halves = (mine, over_square_2(mine))
        joint_sum = wide(
            jnp.where(
                half(r, c) == 0,
                jnp.concatenate(halves, axis=1),
                jnp.concatenate(halves[::-1], axis=1),
            )
        )
        summed = (joint_sum, out_sum, gate_sum, up_sum, down_sum, vector_sum)
    else:
        share_down = spread(weight_grad(product, dfeed))
        share_gate = spread(weight_grad(hidden_low, dgate))
        share_up = spread(weight_grad(hidden_low, dlift))
        share_out = spread(weight_grad(attended, dbranch))
        share_gains = lax.psum_scatter(gains, "fsdp", scatter_dimension=1, tiled=True)
        dq, dkv, to_mate, to_cross = attend_back(ids, bounds, *given, 0, 4, (0, 4))
        edges_1 = swap_edges(to_mate, to_cross)
        dq, dkv, to_mate, to_cross = attend_back(ids, bounds, *given, 4, 2, (4, 2), (dq, dkv))
        edges_2 = swap_edges(to_mate, to_cross)
        djoint = joint(ids, dq, dkv, [edges_1, edges_2], cosine, sine)
        share_qkv = spread(weight_grad(tokens, djoint))
        grad_tokens = input_grad(djoint, dz1, joint_weights)
        summed = lax.psum(
            tuple(
                s.astype(full)
                for s in (share_qkv, share_out, share_gate, share_up, share_down, share_gains)
            ),
            "rep",
        )
    return (result, grad_tokens, *summed[:5], *(summed[5][i] for i in range(4)))


def solution(mesh):
    rows = P(("rep", "fsdp"), None)
    matrix = P("fsdp", None)
    vector = P("fsdp")
    custom = (mesh.shape["rep"], mesh.shape["fsdp"]) == (4, 8)
    return jax.shard_map(
        functools.partial(shards, custom and not FORCE_WHOLE),
        mesh=mesh,
        in_specs=(rows, P("rep", None)) + (matrix,) * 5 + (vector,) * 4 + (rows,),
        out_specs=(rows, rows) + (matrix,) * 5 + (vector,) * 4,
        check_vma=False,
    )
```

```python
import functools
import math

import jax
import jax.numpy as jnp
from jax import lax
from jax.experimental import pallas as pl
from jax.experimental.pallas import tpu as pltpu
from jax.sharding import PartitionSpec as P

HEADS = 12
WINDOW = 1024
REACH = WINDOW // 2
HEAD = 64
PAIR = 2 * HEAD
QUERY_BLOCK = 256
TOKEN_BLOCK = 256
FORCE_WHOLE = False

epsilon = 1e-06
rope_base = 1000.0
masked_score = -1e30
low = jnp.bfloat16
full = jnp.float32


def dot_nn(a, b):
    return lax.dot_general(a, b, (((1,), (0,)), ((), ())), preferred_element_type=full)


def dot_nt(a, b):
    return lax.dot_general(a, b, (((1,), (1,)), ((), ())), preferred_element_type=full)


def dot_tn(a, b):
    return lax.dot_general(a, b, (((0,), (0,)), ((), ())), preferred_element_type=full)


def params(megabytes=56):
    return pltpu.CompilerParams(vmem_limit_bytes=megabytes * 1024 * 1024)


def after(value, *others):
    return lax.optimization_barrier((value, *others))[0]


def shape(dims, dtype):
    return jax.ShapeDtypeStruct(dims, dtype)


def cost(micros):
    return pl.CostEstimate(flops=int(micros * 0.575e9), bytes_accessed=1, transcendentals=0)


def tables(position):
    lane = jnp.arange(PAIR, dtype=jnp.int32) % HEAD
    half = HEAD // 2
    frequency = rope_base ** (-2.0 * (lane % half).astype(full) / HEAD)
    angle = position.astype(full)[:, None] * frequency[None, :]
    sign = jnp.where(lane < half, -1.0, 1.0).astype(full)
    return jnp.cos(angle), jnp.sin(angle) * sign[None, :]


def partner(x):
    half = HEAD // 2
    lane = lax.broadcasted_iota(jnp.int32, x.shape, 1) % HEAD
    return jnp.where(lane < half, pltpu.roll(x, PAIR - half, 1), pltpu.roll(x, half, 1))


def turn(x, cosine, sine):
    return x * cosine + partner(x) * sine


def turn_back(x, cosine, sine):
    return x * cosine - partner(x) * sine


def project_kernel(
    plan, sources, first, count, ids, mate_ref, tok_ref, cross_ref, cos_ref, sin_ref, *refs
):
    srcs = refs[:sources]
    q_ref, k_ref, v_ref, weight, sems = refs[sources:]
    step = pl.program_id(0)

    @pl.when(step == 0)
    def _():
        for copy in plan(ids, srcs, weight, sems.at[0]):
            copy.start()
        pltpu.make_async_copy(weight, weight, sems.at[0]).wait()

    width = tok_ref.shape[1]
    inside = (step >= first) & (step < first + count)
    by_mate = (step < first) == (ids[2] == 1)
    rows = jnp.where(
        inside, tok_ref[...], jnp.where(by_mate, mate_ref[...], cross_ref[...])
    )
    cosine = cos_ref[...]
    sine = sin_ref[...]
    keys = dot_nn(rows, weight[1])
    for at in range(0, width, PAIR):
        k_ref[:, at : at + PAIR] = turn(keys[:, at : at + PAIR], cosine, sine).astype(low)
    v_ref[...] = dot_nn(rows, weight[2]).astype(low)

    @pl.when((step >= first) & (step < first + count))
    def _():
        queries = dot_nn(rows, weight[0])
        for at in range(0, width, PAIR):
            turned = turn(queries[:, at : at + PAIR], cosine, sine).astype(low)
            q_ref[:, at : at + PAIR] = (turned.astype(full) * (1.0 / math.sqrt(HEAD))).astype(low)


def project(plan, ids, edges, tokens, cosine, sine, sources):
    rows, width = tokens.shape
    mate, cross = edges
    ext = rows + 2 * mate.shape[0]
    block = 2 * TOKEN_BLOCK
    first, count = mate.shape[0] // block, rows // block
    tile = lambda w: pl.BlockSpec((block, w), lambda i, *_: (i, 0))
    inner = pl.BlockSpec((block, width), lambda i, *_: (jnp.clip(i - first, 0, count - 1), 0))
    edge = lambda core: pl.BlockSpec(
        (block, width),
        lambda i, ids: (
            jnp.where(
                ids[2] == core, jnp.minimum(i, first - 1), jnp.maximum(i - first - count, 0)
            ),
            0,
        ),
    )
    return pl.pallas_call(
        functools.partial(project_kernel, plan, len(sources), first, count),
        grid_spec=pltpu.PrefetchScalarGridSpec(
            num_scalar_prefetch=1,
            grid=(ext // block,),
            in_specs=[
                edge(1),
                inner,
                edge(0),
                tile(PAIR),
                tile(PAIR),
            ]
            + [pl.BlockSpec(memory_space=pl.ANY)] * len(sources),
            out_specs=[
                inner,
                tile(width),
                tile(width),
                pl.BlockSpec((4, width, width), lambda i, *_: (0, 0, 0)),
            ],
            scratch_shapes=[pltpu.SemaphoreType.DMA((1,))],
        ),
        out_shape=[
            shape((rows, width), low),
            shape((ext, width), low),
            shape((ext, width), low),
            shape((4, width, width), low),
        ],
        compiler_params=params(),
        cost_estimate=cost(0.1),
        name="project",
    )(ids, mate, tokens, cross, cosine, sine, *sources)


def fill_bias(bounds_ref, bias_ref, blocks, span):
    for b in range(blocks):
        lo = bounds_ref[0:1, b * QUERY_BLOCK : (b + 1) * QUERY_BLOCK] - b * QUERY_BLOCK
        hi = bounds_ref[1:2, b * QUERY_BLOCK : (b + 1) * QUERY_BLOCK] - b * QUERY_BLOCK
        at = lax.broadcasted_iota(jnp.int32, (span, QUERY_BLOCK), 0)
        bias_ref[b] = jnp.where((at >= lo) & (at < hi), 0.0, masked_score)


def only(x, head):
    lane = lax.broadcasted_iota(jnp.int32, x.shape, 1)
    return jnp.where((lane >= HEAD) if head else (lane < HEAD), x, jnp.zeros_like(x))


def attend_kernel(chunk, bounds_ref, q_ref, k_ref, v_ref, *refs):
    o_ref, lse_ref, bias_ref, vt_ref, s_ref = refs[-5:]
    rows = q_ref.shape[0]
    block = QUERY_BLOCK
    blocks = rows // block
    span = k_ref.shape[0] - rows + block

    @pl.when(pl.program_id(0) == 0)
    def _():
        fill_bias(bounds_ref, bias_ref, blocks, span)

    vt_ref[...] = v_ref[...].T
    chunks = [(c, min(chunk, span - c)) for c in range(0, span, chunk)]
    steps = [(b, h) for b in range(blocks) for h in range(2)]
    fold = lambda x, by: by(x.reshape(x.shape[0] // 64, 64, block), axis=0)
    add = lambda old, new: new if old is None else old + new

    def begin(i):
        b, h = steps[i]
        return {"query": only(q_ref[b * block : (b + 1) * block, :], h), "top": None}

    def score(i, c, n, state):
        b, _ = steps[i]
        s = dot_nt(k_ref[b * block + c : b * block + c + n, :], state["query"])
        s = s + bias_ref[b, c : c + n, :]
        s_ref[i % 2, c : c + n, :] = s
        top = fold(s, jnp.max)
        state["top"] = top if state["top"] is None else jnp.maximum(state["top"], top)

    def weigh(i, c, n, state):
        b, h = steps[i]
        e = jnp.exp(s_ref[i % 2, c : c + n, :] - state["peak"])
        state["total"] = add(state.get("total"), fold(e, jnp.sum))
        lanes = slice(b * block + c, b * block + c + n)
        mixed = dot_nn(vt_ref[h * HEAD : (h + 1) * HEAD, lanes], e.astype(low))
        state["mixed"] = add(state.get("mixed"), mixed)

    state = begin(0)
    for c, n in chunks:
        score(0, c, n, state)
    out = []
    for i, (b, h) in enumerate(steps):
        state["peak"] = jnp.max(state["top"], axis=0, keepdims=True)
        following = begin(i + 1) if i + 1 < len(steps) else None
        for c, n in chunks:
            if following is not None:
                score(i + 1, c, n, following)
            weigh(i, c, n, state)
        total = jnp.sum(state["total"], axis=0, keepdims=True)
        out.append(state["mixed"] / total)
        at = slice(b * block, (b + 1) * block)
        lse_ref[0, h : h + 1, at] = state["peak"] + jnp.log(total)
        if h == 1:
            o_ref[at, :] = jnp.concatenate(out, axis=0).T.astype(low)
            out = []
        state = following


def attend(bounds, q, k, v, first, pairs, before=None, chunk=640):
    rows, width = q.shape
    ext = k.shape[0]
    blocks = rows // QUERY_BLOCK
    span = ext - rows + QUERY_BLOCK
    own = pl.BlockSpec((rows, PAIR), lambda p: (0, p + first))
    wide = pl.BlockSpec((ext, PAIR), lambda p: (0, p + first))
    before = () if before is None else tuple(before)
    return pl.pallas_call(
        functools.partial(attend_kernel, chunk),
        grid=(pairs,),
        in_specs=[pl.BlockSpec((2, rows), lambda p: (0, 0)), own, wide, wide]
        + [pl.BlockSpec(memory_space=pl.ANY)] * len(before),
        out_specs=[own, pl.BlockSpec((1, 2, rows), lambda p: (p + first, 0, 0))],
        out_shape=[shape((rows, width), low), shape((width // PAIR, 2, rows), full)],
        input_output_aliases={4 + i: i for i in range(len(before))},
        scratch_shapes=[
            pltpu.VMEM((blocks, span, QUERY_BLOCK), full),
            pltpu.VMEM((PAIR, ext), low),
            pltpu.VMEM((2, span, QUERY_BLOCK), full),
        ],
        compiler_params=params(),
        cost_estimate=cost(2 * pairs),
        name="attend",
    )(bounds, q, k, v, *before)


def attend_back_kernel(
    chunk,
    ids,
    bounds_ref,
    q_ref,
    k_ref,
    v_ref,
    o_ref,
    do_ref,
    lse_ref,
    *refs,
):
    cos_ref, sin_ref = refs[:2]
    dq_ref, own_ref, mate_ref, cross_ref = refs[-10:-6]
    bias_ref, kt_ref, dk_ref, dv_ref, p_ref, ds_ref = refs[-6:]
    rows = q_ref.shape[0]
    ext = k_ref.shape[0]
    block = QUERY_BLOCK
    blocks = rows // block
    reach = (ext - rows) // 2
    span = ext - rows + block

    @pl.when(pl.program_id(0) == 0)
    def _():
        fill_bias(bounds_ref, bias_ref, blocks, span)

    kt_ref[...] = k_ref[...].T
    dk_ref[...] = jnp.zeros_like(dk_ref)
    dv_ref[...] = jnp.zeros_like(dv_ref)
    chunks = [(c, min(chunk, span - c)) for c in range(0, span, chunk)]

    def begin(b):
        at = slice(b * block, (b + 1) * block)
        q = q_ref[at, :]
        do = do_ref[at, :]
        product = (do.astype(full) * o_ref[at, :].astype(full)).T
        heads = range(2)
        return {
            "query": [only(q, h) for h in heads],
            "grad": [only(do, h) for h in heads],
            "delta": [
                jnp.sum(product[h * HEAD : (h + 1) * HEAD], axis=0, keepdims=True) for h in heads
            ],
            "lse": [lse_ref[0, h : h + 1, at] for h in heads],
            "dq": [None, None],
        }

    def score(b, h, c, n, state):
        rows_of = slice(b * block + c, b * block + c + n)
        lanes = slice(h * block, (h + 1) * block)
        s = dot_nt(k_ref[rows_of, :], state["query"][h]) + bias_ref[b, c : c + n, :]
        p = jnp.exp(s - state["lse"][h])
        dp = dot_nt(v_ref[rows_of, :], state["grad"][h])
        p_ref[b % 2, c : c + n, lanes] = p.astype(low)
        ds_ref[b % 2, c : c + n, lanes] = (p * (dp - state["delta"][h])).astype(low)

    def spread(b, h, c, n, state):
        rows_of = slice(b * block + c, b * block + c + n)
        if h == 0:
            both = jnp.concatenate(state["grad"], axis=0)
            dv_ref[rows_of, :] += dot_nn(p_ref[b % 2, c : c + n, :], both)
        else:
            both = jnp.concatenate(state["query"], axis=0)
            dk_ref[rows_of, :] += dot_nn(ds_ref[b % 2, c : c + n, :], both)
        ds = ds_ref[b % 2, c : c + n, h * block : (h + 1) * block]
        t = dot_nn(kt_ref[h * HEAD : (h + 1) * HEAD, rows_of], ds)
        state["dq"][h] = t if state["dq"][h] is None else state["dq"][h] + t

    state = begin(0)
    for h in range(2):
        for c, n in chunks:
            score(0, h, c, n, state)
    for b in range(blocks):
        following = begin(b + 1) if b + 1 < blocks else None
        for h in range(2):
            for c, n in chunks:
                if following is not None:
                    score(b + 1, h, c, n, following)
                spread(b, h, c, n, state)
        at = slice(b * block, (b + 1) * block)
        turned = turn_back(jnp.concatenate(state["dq"], axis=0).T, cos_ref[at, :], sin_ref[at, :])
        dq_ref[at, :] = (turned * (1.0 / math.sqrt(HEAD))).astype(low)
        state = following
    first = ids[2] == 0
    for i, ref in enumerate((dk_ref, dv_ref)):
        prior = ref[:reach, :].astype(low)
        following = ref[reach + rows :, :].astype(low)
        own_ref[i] = ref[reach : reach + rows, :].astype(low)
        mate_ref[i] = jnp.where(first, following, prior)
        cross_ref[i] = jnp.where(first, prior, following)


def attend_back(ids, bounds, q, k, v, o, do, lse, cosine, sine, first, pairs, halo, before=None, chunk=256):
    rows, width = q.shape
    ext = k.shape[0]
    blocks = rows // QUERY_BLOCK
    reach = (ext - rows) // 2
    span = ext - rows + QUERY_BLOCK
    halo_first, halo_pairs = halo
    before = () if before is None else tuple(before)
    own = pl.BlockSpec((rows, PAIR), lambda p, ids: (0, p + first))
    wide = pl.BlockSpec((ext, PAIR), lambda p, ids: (0, p + first))
    edge = pl.BlockSpec((2, reach, PAIR), lambda p, ids: (0, 0, p + first - halo_first))
    return pl.pallas_call(
        functools.partial(attend_back_kernel, chunk),
        grid_spec=pltpu.PrefetchScalarGridSpec(
            num_scalar_prefetch=1,
            grid=(pairs,),
            in_specs=[
            pl.BlockSpec((2, rows), lambda p, ids: (0, 0)),
            own,
            wide,
            wide,
            own,
            own,
            pl.BlockSpec((1, 2, rows), lambda p, ids: (p + first, 0, 0)),
            pl.BlockSpec((rows, PAIR), lambda p, ids: (0, 0)),
            pl.BlockSpec((rows, PAIR), lambda p, ids: (0, 0)),
        ]
        + [pl.BlockSpec(memory_space=pl.ANY)] * len(before),
        out_specs=[
            own,
            pl.BlockSpec((2, rows, PAIR), lambda p, ids: (0, 0, p + first)),
            edge,
            edge,
        ],
        scratch_shapes=[
            pltpu.VMEM((blocks, span, QUERY_BLOCK), full),
            pltpu.VMEM((PAIR, ext), low),
            pltpu.VMEM((ext, PAIR), full),
            pltpu.VMEM((ext, PAIR), full),
            pltpu.VMEM((2, span, 2 * QUERY_BLOCK), low),
            pltpu.VMEM((2, span, 2 * QUERY_BLOCK), low),
        ],
        ),
        out_shape=[
            shape((rows, width), low),
            shape((2, rows, width), low),
            shape((2, reach, halo_pairs * PAIR), low),
            shape((2, reach, halo_pairs * PAIR), low),
        ],
        input_output_aliases={10 + i: i for i in range(len(before))},
        compiler_params=params(),
        cost_estimate=cost(9 * pairs),
        name="attend_back",
    )(ids, bounds, q, k, v, o, do, lse, cosine, sine, *before)


def mean(x):
    return jnp.mean(x, axis=-1, keepdims=True)


def norm(x):
    centred = x - mean(x)
    inverse = lax.rsqrt(mean(centred * centred) + epsilon)
    return centred * inverse, inverse


def norm_back(scaled, normed, inverse):
    return inverse * (scaled - mean(scaled) - normed * mean(scaled * normed))


def position(j, core):
    return jnp.where(core == 0, j, (j & 1) * 2 + (j >> 1))


def gather_vectors(ids, vec_ref, width):
    count = vec_ref.shape[0]
    if count == 1:
        return vec_ref[0].astype(full)[:8]
    size = width // (2 * count)
    row = lax.broadcasted_iota(jnp.int32, (PAIR, width), 0)
    column = lax.broadcasted_iota(jnp.int32, (PAIR, width), 1)
    half = lax.broadcasted_iota(jnp.int32, (16, PAIR), 0) // 8
    out = jnp.zeros((16, width), full)
    for at in range(count):
        found = vec_ref[at].astype(full)
        for i in range(2):
            f = 2 * (ids[1] ^ position(at, ids[2])) + (ids[2] ^ i)
            place = ((column - f * size == row) & (row < size)).astype(full).astype(low)
            out = out + dot_nn(jnp.where(half == i, found, 0.0).astype(low), place)
    return out[:8] + out[8:]


def middle_kernel(plan, sources, ids, at_ref, tok_ref, cot_ref, *refs):
    vec_ref, refs = refs[0], refs[1:]
    srcs = refs[:sources]
    (
        out_ref,
        dz1_ref,
        da_ref,
        hidden_ref,
        product_ref,
        dfeed_ref,
        dgate_ref,
        dlift_ref,
        dbranch_ref,
        gains_ref,
        parts_ref,
        out_w,
        gate_w,
        up_w,
        down_w,
        lift_factor,
        gate_factor,
        vectors,
        sems,
    ) = refs[sources:]
    step = pl.program_id(0)
    weights = (out_w, gate_w, up_w, down_w)

    @pl.when(step == 0)
    def _():
        for copy in plan(ids, srcs, weights, sems):
            copy.start()
        gains_ref[...] = jnp.zeros_like(gains_ref)

    def ready(*which):
        @pl.when(step == 0)
        def _():
            for i in which:
                pltpu.make_async_copy(weights[i], weights[i], sems.at[i]).wait()

    parts, _, width = gate_w.shape

    @pl.when(step == 0)
    def _():
        vectors[...] = gather_vectors(ids, vec_ref, width)

    gain1, bias1, gain2, bias2 = (vectors[i : i + 1] for i in range(4))
    ready(0)
    normed1, inverse1 = norm(tok_ref[...].astype(full) + dot_nn(at_ref[...], out_w[...]))
    hidden = normed1 * gain1 + bias1
    hidden_low = hidden.astype(low)
    hidden_ref[...] = hidden_low
    ready(1, 2)
    feed = None
    for part in range(parts):
        at = slice(part * width, (part + 1) * width)
        gate = dot_nn(hidden_low, gate_w[part])
        lift = dot_nn(hidden_low, up_w[part])
        sigma = jax.nn.sigmoid(gate)
        opened = gate * sigma
        product = (opened * lift).astype(low)
        product_ref[:, at] = product
        lift_factor[:, at] = opened
        gate_factor[:, at] = lift * sigma * (1.0 + gate * (1.0 - sigma))
        if part == 0:
            ready(3)
        term = dot_nn(product, down_w[at, :])
        feed = term if feed is None else feed + term
    normed2, inverse2 = norm(hidden + feed)
    out_ref[...] = (normed2 * gain2 + bias2).astype(low)
    cot = cot_ref[...].astype(full)
    gains_ref[2:3] += jnp.sum(cot * normed2, axis=0, keepdims=True)
    gains_ref[3:4] += jnp.sum(cot, axis=0, keepdims=True)
    grad = norm_back(cot * gain2, normed2, inverse2)
    dfeed = grad.astype(low)
    dfeed_ref[...] = dfeed
    for part in range(parts):
        at = slice(part * width, (part + 1) * width)
        dproduct = dot_nt(dfeed, down_w[at, :])
        dgate = (dproduct * gate_factor[:, at]).astype(low)
        dlift = (dproduct * lift_factor[:, at]).astype(low)
        dgate_ref[:, at] = dgate
        dlift_ref[:, at] = dlift
        grad = grad + dot_nt(dgate, gate_w[part]) + dot_nt(dlift, up_w[part])
    gains_ref[0:1] += jnp.sum(grad * normed1, axis=0, keepdims=True)
    gains_ref[1:2] += jnp.sum(grad, axis=0, keepdims=True)
    grad = norm_back(grad * gain1, normed1, inverse1)
    dz1_ref[...] = grad
    dbranch = grad.astype(low)
    dbranch_ref[...] = dbranch
    da_ref[...] = dot_nt(dbranch, out_w[...]).astype(low)

    @pl.when(step == pl.num_programs(0) - 1)
    def _():
        sums = gains_ref[...].astype(low)
        size = width // 8
        row = lax.broadcasted_iota(jnp.int32, (width, PAIR), 0)
        column = lax.broadcasted_iota(jnp.int32, (width, PAIR), 1)
        for f in range(8):
            place = ((row - f * size == column) & (column < size)).astype(full).astype(low)
            parts_ref[f] = dot_nn(sums, place)


def middle(plan, ids, attended, tokens, cot, vectors, sources, hidden):
    rows, width = tokens.shape
    block = TOKEN_BLOCK
    tile = lambda w: pl.BlockSpec((block, w), lambda i, *_: (i, 0))
    whole = pl.BlockSpec((8, width), lambda i, *_: (0, 0))
    return pl.pallas_call(
        functools.partial(middle_kernel, plan, len(sources)),
        grid_spec=pltpu.PrefetchScalarGridSpec(
            num_scalar_prefetch=1,
            grid=(rows // block,),
            in_specs=[
                tile(width),
                tile(width),
                tile(width),
            ]
            + [pl.BlockSpec(vectors.shape, lambda i, *_: (0, 0, 0))]
            + [pl.BlockSpec(memory_space=pl.ANY)] * len(sources),
            out_specs=[
                tile(width),
                tile(width),
                tile(width),
                tile(width),
                tile(hidden),
                tile(width),
                tile(hidden),
                tile(hidden),
                tile(width),
                whole,
                pl.BlockSpec((8, 8, PAIR), lambda i, *_: (0, 0, 0)),
            ],
            scratch_shapes=[
                pltpu.VMEM((width, width), low),
                pltpu.VMEM((hidden // width, width, width), low),
                pltpu.VMEM((hidden // width, width, width), low),
                pltpu.VMEM((hidden, width), low),
                pltpu.VMEM((block, hidden), full),
                pltpu.VMEM((block, hidden), full),
                pltpu.VMEM((8, width), full),
                pltpu.SemaphoreType.DMA((4,)),
            ],
        ),
        out_shape=[
            shape((rows, width), low),
            shape((rows, width), full),
            shape((rows, width), low),
            shape((rows, width), low),
            shape((rows, hidden), low),
            shape((rows, width), low),
            shape((rows, hidden), low),
            shape((rows, hidden), low),
            shape((rows, width), low),
            shape((8, width), full),
            shape((8, 8, PAIR), full),
        ],
        compiler_params=params(),
        cost_estimate=cost(53),
        name="middle",
    )(ids, attended, tokens, cot, vectors, *sources)


def weight_grad_kernel(a_ref, b_ref, o_ref):
    o_ref[...] = dot_tn(a_ref[...], b_ref[...]).astype(o_ref.dtype)


def weight_grad(a, b, tile_a=768, tile_b=768):
    rows, size_a = a.shape
    size_b = b.shape[1]
    return pl.pallas_call(
        weight_grad_kernel,
        grid=(size_a // tile_a, size_b // tile_b),
        in_specs=[
            pl.BlockSpec((rows, tile_a), lambda i, j: (0, i)),
            pl.BlockSpec((rows, tile_b), lambda i, j: (0, j)),
        ],
        out_specs=pl.BlockSpec((tile_a, tile_b), lambda i, j: (i, j)),
        out_shape=shape((size_a, size_b), low),
        compiler_params=params(),
        cost_estimate=cost(9),
        name="weight_grad",
    )(a, b)


def joint_kernel(halos, ids, dq_ref, own_ref, cos_ref, sin_ref, *refs):
    by_mate = (pl.program_id(0) < pl.num_programs(0) // 2) == (ids[2] == 1)
    cosine = cos_ref[...]
    sine = sin_ref[...]
    dj_ref = refs[-1]
    width = dq_ref.shape[1]
    start = 0
    for mate_ref, cross_ref in zip(refs[:halos], refs[halos : 2 * halos]):
        for at in range(0, mate_ref.shape[2], PAIR):
            near = [
                jnp.where(
                    by_mate, mate_ref[i, :, at : at + PAIR], cross_ref[i, :, at : at + PAIR]
                ).astype(full)
                for i in range(2)
            ]
            lanes = slice(start, start + PAIR)
            keys = turn_back(own_ref[0, :, lanes].astype(full) + near[0], cosine, sine)
            values = own_ref[1, :, lanes].astype(full) + near[1]
            for i, x in enumerate((dq_ref[:, lanes], keys, values)):
                dj_ref[:, i * width + start : i * width + start + PAIR] = x.astype(low)
            start += PAIR


def joint(ids, dq, own, edges, cosine, sine):
    rows, width = dq.shape
    mates, crosses = zip(*edges)
    block = TOKEN_BLOCK
    half = mates[0].shape[1] // block
    inner = pl.BlockSpec((block, PAIR), lambda i, ids: (i + half, 0))
    tile = lambda w: pl.BlockSpec((block, w), lambda i, ids: (i, 0))
    edge = lambda size, core: pl.BlockSpec(
        (2, block, size),
        lambda i, ids: (
            0,
            jnp.where(ids[2] == core, jnp.minimum(i, half - 1), jnp.maximum(i - half, 0)),
            0,
        ),
    )
    return pl.pallas_call(
        functools.partial(joint_kernel, len(edges)),
        grid_spec=pltpu.PrefetchScalarGridSpec(
            num_scalar_prefetch=1,
            grid=(rows // block,),
            in_specs=[
                tile(width),
                pl.BlockSpec((2, block, width), lambda i, ids: (0, i, 0)),
                inner,
                inner,
            ]
            + [edge(m.shape[2], 1) for m in mates]
            + [edge(m.shape[2], 0) for m in crosses],
            out_specs=tile(3 * width),
        ),
        out_shape=shape((rows, 3 * width), low),
        compiler_params=params(32),
        cost_estimate=cost(0.01),
        name="joint",
    )(ids, dq, own, cosine, sine, *mates, *crosses)


def input_grad_kernel(dj_ref, dz1_ref, weight_ref, out_ref):
    width = dz1_ref.shape[1]
    out = dz1_ref[...]
    for i in range(3):
        out = out + dot_nt(dj_ref[:, i * width : (i + 1) * width], weight_ref[i])
    out_ref[...] = out


def input_grad(djoint, dz1, weights):
    rows, width = dz1.shape
    block = 2 * TOKEN_BLOCK
    tile = lambda w: pl.BlockSpec((block, w), lambda i: (i, 0))
    return pl.pallas_call(
        input_grad_kernel,
        grid=(rows // block,),
        in_specs=[
            tile(3 * width),
            tile(width),
            pl.BlockSpec((3, width, width), lambda i: (0, 0, 0)),
        ],
        out_specs=tile(width),
        out_shape=shape((rows, width), full),
        compiler_params=params(32),
        cost_estimate=cost(24),
        name="input_grad",
    )(djoint, dz1, weights)


def whole_joint_plan(ids, srcs, weight, sem):
    width = weight.shape[1]
    return [
        pltpu.make_async_copy(srcs[0].at[:, i * width : (i + 1) * width], weight.at[i], sem)
        for i in range(3)
    ] + [pltpu.make_async_copy(srcs[1], weight.at[3], sem)]


def whole_middle_plan(ids, srcs, weights, sems):
    out_w, gate_w, up_w, down_w = weights
    parts, _, width = gate_w.shape
    columns = lambda src, dst, sem: [
        pltpu.make_async_copy(src.at[:, i * width : (i + 1) * width], dst.at[i], sem)
        for i in range(parts)
    ]
    return (
        [pltpu.make_async_copy(srcs[0].at[3], out_w, sems.at[0])]
        + columns(srcs[1], gate_w, sems.at[1])
        + columns(srcs[2], up_w, sems.at[2])
        + [pltpu.make_async_copy(srcs[3], down_w, sems.at[3])]
    )


def swap_with(value, place):
    pairs = []
    for r in range(4):
        for z in range(4):
            for c in range(2):
                to_r, to_z, to_c = place(r, z, c)
                pairs.append(((r * 4 + z) * 2 + c, (to_r * 4 + to_z) * 2 + to_c))
    return lax.ppermute(value, ("rep", "fsdp"), pairs)


def over_core(value):
    return swap_with(value, lambda r, z, c: (r, z, 1 - c))


def over_square_1(value):
    return swap_with(value, lambda r, z, c: (r ^ (1 + c), z, c))


def over_square_2(value):
    return swap_with(value, lambda r, z, c: (r ^ (2 - c), z, c))


def over_z_1(value):
    return swap_with(value, lambda r, z, c: (r, z ^ (2 - c), c))


def over_z_2(value):
    return swap_with(value, lambda r, z, c: (r, z ^ (1 + c), c))


def pieces(ids, srcs):
    r, z, c = ids[0], ids[1], ids[2]
    found = []
    for i in range(2):
        core = (1 - c) if i else c
        bit1, bit2 = 1 + core, 2 - core
        for quarter in range(4):
            found.append((srcs[i][0].at[quarter], quarter, z, core))
        for ref, quarter in zip(srcs[i][1:], (r, r ^ bit1, r ^ bit2, r ^ 3)):
            for k in range(1, 4):
                found.append((ref.at[k - 1], quarter, z ^ position(k, core), core))
    return found


def piece_joint_plan(ids, srcs, weight, sem):
    size = srcs[0].shape[1]
    copies = []
    found = [
        [srcs[i]] + [srcs[k].at[j] for k in (2 + i, 4 + i) for j in range(2)] for i in range(2)
    ]
    for ref, quarter, z, core in pieces(ids, found):
        at = pl.multiple_of((2 * z + core) * size, size)
        copies.append(pltpu.make_async_copy(ref, weight.at[quarter, pl.ds(at, size)], sem))
    return copies


def piece_middle_plan(ids, srcs, weights, sems):
    out_w, gate_w, up_w, down_w = weights
    size = srcs[1].shape[1] // 3
    copies = [pltpu.make_async_copy(srcs[0].at[3], out_w, sems.at[0])]
    found = pieces(ids, [srcs[1::2], srcs[2::2]])
    for i, target in enumerate((gate_w, up_w)):
        for ref, quarter, z, core in found:
            at = pl.multiple_of((2 * z + core) * size, size)
            copies.append(
                pltpu.make_async_copy(
                    ref.at[i * size : (i + 1) * size],
                    target.at[quarter, pl.ds(at, size)],
                    sems.at[1 + i],
                )
            )
    for ref, quarter, z, core in found:
        at = pl.multiple_of(((2 * z + core) * 4 + quarter) * size, size)
        copies.append(
            pltpu.make_async_copy(
                ref.at[2 * size : 3 * size], down_w.at[pl.ds(at, size)], sems.at[3]
            )
        )
    return copies


def put_pieces(ids, block_ref, own_ref, other_ref, first, size):
    z, c = ids[1], ids[2]
    for ref, core in ((own_ref, c), (other_ref, 1 - c)):
        for k in range(4):
            at = pl.multiple_of((2 * (z ^ position(k, core)) + core) * size, 8)
            ref[0, k, first : first + size, :] = block_ref[pl.ds(at, size), :].astype(low)


def gate_up_grad_kernel(
        ids,
    hidden_ref,
    dgate_ref,
    dlift_ref,
    at_ref,
    db_ref,
    gains_ref,
    own_ref,
    other_ref,
    block_ref,
    second_ref,
    out_ref,
):
    size = block_ref.shape[0] // 8
    slim = size // 4
    z, c = ids[1], ids[2]
    quarter = ids[0] ^ pl.program_id(0)

    @pl.when(pl.program_id(0) == 0)
    def _():
        out_ref[...] = dot_tn(at_ref[...], db_ref[...])

    block_ref[...] = dot_tn(hidden_ref[...], dgate_ref[...])
    second_ref[...] = dot_tn(hidden_ref[...], dlift_ref[...])
    put_pieces(ids, block_ref, own_ref, other_ref, 0, size)
    put_pieces(ids, second_ref, own_ref, other_ref, size, size)
    for ref, core in ((own_ref, c), (other_ref, 1 - c)):
        for k in range(4):
            f = 2 * (z ^ position(k, core)) + core
            at = pl.multiple_of(f * size + quarter * slim, 8)
            sums = gains_ref[f]
            chosen = lax.broadcasted_iota(jnp.int32, sums.shape, 0) == quarter
            sums = jnp.sum(jnp.where(chosen, sums, 0.0), axis=0, keepdims=True)
            sums = jnp.pad(sums, ((0, 7), (0, ref.shape[3] - PAIR)))
            rest = jnp.concatenate([out_ref[pl.ds(at, slim), :], sums])
            ref[0, k, 2 * size :, :] = rest.astype(low)


def grad_specs(size, width):
    own = pl.BlockSpec((1, 4, size, width), lambda j, ids: (position(j, ids[2]), 0, 0, 0))
    other = pl.BlockSpec((1, 4, size, width), lambda j, ids: (position(j, 1 - ids[2]), 0, 0, 0))
    return [own, other], [shape((4, 4, size, width), low)] * 2


def gate_up_grad(ids, hidden_low, dgate, dlift, attended, dbranch, gains):
    rows, width = hidden_low.shape
    size = width // 8
    out_specs, out_shape = grad_specs(2 * size + size // 4 + 8, width)
    column = pl.BlockSpec((rows, width), lambda j, ids: (0, ids[0] ^ j))
    whole = pl.BlockSpec((rows, width), lambda j, ids: (0, 0))
    return pl.pallas_call(
        gate_up_grad_kernel,
        grid_spec=pltpu.PrefetchScalarGridSpec(
            num_scalar_prefetch=1,
            grid=(4,),
            in_specs=[
                whole,
                column,
                column,
                whole,
                whole,
                pl.BlockSpec(gains.shape, lambda j, ids: (0, 0, 0)),
            ],
            out_specs=out_specs,
            scratch_shapes=[pltpu.VMEM((width, width), full)] * 3,
        ),
        out_shape=out_shape,
        compiler_params=params(),
        cost_estimate=cost(18),
        name="gate_up_grad",
    )(ids, hidden_low, dgate, dlift, attended, dbranch, gains)


def down_grad_kernel(ids, product_ref, dfeed_ref, own_ref, other_ref, block_ref):
    size = own_ref.shape[2]
    r, z, c = ids[0], ids[1], ids[2]
    step = pl.program_id(0)
    block_ref[...] = dot_tn(product_ref[...], dfeed_ref[...])
    for ref, core in ((own_ref, c), (other_ref, 1 - c)):
        for j in range(4):
            at = pl.multiple_of((core * 4 + (r ^ position(j, core))) * size, 8)
            ref[j, 0] = block_ref[pl.ds(at, size), :].astype(low)


def down_grad(ids, product, dfeed):
    rows, hidden = product.shape
    width = dfeed.shape[1]
    size = hidden // 32
    out = lambda core: pl.BlockSpec(
        (4, 1, size, width),
        lambda j, ids: (0, position(ids[1] ^ j, (1 - ids[2]) if core else ids[2]), 0, 0),
    )
    return pl.pallas_call(
        down_grad_kernel,
        grid_spec=pltpu.PrefetchScalarGridSpec(
            num_scalar_prefetch=1,
            grid=(4,),
            in_specs=[
                pl.BlockSpec((rows, hidden // 4), lambda j, ids: (0, j)),
                pl.BlockSpec((rows, width), lambda j, ids: (0, 0)),
            ],
            out_specs=[out(0), out(1)],
            scratch_shapes=[pltpu.VMEM((hidden // 4, width), full)],
        ),
        out_shape=[shape((4, 4, size, width), low)] * 2,
        compiler_params=params(),
        cost_estimate=cost(10),
        name="down_grad",
    )(ids, product, dfeed)


def half(r, core):
    return jnp.where(core == 0, r >> 1, r & 1)


def joint_grad_kernel(ids, tok_ref, dj_ref, *refs):
    own_refs, other_refs, block_ref = refs[:2], refs[2:5], refs[5]
    r, z, c = ids[0], ids[1], ids[2]
    size = block_ref.shape[0] // 8
    block_ref[...] = dot_tn(tok_ref[...], dj_ref[...])

    def put(targets, core):
        for k, (ref, at) in enumerate(targets):
            first = pl.multiple_of((2 * (z ^ position(k, core)) + core) * size, 8)
            ref[at] = block_ref[pl.ds(first, size), :].astype(low)

    def whole(ref):
        return [(ref, k) for k in range(4)]

    sent = [(other_refs[1 + k // 2], k % 2) for k in range(4)]
    for kept_to, sent_to, core in (
        (whole(own_refs[0]), whole(own_refs[1]), c),
        (whole(other_refs[0]), sent, 1 - c),
    ):
        kept = pl.program_id(0) == half(r, core)
        pl.when(kept)(functools.partial(put, kept_to, core))
        pl.when(jnp.logical_not(kept))(functools.partial(put, sent_to, core))


def joint_grad(ids, tokens, djoint):
    rows, width = tokens.shape
    part = djoint.shape[1] // 2
    size = width // 8
    out = lambda n: pl.BlockSpec((n, size, part), lambda j, ids: (0, 0, 0))
    counts = (4, 4, 4, 2, 2)
    return pl.pallas_call(
        joint_grad_kernel,
        grid_spec=pltpu.PrefetchScalarGridSpec(
            num_scalar_prefetch=1,
            grid=(2,),
            in_specs=[
                pl.BlockSpec((rows, width), lambda j, ids: (0, 0)),
                pl.BlockSpec((rows, part), lambda j, ids: (0, j)),
            ],
            out_specs=[out(n) for n in counts],
            scratch_shapes=[pltpu.VMEM((width, part), full)],
        ),
        out_shape=[shape((n, size, part), low) for n in counts],
        compiler_params=params(32),
        cost_estimate=cost(0.01),
        name="joint_grad",
    )(ids, tokens, djoint)


def wide(v):
    return v.astype(full)


def sum_core(own, mate):
    return (wide(own[2:]) + wide(mate[2:])).astype(low)


def sum_square(own, mate, b):
    return (wide(own[1]) + wide(mate[1]) + wide(b[1])).astype(low)


def sum_rest(own, mate, b, d):
    return wide(own[0]) + wide(mate[0]) + wide(b[0]) + wide(d)


def sum_z(kept, e, f):
    return (kept[0] + wide(e[0]) + wide(f)).astype(low)


def place(ids, quarter):
    return position(quarter ^ ids[0], ids[2])


def finish_kernel(ids, near_ref, far_ref, gate_ref, up_ref, down_ref, out_ref, vec_ref):
    size, width = gate_ref.shape
    slim = out_ref.shape[0]
    at = place(ids, pl.program_id(0))

    def put(ref):
        piece = ref[at & 1].astype(full)
        gate_ref[...] = piece[:size]
        up_ref[...] = piece[size : 2 * size]
        out_ref[...] = piece[2 * size : 2 * size + slim]
        vec_ref[0] = piece[2 * size + slim : 2 * size + slim + 8, :PAIR]
        down_ref[...] = piece[2 * size + slim + 8 :]

    pl.when(at < 2)(lambda: put(near_ref))
    pl.when(at >= 2)(lambda: put(far_ref))


def finish(ids, near, far, size):
    width = near.shape[2]
    whole = pl.BlockSpec(near.shape, lambda j, ids: (0, 0, 0))
    column = pl.BlockSpec((size, width), lambda j, ids: (0, j))
    gate, up, down, out, vectors = pl.pallas_call(
        finish_kernel,
        grid_spec=pltpu.PrefetchScalarGridSpec(
            num_scalar_prefetch=1,
            grid=(4,),
            in_specs=[whole, whole],
            out_specs=[
                column,
                column,
                pl.BlockSpec((size, width), lambda j, ids: (j, 0)),
                pl.BlockSpec((size // 4, width), lambda j, ids: (j, 0)),
                pl.BlockSpec((1, 8, PAIR), lambda j, ids: (j, 0, 0)),
            ],
        ),
        out_shape=[shape((size, 4 * width), full)] * 2
        + [
            shape((4 * size, width), full),
            shape((size, width), full),
            shape((4, 8, PAIR), full),
        ],
        compiler_params=params(24),
        cost_estimate=cost(5),
        name="finish",
    )(ids, near, far)
    return gate, up, down, out, vectors[:, 0, :size]


def shards(
    custom,
    tokens,
    lengths,
    qkv_weight,
    out_weight,
    gate_weight,
    up_weight,
    down_weight,
    norm1_gain,
    norm1_bias,
    norm2_gain,
    norm2_bias,
    cotangent,
):
    rows, width = tokens.shape
    hidden = gate_weight.shape[1]
    size = lax.axis_size("fsdp")
    me = lax.axis_index("fsdp")
    r = lax.axis_index("rep")
    z, c = me // 2, me % 2
    ids = jnp.stack([r, z, c]).astype(jnp.int32)
    vectors = jnp.stack([norm1_gain, norm1_bias, norm2_gain, norm2_bias]).astype(low)

    mates = [(i, i ^ 1) for i in range(size)]
    crossed = [(i, i + 1 if i % 2 else i - 1) for i in range(1, size - 1)]
    swap_edges = lambda to_mate, to_cross: (
        lax.ppermute(to_mate, "fsdp", mates),
        lax.ppermute(to_cross, "fsdp", crossed),
    )
    edges = (tokens[rows - REACH :], tokens[:REACH])
    edges = (jnp.where(c == 0, *edges), jnp.where(c == 0, *edges[::-1]))
    if custom:
        part = qkv_weight.shape[0]
        columns = lambda w: jnp.swapaxes(w.astype(low).reshape(part, -1, width), 0, 1)
        column = lambda w, i: lax.dynamic_slice_in_dim(w, i * width, width, 1).astype(low)
        mine = jnp.where(
            r == 3, out_weight.astype(low), column(qkv_weight, jnp.minimum(r, 2))
        )
        first = over_z_2(mine)
        second = over_z_1(jnp.stack([mine, first]))
        rows_of = jnp.pad(vectors, ((0, 4), (0, width - part)))
        mine_2 = jnp.concatenate(
            [
                column(gate_weight, r),
                column(up_weight, r),
                lax.dynamic_slice_in_dim(down_weight, r * part, part, 0).astype(low),
                rows_of,
                over_core(rows_of),
            ]
        )
        shard_1 = jnp.concatenate([columns(qkv_weight), out_weight.astype(low)[None]])
        shard_2 = jnp.concatenate(
            [
                columns(gate_weight),
                columns(up_weight),
                down_weight.astype(low).reshape(4, part, width),
            ],
            axis=1,
        )
        mate_shard_1 = over_core(shard_1)
        own_1 = jnp.concatenate([first[None], after(second, mine_2, mate_shard_1)])
        first_2 = over_z_2(after(mine_2, own_1))
        other_1 = over_square_1(own_1)
        edges = swap_edges(*after(edges, first))
        mate_shard_2 = over_core(after(shard_2, own_1))
        near_1 = jnp.stack([own_1, after(other_1, shard_2, *edges)])
        far_1 = over_square_2(near_1)
        mate_near_1 = over_core(near_1)
        joint_sources = [shard_1, mate_shard_1, near_1, mate_near_1, far_1]
        joint_plan = piece_joint_plan
    else:
        edges = swap_edges(*edges)
        gather = lambda w: lax.all_gather(w.astype(low), "fsdp", axis=0, tiled=True)
        joint_sources = [gather(qkv_weight), gather(out_weight)]
        joint_plan = whole_joint_plan
        middle_sources = [gather(w) for w in (gate_weight, up_weight, down_weight)]
        vectors = lax.all_gather(vectors, "fsdp", axis=1, tiled=True)
        found = jnp.pad(vectors, ((0, 12), (0, 0)))[None]
        middle_plan = whole_middle_plan

    doc_lengths = lengths[0]
    ends = jnp.cumsum(doc_lengths)
    index = me * rows - REACH + jnp.arange(rows + 2 * REACH, dtype=jnp.int32)
    if custom:
        index = after(index, near_1)
    passed = (index[:, None] >= ends[None, :]).astype(jnp.int32)
    starts = jnp.sum(passed * doc_lengths[None, :], axis=1)
    cosine, sine = tables(index - starts)
    if custom:
        pair_2 = jnp.stack([mine_2, after(first_2, cosine)])
        second_2 = over_z_1(pair_2)
        mate_far_1 = over_core(after(far_1, pair_2))
        joint_sources.append(mate_far_1)
    own_starts = starts[REACH : REACH + rows]
    own_index = index[REACH : REACH + rows]
    stops = jnp.min(
        jnp.where(ends[None, :] > own_index[:, None], ends[None, :], size * rows), axis=1
    )
    base = me * rows - REACH
    bounds = jnp.stack(
        [
            jnp.maximum(own_starts, own_index - REACH) - base,
            jnp.minimum(stops, own_index + REACH + 1) - base,
        ]
    ).astype(jnp.int32)

    queries, keys, values, joint_weights = project(
        joint_plan, ids, edges, tokens, cosine, sine, joint_sources
    )
    given = (queries, keys, values)
    if custom:
        second_2 = after(second_2, queries)
        own_2 = jnp.concatenate([first_2[None, : 3 * part], second_2[:, : 3 * part]])
        found = jnp.concatenate([pair_2[:, 3 * part :, :PAIR], second_2[:, 3 * part :, :PAIR]])
        other_2 = over_square_1(own_2)
        done = attend(after(bounds, own_2, mate_shard_2), *given, 0, 2)
        tables_own = after((cosine, sine), done[1])
        tables_own = tuple(t[REACH : REACH + rows] for t in tables_own)
        other_2 = after(other_2, done[1], *tables_own)
        far_2 = over_square_2(after(own_2, other_2))
        across_2 = over_square_2(other_2)
        mate_own_2 = over_core(own_2)
        mate_other_2 = over_core(other_2)
        done = attend(after(bounds, other_2), *given, 2, 2, done)
        far_2 = after(far_2, done[1], mate_other_2, mate_own_2)
        mate_far_2 = over_core(far_2)
        attended, lse = attend(after(bounds, far_2), *given, 4, 2, done)
        across_2 = after(across_2, lse, mate_far_2)
        mate_across_2 = over_core(across_2)
        middle_sources = [shard_2, mate_shard_2, own_2, mate_own_2, other_2, mate_other_2]
        middle_sources += [far_2, mate_far_2, across_2, mate_across_2]
        middle_plan = piece_middle_plan
    else:
        done = None
        for first in (0, 2, 4):
            done = attend(bounds, *given, first, 2, done)
        attended, lse = done
        tables_own = tuple(t[REACH : REACH + rows] for t in (cosine, sine))
    result, dz1, dattended, hidden_low, product, dfeed, dgate, dlift, dbranch, *gains = middle(
        middle_plan,
        ids,
        attended,
        tokens,
        cotangent,
        found,
        [joint_weights, *middle_sources],
        hidden,
    )
    given = (queries, keys, values, attended, dattended, lse)
    given += tables_own
    spread = lambda g: lax.psum_scatter(g, "fsdp", scatter_dimension=0, tiled=True)
    if custom:
        own, other = gate_up_grad(ids, hidden_low, dgate, dlift, attended, dbranch, gains[1])
        mate = over_core(other)
        own_d, other_d = down_grad(ids, after(product, own), dfeed)
        sent = sum_core(own, after(mate, own_d))
        b = over_square_2(sent)
        mate_d = over_core(other_d)
        sent = sum_core(own_d, after(mate_d, sent))
        b_d = over_square_2(sent)
        dq, dkv, to_mate, to_cross = attend_back(ids, after(bounds, sent), *given, 0, 5, (0, 5))
        edges = [swap_edges(to_mate, to_cross)]
        sent = sum_square(own, mate, after(b, dq))
        d = over_square_1(sent)
        sent_d = sum_square(own_d, mate_d, after(b_d, sent))
        d_d = over_square_1(sent_d)
        dq, dkv, to_mate, to_cross = attend_back(
            ids, after(bounds, sent_d), *given, 5, 1, (5, 1), (dq, dkv)
        )
        edges_2 = [swap_edges(to_mate, to_cross)]
        kept = sum_rest(own, mate, b, after(d, dq, *edges[0]))
        kept = jnp.concatenate(
            [kept, sum_rest(own_d, mate_d, b_d, after(d_d, kept, *edges_2[0]))], axis=1
        )
        sent = kept[2:].astype(low)
        e = over_z_1(sent)
        djoint = joint(ids, after(dq, sent), dkv, edges + edges_2, cosine, sine)
        own_k, own_s, other_k, *other_s = joint_grad(ids, tokens, djoint)
        mate_s = jnp.concatenate([over_core(v) for v in other_s])
        sent = (wide(own_s) + wide(mate_s)).astype(low)
        b_1 = over_square_2(sent)
        e = after(e, sent)
        mate_k = over_core(after(other_k, e))
        sent = (kept[1] + wide(e[1])).astype(low)
        f = over_z_2(sent)
        grad_tokens = input_grad(after(djoint, sent), dz1, joint_weights)
        kept_1 = wide(own_k) + wide(mate_k) + wide(after(b_1, grad_tokens))
        sent = kept_1[2:].astype(low)
        e_1 = over_z_1(sent)
        mine = sum_z(kept, e, after(f, sent))
        got = over_square_1(mine)
        near = jnp.stack([mine, after(got, sent)])
        far = over_square_2(near)
        f_1 = over_z_2((kept_1[1] + wide(after(e_1, near)[1])).astype(low))
        mine = sum_z(kept_1, e_1, f_1)
        got = over_square_1(mine)
        gate_sum, up_sum, down_sum, out_sum, vector_sum = finish(
            ids, near, after(far, mine), part
        )
        mine = (wide(mine) + wide(after(got, gate_sum))).astype(low)
        halves = (mine, over_square_2(mine))
        joint_sum = wide(
            jnp.where(
                half(r, c) == 0,
                jnp.concatenate(halves, axis=1),
                jnp.concatenate(halves[::-1], axis=1),
            )
        )
        summed = (joint_sum, out_sum, gate_sum, up_sum, down_sum, vector_sum)
    else:
        share_down = spread(weight_grad(product, dfeed))
        share_gate = spread(weight_grad(hidden_low, dgate))
        share_up = spread(weight_grad(hidden_low, dlift))
        share_out = spread(weight_grad(attended, dbranch))
        share_gains = lax.psum_scatter(gains[0][:4], "fsdp", scatter_dimension=1, tiled=True)
        dq, dkv, to_mate, to_cross = attend_back(ids, bounds, *given, 0, 4, (0, 4))
        edges_1 = swap_edges(to_mate, to_cross)
        dq, dkv, to_mate, to_cross = attend_back(ids, bounds, *given, 4, 2, (4, 2), (dq, dkv))
        edges_2 = swap_edges(to_mate, to_cross)
        djoint = joint(ids, dq, dkv, [edges_1, edges_2], cosine, sine)
        share_qkv = spread(weight_grad(tokens, djoint))
        grad_tokens = input_grad(djoint, dz1, joint_weights)
        summed = lax.psum(
            tuple(
                s.astype(full)
                for s in (share_qkv, share_out, share_gate, share_up, share_down, share_gains)
            ),
            "rep",
        )
    return (result, grad_tokens, *summed[:5], *(summed[5][i] for i in range(4)))


def solution(mesh):
    rows = P(("rep", "fsdp"), None)
    matrix = P("fsdp", None)
    vector = P("fsdp")
    custom = (mesh.shape["rep"], mesh.shape["fsdp"]) == (4, 8)
    return jax.shard_map(
        functools.partial(shards, custom and not FORCE_WHOLE),
        mesh=mesh,
        in_specs=(rows, P("rep", None)) + (matrix,) * 5 + (vector,) * 4 + (rows,),
        out_specs=(rows, rows) + (matrix,) * 5 + (vector,) * 4,
        check_vma=False,
    )
```

```python
import functools
import math

import jax
import jax.numpy as jnp
from jax import lax
from jax.experimental import pallas as pl
from jax.experimental.pallas import tpu as pltpu
from jax.sharding import PartitionSpec as P

HEADS = 12
WINDOW = 1024
REACH = WINDOW // 2
HEAD = 64
PAIR = 2 * HEAD
QUERY_BLOCK = 256
TOKEN_BLOCK = 256
FORCE_WHOLE = False

epsilon = 1e-06
rope_base = 1000.0
masked_score = -1e30
low = jnp.bfloat16
full = jnp.float32


def dot_nn(a, b):
    return lax.dot_general(a, b, (((1,), (0,)), ((), ())), preferred_element_type=full)


def dot_nt(a, b):
    return lax.dot_general(a, b, (((1,), (1,)), ((), ())), preferred_element_type=full)


def dot_tn(a, b):
    return lax.dot_general(a, b, (((0,), (0,)), ((), ())), preferred_element_type=full)


def params(megabytes=56):
    return pltpu.CompilerParams(vmem_limit_bytes=megabytes * 1024 * 1024)


def after(value, *others):
    return lax.optimization_barrier((value, *others))[0]


def shape(dims, dtype):
    return jax.ShapeDtypeStruct(dims, dtype)


def cost(micros):
    return pl.CostEstimate(flops=int(micros * 0.575e9), bytes_accessed=1, transcendentals=0)


def tables(position):
    lane = jnp.arange(PAIR, dtype=jnp.int32) % HEAD
    half = HEAD // 2
    frequency = rope_base ** (-2.0 * (lane % half).astype(full) / HEAD)
    angle = position.astype(full)[:, None] * frequency[None, :]
    sign = jnp.where(lane < half, -1.0, 1.0).astype(full)
    return jnp.cos(angle), jnp.sin(angle) * sign[None, :]


def partner(x):
    half = HEAD // 2
    lane = lax.broadcasted_iota(jnp.int32, x.shape, 1) % HEAD
    return jnp.where(lane < half, pltpu.roll(x, PAIR - half, 1), pltpu.roll(x, half, 1))


def turn(x, cosine, sine):
    return x * cosine + partner(x) * sine


def turn_back(x, cosine, sine):
    return x * cosine - partner(x) * sine


def project_kernel(
    plan, sources, first, count, ids, mate_ref, tok_ref, cross_ref, cos_ref, sin_ref, *refs
):
    srcs = refs[:sources]
    q_ref, k_ref, v_ref, weight, sems = refs[sources:]
    step = pl.program_id(0)

    @pl.when(step == 0)
    def _():
        for copy in plan(ids, srcs, weight, sems.at[0]):
            copy.start()
        pltpu.make_async_copy(weight, weight, sems.at[0]).wait()

    width = tok_ref.shape[1]
    inside = (step >= first) & (step < first + count)
    by_mate = (step < first) == (ids[2] == 1)
    rows = jnp.where(
        inside, tok_ref[...], jnp.where(by_mate, mate_ref[...], cross_ref[...])
    )
    cosine = cos_ref[...]
    sine = sin_ref[...]
    keys = dot_nn(rows, weight[1])
    for at in range(0, width, PAIR):
        k_ref[:, at : at + PAIR] = turn(keys[:, at : at + PAIR], cosine, sine).astype(low)
    v_ref[...] = dot_nn(rows, weight[2]).astype(low)

    @pl.when((step >= first) & (step < first + count))
    def _():
        queries = dot_nn(rows, weight[0])
        for at in range(0, width, PAIR):
            turned = turn(queries[:, at : at + PAIR], cosine, sine).astype(low)
            q_ref[:, at : at + PAIR] = (turned.astype(full) * (1.0 / math.sqrt(HEAD))).astype(low)


def project(plan, ids, edges, tokens, cosine, sine, sources):
    rows, width = tokens.shape
    mate, cross = edges
    ext = rows + 2 * mate.shape[0]
    block = 2 * TOKEN_BLOCK
    first, count = mate.shape[0] // block, rows // block
    tile = lambda w: pl.BlockSpec((block, w), lambda i, *_: (i, 0))
    inner = pl.BlockSpec((block, width), lambda i, *_: (jnp.clip(i - first, 0, count - 1), 0))
    edge = lambda core: pl.BlockSpec(
        (block, width),
        lambda i, ids: (
            jnp.where(
                ids[2] == core, jnp.minimum(i, first - 1), jnp.maximum(i - first - count, 0)
            ),
            0,
        ),
    )
    return pl.pallas_call(
        functools.partial(project_kernel, plan, len(sources), first, count),
        grid_spec=pltpu.PrefetchScalarGridSpec(
            num_scalar_prefetch=1,
            grid=(ext // block,),
            in_specs=[
                edge(1),
                inner,
                edge(0),
                tile(PAIR),
                tile(PAIR),
            ]
            + [pl.BlockSpec(memory_space=pl.ANY)] * len(sources),
            out_specs=[
                inner,
                tile(width),
                tile(width),
                pl.BlockSpec((4, width, width), lambda i, *_: (0, 0, 0)),
            ],
            scratch_shapes=[pltpu.SemaphoreType.DMA((1,))],
        ),
        out_shape=[
            shape((rows, width), low),
            shape((ext, width), low),
            shape((ext, width), low),
            shape((4, width, width), low),
        ],
        compiler_params=params(),
        cost_estimate=cost(0.1),
        name="project",
    )(ids, mate, tokens, cross, cosine, sine, *sources)


def fill_bias(bounds_ref, bias_ref, blocks, span):
    for b in range(blocks):
        lo = bounds_ref[0:1, b * QUERY_BLOCK : (b + 1) * QUERY_BLOCK] - b * QUERY_BLOCK
        hi = bounds_ref[1:2, b * QUERY_BLOCK : (b + 1) * QUERY_BLOCK] - b * QUERY_BLOCK
        at = lax.broadcasted_iota(jnp.int32, (span, QUERY_BLOCK), 0)
        bias_ref[b] = jnp.where((at >= lo) & (at < hi), 0.0, masked_score)


def only(x, head):
    lane = lax.broadcasted_iota(jnp.int32, x.shape, 1)
    return jnp.where((lane >= HEAD) if head else (lane < HEAD), x, jnp.zeros_like(x))


def attend_kernel(chunk, bounds_ref, q_ref, k_ref, v_ref, *refs):
    o_ref, lse_ref, bias_ref, vt_ref, s_ref = refs[-5:]
    rows = q_ref.shape[0]
    block = QUERY_BLOCK
    blocks = rows // block
    span = k_ref.shape[0] - rows + block

    @pl.when(pl.program_id(0) == 0)
    def _():
        fill_bias(bounds_ref, bias_ref, blocks, span)

    vt_ref[...] = v_ref[...].T
    chunks = [(c, min(chunk, span - c)) for c in range(0, span, chunk)]
    steps = [(b, h) for b in range(blocks) for h in range(2)]
    fold = lambda x, by: by(x.reshape(x.shape[0] // 64, 64, block), axis=0)
    add = lambda old, new: new if old is None else old + new

    def begin(i):
        b, h = steps[i]
        return {"query": only(q_ref[b * block : (b + 1) * block, :], h), "top": None}

    def score(i, c, n, state):
        b, _ = steps[i]
        s = dot_nt(k_ref[b * block + c : b * block + c + n, :], state["query"])
        s = s + bias_ref[b, c : c + n, :]
        s_ref[i % 2, c : c + n, :] = s
        top = fold(s, jnp.max)
        state["top"] = top if state["top"] is None else jnp.maximum(state["top"], top)

    def weigh(i, c, n, state):
        b, h = steps[i]
        e = jnp.exp(s_ref[i % 2, c : c + n, :] - state["peak"])
        state["total"] = add(state.get("total"), fold(e, jnp.sum))
        lanes = slice(b * block + c, b * block + c + n)
        mixed = dot_nn(vt_ref[h * HEAD : (h + 1) * HEAD, lanes], e.astype(low))
        state["mixed"] = add(state.get("mixed"), mixed)

    state = begin(0)
    for c, n in chunks:
        score(0, c, n, state)
    out = []
    for i, (b, h) in enumerate(steps):
        state["peak"] = jnp.max(state["top"], axis=0, keepdims=True)
        following = begin(i + 1) if i + 1 < len(steps) else None
        for c, n in chunks:
            if following is not None:
                score(i + 1, c, n, following)
            weigh(i, c, n, state)
        total = jnp.sum(state["total"], axis=0, keepdims=True)
        out.append(state["mixed"] / total)
        at = slice(b * block, (b + 1) * block)
        lse_ref[0, h : h + 1, at] = state["peak"] + jnp.log(total)
        if h == 1:
            o_ref[at, :] = jnp.concatenate(out, axis=0).T.astype(low)
            out = []
        state = following


def attend(bounds, q, k, v, first, pairs, before=None, chunk=640):
    rows, width = q.shape
    ext = k.shape[0]
    blocks = rows // QUERY_BLOCK
    span = ext - rows + QUERY_BLOCK
    own = pl.BlockSpec((rows, PAIR), lambda p: (0, p + first))
    wide = pl.BlockSpec((ext, PAIR), lambda p: (0, p + first))
    before = () if before is None else tuple(before)
    return pl.pallas_call(
        functools.partial(attend_kernel, chunk),
        grid=(pairs,),
        in_specs=[pl.BlockSpec((2, rows), lambda p: (0, 0)), own, wide, wide]
        + [pl.BlockSpec(memory_space=pl.ANY)] * len(before),
        out_specs=[own, pl.BlockSpec((1, 2, rows), lambda p: (p + first, 0, 0))],
        out_shape=[shape((rows, width), low), shape((width // PAIR, 2, rows), full)],
        input_output_aliases={4 + i: i for i in range(len(before))},
        scratch_shapes=[
            pltpu.VMEM((blocks, span, QUERY_BLOCK), full),
            pltpu.VMEM((PAIR, ext), low),
            pltpu.VMEM((2, span, QUERY_BLOCK), full),
        ],
        compiler_params=params(),
        cost_estimate=cost(2 * pairs),
        name="attend",
    )(bounds, q, k, v, *before)


def attend_back_kernel(
    chunk,
    ids,
    bounds_ref,
    q_ref,
    k_ref,
    v_ref,
    o_ref,
    do_ref,
    lse_ref,
    *refs,
):
    cos_ref, sin_ref = refs[:2]
    dq_ref, own_ref, mate_ref, cross_ref = refs[-10:-6]
    bias_ref, kt_ref, dk_ref, dv_ref, p_ref, ds_ref = refs[-6:]
    rows = q_ref.shape[0]
    ext = k_ref.shape[0]
    block = QUERY_BLOCK
    blocks = rows // block
    reach = (ext - rows) // 2
    span = ext - rows + block

    @pl.when(pl.program_id(0) == 0)
    def _():
        fill_bias(bounds_ref, bias_ref, blocks, span)

    kt_ref[...] = k_ref[...].T
    dk_ref[...] = jnp.zeros_like(dk_ref)
    dv_ref[...] = jnp.zeros_like(dv_ref)
    chunks = [(c, min(chunk, span - c)) for c in range(0, span, chunk)]

    def begin(b):
        at = slice(b * block, (b + 1) * block)
        q = q_ref[at, :]
        do = do_ref[at, :]
        product = (do.astype(full) * o_ref[at, :].astype(full)).T
        heads = range(2)
        return {
            "query": [only(q, h) for h in heads],
            "grad": [only(do, h) for h in heads],
            "delta": [
                jnp.sum(product[h * HEAD : (h + 1) * HEAD], axis=0, keepdims=True) for h in heads
            ],
            "lse": [lse_ref[0, h : h + 1, at] for h in heads],
            "dq": [None, None],
        }

    def score(b, h, c, n, state):
        rows_of = slice(b * block + c, b * block + c + n)
        lanes = slice(h * block, (h + 1) * block)
        s = dot_nt(k_ref[rows_of, :], state["query"][h]) + bias_ref[b, c : c + n, :]
        p = jnp.exp(s - state["lse"][h])
        dp = dot_nt(v_ref[rows_of, :], state["grad"][h])
        p_ref[b % 2, c : c + n, lanes] = p.astype(low)
        ds_ref[b % 2, c : c + n, lanes] = (p * (dp - state["delta"][h])).astype(low)

    def spread(b, h, c, n, state):
        rows_of = slice(b * block + c, b * block + c + n)
        if h == 0:
            both = jnp.concatenate(state["grad"], axis=0)
            dv_ref[rows_of, :] += dot_nn(p_ref[b % 2, c : c + n, :], both)
        else:
            both = jnp.concatenate(state["query"], axis=0)
            dk_ref[rows_of, :] += dot_nn(ds_ref[b % 2, c : c + n, :], both)
        ds = ds_ref[b % 2, c : c + n, h * block : (h + 1) * block]
        t = dot_nn(kt_ref[h * HEAD : (h + 1) * HEAD, rows_of], ds)
        state["dq"][h] = t if state["dq"][h] is None else state["dq"][h] + t

    state = begin(0)
    for h in range(2):
        for c, n in chunks:
            score(0, h, c, n, state)
    for b in range(blocks):
        following = begin(b + 1) if b + 1 < blocks else None
        for h in range(2):
            for c, n in chunks:
                if following is not None:
                    score(b + 1, h, c, n, following)
                spread(b, h, c, n, state)
        at = slice(b * block, (b + 1) * block)
        turned = turn_back(jnp.concatenate(state["dq"], axis=0).T, cos_ref[at, :], sin_ref[at, :])
        dq_ref[at, :] = (turned * (1.0 / math.sqrt(HEAD))).astype(low)
        state = following
    first = ids[2] == 0
    for i, ref in enumerate((dk_ref, dv_ref)):
        prior = ref[:reach, :].astype(low)
        following = ref[reach + rows :, :].astype(low)
        own_ref[i] = ref[reach : reach + rows, :].astype(low)
        mate_ref[i] = jnp.where(first, following, prior)
        cross_ref[i] = jnp.where(first, prior, following)


def attend_back(ids, bounds, q, k, v, o, do, lse, cosine, sine, first, pairs, halo, before=None, chunk=256):
    rows, width = q.shape
    ext = k.shape[0]
    blocks = rows // QUERY_BLOCK
    reach = (ext - rows) // 2
    span = ext - rows + QUERY_BLOCK
    halo_first, halo_pairs = halo
    before = () if before is None else tuple(before)
    own = pl.BlockSpec((rows, PAIR), lambda p, ids: (0, p + first))
    wide = pl.BlockSpec((ext, PAIR), lambda p, ids: (0, p + first))
    edge = pl.BlockSpec((2, reach, PAIR), lambda p, ids: (0, 0, p + first - halo_first))
    return pl.pallas_call(
        functools.partial(attend_back_kernel, chunk),
        grid_spec=pltpu.PrefetchScalarGridSpec(
            num_scalar_prefetch=1,
            grid=(pairs,),
            in_specs=[
            pl.BlockSpec((2, rows), lambda p, ids: (0, 0)),
            own,
            wide,
            wide,
            own,
            own,
            pl.BlockSpec((1, 2, rows), lambda p, ids: (p + first, 0, 0)),
            pl.BlockSpec((rows, PAIR), lambda p, ids: (0, 0)),
            pl.BlockSpec((rows, PAIR), lambda p, ids: (0, 0)),
        ]
        + [pl.BlockSpec(memory_space=pl.ANY)] * len(before),
        out_specs=[
            own,
            pl.BlockSpec((2, rows, PAIR), lambda p, ids: (0, 0, p + first)),
            edge,
            edge,
        ],
        scratch_shapes=[
            pltpu.VMEM((blocks, span, QUERY_BLOCK), full),
            pltpu.VMEM((PAIR, ext), low),
            pltpu.VMEM((ext, PAIR), full),
            pltpu.VMEM((ext, PAIR), full),
            pltpu.VMEM((2, span, 2 * QUERY_BLOCK), low),
            pltpu.VMEM((2, span, 2 * QUERY_BLOCK), low),
        ],
        ),
        out_shape=[
            shape((rows, width), low),
            shape((2, rows, width), low),
            shape((2, reach, halo_pairs * PAIR), low),
            shape((2, reach, halo_pairs * PAIR), low),
        ],
        input_output_aliases={10 + i: i for i in range(len(before))},
        compiler_params=params(),
        cost_estimate=cost(9 * pairs),
        name="attend_back",
    )(ids, bounds, q, k, v, o, do, lse, cosine, sine, *before)


def mean(x):
    return jnp.mean(x, axis=-1, keepdims=True)


def norm(x):
    centred = x - mean(x)
    inverse = lax.rsqrt(mean(centred * centred) + epsilon)
    return centred * inverse, inverse


def norm_back(scaled, normed, inverse):
    return inverse * (scaled - mean(scaled) - normed * mean(scaled * normed))


def position(j, core):
    return jnp.where(core == 0, j, (j & 1) * 2 + (j >> 1))


def gather_vectors(ids, vec_ref, width):
    count = vec_ref.shape[0]
    if count == 1:
        return vec_ref[0].astype(full)[:8]
    size = width // (2 * count)
    row = lax.broadcasted_iota(jnp.int32, (PAIR, width), 0)
    column = lax.broadcasted_iota(jnp.int32, (PAIR, width), 1)
    half = lax.broadcasted_iota(jnp.int32, (16, PAIR), 0) // 8
    out = jnp.zeros((16, width), full)
    for at in range(count):
        found = vec_ref[at].astype(full)
        for i in range(2):
            f = 2 * (ids[1] ^ position(at, ids[2])) + (ids[2] ^ i)
            place = ((column - f * size == row) & (row < size)).astype(full).astype(low)
            out = out + dot_nn(jnp.where(half == i, found, 0.0).astype(low), place)
    return out[:8] + out[8:]


def middle_kernel(plan, sources, ids, at_ref, tok_ref, cot_ref, *refs):
    vec_ref, refs = refs[0], refs[1:]
    srcs = refs[:sources]
    (
        out_ref,
        dz1_ref,
        da_ref,
        hidden_ref,
        product_ref,
        dfeed_ref,
        dgate_ref,
        dlift_ref,
        dbranch_ref,
        gains_ref,
        parts_ref,
        out_w,
        gate_w,
        up_w,
        down_w,
        lift_factor,
        gate_factor,
        vectors,
        sems,
    ) = refs[sources:]
    step = pl.program_id(0)
    weights = (out_w, gate_w, up_w, down_w)

    @pl.when(step == 0)
    def _():
        for copy in plan(ids, srcs, weights, sems):
            copy.start()
        gains_ref[...] = jnp.zeros_like(gains_ref)

    def ready(*which):
        @pl.when(step == 0)
        def _():
            for i in which:
                pltpu.make_async_copy(weights[i], weights[i], sems.at[i]).wait()

    parts, _, width = gate_w.shape

    @pl.when(step == 0)
    def _():
        vectors[...] = gather_vectors(ids, vec_ref, width)

    gain1, bias1, gain2, bias2 = (vectors[i : i + 1] for i in range(4))
    ready(0)
    normed1, inverse1 = norm(tok_ref[...].astype(full) + dot_nn(at_ref[...], out_w[...]))
    hidden = normed1 * gain1 + bias1
    hidden_low = hidden.astype(low)
    hidden_ref[...] = hidden_low
    ready(1, 2)
    feed = None
    for part in range(parts):
        at = slice(part * width, (part + 1) * width)
        gate = dot_nn(hidden_low, gate_w[part])
        lift = dot_nn(hidden_low, up_w[part])
        sigma = jax.nn.sigmoid(gate)
        opened = gate * sigma
        product = (opened * lift).astype(low)
        product_ref[:, at] = product
        lift_factor[:, at] = opened
        gate_factor[:, at] = lift * sigma * (1.0 + gate * (1.0 - sigma))
        if part == 0:
            ready(3)
        term = dot_nn(product, down_w[at, :])
        feed = term if feed is None else feed + term
    normed2, inverse2 = norm(hidden + feed)
    out_ref[...] = (normed2 * gain2 + bias2).astype(low)
    cot = cot_ref[...].astype(full)
    gains_ref[2:3] += jnp.sum(cot * normed2, axis=0, keepdims=True)
    gains_ref[3:4] += jnp.sum(cot, axis=0, keepdims=True)
    grad = norm_back(cot * gain2, normed2, inverse2)
    dfeed = grad.astype(low)
    dfeed_ref[...] = dfeed
    for part in range(parts):
        at = slice(part * width, (part + 1) * width)
        dproduct = dot_nt(dfeed, down_w[at, :])
        dgate = (dproduct * gate_factor[:, at]).astype(low)
        dlift = (dproduct * lift_factor[:, at]).astype(low)
        dgate_ref[:, at] = dgate
        dlift_ref[:, at] = dlift
        grad = grad + dot_nt(dgate, gate_w[part]) + dot_nt(dlift, up_w[part])
    gains_ref[0:1] += jnp.sum(grad * normed1, axis=0, keepdims=True)
    gains_ref[1:2] += jnp.sum(grad, axis=0, keepdims=True)
    grad = norm_back(grad * gain1, normed1, inverse1)
    dz1_ref[...] = grad
    dbranch = grad.astype(low)
    dbranch_ref[...] = dbranch
    da_ref[...] = dot_nt(dbranch, out_w[...]).astype(low)

    @pl.when(step == pl.num_programs(0) - 1)
    def _():
        sums = gains_ref[...].astype(low)
        size = width // 8
        row = lax.broadcasted_iota(jnp.int32, (width, PAIR), 0)
        column = lax.broadcasted_iota(jnp.int32, (width, PAIR), 1)
        for f in range(8):
            place = ((row - f * size == column) & (column < size)).astype(full).astype(low)
            parts_ref[f] = dot_nn(sums, place)


def middle(plan, ids, attended, tokens, cot, vectors, sources, hidden):
    rows, width = tokens.shape
    block = TOKEN_BLOCK
    tile = lambda w: pl.BlockSpec((block, w), lambda i, *_: (i, 0))
    whole = pl.BlockSpec((8, width), lambda i, *_: (0, 0))
    return pl.pallas_call(
        functools.partial(middle_kernel, plan, len(sources)),
        grid_spec=pltpu.PrefetchScalarGridSpec(
            num_scalar_prefetch=1,
            grid=(rows // block,),
            in_specs=[
                tile(width),
                tile(width),
                tile(width),
            ]
            + [pl.BlockSpec(vectors.shape, lambda i, *_: (0, 0, 0))]
            + [pl.BlockSpec(memory_space=pl.ANY)] * len(sources),
            out_specs=[
                tile(width),
                tile(width),
                tile(width),
                tile(width),
                tile(hidden),
                tile(width),
                tile(hidden),
                tile(hidden),
                tile(width),
                whole,
                pl.BlockSpec((8, 8, PAIR), lambda i, *_: (0, 0, 0)),
            ],
            scratch_shapes=[
                pltpu.VMEM((width, width), low),
                pltpu.VMEM((hidden // width, width, width), low),
                pltpu.VMEM((hidden // width, width, width), low),
                pltpu.VMEM((hidden, width), low),
                pltpu.VMEM((block, hidden), full),
                pltpu.VMEM((block, hidden), full),
                pltpu.VMEM((8, width), full),
                pltpu.SemaphoreType.DMA((4,)),
            ],
        ),
        out_shape=[
            shape((rows, width), low),
            shape((rows, width), full),
            shape((rows, width), low),
            shape((rows, width), low),
            shape((rows, hidden), low),
            shape((rows, width), low),
            shape((rows, hidden), low),
            shape((rows, hidden), low),
            shape((rows, width), low),
            shape((8, width), full),
            shape((8, 8, PAIR), full),
        ],
        compiler_params=params(),
        cost_estimate=cost(53),
        name="middle",
    )(ids, attended, tokens, cot, vectors, *sources)


def weight_grad_kernel(a_ref, b_ref, o_ref):
    o_ref[...] = dot_tn(a_ref[...], b_ref[...]).astype(o_ref.dtype)


def weight_grad(a, b, tile_a=768, tile_b=768):
    rows, size_a = a.shape
    size_b = b.shape[1]
    return pl.pallas_call(
        weight_grad_kernel,
        grid=(size_a // tile_a, size_b // tile_b),
        in_specs=[
            pl.BlockSpec((rows, tile_a), lambda i, j: (0, i)),
            pl.BlockSpec((rows, tile_b), lambda i, j: (0, j)),
        ],
        out_specs=pl.BlockSpec((tile_a, tile_b), lambda i, j: (i, j)),
        out_shape=shape((size_a, size_b), low),
        compiler_params=params(),
        cost_estimate=cost(9),
        name="weight_grad",
    )(a, b)


def joint_kernel(halos, ids, dq_ref, own_ref, cos_ref, sin_ref, *refs):
    by_mate = (pl.program_id(0) < pl.num_programs(0) // 2) == (ids[2] == 1)
    cosine = cos_ref[...]
    sine = sin_ref[...]
    dj_ref = refs[-1]
    width = dq_ref.shape[1]
    start = 0
    for mate_ref, cross_ref in zip(refs[:halos], refs[halos : 2 * halos]):
        for at in range(0, mate_ref.shape[2], PAIR):
            near = [
                jnp.where(
                    by_mate, mate_ref[i, :, at : at + PAIR], cross_ref[i, :, at : at + PAIR]
                ).astype(full)
                for i in range(2)
            ]
            lanes = slice(start, start + PAIR)
            keys = turn_back(own_ref[0, :, lanes].astype(full) + near[0], cosine, sine)
            values = own_ref[1, :, lanes].astype(full) + near[1]
            for i, x in enumerate((dq_ref[:, lanes], keys, values)):
                dj_ref[:, i * width + start : i * width + start + PAIR] = x.astype(low)
            start += PAIR


def joint(ids, dq, own, edges, cosine, sine):
    rows, width = dq.shape
    mates, crosses = zip(*edges)
    block = TOKEN_BLOCK
    half = mates[0].shape[1] // block
    inner = pl.BlockSpec((block, PAIR), lambda i, ids: (i + half, 0))
    tile = lambda w: pl.BlockSpec((block, w), lambda i, ids: (i, 0))
    edge = lambda size, core: pl.BlockSpec(
        (2, block, size),
        lambda i, ids: (
            0,
            jnp.where(ids[2] == core, jnp.minimum(i, half - 1), jnp.maximum(i - half, 0)),
            0,
        ),
    )
    return pl.pallas_call(
        functools.partial(joint_kernel, len(edges)),
        grid_spec=pltpu.PrefetchScalarGridSpec(
            num_scalar_prefetch=1,
            grid=(rows // block,),
            in_specs=[
                tile(width),
                pl.BlockSpec((2, block, width), lambda i, ids: (0, i, 0)),
                inner,
                inner,
            ]
            + [edge(m.shape[2], 1) for m in mates]
            + [edge(m.shape[2], 0) for m in crosses],
            out_specs=tile(3 * width),
        ),
        out_shape=shape((rows, 3 * width), low),
        compiler_params=params(32),
        cost_estimate=cost(0.01),
        name="joint",
    )(ids, dq, own, cosine, sine, *mates, *crosses)


def input_grad_kernel(dj_ref, dz1_ref, weight_ref, out_ref):
    width = dz1_ref.shape[1]
    out = dz1_ref[...]
    for i in range(3):
        out = out + dot_nt(dj_ref[:, i * width : (i + 1) * width], weight_ref[i])
    out_ref[...] = out


def input_grad(djoint, dz1, weights):
    rows, width = dz1.shape
    block = 2 * TOKEN_BLOCK
    tile = lambda w: pl.BlockSpec((block, w), lambda i: (i, 0))
    return pl.pallas_call(
        input_grad_kernel,
        grid=(rows // block,),
        in_specs=[
            tile(3 * width),
            tile(width),
            pl.BlockSpec((3, width, width), lambda i: (0, 0, 0)),
        ],
        out_specs=tile(width),
        out_shape=shape((rows, width), full),
        compiler_params=params(32),
        cost_estimate=cost(24),
        name="input_grad",
    )(djoint, dz1, weights)


def whole_joint_plan(ids, srcs, weight, sem):
    width = weight.shape[1]
    return [
        pltpu.make_async_copy(srcs[0].at[:, i * width : (i + 1) * width], weight.at[i], sem)
        for i in range(3)
    ] + [pltpu.make_async_copy(srcs[1], weight.at[3], sem)]


def whole_middle_plan(ids, srcs, weights, sems):
    out_w, gate_w, up_w, down_w = weights
    parts, _, width = gate_w.shape
    columns = lambda src, dst, sem: [
        pltpu.make_async_copy(src.at[:, i * width : (i + 1) * width], dst.at[i], sem)
        for i in range(parts)
    ]
    return (
        [pltpu.make_async_copy(srcs[0].at[3], out_w, sems.at[0])]
        + columns(srcs[1], gate_w, sems.at[1])
        + columns(srcs[2], up_w, sems.at[2])
        + [pltpu.make_async_copy(srcs[3], down_w, sems.at[3])]
    )


def swap_with(value, place):
    pairs = []
    for r in range(4):
        for z in range(4):
            for c in range(2):
                to_r, to_z, to_c = place(r, z, c)
                pairs.append(((r * 4 + z) * 2 + c, (to_r * 4 + to_z) * 2 + to_c))
    return lax.ppermute(value, ("rep", "fsdp"), pairs)


def over_core(value):
    return swap_with(value, lambda r, z, c: (r, z, 1 - c))


def over_square_1(value):
    return swap_with(value, lambda r, z, c: (r ^ (1 + c), z, c))


def over_square_2(value):
    return swap_with(value, lambda r, z, c: (r ^ (2 - c), z, c))


def over_z_1(value):
    return swap_with(value, lambda r, z, c: (r, z ^ (2 - c), c))


def over_z_2(value):
    return swap_with(value, lambda r, z, c: (r, z ^ (1 + c), c))


def pieces(ids, srcs):
    r, z, c = ids[0], ids[1], ids[2]
    found = []
    for i in range(2):
        core = (1 - c) if i else c
        bit1, bit2 = 1 + core, 2 - core
        for quarter in range(4):
            found.append((srcs[i][0].at[quarter], quarter, z, core))
        for ref, quarter in zip(srcs[i][1:], (r, r ^ bit1, r ^ bit2, r ^ 3)):
            for k in range(1, 4):
                found.append((ref.at[k - 1], quarter, z ^ position(k, core), core))
    return found


def piece_joint_plan(ids, srcs, weight, sem):
    size = srcs[0].shape[1]
    copies = []
    found = [
        [srcs[i]] + [srcs[k].at[j] for k in (2 + i, 4 + i) for j in range(2)] for i in range(2)
    ]
    for ref, quarter, z, core in pieces(ids, found):
        at = pl.multiple_of((2 * z + core) * size, size)
        copies.append(pltpu.make_async_copy(ref, weight.at[quarter, pl.ds(at, size)], sem))
    return copies


def piece_middle_plan(ids, srcs, weights, sems):
    out_w, gate_w, up_w, down_w = weights
    size = srcs[1].shape[1] // 3
    copies = [pltpu.make_async_copy(srcs[0].at[3], out_w, sems.at[0])]
    found = pieces(ids, [srcs[1::2], srcs[2::2]])
    for i, target in enumerate((gate_w, up_w)):
        for ref, quarter, z, core in found:
            at = pl.multiple_of((2 * z + core) * size, size)
            copies.append(
                pltpu.make_async_copy(
                    ref.at[i * size : (i + 1) * size],
                    target.at[quarter, pl.ds(at, size)],
                    sems.at[1 + i],
                )
            )
    for ref, quarter, z, core in found:
        at = pl.multiple_of(((2 * z + core) * 4 + quarter) * size, size)
        copies.append(
            pltpu.make_async_copy(
                ref.at[2 * size : 3 * size], down_w.at[pl.ds(at, size)], sems.at[3]
            )
        )
    return copies


def put_pieces(ids, block_ref, own_ref, other_ref, first, size):
    z, c = ids[1], ids[2]
    for ref, core in ((own_ref, c), (other_ref, 1 - c)):
        for k in range(4):
            at = pl.multiple_of((2 * (z ^ position(k, core)) + core) * size, 8)
            ref[0, k, first : first + size, :] = block_ref[pl.ds(at, size), :].astype(low)


def gate_up_grad_kernel(
        ids,
    hidden_ref,
    dgate_ref,
    dlift_ref,
    at_ref,
    db_ref,
    gains_ref,
    own_ref,
    other_ref,
    block_ref,
    second_ref,
    out_ref,
):
    size = block_ref.shape[0] // 8
    slim = size // 4
    z, c = ids[1], ids[2]
    quarter = ids[0] ^ pl.program_id(0)

    @pl.when(pl.program_id(0) == 0)
    def _():
        out_ref[...] = dot_tn(at_ref[...], db_ref[...])

    block_ref[...] = dot_tn(hidden_ref[...], dgate_ref[...])
    second_ref[...] = dot_tn(hidden_ref[...], dlift_ref[...])
    put_pieces(ids, block_ref, own_ref, other_ref, 0, size)
    put_pieces(ids, second_ref, own_ref, other_ref, size, size)
    for ref, core in ((own_ref, c), (other_ref, 1 - c)):
        for k in range(4):
            f = 2 * (z ^ position(k, core)) + core
            at = pl.multiple_of(f * size + quarter * slim, 8)
            sums = gains_ref[f]
            chosen = lax.broadcasted_iota(jnp.int32, sums.shape, 0) == quarter
            sums = jnp.sum(jnp.where(chosen, sums, 0.0), axis=0, keepdims=True)
            sums = jnp.pad(sums, ((0, 7), (0, ref.shape[3] - PAIR)))
            rest = jnp.concatenate([out_ref[pl.ds(at, slim), :], sums])
            ref[0, k, 2 * size :, :] = rest.astype(low)


def grad_specs(size, width):
    own = pl.BlockSpec((1, 4, size, width), lambda j, ids: (position(j, ids[2]), 0, 0, 0))
    other = pl.BlockSpec((1, 4, size, width), lambda j, ids: (position(j, 1 - ids[2]), 0, 0, 0))
    return [own, other], [shape((4, 4, size, width), low)] * 2


def gate_up_grad(ids, hidden_low, dgate, dlift, attended, dbranch, gains):
    rows, width = hidden_low.shape
    size = width // 8
    out_specs, out_shape = grad_specs(2 * size + size // 4 + 8, width)
    column = pl.BlockSpec((rows, width), lambda j, ids: (0, ids[0] ^ j))
    whole = pl.BlockSpec((rows, width), lambda j, ids: (0, 0))
    return pl.pallas_call(
        gate_up_grad_kernel,
        grid_spec=pltpu.PrefetchScalarGridSpec(
            num_scalar_prefetch=1,
            grid=(4,),
            in_specs=[
                whole,
                column,
                column,
                whole,
                whole,
                pl.BlockSpec(gains.shape, lambda j, ids: (0, 0, 0)),
            ],
            out_specs=out_specs,
            scratch_shapes=[pltpu.VMEM((width, width), full)] * 3,
        ),
        out_shape=out_shape,
        compiler_params=params(),
        cost_estimate=cost(18),
        name="gate_up_grad",
    )(ids, hidden_low, dgate, dlift, attended, dbranch, gains)


def down_grad_kernel(ids, product_ref, dfeed_ref, own_ref, other_ref, block_ref):
    size = own_ref.shape[2]
    r, z, c = ids[0], ids[1], ids[2]
    step = pl.program_id(0)
    block_ref[...] = dot_tn(product_ref[...], dfeed_ref[...])
    for ref, core in ((own_ref, c), (other_ref, 1 - c)):
        for j in range(4):
            at = pl.multiple_of((core * 4 + (r ^ position(j, core))) * size, 8)
            ref[j, 0] = block_ref[pl.ds(at, size), :].astype(low)


def down_grad(ids, product, dfeed):
    rows, hidden = product.shape
    width = dfeed.shape[1]
    size = hidden // 32
    out = lambda core: pl.BlockSpec(
        (4, 1, size, width),
        lambda j, ids: (0, position(ids[1] ^ j, (1 - ids[2]) if core else ids[2]), 0, 0),
    )
    return pl.pallas_call(
        down_grad_kernel,
        grid_spec=pltpu.PrefetchScalarGridSpec(
            num_scalar_prefetch=1,
            grid=(4,),
            in_specs=[
                pl.BlockSpec((rows, hidden // 4), lambda j, ids: (0, j)),
                pl.BlockSpec((rows, width), lambda j, ids: (0, 0)),
            ],
            out_specs=[out(0), out(1)],
            scratch_shapes=[pltpu.VMEM((hidden // 4, width), full)],
        ),
        out_shape=[shape((4, 4, size, width), low)] * 2,
        compiler_params=params(),
        cost_estimate=cost(10),
        name="down_grad",
    )(ids, product, dfeed)


def half(r, core):
    return jnp.where(core == 0, r >> 1, r & 1)


def joint_grad_kernel(ids, tok_ref, dj_ref, *refs):
    own_refs, other_refs, block_ref = refs[:2], refs[2:5], refs[5]
    r, z, c = ids[0], ids[1], ids[2]
    size = block_ref.shape[0] // 8
    block_ref[...] = dot_tn(tok_ref[...], dj_ref[...])

    def put(targets, core):
        for k, (ref, at) in enumerate(targets):
            first = pl.multiple_of((2 * (z ^ position(k, core)) + core) * size, 8)
            ref[at] = block_ref[pl.ds(first, size), :].astype(low)

    def whole(ref):
        return [(ref, k) for k in range(4)]

    sent = [(other_refs[1 + k // 2], k % 2) for k in range(4)]
    for kept_to, sent_to, core in (
        (whole(own_refs[0]), whole(own_refs[1]), c),
        (whole(other_refs[0]), sent, 1 - c),
    ):
        kept = pl.program_id(0) == half(r, core)
        pl.when(kept)(functools.partial(put, kept_to, core))
        pl.when(jnp.logical_not(kept))(functools.partial(put, sent_to, core))


def joint_grad(ids, tokens, djoint):
    rows, width = tokens.shape
    part = djoint.shape[1] // 2
    size = width // 8
    out = lambda n: pl.BlockSpec((n, size, part), lambda j, ids: (0, 0, 0))
    counts = (4, 4, 4, 2, 2)
    return pl.pallas_call(
        joint_grad_kernel,
        grid_spec=pltpu.PrefetchScalarGridSpec(
            num_scalar_prefetch=1,
            grid=(2,),
            in_specs=[
                pl.BlockSpec((rows, width), lambda j, ids: (0, 0)),
                pl.BlockSpec((rows, part), lambda j, ids: (0, j)),
            ],
            out_specs=[out(n) for n in counts],
            scratch_shapes=[pltpu.VMEM((width, part), full)],
        ),
        out_shape=[shape((n, size, part), low) for n in counts],
        compiler_params=params(32),
        cost_estimate=cost(0.01),
        name="joint_grad",
    )(ids, tokens, djoint)


def wide(v):
    return v.astype(full)


def sum_core(own, mate):
    return (wide(own[2:]) + wide(mate[2:])).astype(low)


def sum_square(own, mate, b):
    return (wide(own[1]) + wide(mate[1]) + wide(b[1])).astype(low)


def sum_rest(own, mate, b, d):
    return wide(own[0]) + wide(mate[0]) + wide(b[0]) + wide(d)


def sum_z(kept, e, f):
    return (kept[0] + wide(e[0]) + wide(f)).astype(low)


def place(ids, quarter):
    return position(quarter ^ ids[0], ids[2])


def finish_kernel(ids, near_ref, far_ref, gate_ref, up_ref, down_ref, out_ref, vec_ref):
    size, width = gate_ref.shape
    slim = out_ref.shape[0]
    at = place(ids, pl.program_id(0))

    def put(ref):
        piece = ref[at & 1].astype(full)
        gate_ref[...] = piece[:size]
        up_ref[...] = piece[size : 2 * size]
        out_ref[...] = piece[2 * size : 2 * size + slim]
        vec_ref[0] = piece[2 * size + slim : 2 * size + slim + 8, :PAIR]
        down_ref[...] = piece[2 * size + slim + 8 :]

    pl.when(at < 2)(lambda: put(near_ref))
    pl.when(at >= 2)(lambda: put(far_ref))


def finish(ids, near, far, size):
    width = near.shape[2]
    whole = pl.BlockSpec(near.shape, lambda j, ids: (0, 0, 0))
    column = pl.BlockSpec((size, width), lambda j, ids: (0, j))
    gate, up, down, out, vectors = pl.pallas_call(
        finish_kernel,
        grid_spec=pltpu.PrefetchScalarGridSpec(
            num_scalar_prefetch=1,
            grid=(4,),
            in_specs=[whole, whole],
            out_specs=[
                column,
                column,
                pl.BlockSpec((size, width), lambda j, ids: (j, 0)),
                pl.BlockSpec((size // 4, width), lambda j, ids: (j, 0)),
                pl.BlockSpec((1, 8, PAIR), lambda j, ids: (j, 0, 0)),
            ],
        ),
        out_shape=[shape((size, 4 * width), full)] * 2
        + [
            shape((4 * size, width), full),
            shape((size, width), full),
            shape((4, 8, PAIR), full),
        ],
        compiler_params=params(24),
        cost_estimate=cost(5),
        name="finish",
    )(ids, near, far)
    return gate, up, down, out, vectors[:, 0, :size]


def shards(
    custom,
    tokens,
    lengths,
    qkv_weight,
    out_weight,
    gate_weight,
    up_weight,
    down_weight,
    norm1_gain,
    norm1_bias,
    norm2_gain,
    norm2_bias,
    cotangent,
):
    rows, width = tokens.shape
    hidden = gate_weight.shape[1]
    size = lax.axis_size("fsdp")
    me = lax.axis_index("fsdp")
    r = lax.axis_index("rep")
    z, c = me // 2, me % 2
    ids = jnp.stack([r, z, c]).astype(jnp.int32)
    vectors = jnp.stack([norm1_gain, norm1_bias, norm2_gain, norm2_bias]).astype(low)

    mates = [(i, i ^ 1) for i in range(size)]
    crossed = [(i, i + 1 if i % 2 else i - 1) for i in range(1, size - 1)]
    swap_edges = lambda to_mate, to_cross: (
        lax.ppermute(to_mate, "fsdp", mates),
        lax.ppermute(to_cross, "fsdp", crossed),
    )
    edges = (tokens[rows - REACH :], tokens[:REACH])
    edges = (jnp.where(c == 0, *edges), jnp.where(c == 0, *edges[::-1]))
    if custom:
        part = qkv_weight.shape[0]
        columns = lambda w: jnp.swapaxes(w.astype(low).reshape(part, -1, width), 0, 1)
        column = lambda w, i: lax.dynamic_slice_in_dim(w, i * width, width, 1).astype(low)
        mine = jnp.where(
            r == 3, out_weight.astype(low), column(qkv_weight, jnp.minimum(r, 2))
        )
        first = over_z_2(mine)
        second = over_z_1(mine)
        third = over_z_1(first)
        rows_of = jnp.pad(vectors, ((0, 4), (0, width - part)))
        mine_2 = jnp.concatenate(
            [
                column(gate_weight, r),
                column(up_weight, r),
                lax.dynamic_slice_in_dim(down_weight, r * part, part, 0).astype(low),
                rows_of,
                over_core(rows_of),
            ]
        )
        shard_1 = jnp.concatenate([columns(qkv_weight), out_weight.astype(low)[None]])
        shard_2 = jnp.concatenate(
            [
                columns(gate_weight),
                columns(up_weight),
                down_weight.astype(low).reshape(4, part, width),
            ],
            axis=1,
        )
        mate_shard_1 = over_core(shard_1)
        own_1 = jnp.stack([first, second, after(third, mine_2, mate_shard_1)])
        first_2 = over_z_2(after(mine_2, own_1))
        other_1 = over_square_1(own_1)
        edges = swap_edges(*after(edges, first))
        mate_shard_2 = over_core(after(shard_2, own_1))
        near_1 = jnp.stack([own_1, after(other_1, shard_2, *edges)])
        far_1 = over_square_2(near_1)
        mate_near_1 = over_core(near_1)
        joint_sources = [shard_1, mate_shard_1, near_1, mate_near_1, far_1]
        joint_plan = piece_joint_plan
    else:
        edges = swap_edges(*edges)
        gather = lambda w: lax.all_gather(w.astype(low), "fsdp", axis=0, tiled=True)
        joint_sources = [gather(qkv_weight), gather(out_weight)]
        joint_plan = whole_joint_plan
        middle_sources = [gather(w) for w in (gate_weight, up_weight, down_weight)]
        vectors = lax.all_gather(vectors, "fsdp", axis=1, tiled=True)
        found = jnp.pad(vectors, ((0, 12), (0, 0)))[None]
        middle_plan = whole_middle_plan

    doc_lengths = lengths[0]
    ends = jnp.cumsum(doc_lengths)
    index = me * rows - REACH + jnp.arange(rows + 2 * REACH, dtype=jnp.int32)
    if custom:
        index = after(index, near_1)
    passed = (index[:, None] >= ends[None, :]).astype(jnp.int32)
    starts = jnp.sum(passed * doc_lengths[None, :], axis=1)
    cosine, sine = tables(index - starts)
    if custom:
        pair_2 = jnp.stack([mine_2, after(first_2, cosine)])
        second_2 = over_z_1(pair_2)
        mate_far_1 = over_core(after(far_1, pair_2))
        joint_sources.append(mate_far_1)
    own_starts = starts[REACH : REACH + rows]
    own_index = index[REACH : REACH + rows]
    stops = jnp.min(
        jnp.where(ends[None, :] > own_index[:, None], ends[None, :], size * rows), axis=1
    )
    base = me * rows - REACH
    bounds = jnp.stack(
        [
            jnp.maximum(own_starts, own_index - REACH) - base,
            jnp.minimum(stops, own_index + REACH + 1) - base,
        ]
    ).astype(jnp.int32)

    queries, keys, values, joint_weights = project(
        joint_plan, ids, edges, tokens, cosine, sine, joint_sources
    )
    given = (queries, keys, values)
    if custom:
        second_2 = after(second_2, queries)
        own_2 = jnp.concatenate([first_2[None, : 3 * part], second_2[:, : 3 * part]])
        found = jnp.concatenate([pair_2[:, 3 * part :, :PAIR], second_2[:, 3 * part :, :PAIR]])
        other_2 = over_square_1(own_2)
        done = attend(after(bounds, own_2, mate_shard_2), *given, 0, 2)
        tables_own = after((cosine, sine), done[1])
        tables_own = tuple(t[REACH : REACH + rows] for t in tables_own)
        other_2 = after(other_2, done[1], *tables_own)
        far_2 = over_square_2(after(own_2, other_2))
        across_2 = over_square_2(other_2)
        mate_own_2 = over_core(own_2)
        mate_other_2 = over_core(other_2)
        done = attend(after(bounds, other_2), *given, 2, 2, done)
        far_2 = after(far_2, done[1], mate_other_2, mate_own_2)
        mate_far_2 = over_core(far_2)
        attended, lse = attend(after(bounds, far_2), *given, 4, 2, done)
        across_2 = after(across_2, lse, mate_far_2)
        mate_across_2 = over_core(across_2)
        middle_sources = [shard_2, mate_shard_2, own_2, mate_own_2, other_2, mate_other_2]
        middle_sources += [far_2, mate_far_2, across_2, mate_across_2]
        middle_plan = piece_middle_plan
    else:
        done = None
        for first in (0, 2, 4):
            done = attend(bounds, *given, first, 2, done)
        attended, lse = done
        tables_own = tuple(t[REACH : REACH + rows] for t in (cosine, sine))
    result, dz1, dattended, hidden_low, product, dfeed, dgate, dlift, dbranch, *gains = middle(
        middle_plan,
        ids,
        attended,
        tokens,
        cotangent,
        found,
        [joint_weights, *middle_sources],
        hidden,
    )
    given = (queries, keys, values, attended, dattended, lse)
    given += tables_own
    spread = lambda g: lax.psum_scatter(g, "fsdp", scatter_dimension=0, tiled=True)
    if custom:
        own, other = gate_up_grad(ids, hidden_low, dgate, dlift, attended, dbranch, gains[1])
        mate = over_core(other)
        own_d, other_d = down_grad(ids, after(product, own), dfeed)
        sent = sum_core(own, after(mate, own_d))
        b = over_square_2(sent)
        mate_d = over_core(other_d)
        sent = sum_core(own_d, after(mate_d, sent))
        b_d = over_square_2(sent)
        dq, dkv, to_mate, to_cross = attend_back(ids, after(bounds, sent), *given, 0, 5, (0, 5))
        edges = [swap_edges(to_mate, to_cross)]
        sent = sum_square(own, mate, after(b, dq))
        d = over_square_1(sent)
        sent_d = sum_square(own_d, mate_d, after(b_d, sent))
        d_d = over_square_1(sent_d)
        dq, dkv, to_mate, to_cross = attend_back(
            ids, after(bounds, sent_d), *given, 5, 1, (5, 1), (dq, dkv)
        )
        edges_2 = [swap_edges(to_mate, to_cross)]
        kept = sum_rest(own, mate, b, after(d, dq, *edges[0]))
        kept = jnp.concatenate(
            [kept, sum_rest(own_d, mate_d, b_d, after(d_d, kept, *edges_2[0]))], axis=1
        )
        sent = kept[2:].astype(low)
        e = over_z_1(sent)
        djoint = joint(ids, after(dq, sent), dkv, edges + edges_2, cosine, sine)
        own_k, own_s, other_k, *other_s = joint_grad(ids, tokens, djoint)
        mate_s = jnp.concatenate([over_core(v) for v in other_s])
        sent = (wide(own_s) + wide(mate_s)).astype(low)
        b_1 = over_square_2(sent)
        e = after(e, sent)
        mate_k = over_core(after(other_k, e))
        sent = (kept[1] + wide(e[1])).astype(low)
        f = over_z_2(sent)
        grad_tokens = input_grad(after(djoint, sent), dz1, joint_weights)
        kept_1 = wide(own_k) + wide(mate_k) + wide(after(b_1, grad_tokens))
        sent = kept_1[2:].astype(low)
        e_1 = over_z_1(sent)
        mine = sum_z(kept, e, after(f, sent))
        got = over_square_1(mine)
        near = jnp.stack([mine, after(got, sent)])
        far = over_square_2(near)
        f_1 = over_z_2((kept_1[1] + wide(after(e_1, near)[1])).astype(low))
        mine = sum_z(kept_1, e_1, f_1)
        got = over_square_1(mine)
        gate_sum, up_sum, down_sum, out_sum, vector_sum = finish(
            ids, near, after(far, mine), part
        )
        mine = (wide(mine) + wide(after(got, gate_sum))).astype(low)
        halves = (mine, over_square_2(mine))
        joint_sum = wide(
            jnp.where(
                half(r, c) == 0,
                jnp.concatenate(halves, axis=1),
                jnp.concatenate(halves[::-1], axis=1),
            )
        )
        summed = (joint_sum, out_sum, gate_sum, up_sum, down_sum, vector_sum)
    else:
        share_down = spread(weight_grad(product, dfeed))
        share_gate = spread(weight_grad(hidden_low, dgate))
        share_up = spread(weight_grad(hidden_low, dlift))
        share_out = spread(weight_grad(attended, dbranch))
        share_gains = lax.psum_scatter(gains[0][:4], "fsdp", scatter_dimension=1, tiled=True)
        dq, dkv, to_mate, to_cross = attend_back(ids, bounds, *given, 0, 4, (0, 4))
        edges_1 = swap_edges(to_mate, to_cross)
        dq, dkv, to_mate, to_cross = attend_back(ids, bounds, *given, 4, 2, (4, 2), (dq, dkv))
        edges_2 = swap_edges(to_mate, to_cross)
        djoint = joint(ids, dq, dkv, [edges_1, edges_2], cosine, sine)
        share_qkv = spread(weight_grad(tokens, djoint))
        grad_tokens = input_grad(djoint, dz1, joint_weights)
        summed = lax.psum(
            tuple(
                s.astype(full)
                for s in (share_qkv, share_out, share_gate, share_up, share_down, share_gains)
            ),
            "rep",
        )
    return (result, grad_tokens, *summed[:5], *(summed[5][i] for i in range(4)))


def solution(mesh):
    rows = P(("rep", "fsdp"), None)
    matrix = P("fsdp", None)
    vector = P("fsdp")
    custom = (mesh.shape["rep"], mesh.shape["fsdp"]) == (4, 8)
    return jax.shard_map(
        functools.partial(shards, custom and not FORCE_WHOLE),
        mesh=mesh,
        in_specs=(rows, P("rep", None)) + (matrix,) * 5 + (vector,) * 4 + (rows,),
        out_specs=(rows, rows) + (matrix,) * 5 + (vector,) * 4,
        check_vma=False,
    )
```

```python
import functools
import math

import jax
import jax.numpy as jnp
from jax import lax
from jax.experimental import pallas as pl
from jax.experimental.pallas import tpu as pltpu
from jax.sharding import PartitionSpec as P

HEADS = 12
WINDOW = 1024
REACH = WINDOW // 2
HEAD = 64
PAIR = 2 * HEAD
QUERY_BLOCK = 256
TOKEN_BLOCK = 256
FORCE_WHOLE = False

epsilon = 1e-06
rope_base = 1000.0
masked_score = -1e30
low = jnp.bfloat16
full = jnp.float32


def dot_nn(a, b):
    return lax.dot_general(a, b, (((1,), (0,)), ((), ())), preferred_element_type=full)


def dot_nt(a, b):
    return lax.dot_general(a, b, (((1,), (1,)), ((), ())), preferred_element_type=full)


def dot_tn(a, b):
    return lax.dot_general(a, b, (((0,), (0,)), ((), ())), preferred_element_type=full)


def params(megabytes=56):
    return pltpu.CompilerParams(vmem_limit_bytes=megabytes * 1024 * 1024)


def after(value, *others):
    return lax.optimization_barrier((value, *others))[0]


def shape(dims, dtype):
    return jax.ShapeDtypeStruct(dims, dtype)


def cost(micros):
    return pl.CostEstimate(flops=int(micros * 0.575e9), bytes_accessed=1, transcendentals=0)


def tables(position):
    lane = jnp.arange(PAIR, dtype=jnp.int32) % HEAD
    half = HEAD // 2
    frequency = rope_base ** (-2.0 * (lane % half).astype(full) / HEAD)
    angle = position.astype(full)[:, None] * frequency[None, :]
    sign = jnp.where(lane < half, -1.0, 1.0).astype(full)
    return jnp.cos(angle), jnp.sin(angle) * sign[None, :]


def partner(x):
    half = HEAD // 2
    lane = lax.broadcasted_iota(jnp.int32, x.shape, 1) % HEAD
    return jnp.where(lane < half, pltpu.roll(x, PAIR - half, 1), pltpu.roll(x, half, 1))


def turn(x, cosine, sine):
    return x * cosine + partner(x) * sine


def turn_back(x, cosine, sine):
    return x * cosine - partner(x) * sine


def project_kernel(
    plan, sources, first, count, ids, mate_ref, tok_ref, cross_ref, cos_ref, sin_ref, *refs
):
    srcs = refs[:sources]
    q_ref, k_ref, v_ref, weight, sems = refs[sources:]
    step = pl.program_id(0)

    @pl.when(step == 0)
    def _():
        for copy in plan(ids, srcs, weight, sems.at[0]):
            copy.start()
        pltpu.make_async_copy(weight, weight, sems.at[0]).wait()

    width = tok_ref.shape[1]
    inside = (step >= first) & (step < first + count)
    by_mate = (step < first) == (ids[2] == 1)
    rows = jnp.where(
        inside, tok_ref[...], jnp.where(by_mate, mate_ref[...], cross_ref[...])
    )
    cosine = cos_ref[...]
    sine = sin_ref[...]
    keys = dot_nn(rows, weight[1])
    for at in range(0, width, PAIR):
        k_ref[:, at : at + PAIR] = turn(keys[:, at : at + PAIR], cosine, sine).astype(low)
    v_ref[...] = dot_nn(rows, weight[2]).astype(low)

    @pl.when((step >= first) & (step < first + count))
    def _():
        queries = dot_nn(rows, weight[0])
        for at in range(0, width, PAIR):
            turned = turn(queries[:, at : at + PAIR], cosine, sine).astype(low)
            q_ref[:, at : at + PAIR] = (turned.astype(full) * (1.0 / math.sqrt(HEAD))).astype(low)


def project(plan, ids, edges, tokens, cosine, sine, sources):
    rows, width = tokens.shape
    mate, cross = edges
    ext = rows + 2 * mate.shape[0]
    block = 2 * TOKEN_BLOCK
    first, count = mate.shape[0] // block, rows // block
    tile = lambda w: pl.BlockSpec((block, w), lambda i, *_: (i, 0))
    inner = pl.BlockSpec((block, width), lambda i, *_: (jnp.clip(i - first, 0, count - 1), 0))
    edge = lambda core: pl.BlockSpec(
        (block, width),
        lambda i, ids: (
            jnp.where(
                ids[2] == core, jnp.minimum(i, first - 1), jnp.maximum(i - first - count, 0)
            ),
            0,
        ),
    )
    return pl.pallas_call(
        functools.partial(project_kernel, plan, len(sources), first, count),
        grid_spec=pltpu.PrefetchScalarGridSpec(
            num_scalar_prefetch=1,
            grid=(ext // block,),
            in_specs=[
                edge(1),
                inner,
                edge(0),
                tile(PAIR),
                tile(PAIR),
            ]
            + [pl.BlockSpec(memory_space=pl.ANY)] * len(sources),
            out_specs=[
                inner,
                tile(width),
                tile(width),
                pl.BlockSpec((4, width, width), lambda i, *_: (0, 0, 0)),
            ],
            scratch_shapes=[pltpu.SemaphoreType.DMA((1,))],
        ),
        out_shape=[
            shape((rows, width), low),
            shape((ext, width), low),
            shape((ext, width), low),
            shape((4, width, width), low),
        ],
        compiler_params=params(),
        cost_estimate=cost(0.1),
        name="project",
    )(ids, mate, tokens, cross, cosine, sine, *sources)


def fill_bias(bounds_ref, bias_ref, blocks, span):
    for b in range(blocks):
        lo = bounds_ref[0:1, b * QUERY_BLOCK : (b + 1) * QUERY_BLOCK] - b * QUERY_BLOCK
        hi = bounds_ref[1:2, b * QUERY_BLOCK : (b + 1) * QUERY_BLOCK] - b * QUERY_BLOCK
        at = lax.broadcasted_iota(jnp.int32, (span, QUERY_BLOCK), 0)
        bias_ref[b] = jnp.where((at >= lo) & (at < hi), 0.0, masked_score)


def only(x, head):
    lane = lax.broadcasted_iota(jnp.int32, x.shape, 1)
    return jnp.where((lane >= HEAD) if head else (lane < HEAD), x, jnp.zeros_like(x))


def attend_kernel(chunk, bounds_ref, q_ref, k_ref, v_ref, *refs):
    o_ref, lse_ref, bias_ref, vt_ref, s_ref = refs[-5:]
    rows = q_ref.shape[0]
    block = QUERY_BLOCK
    blocks = rows // block
    span = k_ref.shape[0] - rows + block

    @pl.when(pl.program_id(0) == 0)
    def _():
        fill_bias(bounds_ref, bias_ref, blocks, span)

    vt_ref[...] = v_ref[...].T
    chunks = [(c, min(chunk, span - c)) for c in range(0, span, chunk)]
    steps = [(b, h) for b in range(blocks) for h in range(2)]
    fold = lambda x, by: by(x.reshape(x.shape[0] // 64, 64, block), axis=0)
    add = lambda old, new: new if old is None else old + new

    def begin(i):
        b, h = steps[i]
        return {"query": only(q_ref[b * block : (b + 1) * block, :], h), "top": None}

    def score(i, c, n, state):
        b, _ = steps[i]
        s = dot_nt(k_ref[b * block + c : b * block + c + n, :], state["query"])
        s = s + bias_ref[b, c : c + n, :]
        s_ref[i % 2, c : c + n, :] = s
        top = fold(s, jnp.max)
        state["top"] = top if state["top"] is None else jnp.maximum(state["top"], top)

    def weigh(i, c, n, state):
        b, h = steps[i]
        e = jnp.exp(s_ref[i % 2, c : c + n, :] - state["peak"])
        state["total"] = add(state.get("total"), fold(e, jnp.sum))
        lanes = slice(b * block + c, b * block + c + n)
        mixed = dot_nn(vt_ref[h * HEAD : (h + 1) * HEAD, lanes], e.astype(low))
        state["mixed"] = add(state.get("mixed"), mixed)

    state = begin(0)
    for c, n in chunks:
        score(0, c, n, state)
    out = []
    for i, (b, h) in enumerate(steps):
        state["peak"] = jnp.max(state["top"], axis=0, keepdims=True)
        following = begin(i + 1) if i + 1 < len(steps) else None
        for c, n in chunks:
            if following is not None:
                score(i + 1, c, n, following)
            weigh(i, c, n, state)
        total = jnp.sum(state["total"], axis=0, keepdims=True)
        out.append(state["mixed"] / total)
        at = slice(b * block, (b + 1) * block)
        lse_ref[0, h : h + 1, at] = state["peak"] + jnp.log(total)
        if h == 1:
            o_ref[at, :] = jnp.concatenate(out, axis=0).T.astype(low)
            out = []
        state = following


def attend(bounds, q, k, v, first, pairs, before=None, chunk=640):
    rows, width = q.shape
    ext = k.shape[0]
    blocks = rows // QUERY_BLOCK
    span = ext - rows + QUERY_BLOCK
    own = pl.BlockSpec((rows, PAIR), lambda p: (0, p + first))
    wide = pl.BlockSpec((ext, PAIR), lambda p: (0, p + first))
    before = () if before is None else tuple(before)
    return pl.pallas_call(
        functools.partial(attend_kernel, chunk),
        grid=(pairs,),
        in_specs=[pl.BlockSpec((2, rows), lambda p: (0, 0)), own, wide, wide]
        + [pl.BlockSpec(memory_space=pl.ANY)] * len(before),
        out_specs=[own, pl.BlockSpec((1, 2, rows), lambda p: (p + first, 0, 0))],
        out_shape=[shape((rows, width), low), shape((width // PAIR, 2, rows), full)],
        input_output_aliases={4 + i: i for i in range(len(before))},
        scratch_shapes=[
            pltpu.VMEM((blocks, span, QUERY_BLOCK), full),
            pltpu.VMEM((PAIR, ext), low),
            pltpu.VMEM((2, span, QUERY_BLOCK), full),
        ],
        compiler_params=params(),
        cost_estimate=cost(2 * pairs),
        name="attend",
    )(bounds, q, k, v, *before)


def attend_back_kernel(
    chunk,
    ids,
    bounds_ref,
    q_ref,
    k_ref,
    v_ref,
    o_ref,
    do_ref,
    lse_ref,
    *refs,
):
    cos_ref, sin_ref = refs[:2]
    dq_ref, own_ref, mate_ref, cross_ref = refs[-10:-6]
    bias_ref, kt_ref, dk_ref, dv_ref, p_ref, ds_ref = refs[-6:]
    rows = q_ref.shape[0]
    ext = k_ref.shape[0]
    block = QUERY_BLOCK
    blocks = rows // block
    reach = (ext - rows) // 2
    span = ext - rows + block

    @pl.when(pl.program_id(0) == 0)
    def _():
        fill_bias(bounds_ref, bias_ref, blocks, span)

    kt_ref[...] = k_ref[...].T
    dk_ref[...] = jnp.zeros_like(dk_ref)
    dv_ref[...] = jnp.zeros_like(dv_ref)
    chunks = [(c, min(chunk, span - c)) for c in range(0, span, chunk)]

    def begin(b):
        at = slice(b * block, (b + 1) * block)
        q = q_ref[at, :]
        do = do_ref[at, :]
        product = (do.astype(full) * o_ref[at, :].astype(full)).T
        heads = range(2)
        return {
            "query": [only(q, h) for h in heads],
            "grad": [only(do, h) for h in heads],
            "delta": [
                jnp.sum(product[h * HEAD : (h + 1) * HEAD], axis=0, keepdims=True) for h in heads
            ],
            "lse": [lse_ref[0, h : h + 1, at] for h in heads],
            "dq": [None, None],
        }

    def score(b, h, c, n, state):
        rows_of = slice(b * block + c, b * block + c + n)
        lanes = slice(h * block, (h + 1) * block)
        s = dot_nt(k_ref[rows_of, :], state["query"][h]) + bias_ref[b, c : c + n, :]
        p = jnp.exp(s - state["lse"][h])
        dp = dot_nt(v_ref[rows_of, :], state["grad"][h])
        p_ref[b % 2, c : c + n, lanes] = p.astype(low)
        ds_ref[b % 2, c : c + n, lanes] = (p * (dp - state["delta"][h])).astype(low)

    def spread(b, h, c, n, state):
        rows_of = slice(b * block + c, b * block + c + n)
        if h == 0:
            both = jnp.concatenate(state["grad"], axis=0)
            dv_ref[rows_of, :] += dot_nn(p_ref[b % 2, c : c + n, :], both)
        else:
            both = jnp.concatenate(state["query"], axis=0)
            dk_ref[rows_of, :] += dot_nn(ds_ref[b % 2, c : c + n, :], both)
        ds = ds_ref[b % 2, c : c + n, h * block : (h + 1) * block]
        t = dot_nn(kt_ref[h * HEAD : (h + 1) * HEAD, rows_of], ds)
        state["dq"][h] = t if state["dq"][h] is None else state["dq"][h] + t

    state = begin(0)
    for h in range(2):
        for c, n in chunks:
            score(0, h, c, n, state)
    for b in range(blocks):
        following = begin(b + 1) if b + 1 < blocks else None
        for h in range(2):
            for c, n in chunks:
                if following is not None:
                    score(b + 1, h, c, n, following)
                spread(b, h, c, n, state)
        at = slice(b * block, (b + 1) * block)
        turned = turn_back(jnp.concatenate(state["dq"], axis=0).T, cos_ref[at, :], sin_ref[at, :])
        dq_ref[at, :] = (turned * (1.0 / math.sqrt(HEAD))).astype(low)
        state = following
    first = ids[2] == 0
    for i, ref in enumerate((dk_ref, dv_ref)):
        prior = ref[:reach, :].astype(low)
        following = ref[reach + rows :, :].astype(low)
        own_ref[i] = ref[reach : reach + rows, :].astype(low)
        mate_ref[i] = jnp.where(first, following, prior)
        cross_ref[i] = jnp.where(first, prior, following)


def attend_back(ids, bounds, q, k, v, o, do, lse, cosine, sine, first, pairs, halo, before=None, chunk=256):
    rows, width = q.shape
    ext = k.shape[0]
    blocks = rows // QUERY_BLOCK
    reach = (ext - rows) // 2
    span = ext - rows + QUERY_BLOCK
    halo_first, halo_pairs = halo
    before = () if before is None else tuple(before)
    own = pl.BlockSpec((rows, PAIR), lambda p, ids: (0, p + first))
    wide = pl.BlockSpec((ext, PAIR), lambda p, ids: (0, p + first))
    edge = pl.BlockSpec((2, reach, PAIR), lambda p, ids: (0, 0, p + first - halo_first))
    return pl.pallas_call(
        functools.partial(attend_back_kernel, chunk),
        grid_spec=pltpu.PrefetchScalarGridSpec(
            num_scalar_prefetch=1,
            grid=(pairs,),
            in_specs=[
            pl.BlockSpec((2, rows), lambda p, ids: (0, 0)),
            own,
            wide,
            wide,
            own,
            own,
            pl.BlockSpec((1, 2, rows), lambda p, ids: (p + first, 0, 0)),
            pl.BlockSpec((rows, PAIR), lambda p, ids: (0, 0)),
            pl.BlockSpec((rows, PAIR), lambda p, ids: (0, 0)),
        ]
        + [pl.BlockSpec(memory_space=pl.ANY)] * len(before),
        out_specs=[
            own,
            pl.BlockSpec((2, rows, PAIR), lambda p, ids: (0, 0, p + first)),
            edge,
            edge,
        ],
        scratch_shapes=[
            pltpu.VMEM((blocks, span, QUERY_BLOCK), full),
            pltpu.VMEM((PAIR, ext), low),
            pltpu.VMEM((ext, PAIR), full),
            pltpu.VMEM((ext, PAIR), full),
            pltpu.VMEM((2, span, 2 * QUERY_BLOCK), low),
            pltpu.VMEM((2, span, 2 * QUERY_BLOCK), low),
        ],
        ),
        out_shape=[
            shape((rows, width), low),
            shape((2, rows, width), low),
            shape((2, reach, halo_pairs * PAIR), low),
            shape((2, reach, halo_pairs * PAIR), low),
        ],
        input_output_aliases={10 + i: i for i in range(len(before))},
        compiler_params=params(),
        cost_estimate=cost(9 * pairs),
        name="attend_back",
    )(ids, bounds, q, k, v, o, do, lse, cosine, sine, *before)


def mean(x):
    return jnp.mean(x, axis=-1, keepdims=True)


def norm(x):
    centred = x - mean(x)
    inverse = lax.rsqrt(mean(centred * centred) + epsilon)
    return centred * inverse, inverse


def norm_back(scaled, normed, inverse):
    return inverse * (scaled - mean(scaled) - normed * mean(scaled * normed))


def position(j, core):
    return jnp.where(core == 0, j, (j & 1) * 2 + (j >> 1))


def gather_vectors(ids, vec_ref, width):
    count = vec_ref.shape[0]
    if count == 1:
        return vec_ref[0].astype(full)[:8]
    size = width // (2 * count)
    row = lax.broadcasted_iota(jnp.int32, (PAIR, width), 0)
    column = lax.broadcasted_iota(jnp.int32, (PAIR, width), 1)
    half = lax.broadcasted_iota(jnp.int32, (16, PAIR), 0) // 8
    out = jnp.zeros((16, width), full)
    for at in range(count):
        found = vec_ref[at].astype(full)
        for i in range(2):
            f = 2 * (ids[1] ^ position(at, ids[2])) + (ids[2] ^ i)
            place = ((column - f * size == row) & (row < size)).astype(full).astype(low)
            out = out + dot_nn(jnp.where(half == i, found, 0.0).astype(low), place)
    return out[:8] + out[8:]


def middle_kernel(plan, sources, ids, at_ref, tok_ref, cot_ref, *refs):
    vec_ref, refs = refs[0], refs[1:]
    srcs = refs[:sources]
    (
        out_ref,
        dz1_ref,
        da_ref,
        hidden_ref,
        product_ref,
        dfeed_ref,
        dgate_ref,
        dlift_ref,
        dbranch_ref,
        gains_ref,
        parts_ref,
        out_w,
        gate_w,
        up_w,
        down_w,
        lift_factor,
        gate_factor,
        vectors,
        sems,
    ) = refs[sources:]
    step = pl.program_id(0)
    weights = (out_w, gate_w, up_w, down_w)

    @pl.when(step == 0)
    def _():
        for copy in plan(ids, srcs, weights, sems):
            copy.start()
        gains_ref[...] = jnp.zeros_like(gains_ref)

    def ready(*which):
        @pl.when(step == 0)
        def _():
            for i in which:
                pltpu.make_async_copy(weights[i], weights[i], sems.at[i]).wait()

    parts, _, width = gate_w.shape

    @pl.when(step == 0)
    def _():
        vectors[...] = gather_vectors(ids, vec_ref, width)

    gain1, bias1, gain2, bias2 = (vectors[i : i + 1] for i in range(4))
    ready(0)
    normed1, inverse1 = norm(tok_ref[...].astype(full) + dot_nn(at_ref[...], out_w[...]))
    hidden = normed1 * gain1 + bias1
    hidden_low = hidden.astype(low)
    hidden_ref[...] = hidden_low
    ready(1, 2)
    feed = None
    for part in range(parts):
        at = slice(part * width, (part + 1) * width)
        gate = dot_nn(hidden_low, gate_w[part])
        lift = dot_nn(hidden_low, up_w[part])
        sigma = jax.nn.sigmoid(gate)
        opened = gate * sigma
        product = (opened * lift).astype(low)
        product_ref[:, at] = product
        lift_factor[:, at] = opened
        gate_factor[:, at] = lift * sigma * (1.0 + gate * (1.0 - sigma))
        if part == 0:
            ready(3)
        term = dot_nn(product, down_w[at, :])
        feed = term if feed is None else feed + term
    normed2, inverse2 = norm(hidden + feed)
    out_ref[...] = (normed2 * gain2 + bias2).astype(low)
    cot = cot_ref[...].astype(full)
    gains_ref[2:3] += jnp.sum(cot * normed2, axis=0, keepdims=True)
    gains_ref[3:4] += jnp.sum(cot, axis=0, keepdims=True)
    grad = norm_back(cot * gain2, normed2, inverse2)
    dfeed = grad.astype(low)
    dfeed_ref[...] = dfeed
    for part in range(parts):
        at = slice(part * width, (part + 1) * width)
        dproduct = dot_nt(dfeed, down_w[at, :])
        dgate = (dproduct * gate_factor[:, at]).astype(low)
        dlift = (dproduct * lift_factor[:, at]).astype(low)
        dgate_ref[:, at] = dgate
        dlift_ref[:, at] = dlift
        grad = grad + dot_nt(dgate, gate_w[part]) + dot_nt(dlift, up_w[part])
    gains_ref[0:1] += jnp.sum(grad * normed1, axis=0, keepdims=True)
    gains_ref[1:2] += jnp.sum(grad, axis=0, keepdims=True)
    grad = norm_back(grad * gain1, normed1, inverse1)
    dz1_ref[...] = grad
    dbranch = grad.astype(low)
    dbranch_ref[...] = dbranch
    da_ref[...] = dot_nt(dbranch, out_w[...]).astype(low)

    @pl.when(step == pl.num_programs(0) - 1)
    def _():
        sums = gains_ref[...].astype(low)
        size = width // 8
        row = lax.broadcasted_iota(jnp.int32, (width, PAIR), 0)
        column = lax.broadcasted_iota(jnp.int32, (width, PAIR), 1)
        for f in range(8):
            place = ((row - f * size == column) & (column < size)).astype(full).astype(low)
            parts_ref[f] = dot_nn(sums, place)


def middle(plan, ids, attended, tokens, cot, vectors, sources, hidden):
    rows, width = tokens.shape
    block = TOKEN_BLOCK
    tile = lambda w: pl.BlockSpec((block, w), lambda i, *_: (i, 0))
    whole = pl.BlockSpec((8, width), lambda i, *_: (0, 0))
    return pl.pallas_call(
        functools.partial(middle_kernel, plan, len(sources)),
        grid_spec=pltpu.PrefetchScalarGridSpec(
            num_scalar_prefetch=1,
            grid=(rows // block,),
            in_specs=[
                tile(width),
                tile(width),
                tile(width),
            ]
            + [pl.BlockSpec(vectors.shape, lambda i, *_: (0, 0, 0))]
            + [pl.BlockSpec(memory_space=pl.ANY)] * len(sources),
            out_specs=[
                tile(width),
                tile(width),
                tile(width),
                tile(width),
                tile(hidden),
                tile(width),
                tile(hidden),
                tile(hidden),
                tile(width),
                whole,
                pl.BlockSpec((8, 8, PAIR), lambda i, *_: (0, 0, 0)),
            ],
            scratch_shapes=[
                pltpu.VMEM((width, width), low),
                pltpu.VMEM((hidden // width, width, width), low),
                pltpu.VMEM((hidden // width, width, width), low),
                pltpu.VMEM((hidden, width), low),
                pltpu.VMEM((block, hidden), full),
                pltpu.VMEM((block, hidden), full),
                pltpu.VMEM((8, width), full),
                pltpu.SemaphoreType.DMA((4,)),
            ],
        ),
        out_shape=[
            shape((rows, width), low),
            shape((rows, width), full),
            shape((rows, width), low),
            shape((rows, width), low),
            shape((rows, hidden), low),
            shape((rows, width), low),
            shape((rows, hidden), low),
            shape((rows, hidden), low),
            shape((rows, width), low),
            shape((8, width), full),
            shape((8, 8, PAIR), full),
        ],
        compiler_params=params(),
        cost_estimate=cost(53),
        name="middle",
    )(ids, attended, tokens, cot, vectors, *sources)


def weight_grad_kernel(a_ref, b_ref, o_ref):
    o_ref[...] = dot_tn(a_ref[...], b_ref[...]).astype(o_ref.dtype)


def weight_grad(a, b, tile_a=768, tile_b=768):
    rows, size_a = a.shape
    size_b = b.shape[1]
    return pl.pallas_call(
        weight_grad_kernel,
        grid=(size_a // tile_a, size_b // tile_b),
        in_specs=[
            pl.BlockSpec((rows, tile_a), lambda i, j: (0, i)),
            pl.BlockSpec((rows, tile_b), lambda i, j: (0, j)),
        ],
        out_specs=pl.BlockSpec((tile_a, tile_b), lambda i, j: (i, j)),
        out_shape=shape((size_a, size_b), low),
        compiler_params=params(),
        cost_estimate=cost(9),
        name="weight_grad",
    )(a, b)


def joint_kernel(halos, ids, dq_ref, own_ref, cos_ref, sin_ref, *refs):
    by_mate = (pl.program_id(0) < pl.num_programs(0) // 2) == (ids[2] == 1)
    cosine = cos_ref[...]
    sine = sin_ref[...]
    dj_ref = refs[-1]
    width = dq_ref.shape[1]
    start = 0
    for mate_ref, cross_ref in zip(refs[:halos], refs[halos : 2 * halos]):
        for at in range(0, mate_ref.shape[2], PAIR):
            near = [
                jnp.where(
                    by_mate, mate_ref[i, :, at : at + PAIR], cross_ref[i, :, at : at + PAIR]
                ).astype(full)
                for i in range(2)
            ]
            lanes = slice(start, start + PAIR)
            keys = turn_back(own_ref[0, :, lanes].astype(full) + near[0], cosine, sine)
            values = own_ref[1, :, lanes].astype(full) + near[1]
            for i, x in enumerate((dq_ref[:, lanes], keys, values)):
                dj_ref[:, i * width + start : i * width + start + PAIR] = x.astype(low)
            start += PAIR


def joint(ids, dq, own, edges, cosine, sine):
    rows, width = dq.shape
    mates, crosses = zip(*edges)
    block = TOKEN_BLOCK
    half = mates[0].shape[1] // block
    inner = pl.BlockSpec((block, PAIR), lambda i, ids: (i + half, 0))
    tile = lambda w: pl.BlockSpec((block, w), lambda i, ids: (i, 0))
    edge = lambda size, core: pl.BlockSpec(
        (2, block, size),
        lambda i, ids: (
            0,
            jnp.where(ids[2] == core, jnp.minimum(i, half - 1), jnp.maximum(i - half, 0)),
            0,
        ),
    )
    return pl.pallas_call(
        functools.partial(joint_kernel, len(edges)),
        grid_spec=pltpu.PrefetchScalarGridSpec(
            num_scalar_prefetch=1,
            grid=(rows // block,),
            in_specs=[
                tile(width),
                pl.BlockSpec((2, block, width), lambda i, ids: (0, i, 0)),
                inner,
                inner,
            ]
            + [edge(m.shape[2], 1) for m in mates]
            + [edge(m.shape[2], 0) for m in crosses],
            out_specs=tile(3 * width),
        ),
        out_shape=shape((rows, 3 * width), low),
        compiler_params=params(32),
        cost_estimate=cost(0.01),
        name="joint",
    )(ids, dq, own, cosine, sine, *mates, *crosses)


def input_grad_kernel(dj_ref, dz1_ref, weight_ref, out_ref):
    width = dz1_ref.shape[1]
    out = dz1_ref[...]
    for i in range(3):
        out = out + dot_nt(dj_ref[:, i * width : (i + 1) * width], weight_ref[i])
    out_ref[...] = out


def input_grad(djoint, dz1, weights):
    rows, width = dz1.shape
    block = 2 * TOKEN_BLOCK
    tile = lambda w: pl.BlockSpec((block, w), lambda i: (i, 0))
    return pl.pallas_call(
        input_grad_kernel,
        grid=(rows // block,),
        in_specs=[
            tile(3 * width),
            tile(width),
            pl.BlockSpec((3, width, width), lambda i: (0, 0, 0)),
        ],
        out_specs=tile(width),
        out_shape=shape((rows, width), full),
        compiler_params=params(32),
        cost_estimate=cost(24),
        name="input_grad",
    )(djoint, dz1, weights)


def whole_joint_plan(ids, srcs, weight, sem):
    width = weight.shape[1]
    return [
        pltpu.make_async_copy(srcs[0].at[:, i * width : (i + 1) * width], weight.at[i], sem)
        for i in range(3)
    ] + [pltpu.make_async_copy(srcs[1], weight.at[3], sem)]


def whole_middle_plan(ids, srcs, weights, sems):
    out_w, gate_w, up_w, down_w = weights
    parts, _, width = gate_w.shape
    columns = lambda src, dst, sem: [
        pltpu.make_async_copy(src.at[:, i * width : (i + 1) * width], dst.at[i], sem)
        for i in range(parts)
    ]
    return (
        [pltpu.make_async_copy(srcs[0].at[3], out_w, sems.at[0])]
        + columns(srcs[1], gate_w, sems.at[1])
        + columns(srcs[2], up_w, sems.at[2])
        + [pltpu.make_async_copy(srcs[3], down_w, sems.at[3])]
    )


def swap_with(value, place):
    pairs = []
    for r in range(4):
        for z in range(4):
            for c in range(2):
                to_r, to_z, to_c = place(r, z, c)
                pairs.append(((r * 4 + z) * 2 + c, (to_r * 4 + to_z) * 2 + to_c))
    return lax.ppermute(value, ("rep", "fsdp"), pairs)


def over_core(value):
    return swap_with(value, lambda r, z, c: (r, z, 1 - c))


def over_square_1(value):
    return swap_with(value, lambda r, z, c: (r ^ (1 + c), z, c))


def over_square_2(value):
    return swap_with(value, lambda r, z, c: (r ^ (2 - c), z, c))


def over_z_1(value):
    return swap_with(value, lambda r, z, c: (r, z ^ (2 - c), c))


def over_z_2(value):
    return swap_with(value, lambda r, z, c: (r, z ^ (1 + c), c))


def pieces(ids, srcs):
    r, z, c = ids[0], ids[1], ids[2]
    found = []
    for i in range(2):
        core = (1 - c) if i else c
        bit1, bit2 = 1 + core, 2 - core
        for quarter in range(4):
            found.append((srcs[i][0].at[quarter], quarter, z, core))
        for ref, quarter in zip(srcs[i][1:], (r, r ^ bit1, r ^ bit2, r ^ 3)):
            for k in range(1, 4):
                found.append((ref.at[k - 1], quarter, z ^ position(k, core), core))
    return found


def piece_joint_plan(ids, srcs, weight, sem):
    size = srcs[0].shape[1]
    copies = []
    found = [
        [srcs[i]] + [srcs[k].at[j] for k in (2 + i, 4 + i) for j in range(2)] for i in range(2)
    ]
    for ref, quarter, z, core in pieces(ids, found):
        at = pl.multiple_of((2 * z + core) * size, size)
        copies.append(pltpu.make_async_copy(ref, weight.at[quarter, pl.ds(at, size)], sem))
    return copies


def piece_middle_plan(ids, srcs, weights, sems):
    out_w, gate_w, up_w, down_w = weights
    size = srcs[1].shape[1] // 3
    copies = [pltpu.make_async_copy(srcs[0].at[3], out_w, sems.at[0])]
    found = pieces(ids, [srcs[1::2], srcs[2::2]])
    for i, target in enumerate((gate_w, up_w)):
        for ref, quarter, z, core in found:
            at = pl.multiple_of((2 * z + core) * size, size)
            copies.append(
                pltpu.make_async_copy(
                    ref.at[i * size : (i + 1) * size],
                    target.at[quarter, pl.ds(at, size)],
                    sems.at[1 + i],
                )
            )
    for ref, quarter, z, core in found:
        at = pl.multiple_of(((2 * z + core) * 4 + quarter) * size, size)
        copies.append(
            pltpu.make_async_copy(
                ref.at[2 * size : 3 * size], down_w.at[pl.ds(at, size)], sems.at[3]
            )
        )
    return copies


def put_pieces(ids, block_ref, own_ref, other_ref, first, size):
    z, c = ids[1], ids[2]
    for ref, core in ((own_ref, c), (other_ref, 1 - c)):
        for k in range(4):
            at = pl.multiple_of((2 * (z ^ position(k, core)) + core) * size, 8)
            ref[0, k, first : first + size, :] = block_ref[pl.ds(at, size), :].astype(low)


def gate_up_grad_kernel(
        ids,
    hidden_ref,
    dgate_ref,
    dlift_ref,
    at_ref,
    db_ref,
    gains_ref,
    own_ref,
    other_ref,
    block_ref,
    second_ref,
    out_ref,
):
    size = block_ref.shape[0] // 8
    slim = size // 4
    z, c = ids[1], ids[2]
    quarter = ids[0] ^ pl.program_id(0)

    @pl.when(pl.program_id(0) == 0)
    def _():
        out_ref[...] = dot_tn(at_ref[...], db_ref[...])

    block_ref[...] = dot_tn(hidden_ref[...], dgate_ref[...])
    second_ref[...] = dot_tn(hidden_ref[...], dlift_ref[...])
    put_pieces(ids, block_ref, own_ref, other_ref, 0, size)
    put_pieces(ids, second_ref, own_ref, other_ref, size, size)
    for ref, core in ((own_ref, c), (other_ref, 1 - c)):
        for k in range(4):
            f = 2 * (z ^ position(k, core)) + core
            at = pl.multiple_of(f * size + quarter * slim, 8)
            sums = gains_ref[f]
            chosen = lax.broadcasted_iota(jnp.int32, sums.shape, 0) == quarter
            sums = jnp.sum(jnp.where(chosen, sums, 0.0), axis=0, keepdims=True)
            sums = jnp.pad(sums, ((0, 7), (0, ref.shape[3] - PAIR)))
            rest = jnp.concatenate([out_ref[pl.ds(at, slim), :], sums])
            ref[0, k, 2 * size :, :] = rest.astype(low)


def grad_specs(size, width):
    own = pl.BlockSpec((1, 4, size, width), lambda j, ids: (position(j, ids[2]), 0, 0, 0))
    other = pl.BlockSpec((1, 4, size, width), lambda j, ids: (position(j, 1 - ids[2]), 0, 0, 0))
    return [own, other], [shape((4, 4, size, width), low)] * 2


def gate_up_grad(ids, hidden_low, dgate, dlift, attended, dbranch, gains):
    rows, width = hidden_low.shape
    size = width // 8
    out_specs, out_shape = grad_specs(2 * size + size // 4 + 8, width)
    column = pl.BlockSpec((rows, width), lambda j, ids: (0, ids[0] ^ j))
    whole = pl.BlockSpec((rows, width), lambda j, ids: (0, 0))
    return pl.pallas_call(
        gate_up_grad_kernel,
        grid_spec=pltpu.PrefetchScalarGridSpec(
            num_scalar_prefetch=1,
            grid=(4,),
            in_specs=[
                whole,
                column,
                column,
                whole,
                whole,
                pl.BlockSpec(gains.shape, lambda j, ids: (0, 0, 0)),
            ],
            out_specs=out_specs,
            scratch_shapes=[pltpu.VMEM((width, width), full)] * 3,
        ),
        out_shape=out_shape,
        compiler_params=params(),
        cost_estimate=cost(18),
        name="gate_up_grad",
    )(ids, hidden_low, dgate, dlift, attended, dbranch, gains)


def down_grad_kernel(ids, product_ref, dfeed_ref, own_ref, other_ref, block_ref):
    size = own_ref.shape[2]
    r, z, c = ids[0], ids[1], ids[2]
    step = pl.program_id(0)
    block_ref[...] = dot_tn(product_ref[...], dfeed_ref[...])
    for ref, core in ((own_ref, c), (other_ref, 1 - c)):
        for j in range(4):
            at = pl.multiple_of((core * 4 + (r ^ position(j, core))) * size, 8)
            ref[j, 0] = block_ref[pl.ds(at, size), :].astype(low)


def down_grad(ids, product, dfeed):
    rows, hidden = product.shape
    width = dfeed.shape[1]
    size = hidden // 32
    out = lambda core: pl.BlockSpec(
        (4, 1, size, width),
        lambda j, ids: (0, position(ids[1] ^ j, (1 - ids[2]) if core else ids[2]), 0, 0),
    )
    return pl.pallas_call(
        down_grad_kernel,
        grid_spec=pltpu.PrefetchScalarGridSpec(
            num_scalar_prefetch=1,
            grid=(4,),
            in_specs=[
                pl.BlockSpec((rows, hidden // 4), lambda j, ids: (0, j)),
                pl.BlockSpec((rows, width), lambda j, ids: (0, 0)),
            ],
            out_specs=[out(0), out(1)],
            scratch_shapes=[pltpu.VMEM((hidden // 4, width), full)],
        ),
        out_shape=[shape((4, 4, size, width), low)] * 2,
        compiler_params=params(),
        cost_estimate=cost(10),
        name="down_grad",
    )(ids, product, dfeed)


def half(r, core):
    return jnp.where(core == 0, r >> 1, r & 1)


def joint_grad_kernel(ids, tok_ref, dj_ref, *refs):
    own_refs, other_refs, block_ref = refs[:2], refs[2:5], refs[5]
    r, z, c = ids[0], ids[1], ids[2]
    size = block_ref.shape[0] // 8
    block_ref[...] = dot_tn(tok_ref[...], dj_ref[...])

    def put(targets, core):
        for k, (ref, at) in enumerate(targets):
            first = pl.multiple_of((2 * (z ^ position(k, core)) + core) * size, 8)
            ref[at] = block_ref[pl.ds(first, size), :].astype(low)

    def whole(ref):
        return [(ref, k) for k in range(4)]

    sent = [(other_refs[1 + k // 2], k % 2) for k in range(4)]
    for kept_to, sent_to, core in (
        (whole(own_refs[0]), whole(own_refs[1]), c),
        (whole(other_refs[0]), sent, 1 - c),
    ):
        kept = pl.program_id(0) == half(r, core)
        pl.when(kept)(functools.partial(put, kept_to, core))
        pl.when(jnp.logical_not(kept))(functools.partial(put, sent_to, core))


def joint_grad(ids, tokens, djoint):
    rows, width = tokens.shape
    part = djoint.shape[1] // 2
    size = width // 8
    out = lambda n: pl.BlockSpec((n, size, part), lambda j, ids: (0, 0, 0))
    counts = (4, 4, 4, 2, 2)
    return pl.pallas_call(
        joint_grad_kernel,
        grid_spec=pltpu.PrefetchScalarGridSpec(
            num_scalar_prefetch=1,
            grid=(2,),
            in_specs=[
                pl.BlockSpec((rows, width), lambda j, ids: (0, 0)),
                pl.BlockSpec((rows, part), lambda j, ids: (0, j)),
            ],
            out_specs=[out(n) for n in counts],
            scratch_shapes=[pltpu.VMEM((width, part), full)],
        ),
        out_shape=[shape((n, size, part), low) for n in counts],
        compiler_params=params(32),
        cost_estimate=cost(0.01),
        name="joint_grad",
    )(ids, tokens, djoint)


def wide(v):
    return v.astype(full)


def sum_core(own, mate):
    return (wide(own[2:]) + wide(mate[2:])).astype(low)


def sum_square(own, mate, b):
    return (wide(own[1]) + wide(mate[1]) + wide(b[1])).astype(low)


def sum_rest(own, mate, b, d):
    return wide(own[0]) + wide(mate[0]) + wide(b[0]) + wide(d)


def sum_z(kept, e, f):
    return (kept[0] + wide(e[0]) + wide(f)).astype(low)


def place(ids, quarter):
    return position(quarter ^ ids[0], ids[2])


def finish_kernel(ids, near_ref, far_ref, gate_ref, up_ref, down_ref, out_ref, vec_ref):
    size, width = gate_ref.shape
    slim = out_ref.shape[0]
    at = place(ids, pl.program_id(0))

    def put(ref):
        piece = ref[at & 1].astype(full)
        gate_ref[...] = piece[:size]
        up_ref[...] = piece[size : 2 * size]
        out_ref[...] = piece[2 * size : 2 * size + slim]
        vec_ref[0] = piece[2 * size + slim : 2 * size + slim + 8, :PAIR]
        down_ref[...] = piece[2 * size + slim + 8 :]

    pl.when(at < 2)(lambda: put(near_ref))
    pl.when(at >= 2)(lambda: put(far_ref))


def finish(ids, near, far, size):
    width = near.shape[2]
    whole = pl.BlockSpec(near.shape, lambda j, ids: (0, 0, 0))
    column = pl.BlockSpec((size, width), lambda j, ids: (0, j))
    gate, up, down, out, vectors = pl.pallas_call(
        finish_kernel,
        grid_spec=pltpu.PrefetchScalarGridSpec(
            num_scalar_prefetch=1,
            grid=(4,),
            in_specs=[whole, whole],
            out_specs=[
                column,
                column,
                pl.BlockSpec((size, width), lambda j, ids: (j, 0)),
                pl.BlockSpec((size // 4, width), lambda j, ids: (j, 0)),
                pl.BlockSpec((1, 8, PAIR), lambda j, ids: (j, 0, 0)),
            ],
        ),
        out_shape=[shape((size, 4 * width), full)] * 2
        + [
            shape((4 * size, width), full),
            shape((size, width), full),
            shape((4, 8, PAIR), full),
        ],
        compiler_params=params(24),
        cost_estimate=cost(5),
        name="finish",
    )(ids, near, far)
    return gate, up, down, out, vectors[:, 0, :size]


def shards(
    custom,
    tokens,
    lengths,
    qkv_weight,
    out_weight,
    gate_weight,
    up_weight,
    down_weight,
    norm1_gain,
    norm1_bias,
    norm2_gain,
    norm2_bias,
    cotangent,
):
    rows, width = tokens.shape
    hidden = gate_weight.shape[1]
    size = lax.axis_size("fsdp")
    me = lax.axis_index("fsdp")
    r = lax.axis_index("rep")
    z, c = me // 2, me % 2
    ids = jnp.stack([r, z, c]).astype(jnp.int32)
    vectors = jnp.stack([norm1_gain, norm1_bias, norm2_gain, norm2_bias]).astype(low)

    mates = [(i, i ^ 1) for i in range(size)]
    crossed = [(i, i + 1 if i % 2 else i - 1) for i in range(1, size - 1)]
    swap_edges = lambda to_mate, to_cross: (
        lax.ppermute(to_mate, "fsdp", mates),
        lax.ppermute(to_cross, "fsdp", crossed),
    )
    edges = (tokens[rows - REACH :], tokens[:REACH])
    edges = (jnp.where(c == 0, *edges), jnp.where(c == 0, *edges[::-1]))
    if custom:
        part = qkv_weight.shape[0]
        columns = lambda w: jnp.swapaxes(w.astype(low).reshape(part, -1, width), 0, 1)
        column = lambda w, i: lax.dynamic_slice_in_dim(w, i * width, width, 1).astype(low)
        mine = jnp.where(
            r == 3, out_weight.astype(low), column(qkv_weight, jnp.minimum(r, 2))
        )
        first = over_z_2(mine)
        second = over_z_1(mine)
        third = over_z_1(first)
        rows_of = jnp.pad(vectors, ((0, 4), (0, width - part)))
        mine_2 = jnp.concatenate(
            [
                column(gate_weight, r),
                column(up_weight, r),
                lax.dynamic_slice_in_dim(down_weight, r * part, part, 0).astype(low),
                rows_of,
                over_core(rows_of),
            ]
        )
        shard_1 = jnp.concatenate([columns(qkv_weight), out_weight.astype(low)[None]])
        shard_2 = jnp.concatenate(
            [
                columns(gate_weight),
                columns(up_weight),
                down_weight.astype(low).reshape(4, part, width),
            ],
            axis=1,
        )
        mate_shard_1 = over_core(shard_1)
        own_1 = jnp.stack([first, second, after(third, mine_2, mate_shard_1)])
        first_2 = over_z_2(after(mine_2, own_1))
        other_1 = over_square_1(own_1)
        edges = swap_edges(*after(edges, first))
        mate_shard_2 = over_core(after(shard_2, own_1))
        near_1 = jnp.stack([own_1, after(other_1, shard_2, *edges)])
        far_1 = over_square_2(near_1)
        mate_near_1 = over_core(near_1)
        joint_sources = [shard_1, mate_shard_1, near_1, mate_near_1, far_1]
        joint_plan = piece_joint_plan
    else:
        edges = swap_edges(*edges)
        gather = lambda w: lax.all_gather(w.astype(low), "fsdp", axis=0, tiled=True)
        joint_sources = [gather(qkv_weight), gather(out_weight)]
        joint_plan = whole_joint_plan
        middle_sources = [gather(w) for w in (gate_weight, up_weight, down_weight)]
        vectors = lax.all_gather(vectors, "fsdp", axis=1, tiled=True)
        found = jnp.pad(vectors, ((0, 12), (0, 0)))[None]
        middle_plan = whole_middle_plan

    doc_lengths = lengths[0]
    ends = jnp.cumsum(doc_lengths)
    index = me * rows - REACH + jnp.arange(rows + 2 * REACH, dtype=jnp.int32)
    if custom:
        index = after(index, near_1)
    passed = (index[:, None] >= ends[None, :]).astype(jnp.int32)
    starts = jnp.sum(passed * doc_lengths[None, :], axis=1)
    cosine, sine = tables(index - starts)
    if custom:
        pair_2 = jnp.stack([mine_2, after(first_2, cosine)])
        second_2 = over_z_1(pair_2)
        mate_far_1 = over_core(after(far_1, pair_2))
        joint_sources.append(mate_far_1)
    own_starts = starts[REACH : REACH + rows]
    own_index = index[REACH : REACH + rows]
    stops = jnp.min(
        jnp.where(ends[None, :] > own_index[:, None], ends[None, :], size * rows), axis=1
    )
    base = me * rows - REACH
    bounds = jnp.stack(
        [
            jnp.maximum(own_starts, own_index - REACH) - base,
            jnp.minimum(stops, own_index + REACH + 1) - base,
        ]
    ).astype(jnp.int32)

    queries, keys, values, joint_weights = project(
        joint_plan, ids, edges, tokens, cosine, sine, joint_sources
    )
    given = (queries, keys, values)
    if custom:
        second_2 = after(second_2, queries)
        own_2 = jnp.concatenate([first_2[None, : 3 * part], second_2[:, : 3 * part]])
        found = jnp.concatenate([pair_2[:, 3 * part :, :PAIR], second_2[:, 3 * part :, :PAIR]])
        other_2 = over_square_1(own_2)
        done = attend(after(bounds, own_2, mate_shard_2), *given, 0, 2)
        tables_own = after((cosine, sine), done[1])
        tables_own = tuple(t[REACH : REACH + rows] for t in tables_own)
        other_2 = after(other_2, done[1], *tables_own)
        far_2 = over_square_2(after(own_2, other_2))
        across_2 = over_square_2(other_2)
        mate_own_2 = over_core(own_2)
        mate_other_2 = over_core(other_2)
        done = attend(after(bounds, other_2), *given, 2, 2, done)
        far_2 = after(far_2, done[1], mate_other_2, mate_own_2)
        mate_far_2 = over_core(far_2)
        attended, lse = attend(after(bounds, far_2), *given, 4, 2, done)
        across_2 = after(across_2, lse, mate_far_2)
        mate_across_2 = over_core(across_2)
        middle_sources = [shard_2, mate_shard_2, own_2, mate_own_2, other_2, mate_other_2]
        middle_sources += [far_2, mate_far_2, across_2, mate_across_2]
        middle_plan = piece_middle_plan
    else:
        done = None
        for first in (0, 2, 4):
            done = attend(bounds, *given, first, 2, done)
        attended, lse = done
        tables_own = tuple(t[REACH : REACH + rows] for t in (cosine, sine))
    result, dz1, dattended, hidden_low, product, dfeed, dgate, dlift, dbranch, *gains = middle(
        middle_plan,
        ids,
        attended,
        tokens,
        cotangent,
        found,
        [joint_weights, *middle_sources],
        hidden,
    )
    given = (queries, keys, values, attended, dattended, lse)
    given += tables_own
    spread = lambda g: lax.psum_scatter(g, "fsdp", scatter_dimension=0, tiled=True)
    if custom:
        own, other = gate_up_grad(ids, hidden_low, dgate, dlift, attended, dbranch, gains[1])
        mate = over_core(other)
        own_d, other_d = down_grad(ids, after(product, own), dfeed)
        sent = sum_core(own, after(mate, own_d))
        b = over_square_2(sent)
        mate_d = over_core(other_d)
        sent = sum_core(own_d, after(mate_d, sent))
        b_d = over_square_2(sent)
        dq, dkv, to_mate, to_cross = attend_back(ids, after(bounds, sent), *given, 0, 5, (0, 5))
        edges = [swap_edges(to_mate, to_cross)]
        sent_d = sum_square(own_d, mate_d, after(b_d, dq))
        d_d = over_square_1(sent_d)
        sent = sum_square(own, mate, after(b, sent_d))
        d = over_square_1(sent)
        dq, dkv, to_mate, to_cross = attend_back(
            ids, after(bounds, sent), *given, 5, 1, (5, 1), (dq, dkv)
        )
        edges_2 = [swap_edges(to_mate, to_cross)]
        kept = sum_rest(own_d, mate_d, b_d, after(d_d, dq, *edges[0]))
        kept = jnp.concatenate(
            [sum_rest(own, mate, b, after(d, kept, *edges_2[0])), kept], axis=1
        )
        sent = kept[2:].astype(low)
        e = over_z_1(sent)
        djoint = joint(ids, after(dq, sent), dkv, edges + edges_2, cosine, sine)
        own_k, own_s, other_k, *other_s = joint_grad(ids, tokens, djoint)
        mate_s = jnp.concatenate([over_core(v) for v in other_s])
        sent = (wide(own_s) + wide(mate_s)).astype(low)
        b_1 = over_square_2(sent)
        e = after(e, sent)
        mate_k = over_core(after(other_k, e))
        sent = (kept[1] + wide(e[1])).astype(low)
        f = over_z_2(sent)
        grad_tokens = input_grad(after(djoint, sent), dz1, joint_weights)
        kept_1 = wide(own_k) + wide(mate_k) + wide(after(b_1, grad_tokens))
        sent = kept_1[2:].astype(low)
        e_1 = over_z_1(sent)
        mine = sum_z(kept, e, after(f, sent))
        got = over_square_1(mine)
        near = jnp.stack([mine, after(got, sent)])
        far = over_square_2(near)
        f_1 = over_z_2((kept_1[1] + wide(after(e_1, near)[1])).astype(low))
        mine = sum_z(kept_1, e_1, f_1)
        got = over_square_1(mine)
        gate_sum, up_sum, down_sum, out_sum, vector_sum = finish(
            ids, near, after(far, mine), part
        )
        mine = (wide(mine) + wide(after(got, gate_sum))).astype(low)
        halves = (mine, over_square_2(mine))
        joint_sum = wide(
            jnp.where(
                half(r, c) == 0,
                jnp.concatenate(halves, axis=1),
                jnp.concatenate(halves[::-1], axis=1),
            )
        )
        summed = (joint_sum, out_sum, gate_sum, up_sum, down_sum, vector_sum)
    else:
        share_down = spread(weight_grad(product, dfeed))
        share_gate = spread(weight_grad(hidden_low, dgate))
        share_up = spread(weight_grad(hidden_low, dlift))
        share_out = spread(weight_grad(attended, dbranch))
        share_gains = lax.psum_scatter(gains[0][:4], "fsdp", scatter_dimension=1, tiled=True)
        dq, dkv, to_mate, to_cross = attend_back(ids, bounds, *given, 0, 4, (0, 4))
        edges_1 = swap_edges(to_mate, to_cross)
        dq, dkv, to_mate, to_cross = attend_back(ids, bounds, *given, 4, 2, (4, 2), (dq, dkv))
        edges_2 = swap_edges(to_mate, to_cross)
        djoint = joint(ids, dq, dkv, [edges_1, edges_2], cosine, sine)
        share_qkv = spread(weight_grad(tokens, djoint))
        grad_tokens = input_grad(djoint, dz1, joint_weights)
        summed = lax.psum(
            tuple(
                s.astype(full)
                for s in (share_qkv, share_out, share_gate, share_up, share_down, share_gains)
            ),
            "rep",
        )
    return (result, grad_tokens, *summed[:5], *(summed[5][i] for i in range(4)))


def solution(mesh):
    rows = P(("rep", "fsdp"), None)
    matrix = P("fsdp", None)
    vector = P("fsdp")
    custom = (mesh.shape["rep"], mesh.shape["fsdp"]) == (4, 8)
    return jax.shard_map(
        functools.partial(shards, custom and not FORCE_WHOLE),
        mesh=mesh,
        in_specs=(rows, P("rep", None)) + (matrix,) * 5 + (vector,) * 4 + (rows,),
        out_specs=(rows, rows) + (matrix,) * 5 + (vector,) * 4,
        check_vma=False,
    )
```
